32 devices in a mesh: seq: 4 (over x, core), batch: 8 (over z, y).
Axes of the slice: x: 2, y: 2, z: 4, core: 2. Of those that a mesh axis runs over, the one named last changes fastest.
Arguments:
- byte_ids: int32 [8, 1536], P('batch', 'seq'), may hold values from 0 to 255
- embedding: bfloat16 [256, 512], replicated, may hold values from -6 to 6
- norm_gains: float32 [2, 2, 512], replicated, may hold values from 0.5 to 1.5
- norm_biases: float32 [2, 2, 512], replicated, may hold values from -1.2 to 1.2
- qkv_weights: bfloat16 [2, 512, 1536], replicated, may hold values from -0.25 to 0.25
- qkv_biases: float32 [2, 1536], replicated, may hold values from -1.2 to 1.2
- out_weights: bfloat16 [2, 512, 512], replicated, may hold values from -2 to 2
- out_biases: float32 [2, 512], replicated, may hold values from -1.2 to 1.2
- expand_weights: bfloat16 [2, 512, 2048], replicated, may hold values from -0.25 to 0.25
- expand_biases: float32 [2, 2048], replicated, may hold values from -1.8 to 1.8
- reduce_weights: bfloat16 [2, 2048, 512], replicated, may hold values from -0.125 to 0.125
- reduce_biases: float32 [2, 512], replicated, may hold values from -1.2 to 1.2
- pool_weight: bfloat16 [1536, 512], replicated, may hold values from -0.15625 to 0.15625
- pool_bias: float32 [512], replicated, may hold values from -1.2 to 1.2
- upsample_weight: bfloat16 [512, 1536], replicated, may hold values from -0.25 to 0.25
- upsample_bias: float32 [1536], replicated, may hold values from -1.2 to 1.2
- cotangent: bfloat16 [8, 1536, 512], P('batch', 'seq'), may hold values from -6 to 6
Outputs:
- output: float32 [8, 1536, 512], P('batch', 'seq')
- embedding_grad: float32 [256, 512], P('batch')
- norm_gains_grad: float32 [2, 2, 512], P(None, None, 'batch')
- norm_biases_grad: float32 [2, 2, 512], P(None, None, 'batch')
- qkv_weights_grad: float32 [2, 512, 1536], P(None, 'batch')
- qkv_biases_grad: float32 [2, 1536], P(None, 'batch')
- out_weights_grad: float32 [2, 512, 512], P(None, 'batch')
- out_biases_grad: float32 [2, 512], P(None, 'batch')
- expand_weights_grad: float32 [2, 512, 2048], P(None, 'batch')
- expand_biases_grad: float32 [2, 2048], P(None, 'batch')
- reduce_weights_grad: float32 [2, 2048, 512], P(None, 'batch')
- reduce_biases_grad: float32 [2, 512], P(None, 'batch')
- pool_weight_grad: float32 [1536, 512], P('batch')
- pool_bias_grad: float32 [512], P('batch')
- upsample_weight_grad: float32 [512, 1536], P('batch')
- upsample_bias_grad: float32 [1536], P('batch')
The draws below stay inside these ranges and needn't reach their ends.
All inputs are finite; a program needn't handle non-finite values.
Results may differ from the reference program's by a relative error of at most 0.018.
Values may be sent and summed in bfloat16 or wider, within the bound.
No kernel may reach another device: no remote copies, remote signals or barrier semaphores. Data moves between devices by JAX's collectives and lax.ppermute only.
A program may use at most 192 MiB of HBM per device.

```python
import math
import jax
import jax.numpy as jnp
import numpy as np
from jax import lax

D = 512
H = 8
HD = 64
FF = 2048
VOCAB = 256
POOL = 3
SEQ_LEN = 1536
PLEN = 512
SEQUENCES = 8


def plant(array, rng, smallest, largest):
    spot = [jax.random.randint(jax.random.fold_in(rng, axis), (), 0, length) for axis, length in enumerate(array.shape)]
    longest = array.shape.index(max(array.shape))
    next_to = spot[:longest] + [(spot[longest] + 1) % array.shape[longest]] + spot[longest + 1:]
    return array.at[tuple(spot)].set(smallest).at[tuple(next_to)].set(largest)


def levels(own_key, extent, cuts, smallest, top_value):
    gain = 1.0
    for axis_at, blocks in cuts:
        heights = jax.random.uniform(jax.random.fold_in(jax.random.fold_in(own_key, 6), axis_at), (blocks,), jnp.float32, smallest / len(cuts), top_value / len(cuts))
        gain = gain * jnp.repeat(jnp.exp(heights), extent[axis_at] // blocks).reshape((-1,) + (1,) * (len(extent) - 1 - axis_at))
    return gain


def rank_table(amount, slope):
    portions = [(1 << 20) // math.isqrt(standing ** slope) + 1 for standing in range(1, amount + 1)]
    scale = 1 + sum(portions) // (1 << 30)
    return np.cumsum(np.array([max(1, weight // scale) for weight in portions]))


def ranked(stream_key, shape, number_of, slope):
    table = rank_table(number_of, slope)
    ticket = jax.random.randint(jax.random.fold_in(stream_key, 1), shape, 0, int(table[number_of - 1]))
    grade = jnp.searchsorted(jnp.asarray(table, jnp.int32), ticket, side="right")
    return jax.random.permutation(jax.random.fold_in(stream_key, 2), number_of)[grade].astype(jnp.int32)


def gaussian(stream_key, shape, deviation, reach, cuts=(), kind=jnp.bfloat16):
    values = jax.random.normal(stream_key, shape, jnp.float32) * deviation
    if len(cuts) > 0:
        values = levels(stream_key, shape, cuts, -0.22, 0.18) * values
    return jnp.clip(values, min=-reach, max=reach).astype(kind)


def setup_inputs(seed: int = 0) -> dict:
    streams_of = jax.random.split(jax.random.key(seed), 18)
    byte_ids = plant(ranked(streams_of[0], (SEQUENCES, SEQ_LEN), VOCAB, 2), jax.random.fold_in(streams_of[0], 3), 0, VOCAB - 1).astype(jnp.int32)
    embedding = gaussian(streams_of[1], (VOCAB, D), 1.0, 6.0)
    norm_gains = jnp.clip(1.0 + 0.1 * jax.random.normal(streams_of[2], (2, 2, D), jnp.float32), 0.5, 1.5)
    norm_biases = gaussian(streams_of[3], (2, 2, D), 0.2, 1.2, (), jnp.float32)
    qkv_weights = gaussian(streams_of[4], (2, D, 3 * D), D ** -0.5, 0.25)
    qkv_biases = gaussian(streams_of[5], (2, 3 * D), 0.2, 1.2, (), jnp.float32)
    out_weights = gaussian(streams_of[6], (2, D, D), 8 ** -0.5, 2.0)
    out_biases = gaussian(streams_of[7], (2, D), 0.2, 1.2, (), jnp.float32)
    expand_weights = gaussian(streams_of[8], (2, D, FF), D ** -0.5, 0.25)
    expand_biases = gaussian(streams_of[9], (2, FF), 0.3, 1.8, (), jnp.float32)
    reduce_weights = gaussian(streams_of[10], (2, FF, D), FF ** -0.5, 0.125)
    reduce_biases = gaussian(streams_of[11], (2, D), 0.2, 1.2, (), jnp.float32)
    pool_weight = gaussian(streams_of[12], (POOL * D, D), (POOL * D) ** -0.5, 0.15625)
    pool_bias = gaussian(streams_of[13], (D,), 0.2, 1.2, (), jnp.float32)
    upsample_weight = gaussian(streams_of[14], (D, POOL * D), D ** -0.5, 0.25)
    upsample_bias = gaussian(streams_of[15], (POOL * D,), 0.2, 1.2, (), jnp.float32)
    cotangent = gaussian(streams_of[16], (SEQUENCES, SEQ_LEN, D), 1.0, 6.0, ((0, 8), (1, 4)))
    return dict(byte_ids=byte_ids, embedding=embedding, norm_gains=norm_gains, norm_biases=norm_biases, qkv_weights=qkv_weights, qkv_biases=qkv_biases, out_weights=out_weights, out_biases=out_biases, expand_weights=expand_weights, expand_biases=expand_biases, reduce_weights=reduce_weights, reduce_biases=reduce_biases, pool_weight=pool_weight, pool_bias=pool_bias, upsample_weight=upsample_weight, upsample_bias=upsample_bias, cotangent=cotangent)


@jax.custom_vjp
def low(v):
    return lax.optimization_barrier(v.astype(jnp.bfloat16)).astype(jnp.float32)

@jax.custom_vjp
def low_back(v):
    return v

def low_keep(v):
    return (low(v), None)

def low_pass(kept, grad):
    return (grad,)

def back_keep(v):
    return (v, None)

def back_low(kept, grad):
    return (low(grad),)
low.defvjp(low_keep, low_pass)
low_back.defvjp(back_keep, back_low)

def product_hi(left, right):
    return jnp.dot(left, right, precision=lax.Precision.HIGHEST)

def layer_norm(stream, scale_gain, offset):
    centred = stream - lax.optimization_barrier(jnp.mean(stream, axis=-1, keepdims=True))
    spread = lax.optimization_barrier(jnp.mean(centred * centred, axis=-1, keepdims=True))
    return centred * lax.rsqrt(spread + 1e-05) * scale_gain + offset

def rotate_heads(stream, positions):
    row_count = stream.shape[0]
    half_width = HD // 2
    frequency = 10000.0 ** (-jnp.arange(half_width, dtype=jnp.float32) / half_width)
    angles = positions.astype(jnp.float32)[:, None] * frequency[None, :]
    cosine = jnp.cos(angles)[:, None, :]
    sine = 1.0 * jnp.sin(angles)[:, None, :]
    split_heads = stream.reshape(row_count, -1, HD)
    first_half = split_heads[..., :half_width]
    second_half = split_heads[..., half_width:]
    turned = jnp.concatenate([first_half * cosine - second_half * sine, first_half * sine + second_half * cosine], axis=-1)
    return turned.reshape(row_count, -1)

def one_head(pieces):
    queries, key_rows, values = pieces
    row_count = queries.shape[0]
    raw_scores = low_back(product_hi(queries, key_rows.T))
    allowed = jnp.arange(row_count)[:, None] >= jnp.arange(row_count)[None, :]
    scores = jnp.where(allowed, raw_scores * HD ** (-0.5), -1e+30)
    row_peak = lax.optimization_barrier(jnp.max(scores, axis=-1, keepdims=True))
    log_total = row_peak + jnp.log(lax.optimization_barrier(jnp.sum(jnp.exp(scores - row_peak), axis=-1, keepdims=True)))
    weights = low(jnp.exp(scores - log_total))
    return product_hi(weights, values)

def attend(queries, key_rows, values):
    row_count = queries.shape[0]

    def to_heads(member):
        return member.reshape(row_count, H, HD).transpose(1, 0, 2)
    mixed_rows = lax.map(jax.checkpoint(one_head), (to_heads(queries), to_heads(key_rows), to_heads(values)))
    return mixed_rows.transpose(1, 0, 2).reshape(row_count, H * HD)

def layer_apply(stream, params, layer_index, positions):
    gains, shifts, qkv_w, qkv_b, out_w, out_b, expand_w, expand_b, reduce_w, reduce_b = params
    normed = low(layer_norm(stream, gains[layer_index, 0], shifts[layer_index, 0]))
    qkv_rows = low_back(product_hi(normed, qkv_w[layer_index]) + qkv_b[layer_index])
    queries = low(rotate_heads(qkv_rows[:, :D], positions))
    key_rows = low(rotate_heads(qkv_rows[:, D:2 * D], positions))
    values = low(qkv_rows[:, 2 * D:])
    mixed_rows = low(low_back(attend(queries, key_rows, values)))
    middle = stream + low_back(product_hi(mixed_rows, out_w[layer_index]) + out_b[layer_index])
    second = low(layer_norm(middle, gains[layer_index, 1], shifts[layer_index, 1]))
    pre_act = low_back(product_hi(second, expand_w[layer_index]) + expand_b[layer_index])
    activated = low(jax.nn.gelu(pre_act))
    return middle + low_back(product_hi(activated, reduce_w[layer_index]) + reduce_b[layer_index])

def forward(params, tokens):
    table_rows, layer_params, pool_w, pool_b, upsample_w, upsample_b = params
    embedded = table_rows[tokens]
    full_rate = layer_apply(embedded, layer_params, 0, jnp.arange(SEQ_LEN))
    moved = jnp.concatenate([jnp.zeros((POOL - 1, D), jnp.float32), full_rate[:SEQ_LEN - POOL + 1]], axis=0)
    pooled = low(moved.reshape(PLEN, POOL * D))
    shortened = low_back(product_hi(pooled, pool_w) + pool_b)
    shortened = layer_apply(shortened, layer_params, 1, jnp.arange(PLEN))
    raised = low_back(product_hi(low(shortened), upsample_w) + upsample_b)
    return full_rate + raised.reshape(SEQ_LEN, D)

def reference(byte_ids, embedding, norm_gains, norm_biases, qkv_weights, qkv_biases, out_weights, out_biases, expand_weights, expand_biases, reduce_weights, reduce_biases, pool_weight, pool_bias, upsample_weight, upsample_bias, cotangent):
    params = jax.tree.map(lambda member: member.astype(jnp.float32), (embedding, (norm_gains, norm_biases, qkv_weights, qkv_biases, out_weights, out_biases, expand_weights, expand_biases, reduce_weights, reduce_biases), pool_weight, pool_bias, upsample_weight, upsample_bias))
    zero_grads = jax.tree.map(jnp.zeros_like, params)

    def per_sequence(running, pieces):
        tokens, seq_cot = pieces
        result, pullback = jax.vjp(lambda weights: forward(weights, tokens), params)
        gradients = pullback(seq_cot.astype(jnp.float32))[0]
        return (jax.tree.map(jnp.add, running, gradients), result)
    totals, outputs = lax.scan(per_sequence, zero_grads, (byte_ids, cotangent))
    table_grad, layer_grads, pool_w_grad, pool_b_grad, upsample_w_grad, upsample_b_grad = totals
    gains_grad, shifts_grad, qkv_w_grad, qkv_b_grad, out_w_grad, out_b_grad, expand_w_grad, expand_b_grad, reduce_w_grad, reduce_b_grad = layer_grads
    return (outputs, table_grad, gains_grad, shifts_grad, qkv_w_grad, qkv_b_grad, out_w_grad, out_b_grad, expand_w_grad, expand_b_grad, reduce_w_grad, reduce_b_grad, pool_w_grad, pool_b_grad, upsample_w_grad, upsample_b_grad)
```

```python
import functools

import jax
import jax.numpy as jnp
import numpy as np
from jax import lax
from jax.experimental import pallas as pl
from jax.experimental.pallas import tpu as pltpu
from jax.sharding import PartitionSpec as P

HD = 64
POOL = 3
QUAD = 4
LANES = 128
VMEM_LIMIT = 60 * 1024 * 1024
F32 = jnp.float32
BF16 = jnp.bfloat16


def dot(left, right):
    return jnp.dot(left, right, preferred_element_type=F32)


def dot_nt(left, right):
    return lax.dot_general(left, right, (((1,), (1,)), ((), ())), preferred_element_type=F32)


def dot_tn(left, right):
    return lax.dot_general(left, right, (((0,), (0,)), ((), ())), preferred_element_type=F32)


def gelu_parts(pre):
    slope = 0.7978845608028654
    square = pre * pre
    bent = jnp.tanh(slope * pre * (1.0 + 0.044715 * square))
    half = 0.5 * (1.0 + bent)
    value = pre * half
    rate = half + 0.5 * pre * (1.0 - bent * bent) * (slope * (1.0 + 3.0 * 0.044715 * square))
    return (value, rate)


def angle_rows(length):
    frequency = 10000.0 ** (-np.arange(HD // 2, dtype=np.float64) / (HD // 2))
    angles = np.arange(length, dtype=np.float64)[:, None] * frequency[None, :]
    return (np.cos(angles).astype(np.float32), np.sin(angles).astype(np.float32))


def cost(microseconds):
    microseconds *= 10
    return pl.CostEstimate(
        flops=int(microseconds * 1e9), bytes_accessed=int(microseconds * 1e6), transcendentals=0
    )


def grant(megabytes, factor=1):
    return min(int(megabytes * factor), 60) * 1024 * 1024


def copy_in(pairs, sems, start=0):
    moves = [
        pltpu.make_async_copy(src, dst, sems.at[start + i]) for i, (src, dst) in enumerate(pairs)
    ]
    for move in moves:
        move.start()
    return moves


def quad_rows(rows):
    lane = lax.broadcasted_iota(jnp.int32, rows.shape, 1) // HD
    zero = jnp.zeros_like(rows)
    return jnp.concatenate([jnp.where(lane == head, rows, zero) for head in range(QUAD)], axis=0)


def quad_fold(tall):
    count = tall.shape[0] // QUAD
    lane = lax.broadcasted_iota(jnp.int32, (count, tall.shape[1]), 1) // HD
    folded = jnp.zeros((count, tall.shape[1]), tall.dtype)
    for head in range(QUAD):
        folded = jnp.where(lane == head, tall[head * count : (head + 1) * count], folded)
    return folded


def causal(scores, key_start, query_start):
    count = scores.shape[1] // QUAD
    key = key_start + lax.broadcasted_iota(jnp.int32, scores.shape, 0)
    query = lax.broadcasted_iota(jnp.int32, (1, scores.shape[1]), 1)
    for head in range(1, QUAD):
        query = jnp.where(query >= count, query - count, query)
    return jnp.where(key <= query + query_start, scores, -1e30)


def flash_quad(tall_q, keys_at, values_at, full, key_start_last, query_start, state):
    acc, peak, total = state
    scores = causal(dot_nt(keys_at(full), tall_q), key_start_last, query_start)
    top = jnp.max(scores, axis=0, keepdims=True)
    raised = jnp.exp(scores - top)
    peak[...] = top
    total[...] = jnp.sum(raised, axis=0, keepdims=True)
    acc[...] = dot(values_at(full), raised.astype(BF16))

    def block(j, carry):
        scores = dot_nt(keys_at(j), tall_q)
        top = jnp.maximum(peak[...], jnp.max(scores, axis=0, keepdims=True))
        raised = jnp.exp(scores - top)
        shrink = jnp.exp(peak[...] - top)
        peak[...] = top
        total[...] = total[...] * shrink + jnp.sum(raised, axis=0, keepdims=True)
        acc[...] = acc[...] * shrink + dot(values_at(j), raised.astype(BF16))
        return carry

    lax.fori_loop(0, full, block, 0)
    return (quad_fold((acc[...] / total[...]).T), peak[...] + jnp.log(total[...]))


def every_third(split_ref, start, count):
    return jnp.concatenate(
        [split_ref[i, pl.ds(start, count, stride=POOL), :] for i in range(split_ref.shape[0])],
        axis=1,
    )


def unit_rows(stream):
    centred = stream - jnp.mean(stream, axis=-1, keepdims=True)
    inverse = lax.rsqrt(jnp.mean(centred * centred, axis=-1, keepdims=True) + 1e-05)
    return (centred * inverse, inverse)


def outer_forward_kernel(
    index_ref,
    ids_ref,
    emb_ref,
    gains_ref,
    shifts_ref,
    qkv_w_any,
    qkv_b_ref,
    out_w_any,
    out_b_ref,
    expand_w_any,
    expand_b_ref,
    reduce_w_any,
    reduce_b_ref,
    pool_w_any,
    cos_ref,
    sin_ref,
    h1_ref,
    low_ref,
    share_ref,
    q_ref,
    k_ref,
    kt_ref,
    v_ref,
    o_ref,
    lse_ref,
    middle_ref,
    active_ref,
    rate_ref,
    qkv_w,
    out_w,
    expand_w,
    reduce_w,
    pool_w,
    coarse_ref,
    fine_ref,
    vt_ref,
    acc_ref,
    peak_ref,
    total_ref,
    second_ref,
    sum_ref,
    later_ref,
    split_ref,
    sems,
):
    index = index_ref[0]
    rows, width = h1_ref.shape
    vocab = emb_ref.shape[0]
    chunk = rows // 2
    moves = copy_in(
        [
            (qkv_w_any.at[0], qkv_w),
            (out_w_any.at[0], out_w),
            (expand_w_any.at[0], expand_w),
            (reduce_w_any.at[0], reduce_w),
            (pool_w_any, pool_w),
        ],
        sems,
    )

    unit, _ = unit_rows(emb_ref[...].astype(F32))
    normed = (unit * gains_ref[0, 0:1] + shifts_ref[0, 0:1]).astype(BF16)
    moves[0].wait()
    table = (dot(normed, qkv_w[...]) + qkv_b_ref[0:1]).T
    coarse = table.astype(BF16)
    coarse_ref[...] = coarse
    fine_ref[...] = (table[: 2 * width] - coarse[: 2 * width].astype(F32)).astype(BF16)

    def picked(start, hot):
        return dot(coarse_ref[start : start + width], hot) + dot(
            fine_ref[start : start + width], hot
        )

    def turned(member, columns):
        cosine, sine = cos_ref[:, columns], sin_ref[:, columns]
        pieces = []
        for head in range(width // HD):
            first = member[head * HD : head * HD + HD // 2]
            second = member[head * HD + HD // 2 : (head + 1) * HD]
            pieces += [first * cosine - second * sine, first * sine + second * cosine]
        return jnp.concatenate(pieces, axis=0)

    codes = lax.broadcasted_iota(jnp.int32, (vocab, rows), 0)

    def hot_of(columns):
        return (codes == ids_ref[:, columns]).astype(F32).astype(BF16)

    def key_block(j, carry):
        columns = pl.ds(pl.multiple_of(j * rows, rows), rows)
        hot = hot_of(columns)
        keys = turned(picked(width, hot), columns)
        kt_ref[:, columns] = keys.astype(BF16)
        k_ref[columns, :] = keys.T.astype(BF16)
        values = dot(coarse_ref[2 * width : 3 * width], hot)
        vt_ref[:, columns] = values.astype(BF16)
        v_ref[columns, :] = values.T.astype(BF16)
        return carry

    lax.fori_loop(0, index + 1, key_block, 0)
    own = pl.ds(pl.multiple_of(index * rows, rows), rows)
    hot = hot_of(own)
    q_ref[...] = (turned(picked(0, hot), own) * HD**-0.5).T.astype(BF16)
    hot_rows = (codes == ids_ref[:, own]).astype(F32).T.astype(BF16)
    middle_ref[...] = dot(hot_rows, emb_ref[...])

    quads = width // (QUAD * HD)

    def part(it, carry):
        which, quad = it // quads, it % quads
        own_rows = pl.ds(pl.multiple_of(which * chunk, chunk), chunk)
        lanes = pl.ds(pl.multiple_of(quad * QUAD * HD, QUAD * HD), QUAD * HD)

        def keys_at(j):
            return k_ref[pl.ds(pl.multiple_of(j * rows, rows), rows), lanes]

        def values_at(j):
            return vt_ref[lanes, pl.ds(pl.multiple_of(j * rows, rows), rows)]

        mixed, lse = flash_quad(
            quad_rows(q_ref[own_rows, lanes]),
            keys_at,
            values_at,
            index,
            index * rows,
            index * rows + which * chunk,
            (acc_ref, peak_ref, total_ref),
        )
        o_ref[own_rows, lanes] = mixed.astype(BF16)
        lse_ref[pl.ds(it, 1), :] = lse
        return carry

    lax.fori_loop(0, 2 * quads, part, 0)

    moves[1].wait()
    middle = middle_ref[...] + dot(o_ref[...], out_w[...]) + out_b_ref[0:1]
    middle_ref[...] = middle
    unit, _ = unit_rows(middle)
    second_ref[...] = (unit * gains_ref[0, 1:2] + shifts_ref[0, 1:2]).astype(BF16)
    sum_ref[...] = middle + reduce_b_ref[0:1]
    moves[2].wait()
    moves[3].wait()

    def hidden(c, carry):
        columns = pl.ds(pl.multiple_of(c * width, width), width)
        pre = dot(second_ref[...], expand_w[:, columns]) + expand_b_ref[0:1, columns]
        value, rate = gelu_parts(pre)
        value = value.astype(BF16)
        active_ref[:, columns] = value
        rate_ref[:, columns] = rate.astype(BF16)
        sum_ref[...] += dot(value, reduce_w[columns, :])
        return carry

    lax.fori_loop(0, expand_w.shape[1] // width, hidden, 0)
    h1_ref[...] = sum_ref[...]
    low_ref[...] = sum_ref[...].astype(BF16)

    moves[4].wait()
    third = rows // POOL

    for lane in range(width // LANES):
        split_ref[lane] = sum_ref[:, lane * LANES : (lane + 1) * LANES]

    def thirds(start):
        return every_third(split_ref, start, third).astype(BF16)

    later_ref[0:8] = jnp.zeros((8, width), F32)
    later_ref[third : third + 8] = jnp.zeros((8, width), F32)
    later_ref[1 : third + 1] = dot(thirds(1), pool_w[0:width]) + dot(
        thirds(2), pool_w[width : 2 * width]
    )
    same = dot(thirds(0), pool_w[2 * width : 3 * width])
    share_ref[0:third] = (later_ref[0:third] + same).astype(BF16)
    share_ref[third : third + 8] = later_ref[third : third + 8].astype(BF16)


def outer_forward(index, all_ids, embedding, gains, shifts, qkv_w, qkv_b, out_w, out_b, expand_w,
                  expand_b, reduce_w, reduce_b, pool_w, rows):
    length = all_ids.shape[1]
    vocab, width = embedding.shape
    hidden = expand_w.shape[2]
    chunk, quads = rows // 2, width // (QUAD * HD)
    cosine, sine = angle_rows(length)
    vmem = pl.BlockSpec(memory_space=pltpu.VMEM)
    far = pl.BlockSpec(memory_space=pltpu.HBM)
    shape = jax.ShapeDtypeStruct
    third = rows // POOL
    return pl.pallas_call(
        outer_forward_kernel,
        name="outer_forward",
        in_specs=[pl.BlockSpec(memory_space=pltpu.SMEM), vmem, vmem, vmem, vmem, far, vmem,
                  far, vmem, far, vmem, far, vmem, far, vmem, vmem],
        out_specs=[vmem] * 12,
        out_shape=[
            shape((rows, width), F32),
            shape((rows, width), BF16),
            shape((third + 8, width), BF16),
            shape((rows, width), BF16),
            shape((length, width), BF16),
            shape((width, length), BF16),
            shape((length, width), BF16),
            shape((rows, width), BF16),
            shape((2 * quads, QUAD * chunk), F32),
            shape((rows, width), F32),
            shape((rows, hidden), BF16),
            shape((rows, hidden), BF16),
        ],
        scratch_shapes=[
            pltpu.VMEM((width, 3 * width), BF16),
            pltpu.VMEM((width, width), BF16),
            pltpu.VMEM((width, hidden), BF16),
            pltpu.VMEM((hidden, width), BF16),
            pltpu.VMEM((POOL * width, width), BF16),
            pltpu.VMEM((3 * width, vocab), BF16),
            pltpu.VMEM((2 * width, vocab), BF16),
            pltpu.VMEM((width, length), BF16),
            pltpu.VMEM((QUAD * HD, QUAD * chunk), F32),
            pltpu.VMEM((1, QUAD * chunk), F32),
            pltpu.VMEM((1, QUAD * chunk), F32),
            pltpu.VMEM((rows, width), BF16),
            pltpu.VMEM((rows, width), F32),
            pltpu.VMEM((third + 8, width), F32),
            pltpu.VMEM((width // LANES, rows, LANES), F32),
            pltpu.SemaphoreType.DMA((5,)),
        ],
        compiler_params=pltpu.CompilerParams(vmem_limit_bytes=grant(60, length // (4 * rows))),
        cost_estimate=cost(30),
    )(index, all_ids, embedding, gains, shifts, qkv_w, qkv_b, out_w, out_b, expand_w, expand_b,
      reduce_w, reduce_b, pool_w, jnp.asarray(cosine.T), jnp.asarray(sine.T))


def turn_rows(member, cosine, sine):
    pieces = []
    for start in range(0, member.shape[1], LANES):
        tile = member[:, start : start + LANES]
        lane = lax.broadcasted_iota(jnp.int32, tile.shape, 1) % HD
        other = jnp.where(
            lane < HD // 2,
            pltpu.roll(tile, LANES - HD // 2, 1),
            pltpu.roll(tile, HD // 2, 1),
        )
        pieces.append(tile * cosine + other * sine)
    return jnp.concatenate(pieces, axis=1)


def norm_back_rows(grad, unit, inverse, gain):
    scaled = grad * gain
    mean_one = jnp.mean(scaled, axis=-1, keepdims=True)
    mean_two = jnp.mean(scaled * unit, axis=-1, keepdims=True)
    return inverse * (scaled - mean_one - unit * mean_two)


def head_sums(product):
    tall = product.T
    return jnp.concatenate(
        [
            jnp.sum(tall[head * HD : (head + 1) * HD], axis=0, keepdims=True)
            for head in range(QUAD)
        ],
        axis=1,
    )


def back_block(scores, lse, delta, tall_q, tall_g, keys_t, values):
    probs = jnp.exp(scores - lse)
    low = (probs * (dot_nt(values, tall_g) - delta)).astype(BF16)
    return (dot(low, tall_q), dot(probs.astype(BF16), tall_g), dot(keys_t, low))


def share_columns(member_ref, index, parts):
    width = member_ref.shape[1] // parts
    if width % LANES == 0:
        return member_ref[:, pl.ds(pl.multiple_of(index * width, LANES), width)]
    full = member_ref.shape[1]
    row = lax.broadcasted_iota(jnp.int32, (full, width), 0)
    column = lax.broadcasted_iota(jnp.int32, (full, width), 1)
    picks = (row == column + index * width).astype(F32).astype(BF16)
    return dot(member_ref[...], picks).astype(BF16)


def can_pack(shapes, parts, blocks):
    return all(
        rows % (16 * blocks) == 0 and columns % (LANES * parts) == 0 for rows, columns in shapes
    )


def packed_rows(shapes, parts, blocks):
    return sum(rows // blocks * (columns // parts // LANES) for rows, columns in shapes)


def spot_of(block, own_block, blocks):
    distance = jnp.bitwise_xor(own_block, block)
    return distance % 2 * (blocks // 2) + distance // 2


def store_packed(out, start, member, own_block, blocks):
    rows, columns = member.shape[0] // blocks, member.shape[1]
    for block in range(blocks):
        spot = spot_of(block, own_block, blocks)
        for tile in range(columns // LANES):
            out[spot, start + tile * rows : start + (tile + 1) * rows, :] = member[
                block * rows : (block + 1) * rows, tile * LANES : (tile + 1) * LANES
            ]
    return start + rows * (columns // LANES)


def inner_kernel(
    parts,
    blocks,
    packed,
    query_rows,
    index_ref,
    *rest,
):
    shares, rest = rest[:parts], rest[parts:]
    (
    pool_b_ref,
    gains_ref,
    shifts_ref,
    qkv_w_any,
    qkv_b_ref,
    out_w_any,
    out_b_ref,
    expand_w_any,
    expand_b_ref,
    reduce_w_any,
    reduce_b_ref,
    raised_grad_ref,
    grad_ref,
    cos_ref,
    sin_ref,
    ) = rest[:15]
    rest = rest[15:]
    outs = 3 if packed else 5
    low_ref, gz_ref, vec_ref = rest[:3]
    mats = rest[3 : 3 + outs]
    (
        qkv_w,
        out_w,
        expand_w,
        reduce_w,
        stream_ref,
        normed_ref,
        q_ref,
        k_ref,
        kt_ref,
        v_ref,
        vt_ref,
        o_ref,
        lse_ref,
        middle_ref,
        second_ref,
        active_ref,
        rate_ref,
        sum_ref,
        pre_ref,
        att_ref,
        go_ref,
        gk_ref,
        gv_ref,
        acc_ref,
        peak_ref,
        total_ref,
        sems,
        *buffers,
    ) = rest[3 + outs :]
    index, own_block = index_ref[0], index_ref[1]
    rows, width = stream_ref.shape
    hidden_width = expand_w.shape[1]
    gq_ref, gqkv_ref = sum_ref, rate_ref.at[:, 0 : 3 * width]
    quads = width // (QUAD * HD)
    moves = copy_in(
        [
            (qkv_w_any.at[1], qkv_w),
            (out_w_any.at[1], out_w),
            (expand_w_any.at[1], expand_w),
            (reduce_w_any.at[1], reduce_w),
        ],
        sems,
    )
    share = rows // parts
    for distance in range(parts):
        start = pl.multiple_of(jnp.bitwise_xor(index, distance) * share, share)
        stream_ref[pl.ds(start, share)] = shares[distance][:share].astype(F32) + pool_b_ref[...]
    for distance in range(parts):
        part = jnp.bitwise_xor(index, distance)

        @pl.when(part < parts - 1)
        def _():
            head = pl.ds(pl.multiple_of((part + 1) * share, share), 8)
            stream_ref[head] += shares[distance][share : share + 8].astype(F32)

    unit, _ = unit_rows(stream_ref[...])
    normed_ref[...] = (unit * gains_ref[1, 0:1] + shifts_ref[1, 0:1]).astype(BF16)
    moves[0].wait()

    def projected(part):
        columns = slice(part * width, (part + 1) * width)
        return dot(normed_ref[...], qkv_w[:, columns]) + qkv_b_ref[1:2, columns]

    cosine, sine = cos_ref[...], sin_ref[...]
    q_ref[...] = (turn_rows(projected(0), cosine, sine) * HD**-0.5).astype(BF16)
    keys = turn_rows(projected(1), cosine, sine)
    k_ref[...] = keys.astype(BF16)
    kt_ref[...] = keys.T.astype(BF16)
    values = projected(2)
    v_ref[...] = values.astype(BF16)
    vt_ref[...] = values.T.astype(BF16)

    def block_of(j):
        return pl.ds(pl.multiple_of(j * query_rows, query_rows), query_rows)

    def lanes_of(quad):
        return pl.ds(pl.multiple_of(quad * QUAD * HD, QUAD * HD), QUAD * HD)

    def part(it, carry):
        which, quad = it // quads, it % quads
        own_rows, lanes = block_of(which), lanes_of(quad)
        mixed, lse = flash_quad(
            quad_rows(q_ref[own_rows, lanes]),
            lambda j: k_ref[block_of(j), lanes],
            lambda j: vt_ref[lanes, block_of(j)],
            which,
            which * query_rows,
            which * query_rows,
            (acc_ref, peak_ref, total_ref),
        )
        o_ref[own_rows, lanes] = mixed.astype(BF16)
        lse_ref[pl.ds(it, 1), :] = lse
        return carry

    lax.fori_loop(0, rows // query_rows * quads, part, 0)
    moves[1].wait()
    middle = stream_ref[...] + dot(o_ref[...], out_w[...]) + out_b_ref[1:2]
    middle_ref[...] = middle
    unit, _ = unit_rows(middle)
    second_ref[...] = (unit * gains_ref[1, 1:2] + shifts_ref[1, 1:2]).astype(BF16)
    sum_ref[...] = middle + reduce_b_ref[1:2]
    moves[2].wait()
    moves[3].wait()

    def columns_of(c):
        return pl.ds(pl.multiple_of(c * width, width), width)

    def hidden(c, carry):
        columns = columns_of(c)
        pre = dot(second_ref[...], expand_w[:, columns]) + expand_b_ref[1:2, columns]
        value, rate = gelu_parts(pre)
        value = value.astype(BF16)
        active_ref[:, columns] = value
        rate_ref[:, columns] = rate.astype(BF16)
        sum_ref[...] += dot(value, reduce_w[columns, :])
        return carry

    lax.fori_loop(0, hidden_width // width, hidden, 0)
    low_ref[...] = sum_ref[...].astype(BF16)

    vec_ref[...] = jnp.zeros(vec_ref.shape, F32)

    def column_sum(row, member):
        vec_ref[row : row + 1, 0 : member.shape[1]] = jnp.sum(member, axis=0, keepdims=True)

    grad_low = grad_ref[...].astype(BF16)
    column_sum(7, grad_low.astype(F32))
    att_ref[...] = grad_low
    sum_ref[...] = jnp.zeros(sum_ref.shape, F32)

    def hidden_back(c, carry):
        columns = columns_of(c)
        pre = dot_nt(att_ref[...], reduce_w[columns, :]) * rate_ref[:, columns].astype(F32)
        low = pre.astype(BF16)
        pre_ref[:, columns] = low
        vec_ref[6:7, columns] = jnp.sum(low.astype(F32), axis=0, keepdims=True)
        sum_ref[...] += dot_nt(low, expand_w[:, columns])
        return carry

    lax.fori_loop(0, hidden_width // width, hidden_back, 0)
    if packed:
        place = store_packed(
            buffers[0], 0, dot_tn(active_ref[...], share_columns(att_ref, index, parts)).astype(BF16), own_block, blocks
        )
        place = store_packed(
            buffers[0], place, dot_tn(second_ref[...], share_columns(pre_ref, index, parts)).astype(BF16), own_block, blocks
        )
        place = store_packed(
            buffers[0], place, dot_tn(low_ref[...], share_columns(raised_grad_ref, index, parts)).astype(BF16), own_block, blocks
        )
        sent = copy_in(halves_of(buffers[0], mats[0:2]), sems, 4)
    else:
        mats[0][...] = dot_tn(active_ref[...], share_columns(att_ref, index, parts)).astype(BF16)
        mats[1][...] = dot_tn(second_ref[...], share_columns(pre_ref, index, parts)).astype(BF16)
        mats[2][...] = dot_tn(low_ref[...], share_columns(raised_grad_ref, index, parts)).astype(BF16)

    unit, inverse = unit_rows(middle_ref[...])
    grad_second = sum_ref[...]
    column_sum(1, grad_second * unit)
    column_sum(3, grad_second)
    grad_middle = grad_ref[...] + norm_back_rows(grad_second, unit, inverse, gains_ref[1, 1:2])
    middle_ref[...] = grad_middle
    att_ref[...] = grad_middle.astype(BF16)
    column_sum(5, att_ref[...].astype(F32))
    go_ref[...] = dot_nt(att_ref[...], out_w[...]).astype(BF16)
    gk_ref[...] = jnp.zeros(gk_ref.shape, F32)
    gv_ref[...] = jnp.zeros(gv_ref.shape, F32)

    def part_back(it, carry):
        which, quad = it // quads, it % quads
        own_rows, lanes = block_of(which), lanes_of(quad)
        tall_q = quad_rows(q_ref[own_rows, lanes])
        tall_g = quad_rows(go_ref[own_rows, lanes])
        lse = lse_ref[pl.ds(it, 1), :]
        delta = head_sums(o_ref[own_rows, lanes].astype(F32) * go_ref[own_rows, lanes].astype(F32))

        def one(j, masked):
            keys = block_of(j)
            scores = dot_nt(k_ref[keys, lanes], tall_q)
            if masked:
                scores = causal(scores, j * query_rows, which * query_rows)
            add_k, add_v, add_q = back_block(
                scores, lse, delta, tall_q, tall_g, kt_ref[lanes, keys], v_ref[keys, lanes]
            )
            gk_ref[keys, lanes] += add_k
            gv_ref[keys, lanes] += add_v
            return add_q

        acc_ref[...] = one(which, True)

        def full(j, inner_carry):
            acc_ref[...] += one(j, False)
            return inner_carry

        lax.fori_loop(0, which, full, 0)
        gq_ref[own_rows, lanes] = quad_fold(acc_ref[...].T) * HD**-0.5
        return carry

    lax.fori_loop(0, rows // query_rows * quads, part_back, 0)
    sine = -sin_ref[...]
    gqkv_ref[:, 0:width] = turn_rows(gq_ref[...], cosine, sine).astype(BF16)
    gqkv_ref[:, width : 2 * width] = turn_rows(gk_ref[...], cosine, sine).astype(BF16)
    gqkv_ref[:, 2 * width : 3 * width] = gv_ref[...].astype(BF16)
    column_sum(4, gqkv_ref[...].astype(F32))
    if packed:
        place = store_packed(
            mats[2], 0, dot_tn(o_ref[...], share_columns(att_ref, index, parts)).astype(BF16), own_block, blocks
        )
        store_packed(
            mats[2], place, dot_tn(normed_ref[...], share_columns(gqkv_ref, index, parts)).astype(BF16), own_block, blocks
        )
    else:
        mats[3][...] = dot_tn(o_ref[...], share_columns(att_ref, index, parts)).astype(BF16)
        mats[4][...] = dot_tn(normed_ref[...], share_columns(gqkv_ref, index, parts)).astype(BF16)
    grad_normed = dot_nt(gqkv_ref[...], qkv_w[...])
    unit, inverse = unit_rows(stream_ref[...])
    column_sum(0, grad_normed * unit)
    column_sum(2, grad_normed)
    grad_in = middle_ref[...] + norm_back_rows(grad_normed, unit, inverse, gains_ref[1, 0:1])
    grad_in_low = grad_in.astype(BF16)
    gz_ref[0:rows] = grad_in_low
    gz_ref[rows : rows + 16] = jnp.zeros((16, width), BF16)
    column_sum(8, grad_in_low.astype(F32))

    if packed:
        for move in sent:
            move.wait()


def halves_of(buffer, outs):
    half = buffer.shape[0] // 2
    return [(buffer.at[0:half], outs[0]), (buffer.at[half : 2 * half], outs[1])]


def inner_shapes_of(width, hidden):
    return [
        (hidden, width),
        (width, hidden),
        (width, POOL * width),
        (width, width),
        (width, 3 * width),
    ]


def row_tables(length):
    cosine, sine = angle_rows(length)
    repeat = LANES // HD
    return (
        np.tile(np.concatenate([cosine, cosine], axis=1), (1, repeat)),
        np.tile(np.concatenate([-sine, sine], axis=1), (1, repeat)),
    )


def inner_layer(index, shares, pool_b, gains, shifts, qkv_w, qkv_b, out_w, out_b, expand_w, expand_b,
                reduce_w, reduce_b, raised_grad, grad, parts, blocks):
    rows, width = grad.shape
    hidden = expand_w.shape[2]
    quads = width // (QUAD * HD)
    query_rows = 256
    shapes = inner_shapes_of(width, hidden)
    packed = can_pack(shapes, parts, blocks)
    cosine, sine = row_tables(rows)
    vmem = pl.BlockSpec(memory_space=pltpu.VMEM)
    anywhere = pl.BlockSpec(memory_space=pl.ANY)
    far = pl.BlockSpec(memory_space=pltpu.HBM)
    shape = jax.ShapeDtypeStruct
    if packed:
        held = [packed_rows(group, parts, blocks) for group in (shapes[:3], shapes[3:])]
        mats = [
            shape((blocks // 2, held[0], LANES), BF16),
            shape((blocks // 2, held[0], LANES), BF16),
            shape((blocks, held[1], LANES), BF16),
        ]
        buffers = [pltpu.VMEM((blocks, held[0], LANES), BF16)]
        outs = [vmem] * 3 + [anywhere] * 2 + [vmem]
    else:
        mats = [shape((height, columns // parts), BF16) for height, columns in shapes]
        buffers = []
        outs = [vmem] * (3 + len(mats))
    found = pl.pallas_call(
        functools.partial(inner_kernel, parts, blocks, packed, query_rows),
        name="inner_layer",
        in_specs=[pl.BlockSpec(memory_space=pltpu.SMEM)] + [vmem] * parts + [vmem, vmem, vmem, far, vmem,
                  far, vmem, far, vmem, far, vmem, vmem, vmem, vmem, vmem],
        out_specs=outs,
        out_shape=[
            shape((rows, width), BF16),
            shape((rows + 16, width), BF16),
            shape((16, max(hidden, POOL * width)), F32),
        ] + mats,
        scratch_shapes=[
            pltpu.VMEM((width, 3 * width), BF16),
            pltpu.VMEM((width, width), BF16),
            pltpu.VMEM((width, hidden), BF16),
            pltpu.VMEM((hidden, width), BF16),
            pltpu.VMEM((rows, width), F32),
            pltpu.VMEM((rows, width), BF16),
            pltpu.VMEM((rows, width), BF16),
            pltpu.VMEM((rows, width), BF16),
            pltpu.VMEM((width, rows), BF16),
            pltpu.VMEM((rows, width), BF16),
            pltpu.VMEM((width, rows), BF16),
            pltpu.VMEM((rows, width), BF16),
            pltpu.VMEM((rows // query_rows * quads, QUAD * query_rows), F32),
            pltpu.VMEM((rows, width), F32),
            pltpu.VMEM((rows, width), BF16),
            pltpu.VMEM((rows, hidden), BF16),
            pltpu.VMEM((rows, hidden), BF16),
            pltpu.VMEM((rows, width), F32),
            pltpu.VMEM((rows, hidden), BF16),
            pltpu.VMEM((rows, width), BF16),
            pltpu.VMEM((rows, width), BF16),
            pltpu.VMEM((rows, width), F32),
            pltpu.VMEM((rows, width), F32),
            pltpu.VMEM((QUAD * HD, QUAD * query_rows), F32),
            pltpu.VMEM((1, QUAD * query_rows), F32),
            pltpu.VMEM((1, QUAD * query_rows), F32),
            pltpu.SemaphoreType.DMA((6,)),
        ]
        + buffers,
        compiler_params=pltpu.CompilerParams(vmem_limit_bytes=grant(44, rows // 512)),
        cost_estimate=cost(33),
    )(index, *shares, pool_b, gains, shifts, qkv_w, qkv_b, out_w, out_b, expand_w, expand_b, reduce_w,
      reduce_b, raised_grad, grad, jnp.asarray(cosine), jnp.asarray(sine))
    return found[0], found[1], found[2], found[3:], packed


def reversed_bits(value, size):
    found, bit = 0, 1
    while bit < size:
        found = found * 2 + (value // bit) % 2
        bit *= 2
    return found


def store_split(out, index, start, member, own_block, parts, blocks):
    columns = member.shape[1] // parts
    place = start
    for part in range(parts):
        spot = reversed_bits(jnp.bitwise_xor(index, part), parts)
        place = store_packed(
            out.at[spot],
            start,
            member[:, part * columns : (part + 1) * columns],
            own_block,
            blocks,
        )
    return place


def vector_tiles(entries, block, blocks):
    found = []
    for ref, row, length, scale in entries:
        size = length // blocks
        first, last = block * size // LANES, ((block + 1) * size - 1) // LANES
        found += [(ref, row, tile, scale) for tile in range(first, last + 1)]
    return found


def store_vectors(out, index, start, entries, own_block, parts, blocks):
    count = -(-len(vector_tiles(entries, 0, blocks)) // parts)
    for block in range(blocks):
        tiles = vector_tiles(entries, block, blocks)
        for part in range(parts):
            rows = [
                ref[row : row + 1, tile * LANES : (tile + 1) * LANES] * scale
                for ref, row, tile, scale in tiles[part * count : (part + 1) * count]
            ]
            rows += [jnp.zeros((16 - len(rows), LANES), F32)]
            spot = reversed_bits(jnp.bitwise_xor(index, part), parts)
            out[spot, spot_of(block, own_block, blocks), start : start + 16, :] = jnp.concatenate(
                rows, axis=0
            ).astype(BF16)


def split_lanes(split_ref, member):
    for lane in range(split_ref.shape[0]):
        split_ref[lane] = member[:, lane * LANES : (lane + 1) * LANES]


def joined_lanes(split_ref):
    return jnp.concatenate([split_ref[lane] for lane in range(split_ref.shape[0])], axis=1)


def add_third(split_ref, start, member):
    for lane in range(split_ref.shape[0]):
        rows = pl.ds(start, member.shape[0], stride=POOL)
        split_ref[lane, rows, :] = (
            split_ref[lane, rows, :] + member[:, lane * LANES : (lane + 1) * LANES]
        )


def raised_kernel(cot_ref, up_w_ref, joined_ref, grad_ref, sums_ref, split_ref):
    width = grad_ref.shape[1]
    split_lanes(split_ref, cot_ref[...].astype(F32))
    total = jnp.zeros(grad_ref.shape, F32)
    for slot in range(POOL):
        columns = slice(slot * width, (slot + 1) * width)
        rows = every_third(split_ref, slot, grad_ref.shape[0])
        sums_ref[:, columns] = jnp.sum(rows, axis=0, keepdims=True)
        rows = rows.astype(BF16)
        joined_ref[:, columns] = rows
        total += dot_nt(rows, up_w_ref[:, columns])
    grad_ref[...] = total


def raised_back(all_cot, up_w):
    length, width = all_cot.shape
    vmem = pl.BlockSpec(memory_space=pltpu.VMEM)
    shape = jax.ShapeDtypeStruct
    return pl.pallas_call(
        raised_kernel,
        name="raised_back",
        in_specs=[vmem] * 2,
        out_specs=[vmem] * 3,
        out_shape=[
            shape((length // POOL, POOL * width), BF16),
            shape((length // POOL, width), F32),
            shape((1, POOL * width), F32),
        ],
        scratch_shapes=[pltpu.VMEM((width // LANES, length, LANES), F32)],
        compiler_params=pltpu.CompilerParams(vmem_limit_bytes=grant(16, length // 1536)),
        cost_estimate=cost(4),
    )(all_cot, up_w)


def output_kernel(index_ref, h1_ref, low_ref, up_w_ref, up_b_ref, out_ref, split_ref):
    rows, width = h1_ref.shape
    third = rows // POOL
    own = low_ref[pl.ds(pl.multiple_of(index_ref[0] * third, third), third), :]
    split_lanes(split_ref, h1_ref[...])
    for slot in range(POOL):
        columns = slice(slot * width, (slot + 1) * width)
        add_third(split_ref, slot, dot(own, up_w_ref[:, columns]) + up_b_ref[:, columns])
    out_ref[0] = joined_lanes(split_ref)


def raised_output(index, h1, low, up_w, up_b):
    rows, width = h1.shape
    vmem = pl.BlockSpec(memory_space=pltpu.VMEM)
    return pl.pallas_call(
        output_kernel,
        name="raised_output",
        in_specs=[pl.BlockSpec(memory_space=pltpu.SMEM)] + [vmem] * 4,
        out_specs=vmem,
        out_shape=jax.ShapeDtypeStruct((1, rows, width), F32),
        scratch_shapes=[pltpu.VMEM((width // LANES, rows, LANES), F32)],
        compiler_params=pltpu.CompilerParams(vmem_limit_bytes=grant(10)),
        cost_estimate=cost(3),
    )(index, h1, low, up_w, up_b)


def outer_hidden_kernel(
    parts,
    blocks,
    packed,
    index_ref,
    *rest,
):
    lows, rest = rest[:parts], rest[parts:]
    (
    inner_two_any,
    gz_ref,
    inner_vec_ref,
    raised_vec_ref,
    cot_ref,
    middle_in_ref,
    active_ref,
    rate_ref,
    mixed_ref,
    gains_ref,
    shifts_ref,
    pool_w_any,
    reduce_w_any,
    expand_w_any,
    out_w_any,
    ) = rest[:15]
    rest = rest[15:]
    outs = 4
    middle_ref, att_ref, go_ref, vec_ref = rest[:4]
    mats = rest[4 : 4 + outs]
    (
        pool_w,
        reduce_w,
        expand_w,
        out_w,
        split_ref,
        grad_ref,
        low_ref,
        second_ref,
        pre_ref,
        sum_ref,
        pooled_ref,
        sems,
        *buffers,
    ) = rest[4 + outs :]
    index, own_block = index_ref[0], index_ref[1]
    rows, width = cot_ref.shape
    hidden_width = expand_w.shape[1]
    third = rows // POOL
    moves = copy_in(
        [
            (pool_w_any, pool_w),
            (reduce_w_any.at[0], reduce_w),
            (expand_w_any.at[0], expand_w),
            (out_w_any.at[0], out_w),
        ],
        sems,
    )
    if packed:
        two = inner_two_any.shape[1]
        moves += copy_in(
            [
                (inner_two_any.at[0 : blocks // 2], mats[2].at[:, 0:two]),
                (inner_two_any.at[blocks // 2 : blocks], mats[3].at[:, 0:two]),
            ],
            sems,
            6,
        )
    start = pl.multiple_of(index * third, third)
    tall = gz_ref[pl.ds(start, third + 16), :].astype(F32)
    here, after = tall[0:third].astype(BF16), tall[1 : third + 1].astype(BF16)

    split_lanes(split_ref, cot_ref[...].astype(F32))
    moves[0].wait()
    add_third(split_ref, 0, dot_nt(here, pool_w[2 * width : 3 * width]))
    add_third(split_ref, 1, dot_nt(after, pool_w[0:width]))
    add_third(split_ref, 2, dot_nt(after, pool_w[width : 2 * width]))
    grad = joined_lanes(split_ref)
    grad_ref[...] = grad
    low_ref[...] = grad.astype(BF16)
    vec_ref[...] = jnp.zeros(vec_ref.shape, F32)

    def column_sum(row, member):
        vec_ref[row : row + 1, 0 : member.shape[1]] = jnp.sum(member, axis=0, keepdims=True)

    column_sum(3, low_ref[...].astype(F32))

    unit, inverse = unit_rows(middle_in_ref[...])
    second_ref[...] = (unit * gains_ref[0, 1:2] + shifts_ref[0, 1:2]).astype(BF16)
    sum_ref[...] = jnp.zeros(sum_ref.shape, F32)
    moves[1].wait()
    moves[2].wait()
    moves[3].wait()
    tiles = width // LANES

    def hidden_back(c, carry):
        columns = pl.ds(pl.multiple_of(c * width, width), width)
        pre = dot_nt(low_ref[...], reduce_w[columns, :]) * rate_ref[:, columns].astype(F32)
        low = pre.astype(BF16)
        vec_ref[2:3, columns] = jnp.sum(low.astype(F32), axis=0, keepdims=True)
        sum_ref[...] += dot_nt(low, expand_w[:, columns])
        reduce_grad = dot_tn(active_ref[:, columns], low_ref[...]).astype(BF16)
        expand_grad = dot_tn(second_ref[...], low).astype(BF16)
        if packed:
            out = buffers[0]
            height = hidden_width // blocks
            for part in range(parts):
                spot = reversed_bits(jnp.bitwise_xor(index, part), parts)
                for block in range(width // height):
                    place = spot_of(c * (width // height) + block, own_block, blocks)
                    out[spot, place, 0:height, :] = reduce_grad[
                        block * height : (block + 1) * height, part * LANES : (part + 1) * LANES
                    ]
            spot = reversed_bits(jnp.bitwise_xor(index, c), parts)
            store_packed(out.at[spot], height, expand_grad, own_block, blocks)
        else:
            mats[0][columns, :] = reduce_grad
            mats[1][:, columns] = expand_grad
        return carry

    lax.fori_loop(0, hidden_width // width, hidden_back, 0)
    grad_second = sum_ref[...]
    column_sum(0, grad_second * unit)
    column_sum(1, grad_second)
    grad_middle = grad_ref[...] + norm_back_rows(grad_second, unit, inverse, gains_ref[0, 1:2])
    middle_ref[...] = grad_middle
    att_ref[...] = grad_middle.astype(BF16)
    column_sum(4, att_ref[...].astype(F32))
    go_ref[...] = dot_nt(att_ref[...], out_w[...]).astype(BF16)
    out_grad = dot_tn(mixed_ref[...], att_ref[...]).astype(BF16)
    if packed:
        place = hidden_width // blocks + tiles * (width // blocks)
        place = store_split(buffers[0], index, place, out_grad, own_block, parts, blocks)
        entries = early_entries(vec_ref, inner_vec_ref, raised_vec_ref, width, hidden_width, parts)
        store_vectors(buffers[0], index, place, entries, own_block, parts, blocks)
        moves += copy_in(halves_of(buffers[0], mats[0:2]), sems, 4)
    else:
        mats[2][...] = out_grad

    for distance in range(parts):
        split_lanes(split_ref, lows[distance][...].astype(F32))
        own = pl.ds(pl.multiple_of(jnp.bitwise_xor(index, distance) * third, third), third)
        for slot, first in ((0, 1), (1, 2), (2, 0)):
            pooled_ref[own, slot * width : (slot + 1) * width] = every_third(
                split_ref, first, third
            ).astype(BF16)
    shared = share_columns(gz_ref, index, parts).astype(F32)
    count = pooled_ref.shape[0]
    here, after = shared[0:count].astype(BF16), shared[1 : count + 1].astype(BF16)
    pool_grad = jnp.concatenate(
        [
            dot_tn(pooled_ref[:, slot * width : (slot + 1) * width], member).astype(BF16)
            for slot, member in ((0, after), (1, after), (2, here))
        ],
        axis=0,
    )
    if packed:
        store_packed(buffers[1], 0, pool_grad, own_block, blocks)
        half = blocks // 2
        moves += copy_in(
            [
                (buffers[1].at[0:half], mats[2].at[:, two:]),
                (buffers[1].at[half:blocks], mats[3].at[:, two:]),
            ],
            sems,
            8,
        )
        for move in moves[4:]:
            move.wait()
    else:
        mats[3][...] = pool_grad


def early_entries(vec_ref, inner_ref, raised_ref, width, hidden, parts):
    once = 1.0 / parts
    sizes = [width, width, width, width, 3 * width, width, hidden, width, width]
    return (
        [(vec_ref, 0, width, 1.0), (vec_ref, 1, width, 1.0), (vec_ref, 2, hidden, 1.0)]
        + [(vec_ref, 3, width, 1.0), (vec_ref, 4, width, 1.0)]
        + [(inner_ref, row, size, once) for row, size in enumerate(sizes)]
        + [(raised_ref, 0, POOL * width, once)]
    )


def late_entries(vec_ref, width):
    return [(vec_ref, 0, width, 1.0), (vec_ref, 1, width, 1.0), (vec_ref, 2, 3 * width, 1.0)]


def outer_hidden(index, lows, inner_two, gz, inner_vecs, raised_vecs, cot, middle, active, rate, mixed, gains, shifts, pool_w, reduce_w, expand_w,
                 out_w, parts, blocks):
    rows, width = cot.shape
    hidden = expand_w.shape[2]
    shapes = [(hidden, width), (width, hidden), (width, width)]
    packed = can_pack(shapes + [(POOL * width, width)], parts, blocks) and hidden // parts == width and width // parts == LANES
    vmem = pl.BlockSpec(memory_space=pltpu.VMEM)
    anywhere = pl.BlockSpec(memory_space=pl.ANY)
    far = pl.BlockSpec(memory_space=pltpu.HBM)
    shape = jax.ShapeDtypeStruct
    if packed:
        held = packed_rows(shapes, parts, blocks) + 16
        mats = [shape((parts // 2, blocks, held, LANES), BF16) for _ in range(2)]
        buffers = [pltpu.VMEM((parts, blocks, held, LANES), BF16)]
        added = packed_rows([(POOL * width, width)], parts, blocks)
        two = inner_two.shape[1]
        mats += [shape((blocks // 2, two + added, LANES), BF16) for _ in range(2)]
        buffers += [pltpu.VMEM((blocks, added, LANES), BF16)]
    else:
        mats = [shape(member, BF16) for member in shapes]
        mats += [shape((POOL * width, width // parts), BF16)]
        buffers = []
    found = pl.pallas_call(
        functools.partial(outer_hidden_kernel, parts, blocks, packed),
        name="outer_hidden",
        in_specs=[pl.BlockSpec(memory_space=pltpu.SMEM)] + [vmem] * parts + [anywhere] + [vmem] * 10 + [far] * 4,
        out_specs=[vmem] * 4 + [anywhere if packed else vmem] * len(mats),
        out_shape=[
            shape((rows, width), F32),
            shape((rows, width), BF16),
            shape((rows, width), BF16),
            shape((8, hidden), F32),
        ] + mats,
        scratch_shapes=[
            pltpu.VMEM((POOL * width, width), BF16),
            pltpu.VMEM((hidden, width), BF16),
            pltpu.VMEM((width, hidden), BF16),
            pltpu.VMEM((width, width), BF16),
            pltpu.VMEM((width // LANES, rows, LANES), F32),
            pltpu.VMEM((rows, width), F32),
            pltpu.VMEM((rows, width), BF16),
            pltpu.VMEM((rows, width), BF16),
            pltpu.VMEM((rows, hidden), BF16),
            pltpu.VMEM((rows, width), F32),
            pltpu.VMEM((gz.shape[0] - 16, POOL * width), BF16),
            pltpu.SemaphoreType.DMA((10,)),
        ]
        + buffers,
        compiler_params=pltpu.CompilerParams(vmem_limit_bytes=grant(44 if packed else 60)),
        cost_estimate=cost(14),
    )(index, *lows, inner_two, gz, inner_vecs, raised_vecs, cot, middle, active, rate, mixed, gains, shifts, pool_w, reduce_w, expand_w, out_w)
    return found[:4], found[4:], packed, shapes


def store_rows(out, index, first, member, own_block, parts, blocks):
    rows, tiles = member.shape[0] // blocks, member.shape[1] // LANES
    share = rows // parts
    for part in range(parts):
        spot = reversed_bits(jnp.bitwise_xor(index, part), parts)
        for block in range(blocks):
            place = spot_of(block, own_block, blocks)
            start = block * rows + part * share
            for tile in range(tiles):
                out[spot, place, first + tile * share : first + (tile + 1) * share, :] = member[
                    start : start + share, tile * LANES : (tile + 1) * LANES
                ]
    return first + tiles * share


def outer_attention_kernel(
    parts,
    blocks,
    packed,
    quad,
    last,
    anchors,
    index_ref,
    ids_ref,
    emb_ref,
    gains_ref,
    shifts_ref,
    qkv_w_any,
    q_ref,
    k_ref,
    kt_ref,
    v_ref,
    o_ref,
    lse_ref,
    go_ref,
    cos_ref,
    sin_ref,
    *rest,
):
    given = (4 if last else 0) + anchors
    if last:
        middle_ref, sums_in_ref, first_ref, table_in_ref = rest[:4]
    outs = rest[given : given + 3]
    (qkv_w, gq_ref, gk_ref, gv_ref, code_ref, acc_ref, sems, *buffers) = rest[given + 3 :]
    index, own_block = index_ref[0], index_ref[1]
    rows, width = o_ref.shape
    vocab = emb_ref.shape[0]
    chunk = rows // 2
    wide = QUAD * HD
    lanes = slice(quad * wide, (quad + 1) * wide)
    moves = copy_in(
        [
            (
                qkv_w_any.at[0, :, part * width + quad * wide : part * width + (quad + 1) * wide],
                qkv_w.at[part],
            )
            for part in range(3)
        ],
        sems,
    )

    def block_of(j):
        return pl.ds(pl.multiple_of(j * rows, rows), rows)

    def clear(j, carry):
        gk_ref[block_of(j), :] = jnp.zeros((rows, wide), F32)
        gv_ref[block_of(j), :] = jnp.zeros((rows, wide), F32)
        return carry

    lax.fori_loop(0, index + 1, clear, 0)

    def part_back(which, carry):
        own_rows = pl.ds(pl.multiple_of(which * chunk, chunk), chunk)
        tall_q = quad_rows(q_ref[own_rows, lanes])
        tall_g = quad_rows(go_ref[own_rows, lanes])
        lse = lse_ref[pl.ds(which * (width // wide) + quad, 1), :]
        delta = head_sums(o_ref[own_rows, lanes].astype(F32) * go_ref[own_rows, lanes].astype(F32))

        def one(j, masked):
            keys = block_of(j)
            scores = dot_nt(k_ref[keys, lanes], tall_q)
            if masked:
                scores = causal(scores, j * rows, index * rows + which * chunk)
            add_k, add_v, add_q = back_block(
                scores, lse, delta, tall_q, tall_g, kt_ref[lanes, keys], v_ref[keys, lanes]
            )
            gk_ref[keys, :] += add_k
            gv_ref[keys, :] += add_v
            return add_q

        acc_ref[...] = one(index, True)

        def full(j, inner_carry):
            acc_ref[...] += one(j, False)
            return inner_carry

        lax.fori_loop(0, index, full, 0)
        gq_ref[own_rows, :] = quad_fold(acc_ref[...].T) * HD**-0.5
        return carry

    lax.fori_loop(0, 2, part_back, 0)

    codes = lax.broadcasted_iota(jnp.int32, (vocab, rows), 0)
    own = block_of(index)

    def hot_of(columns):
        return (codes == ids_ref[:, columns]).astype(F32).astype(BF16)

    turned = turn_rows(gq_ref[...], cos_ref[own, :], -sin_ref[own, :]).astype(BF16)
    code_ref[:, 0:wide] = dot(hot_of(own), turned)
    code_ref[:, wide : 3 * wide] = jnp.zeros((vocab, 2 * wide), F32)

    def by_code(j, carry):
        columns = block_of(j)
        hot = hot_of(columns)
        turned = turn_rows(gk_ref[columns, :], cos_ref[columns, :], -sin_ref[columns, :])
        code_ref[:, wide : 2 * wide] += dot(hot, turned.astype(BF16))
        code_ref[:, 2 * wide : 3 * wide] += dot(hot, gv_ref[columns, :].astype(BF16))
        return carry

    lax.fori_loop(0, index + 1, by_code, 0)
    code = code_ref[...]
    code_low = code.astype(BF16)
    unit, inverse = unit_rows(emb_ref[...].astype(F32))
    normed = (unit * gains_ref[0, 0:1] + shifts_ref[0, 0:1]).astype(BF16)
    qkv_grad = dot_tn(normed, code_low).astype(BF16)
    grad_table = jnp.zeros((vocab, width), F32)
    for part in range(3):
        moves[part].wait()
        grad_table += dot_nt(code_low[:, part * wide : (part + 1) * wide], qkv_w[part])
    vec_ref = outs[0]
    if last:
        vec_ref[...] = sums_in_ref[...]
    else:
        vec_ref[...] = jnp.zeros(vec_ref.shape, F32)
    for part in range(3):
        start = part * width + quad * wide
        vec_ref[2:3, start : start + wide] = jnp.sum(
            code[:, part * wide : (part + 1) * wide], axis=0, keepdims=True
        )
    if not last:
        outs[1][...] = qkv_grad
        outs[2][...] = grad_table
        return
    grad_table += table_in_ref[...]
    high = middle_ref[...].astype(BF16)
    low = (middle_ref[...] - high.astype(F32)).astype(BF16)
    hot = hot_of(own)
    embed = dot(hot, high) + dot(hot, low)
    embed = embed + norm_back_rows(grad_table, unit, inverse, gains_ref[0, 0:1])
    embed = embed.astype(BF16)
    vec_ref[0:1, 0:width] = jnp.sum(grad_table * unit, axis=0, keepdims=True)
    vec_ref[1:2, 0:width] = jnp.sum(grad_table, axis=0, keepdims=True)
    if packed:
        out = buffers[0]
        place = store_rows(out, index, 0, first_ref[...], own_block, parts, blocks)
        place = store_rows(out, index, place, qkv_grad, own_block, parts, blocks)
        place = store_split(out, index, place, embed, own_block, parts, blocks)
        store_vectors(out, index, place, late_entries(vec_ref, width), own_block, parts, blocks)
        for move in copy_in(halves_of(out, outs[1:]), sems, 3):
            move.wait()
    else:
        outs[1][...] = qkv_grad
        outs[2][...] = embed


def outer_attention(quad, index, all_ids, embedding, gains, shifts, qkv_w, queries, keys, keys_t, values,
                    mixed, lse, go, ending, anchors, parts, blocks):
    rows, width = queries.shape
    length = all_ids.shape[1]
    vocab = embedding.shape[0]
    chunk = rows // 2
    wide = QUAD * HD
    last = ending is not None
    packed = width % (16 * parts * blocks) == 0 and vocab % (16 * blocks) == 0
    packed = packed and width % (LANES * parts) == 0
    cosine, sine = row_tables(length)
    vmem = pl.BlockSpec(memory_space=pltpu.VMEM)
    anywhere = pl.BlockSpec(memory_space=pl.ANY)
    far = pl.BlockSpec(memory_space=pltpu.HBM)
    shape = jax.ShapeDtypeStruct
    outs, buffers = [shape((8, 3 * width), F32)], []
    if not last:
        outs += [shape((width, 3 * wide), BF16), shape((vocab, width), F32)]
    elif packed:
        held = 3 * width // LANES * (width // blocks // parts)
        held += vocab // blocks * (width // parts // LANES) + 16
        outs += [shape((parts // 2, blocks, held, LANES), BF16) for _ in range(2)]
        buffers = [pltpu.VMEM((parts, blocks, held, LANES), BF16)]
    else:
        outs += [shape((width, 3 * wide), BF16), shape((vocab, width), BF16)]
    ending = list(ending) if last else []
    return pl.pallas_call(
        functools.partial(outer_attention_kernel, parts, blocks, packed, quad, last, len(anchors)),
        name="outer_attention",
        in_specs=[pl.BlockSpec(memory_space=pltpu.SMEM)]
        + [vmem] * 4
        + [far]
        + [vmem] * (9 + len(ending))
        + [anywhere] * len(anchors),
        out_specs=[vmem] + [anywhere if buffers else vmem] * 2,
        out_shape=outs,
        scratch_shapes=[
            pltpu.VMEM((3, width, wide), BF16),
            pltpu.VMEM((rows, wide), F32),
            pltpu.VMEM((length, wide), F32),
            pltpu.VMEM((length, wide), F32),
            pltpu.VMEM((vocab, 3 * wide), F32),
            pltpu.VMEM((wide, QUAD * chunk), F32),
            pltpu.SemaphoreType.DMA((5,)),
        ]
        + buffers,
        compiler_params=pltpu.CompilerParams(vmem_limit_bytes=grant(34, length // (4 * rows))),
        cost_estimate=cost(14),
    )(index, all_ids, embedding, gains, shifts, qkv_w, queries, keys, keys_t, values, mixed, lse, go,
      jnp.asarray(cosine), jnp.asarray(sine), *ending, *anchors), packed


def add_kernel(count, anchors, index_slices, *refs):
    sources, outs = refs[:count], refs[count + anchors :]
    for out, piece in zip(outs, index_slices):
        total = sources[0][piece].astype(F32)
        for source in sources[1:]:
            total += source[piece].astype(F32)
        out[...] = total.astype(BF16)


def add(sources, pieces, anchors=()):
    shape = sources[0].shape
    found = [shape[1:] if isinstance(piece, int) else (piece[1] - piece[0], *shape[1:]) for piece in pieces]
    slices = [piece if isinstance(piece, int) else slice(*piece) for piece in pieces]
    vmem = pl.BlockSpec(memory_space=pltpu.VMEM)
    return list(pl.pallas_call(
        functools.partial(add_kernel, len(sources), len(anchors), slices),
        name="add",
        in_specs=[vmem] * len(sources) + [pl.BlockSpec(memory_space=pl.ANY)] * len(anchors),
        out_specs=[vmem] * len(found),
        out_shape=[jax.ShapeDtypeStruct(member, BF16) for member in found],
        compiler_params=pltpu.CompilerParams(vmem_limit_bytes=grant(16)),
        cost_estimate=cost(1),
    )(*sources, *anchors))


def total_kernel(counts, *refs):
    out, start, at = refs[-1], 0, 0
    for count in counts:
        total = refs[at][...].astype(F32)
        for ref in refs[at + 1 : at + count]:
            total += ref[...].astype(F32)
        out[start : start + total.shape[0], :] = total.astype(BF16)
        start, at = start + total.shape[0], at + count


def totals(groups):
    rows = sum(group[0].shape[0] for group in groups)
    vmem = pl.BlockSpec(memory_space=pltpu.VMEM)
    members = [member for group in groups for member in group]
    return pl.pallas_call(
        functools.partial(total_kernel, [len(group) for group in groups]),
        name="totals",
        in_specs=[vmem] * len(members),
        out_specs=vmem,
        out_shape=jax.ShapeDtypeStruct((rows, LANES), BF16),
        compiler_params=pltpu.CompilerParams(vmem_limit_bytes=grant(8)),
        cost_estimate=cost(1),
    )(*members)


def assemble_kernel(parts, blocks, index_ref, *rest):
    groups = [rest[i * parts : (i + 1) * parts] for i in range(3)]
    outs = rest[3 * parts :]
    index, own_block = index_ref[0], index_ref[1]
    (embed, gains, shifts, qkv_w, qkv_b, out_w, out_b, expand_w, expand_b, reduce_w, reduce_b) = outs[:11]
    pool_w, pool_b, up_w, up_b = outs[11:]

    def place(group, start, out, height, columns):
        tiles = columns // parts // LANES
        for distance in range(parts):
            part = jnp.bitwise_xor(index, distance)
            for tile in range(tiles):
                lanes = pl.ds(pl.multiple_of((part * tiles + tile) * LANES, LANES), LANES)
                found = group[distance][start + tile * height : start + (tile + 1) * height]
                out[:, lanes] = found.astype(F32)
        return start + tiles * height

    inner, early, late = groups
    start = 0
    for out in (reduce_w.at[1], expand_w.at[1], up_w, out_w.at[1], qkv_w.at[1], pool_w):
        start = place(inner, start, out, *out.shape)
    start = 0
    for out in (reduce_w.at[0], expand_w.at[0], out_w.at[0]):
        start = place(early, start, out, *out.shape)
    early_start = start
    height, wide = qkv_w.shape[1] // parts, QUAD * HD
    start = 0
    for quad in range(qkv_w.shape[2] // 3 // wide):
        for third in range(3):
            for tile in range(wide // LANES):
                lane = third * (qkv_w.shape[2] // 3) + quad * wide + tile * LANES
                for distance in range(parts):
                    part = jnp.bitwise_xor(index, distance)
                    rows = pl.ds(pl.multiple_of(part * height, height), height)
                    qkv_w[0, rows, lane : lane + LANES] = late[distance][
                        start : start + height
                    ].astype(F32)
                start += height
    late_start = place(late, start, embed, *embed.shape)

    def vectors(group, start, sizes):
        entries = [(None, 0, size * blocks, 1.0) for size in sizes]
        total = len(vector_tiles(entries, 0, blocks))
        count = -(-total // parts)
        tiles = {}
        for distance in range(parts):
            tiles[distance] = group[distance][start : start + 16].astype(F32)
        rows = []
        for number in range(total):
            row = jnp.zeros((1, LANES), F32)
            for distance in range(parts):
                here = jnp.bitwise_xor(index, distance) == number // count
                row = jnp.where(here, tiles[distance][number % count : number % count + 1], row)
            rows.append(row)
        found, number = [], 0
        for size in sizes:
            held = len(vector_tiles([(None, 0, size * blocks, 1.0)], 0, blocks))
            wide = jnp.concatenate(rows[number : number + held], axis=1)
            number += held
            if size % LANES != 0:
                shift = own_block * size % LANES
                wide = pltpu.roll(wide, (wide.shape[1] - shift) % wide.shape[1], 1)
            found.append(wide[:, :size])
        return found

    width_b, hidden_b, three_b = out_b.shape[1], expand_b.shape[1], qkv_b.shape[1]
    low = vectors(
        early,
        early_start,
        [width_b, width_b, hidden_b, width_b, width_b]
        + [width_b] * 4
        + [three_b, width_b, hidden_b, width_b, width_b, three_b],
    )
    high = vectors(late, late_start, [width_b, width_b, three_b])
    gains[0, 0:1], shifts[0, 0:1], qkv_b[0:1] = high
    gains[0, 1:2], shifts[0, 1:2], expand_b[0:1], reduce_b[0:1], out_b[0:1] = low[:5]
    gains[1, 0:1], gains[1, 1:2], shifts[1, 0:1], shifts[1, 1:2] = low[5:9]
    qkv_b[1:2], out_b[1:2], expand_b[1:2], reduce_b[1:2] = low[9:13]
    pool_b[...], up_b[...] = low[13:]


def assemble(index, groups, width, hidden, vocab, parts, blocks):
    vmem = pl.BlockSpec(memory_space=pltpu.VMEM)
    part = width // blocks
    shapes = [
        (vocab // blocks, width),
        (2, 2, part),
        (2, 2, part),
        (2, part, 3 * width),
        (2, 3 * part),
        (2, part, width),
        (2, part),
        (2, part, hidden),
        (2, hidden // blocks),
        (2, hidden // blocks, width),
        (2, part),
        (POOL * part, width),
        (1, part),
        (part, POOL * width),
        (1, POOL * part),
    ]
    return pl.pallas_call(
        functools.partial(assemble_kernel, parts, blocks),
        name="assemble",
        in_specs=[pl.BlockSpec(memory_space=pltpu.SMEM)] + [vmem] * (3 * parts),
        out_specs=[vmem] * 15,
        out_shape=[jax.ShapeDtypeStruct(member, F32) for member in shapes],
        compiler_params=pltpu.CompilerParams(vmem_limit_bytes=grant(16)),
        cost_estimate=cost(4),
    )(index, *[member for group in groups for member in group])


def pack(members, parts, blocks):
    rows = []
    for member in members:
        height, width = member.shape
        split = member.reshape(blocks, height // blocks, parts, width // parts)
        rows.append(split.transpose(2, 0, 1, 3).reshape(parts, blocks, -1))
    buffer = jnp.concatenate(rows, axis=2)
    order = [reversed_bits(spot, parts) for spot in range(parts)]
    index = lax.axis_index("seq")
    buffer = jnp.stack([buffer[jnp.bitwise_xor(index, other)] for other in order])
    return buffer.reshape(parts, blocks, -1, LANES)


def in_spots(buffer):
    blocks = buffer.shape[-3]
    index = lax.axis_index("batch")
    order = [spot * 2 % blocks + spot * 2 // blocks for spot in range(blocks)]
    return jnp.stack(
        [
            lax.dynamic_index_in_dim(buffer, jnp.bitwise_xor(index, other), -3, keepdims=False)
            for other in order
        ],
        axis=-3,
    )


def exchange(member, axis, distance):
    pairs = [(peer, peer ^ distance) for peer in range(lax.axis_size(axis))]
    return lax.ppermute(member, axis, pairs)


def seq_scatter(keep, send, level=1, anchors=()):
    while keep.shape[0] > 1:
        half = keep.shape[0] // 2
        got = exchange(send, "seq", level)
        keep, send = add([keep, got], [(0, half), (half, 2 * half)], anchors)
        level *= 2
    return keep, send, level


def seq_last(keep, send, level):
    half = keep.shape[1] // 2
    return add([keep[0], exchange(send, "seq", level)[0]], [(0, half), (half, 2 * half)])


def batch_halves(keep, send, anchors=()):
    return add([keep, exchange(send, "batch", 1)], list(range(keep.shape[0])), anchors)


def batch_rest(sums):
    return [sums[0]] + [
        exchange(sums[spot], "batch", 2 * spot) for spot in range(1, len(sums))
    ]


def plain_sums(buffer):
    level = 1
    while buffer.shape[0] > 1:
        half = buffer.shape[0] // 2
        got = exchange(buffer[half:], "seq", level)
        buffer = (buffer[:half].astype(F32) + got.astype(F32)).astype(BF16)
        level *= 2
    return plain_batch(buffer[0])


def plain_batch(buffer):
    half = buffer.shape[0] // 2
    got = exchange(buffer[half:], "batch", 1)
    sums = (buffer[:half].astype(F32) + got.astype(F32)).astype(BF16)
    total = sums[0].astype(F32)
    for spot in range(1, half):
        total += exchange(sums[spot], "batch", 2 * spot).astype(F32)
    return total.astype(BF16)


def seq_gather(member):
    parts = lax.axis_size("seq")
    found, level = {0: member}, parts // 2
    while level >= 1:
        for distance, held in list(found.items()):
            found[distance ^ level] = exchange(held, "seq", level)
        level //= 2
    return [found[distance] for distance in range(parts)]


def in_order(found):
    found = jnp.stack(found)
    index = lax.axis_index("seq")
    return jnp.stack([found[jnp.bitwise_xor(index, part)] for part in range(len(found))])


def unpack(gathered, shapes, blocks):
    parts = gathered.shape[0]
    gathered = gathered.reshape(parts, -1)
    found, start = [], 0
    for height, width in shapes:
        height, columns = height // blocks, width // parts
        piece = gathered[:, start : start + height * columns]
        piece = piece.reshape(parts, height, columns).transpose(1, 0, 2)
        start += height * columns
        found.append(piece.reshape(height, width).astype(F32))
    return found


def local(
    byte_ids,
    embedding,
    norm_gains,
    norm_biases,
    qkv_weights,
    qkv_biases,
    out_weights,
    out_biases,
    expand_weights,
    expand_biases,
    reduce_weights,
    reduce_biases,
    pool_weight,
    pool_bias,
    upsample_weight,
    upsample_bias,
    cotangent,
):
    parts, blocks = lax.axis_size("seq"), lax.axis_size("batch")
    rows, width, hidden = byte_ids.shape[1], embedding.shape[1], expand_weights.shape[2]
    index = jnp.stack([lax.axis_index("seq"), lax.axis_index("batch")]).astype(jnp.int32)
    all_ids = lax.all_gather(byte_ids[0], "seq", axis=0, tiled=True).reshape(1, -1)
    all_cot = lax.all_gather(cotangent[0], "seq", axis=0, tiled=True)

    h1, h1_low, share, queries, keys, keys_t, values, mixed, lse, middle, active, rate = outer_forward(
        index, all_ids, embedding, norm_gains, norm_biases, qkv_weights, qkv_biases, out_weights,
        out_biases, expand_weights, expand_biases, reduce_weights, reduce_biases, pool_weight, rows
    )
    shares = seq_gather(share)
    lows = seq_gather(h1_low)
    raised_grad, grad_short, raised_sums = raised_back(all_cot, upsample_weight)
    short_low, gz, inner_vecs, inner_found, inner_packed = inner_layer(
        index, shares, pool_bias.reshape(1, -1), norm_gains, norm_biases, qkv_weights, qkv_biases,
        out_weights, out_biases, expand_weights, expand_biases, reduce_weights, reduce_biases,
        raised_grad, grad_short, parts, blocks
    )
    output = raised_output(index, h1, short_low, upsample_weight, upsample_bias.reshape(1, -1))

    if inner_packed:
        first_sums = batch_halves(*inner_found[0:2])
    (grad_middle, grad_att, grad_mixed, hidden_vecs), early, early_packed, early_shapes = outer_hidden(
        index, lows, inner_found[2], gz, inner_vecs, raised_sums, cotangent[0], middle, active, rate, mixed, norm_gains,
        norm_biases, pool_weight, reduce_weights, expand_weights, out_weights, parts, blocks
    )

    def attention_back(quad, ending, anchors):
        return outer_attention(
            quad, index, all_ids, embedding, norm_gains, norm_biases, qkv_weights, queries, keys,
            keys_t, values, mixed, lse, grad_mixed, ending, anchors, parts, blocks
        )

    ending, late_packed = attention_back(0, None, first_sums if inner_packed else [])
    if inner_packed and early_packed:
        first_total = totals([batch_rest(first_sums)])
        second_sums = batch_halves(*early[2:4], ending[:1])
        early_keep, early_send, level = seq_scatter(*early[0:2], anchors=ending[:1])
        anchors = second_sums + [early_keep, first_total]
    else:
        anchors = []
    (table_vecs, *late), _ = attention_back(1, [grad_middle] + list(ending), anchors)
    if inner_packed and early_packed and late_packed:
        inner_total = totals([[first_total], batch_rest(second_sums)])
        inner_all = seq_gather(inner_total)
        early_halves = seq_last(early_keep, early_send, level)
        late_all = batch_halves(*seq_last(*seq_scatter(*late, anchors=early_halves[:1] + [inner_total])))
        early_all = seq_gather(totals([batch_rest(batch_halves(*early_halves))]))
        late_all = seq_gather(totals([batch_rest(late_all)]))
        found = list(
            assemble(
                index, [inner_all, early_all, late_all], width, hidden, embedding.shape[0], parts, blocks
            )
        )
        found[12], found[14] = found[12][0], found[14][0]
        return (output, *found)

    inner_shapes = inner_shapes_of(width, hidden)
    inner_buffer = jnp.concatenate([member.reshape(blocks, -1) for member in inner_found], axis=1)
    inner_buffer = in_spots(inner_buffer.reshape(blocks, -1, LANES))
    inner_out = unpack(in_order(seq_gather(plain_batch(inner_buffer))), inner_shapes, blocks)
    pool_buffer = in_spots(early[3].reshape(blocks, -1, LANES))
    pool_out = unpack(
        in_order(seq_gather(plain_batch(pool_buffer))), [(POOL * width, width)], blocks
    )
    early_buffer = in_spots(pack(early[:3], parts, blocks))
    early_out = unpack(
        in_order(seq_gather(plain_sums(early_buffer))), early_shapes, blocks
    )
    wide = QUAD * HD
    qkv_grad = jnp.concatenate(
        [
            half[:, part * wide : (part + 1) * wide]
            for part in range(3)
            for half in (ending[1], late[0])
        ],
        axis=1,
    )
    late, late_shapes = [qkv_grad, late[1]], [qkv_grad.shape, late[1].shape]
    late_buffer = in_spots(pack(late, parts, blocks))
    late_out = unpack(
        in_order(seq_gather(plain_sums(late_buffer))), late_shapes, blocks
    )
    once = 1.0 / parts
    vectors = [
        table_vecs[0, :width],
        hidden_vecs[0, :width],
        table_vecs[1, :width],
        hidden_vecs[1, :width],
        table_vecs[2, : 3 * width],
        hidden_vecs[4, :width],
        hidden_vecs[2, :hidden],
        hidden_vecs[3, :width],
        inner_vecs[0, :width] * once,
        inner_vecs[1, :width] * once,
        inner_vecs[2, :width] * once,
        inner_vecs[3, :width] * once,
        inner_vecs[4, : 3 * width] * once,
        inner_vecs[5, :width] * once,
        inner_vecs[6, :hidden] * once,
        inner_vecs[7, :width] * once,
        inner_vecs[8, :width] * once,
        raised_sums[0] * once,
    ]
    flat = jnp.concatenate([member.reshape(blocks, -1) for member in vectors], axis=1)
    flat = lax.psum(flat.astype(BF16), ("seq", "batch")).astype(F32)
    flat = lax.dynamic_index_in_dim(flat, lax.axis_index("batch"), 0, keepdims=False)
    sums, start = [], 0
    for member in vectors:
        sums.append(flat[start : start + member.shape[0] // blocks])
        start += member.shape[0] // blocks
    return (
        output,
        late_out[1],
        jnp.stack([jnp.stack([sums[0], sums[1]]), jnp.stack([sums[8], sums[9]])]),
        jnp.stack([jnp.stack([sums[2], sums[3]]), jnp.stack([sums[10], sums[11]])]),
        jnp.stack([late_out[0], inner_out[4]]),
        jnp.stack([sums[4], sums[12]]),
        jnp.stack([early_out[2], inner_out[3]]),
        jnp.stack([sums[5], sums[13]]),
        jnp.stack([early_out[1], inner_out[1]]),
        jnp.stack([sums[6], sums[14]]),
        jnp.stack([early_out[0], inner_out[0]]),
        jnp.stack([sums[7], sums[15]]),
        pool_out[0],
        sums[16],
        inner_out[2],
        sums[17],
    )


def solution(mesh):
    whole = P()
    return jax.shard_map(
        local,
        mesh=mesh,
        in_specs=(P("batch", "seq"),) + (whole,) * 15 + (P("batch", "seq", None),),
        out_specs=(
            P("batch", "seq", None),
            P("batch", None),
            P(None, None, "batch"),
            P(None, None, "batch"),
            P(None, "batch", None),
            P(None, "batch"),
            P(None, "batch", None),
            P(None, "batch"),
            P(None, "batch", None),
            P(None, "batch"),
            P(None, "batch", None),
            P(None, "batch"),
            P("batch", None),
            P("batch"),
            P("batch", None),
            P("batch"),
        ),
        check_vma=False,
    )
```

```python
import functools

import jax
import jax.numpy as jnp
import numpy as np
from jax import lax
from jax.experimental import pallas as pl
from jax.experimental.pallas import tpu as pltpu
from jax.sharding import PartitionSpec as P

HD = 64
POOL = 3
QUAD = 4
LANES = 128
VMEM_LIMIT = 60 * 1024 * 1024
F32 = jnp.float32
BF16 = jnp.bfloat16


def dot(left, right):
    return jnp.dot(left, right, preferred_element_type=F32)


def dot_nt(left, right):
    return lax.dot_general(left, right, (((1,), (1,)), ((), ())), preferred_element_type=F32)


def dot_tn(left, right):
    return lax.dot_general(left, right, (((0,), (0,)), ((), ())), preferred_element_type=F32)


def gelu_parts(pre):
    slope = 0.7978845608028654
    square = pre * pre
    bent = jnp.tanh(slope * pre * (1.0 + 0.044715 * square))
    half = 0.5 * (1.0 + bent)
    value = pre * half
    rate = half + 0.5 * pre * (1.0 - bent * bent) * (slope * (1.0 + 3.0 * 0.044715 * square))
    return (value, rate)


def angle_rows(length):
    frequency = 10000.0 ** (-np.arange(HD // 2, dtype=np.float64) / (HD // 2))
    angles = np.arange(length, dtype=np.float64)[:, None] * frequency[None, :]
    return (np.cos(angles).astype(np.float32), np.sin(angles).astype(np.float32))


def cost(microseconds):
    microseconds *= 10
    return pl.CostEstimate(
        flops=int(microseconds * 1e9), bytes_accessed=int(microseconds * 1e6), transcendentals=0
    )


def grant(megabytes, factor=1):
    return min(int(megabytes * factor), 60) * 1024 * 1024


def outside(shape, dtype):
    return pltpu.HBM(shape, dtype)


def far_away(member):
    return pltpu.with_memory_space_constraint(member, pltpu.HBM)


def copy_in(pairs, sems, start=0):
    moves = [
        pltpu.make_async_copy(src, dst, sems.at[start + i]) for i, (src, dst) in enumerate(pairs)
    ]
    for move in moves:
        move.start()
    return moves


def chunk_of(index, which, parts):
    return index + which * (2 * parts - 1 - 2 * index)


def by_blocks(index, parts, body):
    if parts != 4:
        full = [chunk_of(index, which, parts) // 2 for which in range(2)]
        body(full, full[1] + 1)
        return

    @pl.when(index < 2)
    def _():
        body([0, 3], 4)

    @pl.when(index >= 2)
    def _():
        body([1, 2], 3)


def each(count, step):
    if isinstance(count, int):
        for i in range(count):
            step(i)
    else:
        lax.fori_loop(0, count, lambda i, carry: (step(i), carry)[1], 0)


def own_lanes(row, index, parts, chunk):
    length = row.shape[1]
    return jnp.concatenate(
        [
            pltpu.roll(row, (length - chunk_of(index, which, parts) * chunk) % length, 1)[:, :chunk]
            for which in range(2)
        ],
        axis=1,
    )


def quad_rows(rows):
    lane = lax.broadcasted_iota(jnp.int32, rows.shape, 1) // HD
    zero = jnp.zeros_like(rows)
    return jnp.concatenate([jnp.where(lane == head, rows, zero) for head in range(QUAD)], axis=0)


def quad_fold(tall):
    count = tall.shape[0] // QUAD
    lane = lax.broadcasted_iota(jnp.int32, (count, tall.shape[1]), 1) // HD
    folded = jnp.zeros((count, tall.shape[1]), tall.dtype)
    for head in range(QUAD):
        folded = jnp.where(lane == head, tall[head * count : (head + 1) * count], folded)
    return folded


def lanes_of(quad):
    return slice(quad * QUAD * HD, (quad + 1) * QUAD * HD)


def causal(scores, key_start, query_start):
    count = scores.shape[1] // QUAD
    key = key_start + lax.broadcasted_iota(jnp.int32, scores.shape, 0)
    query = lax.broadcasted_iota(jnp.int32, (1, scores.shape[1]), 1)
    for head in range(1, QUAD):
        query = jnp.where(query >= count, query - count, query)
    return jnp.where(key <= query + query_start, scores, -1e30)


def flash_quads(tall_q, keys_at, values_at, full, key_start_last, query_start, state):
    quads = range(len(tall_q))
    acc, peak, total = state

    def scores_of(j):
        return [dot_nt(keys_at(j, quad), tall_q[quad]) for quad in quads]

    scores = [causal(member, key_start_last, query_start) for member in scores_of(full)]
    tops = [jnp.max(member, axis=0, keepdims=True) for member in scores]
    raised = [jnp.exp(scores[quad] - tops[quad]) for quad in quads]
    for quad in quads:
        peak[quad] = tops[quad]
        total[quad] = jnp.sum(raised[quad], axis=0, keepdims=True)
        acc[quad] = dot(values_at(full, quad), raised[quad].astype(BF16))

    def block(j):
        scores = scores_of(j)
        tops = [
            jnp.maximum(peak[quad], jnp.max(scores[quad], axis=0, keepdims=True)) for quad in quads
        ]
        raised = [jnp.exp(scores[quad] - tops[quad]) for quad in quads]
        for quad in quads:
            shrink = jnp.exp(peak[quad] - tops[quad])
            peak[quad] = tops[quad]
            total[quad] = total[quad] * shrink + jnp.sum(raised[quad], axis=0, keepdims=True)
            acc[quad] = acc[quad] * shrink + dot(values_at(j, quad), raised[quad].astype(BF16))

    each(full, block)
    return [
        (quad_fold((acc[quad] / total[quad]).T), peak[quad] + jnp.log(total[quad]))
        for quad in quads
    ]


def every_third(split_ref, start, count):
    return jnp.concatenate(
        [split_ref[i, pl.ds(start, count, stride=POOL), :] for i in range(split_ref.shape[0])],
        axis=1,
    )


def unit_rows(stream):
    centred = stream - jnp.mean(stream, axis=-1, keepdims=True)
    inverse = lax.rsqrt(jnp.mean(centred * centred, axis=-1, keepdims=True) + 1e-05)
    return (centred * inverse, inverse)


def table_kernel(emb_ref, gains_ref, shifts_ref, qkv_w_any, qkv_b_ref, coarse_ref, fine_ref, qkv_w, sems):
    width = emb_ref.shape[1]
    moves = copy_in([(qkv_w_any.at[0], qkv_w)], sems)
    unit, _ = unit_rows(emb_ref[...].astype(F32))
    normed = (unit * gains_ref[0, 0:1] + shifts_ref[0, 0:1]).astype(BF16)
    moves[0].wait()
    table = (dot(normed, qkv_w[...]) + qkv_b_ref[0:1]).T
    coarse = table.astype(BF16)
    coarse_ref[...] = coarse
    fine_ref[...] = (table[: 2 * width] - coarse[: 2 * width].astype(F32)).astype(BF16)


def byte_table(embedding, gains, shifts, qkv_w, qkv_b):
    vocab, width = embedding.shape
    vmem = pl.BlockSpec(memory_space=pltpu.VMEM)
    far = pl.BlockSpec(memory_space=pltpu.HBM)
    return pl.pallas_call(
        table_kernel,
        name="byte_table",
        in_specs=[vmem, vmem, vmem, far, vmem],
        out_specs=[vmem, vmem],
        out_shape=[outside((3 * width, vocab), BF16), outside((2 * width, vocab), BF16)],
        scratch_shapes=[pltpu.VMEM((width, 3 * width), BF16), pltpu.SemaphoreType.DMA((1,))],
        compiler_params=pltpu.CompilerParams(vmem_limit_bytes=grant(16)),
        cost_estimate=cost(4),
    )(embedding, gains, shifts, qkv_w, qkv_b)


def outer_forward_kernel(
    parts,
    index_ref,
    *rest,
):
    ids, rest = rest[:parts], rest[parts:]
    (
    emb_ref,
    gains_ref,
    shifts_ref,
    coarse_any,
    fine_any,
    out_w_any,
    out_b_ref,
    expand_w_any,
    expand_b_ref,
    reduce_w_any,
    reduce_b_ref,
    pool_w_any,
    cos_ref,
    sin_ref,
    low_ref,
    share_ref,
    q_any,
    k_any,
    kt_any,
    v_any,
    o_any,
    lse_ref,
    middle_any,
    active_any,
    rate_any,
    ids_ref,
    q_ref,
    k_ref,
    kt_ref,
    v_ref,
    o_ref,
    middle_ref,
    active_ref,
    rate_ref,
    out_w,
    expand_w,
    reduce_w,
    pool_w,
    coarse_ref,
    fine_ref,
    vt_ref,
    acc_ref,
    peak_ref,
    total_ref,
    second_ref,
    sum_ref,
    later_ref,
    split_ref,
    sems,
    ) = rest
    index = index_ref[0]
    rows, width = middle_ref.shape
    vocab = emb_ref.shape[0]
    chunk = rows // 2
    moves = copy_in(
        [
            (coarse_any, coarse_ref),
            (fine_any, fine_ref),
            (out_w_any.at[0], out_w),
            (expand_w_any.at[0], expand_w),
            (reduce_w_any.at[0], reduce_w),
            (pool_w_any, pool_w),
        ],
        sems,
    )

    for distance in range(parts):
        part = jnp.bitwise_xor(index, distance)
        ids_ref[:, pl.ds(pl.multiple_of(part * rows, rows), rows)] = ids[distance][...]
    moves[0].wait()
    moves[1].wait()

    def picked(start, hot):
        return dot(coarse_ref[start : start + width], hot) + dot(
            fine_ref[start : start + width], hot
        )

    def turned(member, cosine, sine):
        pieces = []
        for head in range(width // HD):
            first = member[head * HD : head * HD + HD // 2]
            second = member[head * HD + HD // 2 : (head + 1) * HD]
            pieces += [first * cosine - second * sine, first * sine + second * cosine]
        return jnp.concatenate(pieces, axis=0)

    codes = lax.broadcasted_iota(jnp.int32, (vocab, rows), 0)

    def block_of(j):
        if isinstance(j, int):
            return slice(j * rows, (j + 1) * rows)
        return pl.ds(pl.multiple_of(j * rows, rows), rows)

    def key_block(j):
        columns = block_of(j)
        hot = (codes == ids_ref[:, columns]).astype(F32).astype(BF16)
        keys = turned(picked(width, hot), cos_ref[:, columns], sin_ref[:, columns])
        kt_ref[:, columns] = keys.astype(BF16)
        k_ref[columns, :] = keys.T.astype(BF16)
        values = dot(coarse_ref[2 * width : 3 * width], hot)
        vt_ref[:, columns] = values.astype(BF16)
        v_ref[columns, :] = values.T.astype(BF16)

    by_blocks(index, parts, lambda full, seen: each(seen, key_block))
    moves += copy_in([(k_ref, k_any), (kt_ref, kt_any), (v_ref, v_any)], sems, 6)
    own_ids = own_lanes(jnp.broadcast_to(ids_ref[...], (8, ids_ref.shape[1])), index, parts, chunk)
    own = (codes == own_ids[0:1]).astype(F32)
    queries = turned(
        picked(0, own.astype(BF16)),
        own_lanes(cos_ref[...], index, parts, chunk),
        own_lanes(sin_ref[...], index, parts, chunk),
    )
    q_ref[...] = (queries * HD**-0.5).T.astype(BF16)
    middle_ref[...] = dot(own.T.astype(BF16), emb_ref[...])

    quads = width // (QUAD * HD)

    def attend(full, seen):
        for which in range(2):
            own_rows = slice(which * chunk, (which + 1) * chunk)
            place = chunk_of(index, which, parts)
            found = flash_quads(
                [quad_rows(q_ref[own_rows, lanes_of(quad)]) for quad in range(quads)],
                lambda j, quad: k_ref[block_of(j), lanes_of(quad)],
                lambda j, quad: vt_ref[lanes_of(quad), block_of(j)],
                full[which],
                full[which] * rows,
                place * chunk,
                (acc_ref.at[which], peak_ref.at[which], total_ref.at[which]),
            )
            for quad, (mixed, lse) in enumerate(found):
                o_ref[own_rows, lanes_of(quad)] = mixed.astype(BF16)
                row = which * quads + quad
                lse_ref[row : row + 1, :] = lse

    by_blocks(index, parts, attend)

    moves += copy_in([(q_ref, q_any), (o_ref, o_any)], sems, 9)
    moves[2].wait()
    middle = middle_ref[...] + dot(o_ref[...], out_w[...]) + out_b_ref[0:1]
    middle_ref[...] = middle
    moves += copy_in([(middle_ref, middle_any)], sems, 11)
    unit, _ = unit_rows(middle)
    second_ref[...] = (unit * gains_ref[0, 1:2] + shifts_ref[0, 1:2]).astype(BF16)
    sum_ref[...] = middle + reduce_b_ref[0:1]
    moves[3].wait()
    moves[4].wait()

    for c in range(expand_w.shape[1] // width):
        columns = slice(c * width, (c + 1) * width)
        pre = dot(second_ref[...], expand_w[:, columns]) + expand_b_ref[0:1, columns]
        value, rate = gelu_parts(pre)
        value = value.astype(BF16)
        active_ref[:, columns] = value
        rate_ref[:, columns] = rate.astype(BF16)
        moves += copy_in(
            [
                (active_ref.at[:, columns], active_any.at[:, columns]),
                (rate_ref.at[:, columns], rate_any.at[:, columns]),
            ],
            sems,
            12 + 2 * c,
        )
        sum_ref[...] += dot(value, reduce_w[columns, :])
    low_ref[...] = sum_ref[...].astype(BF16)

    moves[5].wait()
    third = rows // POOL

    for lane in range(width // LANES):
        split_ref[lane] = sum_ref[:, lane * LANES : (lane + 1) * LANES]

    def thirds(start):
        return every_third(split_ref, start, third).astype(BF16)

    later = dot(thirds(1), pool_w[0:width]) + dot(thirds(2), pool_w[width : 2 * width])
    same = dot(thirds(0), pool_w[2 * width : 3 * width])
    half = third // 2
    for which in range(2):
        start = which * (half + 8)
        later_ref[start : start + 8] = jnp.zeros((8, width), F32)
        later_ref[start + half : start + half + 8] = jnp.zeros((8, width), F32)
        later_ref[start + 1 : start + half + 1] = later[which * half : (which + 1) * half]
        share_ref[start : start + half] = (
            later_ref[start : start + half] + same[which * half : (which + 1) * half]
        ).astype(BF16)
        share_ref[start + half : start + half + 8] = later_ref[
            start + half : start + half + 8
        ].astype(BF16)
    for move in moves[6:]:
        move.wait()


def outer_forward(index, ids, embedding, gains, shifts, coarse, fine, out_w, out_b, expand_w,
                  expand_b, reduce_w, reduce_b, pool_w, rows):
    length = rows * len(ids)
    vocab, width = embedding.shape
    hidden = expand_w.shape[2]
    chunk, quads = rows // 2, width // (QUAD * HD)
    cosine, sine = angle_rows(length)
    vmem = pl.BlockSpec(memory_space=pltpu.VMEM)
    far = pl.BlockSpec(memory_space=pltpu.HBM)
    shape = outside
    third = rows // POOL
    kept = [
        shape((rows, width), BF16),
        shape((length, width), BF16),
        shape((width, length), BF16),
        shape((length, width), BF16),
        shape((rows, width), BF16),
        shape((rows, width), F32),
        shape((rows, hidden), BF16),
        shape((rows, hidden), BF16),
    ]
    return pl.pallas_call(
        functools.partial(outer_forward_kernel, length // rows),
        name="outer_forward",
        in_specs=[pl.BlockSpec(memory_space=pltpu.SMEM)] + [vmem] * (len(ids) + 3) + [far, far,
                  far, vmem, far, vmem, far, vmem, far, vmem, vmem],
        out_specs=[vmem] * 2 + [far] * 5 + [vmem] + [far] * 3 + [vmem],
        out_shape=[
            shape((rows, width), BF16),
            shape((third + 16, width), BF16),
        ]
        + kept[:5]
        + [shape((2 * quads, QUAD * chunk), F32)]
        + kept[5:]
        + [shape((1, length), jnp.int32)],
        scratch_shapes=[pltpu.VMEM(member.shape, member.dtype) for member in kept]
        + [
            pltpu.VMEM((width, width), BF16),
            pltpu.VMEM((width, hidden), BF16),
            pltpu.VMEM((hidden, width), BF16),
            pltpu.VMEM((POOL * width, width), BF16),
            pltpu.VMEM((3 * width, vocab), BF16),
            pltpu.VMEM((2 * width, vocab), BF16),
            pltpu.VMEM((width, length), BF16),
            pltpu.VMEM((2, quads, QUAD * HD, QUAD * chunk), F32),
            pltpu.VMEM((2, quads, 1, QUAD * chunk), F32),
            pltpu.VMEM((2, quads, 1, QUAD * chunk), F32),
            pltpu.VMEM((rows, width), BF16),
            pltpu.VMEM((rows, width), F32),
            pltpu.VMEM((third + 16, width), F32),
            pltpu.VMEM((width // LANES, rows, LANES), F32),
            pltpu.SemaphoreType.DMA((12 + 2 * (hidden // width),)),
        ],
        compiler_params=pltpu.CompilerParams(vmem_limit_bytes=grant(60, length // (4 * rows))),
        cost_estimate=cost(30),
    )(index, *ids, embedding, gains, shifts, coarse, fine, out_w, out_b, expand_w, expand_b,
      reduce_w, reduce_b, pool_w, far_away(jnp.asarray(cosine.T)), far_away(jnp.asarray(sine.T)))


def turn_rows(member, cosine, sine):
    pieces = []
    for start in range(0, member.shape[1], LANES):
        tile = member[:, start : start + LANES]
        lane = lax.broadcasted_iota(jnp.int32, tile.shape, 1) % HD
        other = jnp.where(
            lane < HD // 2,
            pltpu.roll(tile, LANES - HD // 2, 1),
            pltpu.roll(tile, HD // 2, 1),
        )
        pieces.append(tile * cosine + other * sine)
    return jnp.concatenate(pieces, axis=1)


def norm_back_rows(grad, unit, inverse, gain):
    scaled = grad * gain
    mean_one = jnp.mean(scaled, axis=-1, keepdims=True)
    mean_two = jnp.mean(scaled * unit, axis=-1, keepdims=True)
    return inverse * (scaled - mean_one - unit * mean_two)


def head_sums(product):
    tall = product.T
    return jnp.concatenate(
        [
            jnp.sum(tall[head * HD : (head + 1) * HD], axis=0, keepdims=True)
            for head in range(QUAD)
        ],
        axis=1,
    )


def back_block(scores, lse, delta, tall_q, tall_g, keys_t, values):
    probs = jnp.exp(scores - lse)
    low = (probs * (dot_nt(values, tall_g) - delta)).astype(BF16)
    return (dot(low, tall_q), dot(probs.astype(BF16), tall_g), dot(keys_t, low))


def share_columns(member_ref, index, parts):
    width = member_ref.shape[1] // parts
    if width % LANES == 0:
        return member_ref[:, pl.ds(pl.multiple_of(index * width, LANES), width)]
    full = member_ref.shape[1]
    row = lax.broadcasted_iota(jnp.int32, (full, width), 0)
    column = lax.broadcasted_iota(jnp.int32, (full, width), 1)
    picks = (row == column + index * width).astype(F32).astype(BF16)
    return dot(member_ref[...], picks).astype(BF16)


def can_pack(shapes, parts, blocks):
    return parts == 4 and all(
        rows % (16 * blocks) == 0 and columns % (LANES * parts) == 0 for rows, columns in shapes
    )


def packed_rows(shapes, parts, blocks):
    return sum(rows // blocks * (columns // parts // LANES) for rows, columns in shapes)


def spot_of(block, own_block, blocks):
    distance = jnp.bitwise_xor(own_block, block)
    return distance % 2 * (blocks // 2) + distance // 2


def store_packed(out, start, member, own_block, blocks):
    rows, columns = member.shape[0] // blocks, member.shape[1]
    for block in range(blocks):
        spot = spot_of(block, own_block, blocks)
        for tile in range(columns // LANES):
            out[spot, start + tile * rows : start + (tile + 1) * rows, :] = member[
                block * rows : (block + 1) * rows, tile * LANES : (tile + 1) * LANES
            ]
    return start + rows * (columns // LANES)


def inner_kernel(
    parts,
    blocks,
    packed,
    query_rows,
    index_ref,
    *rest,
):
    shares, rest = rest[:parts], rest[parts:]
    (
    pool_b_ref,
    gains_ref,
    shifts_ref,
    qkv_w_any,
    qkv_b_ref,
    out_w_any,
    out_b_ref,
    expand_w_any,
    expand_b_ref,
    reduce_w_any,
    reduce_b_ref,
    raised_grad_any,
    grad_any,
    cos_ref,
    sin_ref,
    ) = rest[:15]
    rest = rest[15:]
    outs = 2 if packed else 5
    low_ref, gz_ref, vec_ref = rest[:3]
    mats = rest[3 : 3 + outs]
    (
        qkv_w,
        out_w,
        expand_w,
        reduce_w,
        stream_ref,
        normed_ref,
        q_ref,
        k_ref,
        kt_ref,
        v_ref,
        vt_ref,
        o_ref,
        lse_ref,
        middle_ref,
        second_ref,
        active_ref,
        rate_ref,
        sum_ref,
        pre_ref,
        att_ref,
        go_ref,
        gk_ref,
        gv_ref,
        acc_ref,
        peak_ref,
        total_ref,
        raised_grad_ref,
        grad_ref,
        sems,
        *buffers,
    ) = rest[3 + outs :]
    index, own_block = index_ref[0], index_ref[1]
    rows, width = stream_ref.shape
    hidden_width = expand_w.shape[1]
    gq_ref, gqkv_ref = sum_ref, rate_ref.at[:, 0 : 3 * width]
    quads = width // (QUAD * HD)
    moves = copy_in(
        [
            (qkv_w_any.at[1], qkv_w),
            (out_w_any.at[1], out_w),
            (expand_w_any.at[1], expand_w),
            (reduce_w_any.at[1], reduce_w),
            (grad_any, grad_ref),
            (raised_grad_any, raised_grad_ref),
        ],
        sems,
    )
    share = rows // parts
    half = share // 2
    chunks = [
        (shares[distance], which * (half + 8), chunk_of(jnp.bitwise_xor(index, distance), which, parts))
        for distance in range(parts)
        for which in range(2)
    ]
    for given, start, place in chunks:
        own = pl.ds(pl.multiple_of(place * half, half), half)
        stream_ref[own] = given[start : start + half].astype(F32) + pool_b_ref[...]
    for given, start, place in chunks:

        @pl.when(place < 2 * parts - 1)
        def _():
            head = pl.ds(pl.multiple_of((place + 1) * half, half), 8)
            stream_ref[head] += given[start + half : start + half + 8].astype(F32)

    unit, _ = unit_rows(stream_ref[...])
    normed_ref[...] = (unit * gains_ref[1, 0:1] + shifts_ref[1, 0:1]).astype(BF16)
    moves[0].wait()

    def projected(part):
        columns = slice(part * width, (part + 1) * width)
        return dot(normed_ref[...], qkv_w[:, columns]) + qkv_b_ref[1:2, columns]

    cosine, sine = cos_ref[...], sin_ref[...]
    q_ref[...] = (turn_rows(projected(0), cosine, sine) * HD**-0.5).astype(BF16)
    keys = turn_rows(projected(1), cosine, sine)
    k_ref[...] = keys.astype(BF16)
    kt_ref[...] = keys.T.astype(BF16)
    values = projected(2)
    v_ref[...] = values.astype(BF16)
    vt_ref[...] = values.T.astype(BF16)

    def block_of(j):
        return pl.ds(pl.multiple_of(j * query_rows, query_rows), query_rows)

    def part(which, carry):
        own_rows = block_of(which)
        found = flash_quads(
            [quad_rows(q_ref[own_rows, lanes_of(quad)]) for quad in range(quads)],
            lambda j, quad: k_ref[block_of(j), lanes_of(quad)],
            lambda j, quad: vt_ref[lanes_of(quad), block_of(j)],
            which,
            which * query_rows,
            which * query_rows,
            (acc_ref, peak_ref, total_ref),
        )
        for quad, (mixed, lse) in enumerate(found):
            o_ref[own_rows, lanes_of(quad)] = mixed.astype(BF16)
            lse_ref[pl.ds(which * quads + quad, 1), :] = lse
        return carry

    lax.fori_loop(0, rows // query_rows, part, 0, unroll=parts == 4)
    moves[1].wait()
    middle = stream_ref[...] + dot(o_ref[...], out_w[...]) + out_b_ref[1:2]
    middle_ref[...] = middle
    unit, _ = unit_rows(middle)
    second_ref[...] = (unit * gains_ref[1, 1:2] + shifts_ref[1, 1:2]).astype(BF16)
    sum_ref[...] = middle + reduce_b_ref[1:2]
    moves[2].wait()
    moves[3].wait()

    def columns_of(c):
        return pl.ds(pl.multiple_of(c * width, width), width)

    def hidden(c, carry):
        columns = columns_of(c)
        pre = dot(second_ref[...], expand_w[:, columns]) + expand_b_ref[1:2, columns]
        value, rate = gelu_parts(pre)
        value = value.astype(BF16)
        active_ref[:, columns] = value
        rate_ref[:, columns] = rate.astype(BF16)
        sum_ref[...] += dot(value, reduce_w[columns, :])
        return carry

    lax.fori_loop(0, hidden_width // width, hidden, 0, unroll=parts == 4)
    low_ref[...] = sum_ref[...].astype(BF16)

    vec_ref[...] = jnp.zeros(vec_ref.shape, F32)

    def column_sum(row, member):
        vec_ref[row : row + 1, 0 : member.shape[1]] = jnp.sum(member, axis=0, keepdims=True)

    moves[4].wait()
    moves[5].wait()
    grad_low = grad_ref[...].astype(BF16)
    column_sum(7, grad_low.astype(F32))
    att_ref[...] = grad_low
    sum_ref[...] = jnp.zeros(sum_ref.shape, F32)

    def hidden_back(c, carry):
        columns = columns_of(c)
        pre = dot_nt(att_ref[...], reduce_w[columns, :]) * rate_ref[:, columns].astype(F32)
        low = pre.astype(BF16)
        pre_ref[:, columns] = low
        vec_ref[6:7, columns] = jnp.sum(low.astype(F32), axis=0, keepdims=True)
        sum_ref[...] += dot_nt(low, expand_w[:, columns])
        return carry

    lax.fori_loop(0, hidden_width // width, hidden_back, 0, unroll=parts == 4)
    if packed:
        place = store_packed(
            buffers[0], 0, dot_tn(active_ref[...], share_columns(att_ref, index, parts)).astype(BF16), own_block, blocks
        )
        place = store_packed(
            buffers[0], place, dot_tn(second_ref[...], share_columns(pre_ref, index, parts)).astype(BF16), own_block, blocks
        )
        place = store_packed(
            buffers[0], place, dot_tn(low_ref[...], share_columns(raised_grad_ref, index, parts)).astype(BF16), own_block, blocks
        )
    else:
        mats[0][...] = dot_tn(active_ref[...], share_columns(att_ref, index, parts)).astype(BF16)
        mats[1][...] = dot_tn(second_ref[...], share_columns(pre_ref, index, parts)).astype(BF16)
        mats[2][...] = dot_tn(low_ref[...], share_columns(raised_grad_ref, index, parts)).astype(BF16)

    unit, inverse = unit_rows(middle_ref[...])
    grad_second = sum_ref[...]
    column_sum(1, grad_second * unit)
    column_sum(3, grad_second)
    grad_middle = grad_ref[...] + norm_back_rows(grad_second, unit, inverse, gains_ref[1, 1:2])
    middle_ref[...] = grad_middle
    att_ref[...] = grad_middle.astype(BF16)
    column_sum(5, att_ref[...].astype(F32))
    go_ref[...] = dot_nt(att_ref[...], out_w[...]).astype(BF16)
    gk_ref[...] = jnp.zeros(gk_ref.shape, F32)
    gv_ref[...] = jnp.zeros(gv_ref.shape, F32)

    def part_back(which, carry):
        own_rows = block_of(which)
        every = range(quads)
        lanes = [lanes_of(quad) for quad in every]
        tall_q = [quad_rows(q_ref[own_rows, lane]) for lane in lanes]
        tall_g = [quad_rows(go_ref[own_rows, lane]) for lane in lanes]
        delta = [
            head_sums(o_ref[own_rows, lane].astype(F32) * go_ref[own_rows, lane].astype(F32))
            for lane in lanes
        ]

        def one(j, masked):
            keys = block_of(j)
            scores = [dot_nt(k_ref[keys, lanes[quad]], tall_q[quad]) for quad in every]
            if masked:
                scores = [
                    causal(member, j * query_rows, which * query_rows) for member in scores
                ]
            found = []
            for quad in every:
                lane = lanes[quad]
                add_k, add_v, add_q = back_block(
                    scores[quad],
                    lse_ref[pl.ds(which * quads + quad, 1), :],
                    delta[quad],
                    tall_q[quad],
                    tall_g[quad],
                    kt_ref[lane, keys],
                    v_ref[keys, lane],
                )
                gk_ref[keys, lane] += add_k
                gv_ref[keys, lane] += add_v
                found.append(add_q)
            return found

        for quad, found in enumerate(one(which, True)):
            acc_ref[quad] = found

        def full(j, inner_carry):
            for quad, found in enumerate(one(j, False)):
                acc_ref[quad] += found
            return inner_carry

        lax.fori_loop(0, which, full, 0)
        for quad in every:
            gq_ref[own_rows, lanes[quad]] = quad_fold(acc_ref[quad].T) * HD**-0.5
        return carry

    lax.fori_loop(0, rows // query_rows, part_back, 0, unroll=parts == 4)
    sine = -sin_ref[...]
    gqkv_ref[:, 0:width] = turn_rows(gq_ref[...], cosine, sine).astype(BF16)
    gqkv_ref[:, width : 2 * width] = turn_rows(gk_ref[...], cosine, sine).astype(BF16)
    gqkv_ref[:, 2 * width : 3 * width] = gv_ref[...].astype(BF16)
    column_sum(4, gqkv_ref[...].astype(F32))
    if packed:
        place = store_packed(
            buffers[0], place, dot_tn(o_ref[...], share_columns(att_ref, index, parts)).astype(BF16), own_block, blocks
        )
        store_packed(
            buffers[0], place, dot_tn(normed_ref[...], share_columns(gqkv_ref, index, parts)).astype(BF16), own_block, blocks
        )
    else:
        mats[3][...] = dot_tn(o_ref[...], share_columns(att_ref, index, parts)).astype(BF16)
        mats[4][...] = dot_tn(normed_ref[...], share_columns(gqkv_ref, index, parts)).astype(BF16)
    if packed:
        sent = copy_in(halves_of(buffers[0], mats), sems, 6)
    grad_normed = dot_nt(gqkv_ref[...], qkv_w[...])
    unit, inverse = unit_rows(stream_ref[...])
    column_sum(0, grad_normed * unit)
    column_sum(2, grad_normed)
    grad_in = middle_ref[...] + norm_back_rows(grad_normed, unit, inverse, gains_ref[1, 0:1])
    grad_in_low = grad_in.astype(BF16)
    gz_ref[0:rows] = grad_in_low
    gz_ref[rows : rows + 16] = jnp.zeros((16, width), BF16)
    column_sum(8, grad_in_low.astype(F32))
    if packed:
        for move in sent:
            move.wait()


def halves_of(buffer, outs):
    half = buffer.shape[0] // 2
    return [(buffer.at[0:half], outs[0]), (buffer.at[half : 2 * half], outs[1])]


def inner_shapes_of(width, hidden):
    return [
        (hidden, width),
        (width, hidden),
        (width, POOL * width),
        (width, width),
        (width, 3 * width),
    ]


def row_tables(length):
    cosine, sine = angle_rows(length)
    repeat = LANES // HD
    return (
        np.tile(np.concatenate([cosine, cosine], axis=1), (1, repeat)),
        np.tile(np.concatenate([-sine, sine], axis=1), (1, repeat)),
    )


def inner_layer(index, shares, pool_b, gains, shifts, qkv_w, qkv_b, out_w, out_b, expand_w, expand_b,
                reduce_w, reduce_b, raised_grad, grad, parts, blocks):
    rows, width = grad.shape
    raised_grad, grad = far_away(raised_grad), far_away(grad)
    hidden = expand_w.shape[2]
    quads = width // (QUAD * HD)
    query_rows = 256 if parts == 4 else 128
    shapes = inner_shapes_of(width, hidden)
    packed = can_pack(shapes, parts, blocks)
    cosine, sine = row_tables(rows)
    vmem = pl.BlockSpec(memory_space=pltpu.VMEM)
    anywhere = pl.BlockSpec(memory_space=pl.ANY)
    far = pl.BlockSpec(memory_space=pltpu.HBM)
    shape = outside
    if packed:
        held = packed_rows(shapes, parts, blocks)
        mats = [shape((blocks // 2, held, LANES), BF16) for _ in range(2)]
        buffers = [pltpu.VMEM((blocks, held, LANES), BF16)]
    else:
        mats = [shape((height, columns // parts), BF16) for height, columns in shapes]
        buffers = []
    found = pl.pallas_call(
        functools.partial(inner_kernel, parts, blocks, packed, query_rows),
        name="inner_layer",
        in_specs=[pl.BlockSpec(memory_space=pltpu.SMEM)] + [vmem] * parts + [vmem, vmem, vmem, far, vmem,
                  far, vmem, far, vmem, far, vmem, far, far, vmem, vmem],
        out_specs=[vmem] * 3 + [anywhere if packed else vmem] * len(mats),
        out_shape=[
            shape((rows, width), BF16),
            shape((rows + 16, width), BF16),
            shape((16, max(hidden, POOL * width)), F32),
        ] + mats,
        scratch_shapes=[
            pltpu.VMEM((width, 3 * width), BF16),
            pltpu.VMEM((width, width), BF16),
            pltpu.VMEM((width, hidden), BF16),
            pltpu.VMEM((hidden, width), BF16),
            pltpu.VMEM((rows, width), F32),
            pltpu.VMEM((rows, width), BF16),
            pltpu.VMEM((rows, width), BF16),
            pltpu.VMEM((rows, width), BF16),
            pltpu.VMEM((width, rows), BF16),
            pltpu.VMEM((rows, width), BF16),
            pltpu.VMEM((width, rows), BF16),
            pltpu.VMEM((rows, width), BF16),
            pltpu.VMEM((rows // query_rows * quads, QUAD * query_rows), F32),
            pltpu.VMEM((rows, width), F32),
            pltpu.VMEM((rows, width), BF16),
            pltpu.VMEM((rows, hidden), BF16),
            pltpu.VMEM((rows, hidden), BF16),
            pltpu.VMEM((rows, width), F32),
            pltpu.VMEM((rows, hidden), BF16),
            pltpu.VMEM((rows, width), BF16),
            pltpu.VMEM((rows, width), BF16),
            pltpu.VMEM((rows, width), F32),
            pltpu.VMEM((rows, width), F32),
            pltpu.VMEM((quads, QUAD * HD, QUAD * query_rows), F32),
            pltpu.VMEM((quads, 1, QUAD * query_rows), F32),
            pltpu.VMEM((quads, 1, QUAD * query_rows), F32),
            pltpu.VMEM(raised_grad.shape, BF16),
            pltpu.VMEM(grad.shape, F32),
            pltpu.SemaphoreType.DMA((8,)),
        ]
        + buffers,
        compiler_params=pltpu.CompilerParams(vmem_limit_bytes=grant(60)),
        cost_estimate=cost(33),
    )(index, *shares, pool_b, gains, shifts, qkv_w, qkv_b, out_w, out_b, expand_w, expand_b, reduce_w,
      reduce_b, raised_grad, grad, far_away(jnp.asarray(cosine)), far_away(jnp.asarray(sine)))
    return found[0], found[1], found[2], found[3:], packed


def reversed_bits(value, size):
    found, bit = 0, 1
    while bit < size:
        found = found * 2 + (value // bit) % 2
        bit *= 2
    return found


def store_split(out, index, start, member, own_block, parts, blocks):
    columns = member.shape[1] // parts
    place = start
    for part in range(parts):
        spot = reversed_bits(jnp.bitwise_xor(index, part), parts)
        place = store_packed(
            out.at[spot],
            start,
            member[:, part * columns : (part + 1) * columns],
            own_block,
            blocks,
        )
    return place


def vector_tiles(entries, block, blocks):
    found = []
    for ref, row, length, scale in entries:
        size = length // blocks
        first, last = block * size // LANES, ((block + 1) * size - 1) // LANES
        found += [(ref, row, tile, scale) for tile in range(first, last + 1)]
    return found


def store_vectors(out, index, start, entries, own_block, parts, blocks):
    count = -(-len(vector_tiles(entries, 0, blocks)) // parts)
    for block in range(blocks):
        tiles = vector_tiles(entries, block, blocks)
        for part in range(parts):
            rows = [
                ref[row : row + 1, tile * LANES : (tile + 1) * LANES] * scale
                for ref, row, tile, scale in tiles[part * count : (part + 1) * count]
            ]
            rows += [jnp.zeros((16 - len(rows), LANES), F32)]
            spot = reversed_bits(jnp.bitwise_xor(index, part), parts)
            out[spot, spot_of(block, own_block, blocks), start : start + 16, :] = jnp.concatenate(
                rows, axis=0
            ).astype(BF16)


def split_lanes(split_ref, member):
    for lane in range(split_ref.shape[0]):
        split_ref[lane] = member[:, lane * LANES : (lane + 1) * LANES]


def joined_lanes(split_ref):
    return jnp.concatenate([split_ref[lane] for lane in range(split_ref.shape[0])], axis=1)


def add_third(split_ref, start, member):
    for lane in range(split_ref.shape[0]):
        rows = pl.ds(start, member.shape[0], stride=POOL)
        split_ref[lane, rows, :] = (
            split_ref[lane, rows, :] + member[:, lane * LANES : (lane + 1) * LANES]
        )


def raised_kernel(cot_ref, up_w_ref, joined_ref, grad_ref, sums_ref, split_ref):
    width = grad_ref.shape[1]
    split_lanes(split_ref, cot_ref[...].astype(F32))
    total = jnp.zeros(grad_ref.shape, F32)
    for slot in range(POOL):
        columns = slice(slot * width, (slot + 1) * width)
        rows = every_third(split_ref, slot, grad_ref.shape[0])
        sums_ref[:, columns] = jnp.sum(rows, axis=0, keepdims=True)
        rows = rows.astype(BF16)
        joined_ref[:, columns] = rows
        total += dot_nt(rows, up_w_ref[:, columns])
    grad_ref[...] = total


def raised_back(all_cot, up_w):
    length, width = all_cot.shape
    vmem = pl.BlockSpec(memory_space=pltpu.VMEM)
    shape = outside
    return pl.pallas_call(
        raised_kernel,
        name="raised_back",
        in_specs=[vmem] * 2,
        out_specs=[vmem] * 3,
        out_shape=[
            shape((length // POOL, POOL * width), BF16),
            shape((length // POOL, width), F32),
            shape((1, POOL * width), F32),
        ],
        scratch_shapes=[pltpu.VMEM((width // LANES, length, LANES), F32)],
        compiler_params=pltpu.CompilerParams(vmem_limit_bytes=grant(16, length // 1536)),
        cost_estimate=cost(4),
    )(all_cot, up_w)


def output_kernel(index_ref, lows_ref, low_ref, up_w_ref, up_b_ref, out_ref, split_ref):
    rows, width = out_ref.shape[1:]
    third = rows // POOL
    own = low_ref[pl.ds(pl.multiple_of(index_ref[0] * third, third), third), :]
    parts, chunk = lows_ref.shape[0], rows // 2
    found = []
    for which in range(2):
        place = 2 * index_ref[0] + which
        part = jnp.minimum(place, 2 * parts - 1 - place)
        start = jnp.where(place < parts, 0, chunk)
        found += [lows_ref[part, pl.ds(pl.multiple_of(start, chunk), chunk), :].astype(F32)]
    split_lanes(split_ref, jnp.concatenate(found, axis=0))
    for slot in range(POOL):
        columns = slice(slot * width, (slot + 1) * width)
        add_third(split_ref, slot, dot(own, up_w_ref[:, columns]) + up_b_ref[:, columns])
    out_ref[0] = joined_lanes(split_ref)


def raised_output(index, lows, low, up_w, up_b):
    rows, width = lows.shape[1:]
    vmem = pl.BlockSpec(memory_space=pltpu.VMEM)
    return pl.pallas_call(
        output_kernel,
        name="raised_output",
        in_specs=[pl.BlockSpec(memory_space=pltpu.SMEM)] + [vmem] * 4,
        out_specs=vmem,
        out_shape=jax.ShapeDtypeStruct((1, rows, width), F32),
        scratch_shapes=[pltpu.VMEM((width // LANES, rows, LANES), F32)],
        compiler_params=pltpu.CompilerParams(vmem_limit_bytes=grant(10)),
        cost_estimate=cost(3),
    )(index, lows, low, up_w, up_b)


def outer_hidden_kernel(
    parts,
    blocks,
    packed,
    index_ref,
    *rest,
):
    (
    lows_any,
    gz_any,
    inner_vec_ref,
    raised_vec_ref,
    cot_any,
    middle_in_any,
    active_any,
    rate_any,
    mixed_any,
    gains_ref,
    shifts_ref,
    pool_w_any,
    reduce_w_any,
    expand_w_any,
    out_w_any,
    ) = rest[:15]
    rest = rest[15:]
    outs = 4
    middle_any, go_ref, vec_ref = rest[:3]
    mats = rest[3 : 3 + outs]
    (
        pool_w,
        reduce_w,
        expand_w,
        out_w,
        split_ref,
        grad_ref,
        low_ref,
        second_ref,
        pre_ref,
        sum_ref,
        pooled_ref,
        lows_ref,
        gz_ref,
        middle_in_ref,
        active_ref,
        rate_ref,
        mixed_ref,
        middle_ref,
        att_ref,
        sems,
        *buffers,
    ) = rest[3 + outs :]
    index, own_block = index_ref[0], index_ref[1]
    rows, width = middle_in_ref.shape
    hidden_width = expand_w.shape[1]
    third = rows // POOL
    places = [chunk_of(index, which, parts) for which in range(2)]
    chunk = rows // 2
    coming = [(gz_any, gz_ref)] + [
        (
            cot_any.at[pl.ds(pl.multiple_of(place * chunk, chunk), chunk)],
            low_ref.at[which * chunk : (which + 1) * chunk],
        )
        for which, place in enumerate(places)
    ]
    coming += [
        (pool_w_any, pool_w),
        (rate_any, rate_ref),
        (reduce_w_any.at[0], reduce_w),
        (expand_w_any.at[0], expand_w),
        (middle_in_any, middle_in_ref),
        (active_any, active_ref),
        (out_w_any.at[0], out_w),
        (mixed_any, mixed_ref),
        (lows_any, lows_ref),
    ]
    coming = copy_in(coming, sems)
    moves = []
    half = third // 2
    coming[0].wait()
    tall = [
        gz_ref[pl.ds(pl.multiple_of(place * half, half), half + 16), :].astype(F32)
        for place in places
    ]
    here = jnp.concatenate([member[0:half] for member in tall], axis=0).astype(BF16)
    after = jnp.concatenate([member[1 : half + 1] for member in tall], axis=0).astype(BF16)

    coming[1].wait()
    coming[2].wait()
    split_lanes(split_ref, low_ref[...].astype(F32))
    coming[3].wait()
    add_third(split_ref, 0, dot_nt(here, pool_w[2 * width : 3 * width]))
    add_third(split_ref, 1, dot_nt(after, pool_w[0:width]))
    add_third(split_ref, 2, dot_nt(after, pool_w[width : 2 * width]))
    grad = joined_lanes(split_ref)
    grad_ref[...] = grad
    low_ref[...] = grad.astype(BF16)
    vec_ref[...] = jnp.zeros(vec_ref.shape, F32)

    def column_sum(row, member):
        vec_ref[row : row + 1, 0 : member.shape[1]] = jnp.sum(member, axis=0, keepdims=True)

    column_sum(3, low_ref[...].astype(F32))

    coming[7].wait()
    unit, inverse = unit_rows(middle_in_ref[...])
    second_ref[...] = (unit * gains_ref[0, 1:2] + shifts_ref[0, 1:2]).astype(BF16)
    sum_ref[...] = jnp.zeros(sum_ref.shape, F32)
    for move in coming[4:7] + coming[8:9]:
        move.wait()
    tiles = width // LANES

    def hidden_back(c, carry):
        columns = pl.ds(pl.multiple_of(c * width, width), width)
        pre = dot_nt(low_ref[...], reduce_w[columns, :]) * rate_ref[:, columns].astype(F32)
        low = pre.astype(BF16)
        vec_ref[2:3, columns] = jnp.sum(low.astype(F32), axis=0, keepdims=True)
        sum_ref[...] += dot_nt(low, expand_w[:, columns])
        reduce_grad = dot_tn(active_ref[:, columns], low_ref[...]).astype(BF16)
        expand_grad = dot_tn(second_ref[...], low).astype(BF16)
        if packed:
            out = buffers[0]
            height = hidden_width // blocks
            for part in range(parts):
                spot = reversed_bits(jnp.bitwise_xor(index, part), parts)
                for block in range(width // height):
                    place = spot_of(c * (width // height) + block, own_block, blocks)
                    out[spot, place, 0:height, :] = reduce_grad[
                        block * height : (block + 1) * height, part * LANES : (part + 1) * LANES
                    ]
            spot = reversed_bits(jnp.bitwise_xor(index, c), parts)
            store_packed(out.at[spot], height, expand_grad, own_block, blocks)
        else:
            mats[0][columns, :] = reduce_grad
            mats[1][:, columns] = expand_grad
        return carry

    lax.fori_loop(0, hidden_width // width, hidden_back, 0, unroll=True)
    grad_second = sum_ref[...]
    column_sum(0, grad_second * unit)
    column_sum(1, grad_second)
    grad_middle = grad_ref[...] + norm_back_rows(grad_second, unit, inverse, gains_ref[0, 1:2])
    middle_ref[...] = grad_middle
    moves += copy_in([(middle_ref, middle_any)], sems, 16)
    att_ref[...] = grad_middle.astype(BF16)
    column_sum(4, att_ref[...].astype(F32))
    coming[9].wait()
    coming[10].wait()
    go_ref[...] = dot_nt(att_ref[...], out_w[...]).astype(BF16)
    out_grad = dot_tn(mixed_ref[...], att_ref[...]).astype(BF16)
    if packed:
        place = hidden_width // blocks + tiles * (width // blocks)
        place = store_split(buffers[0], index, place, out_grad, own_block, parts, blocks)
        entries = early_entries(vec_ref, inner_vec_ref, raised_vec_ref, width, hidden_width, parts)
        store_vectors(buffers[0], index, place, entries, own_block, parts, blocks)
        moves += copy_in(halves_of(buffers[0], mats[0:2]), sems, 12)
    else:
        mats[2][...] = out_grad

    coming[11].wait()
    for part in range(parts):
        split_lanes(split_ref, lows_ref[part].astype(F32))
        for slot, first in ((0, 1), (1, 2), (2, 0)):
            found = every_third(split_ref, first, third).astype(BF16)
            for which in range(2):
                place = chunk_of(part, which, parts)
                own = slice(place * half, (place + 1) * half)
                pooled_ref[own, slot * width : (slot + 1) * width] = found[
                    which * half : (which + 1) * half
                ]
    shared = share_columns(gz_ref, index, parts).astype(F32)
    count = pooled_ref.shape[0]
    here, after = shared[0:count].astype(BF16), shared[1 : count + 1].astype(BF16)
    pool_grad = jnp.concatenate(
        [
            dot_tn(pooled_ref[:, slot * width : (slot + 1) * width], member).astype(BF16)
            for slot, member in ((0, after), (1, after), (2, here))
        ],
        axis=0,
    )
    if packed:
        store_packed(buffers[1], 0, pool_grad, own_block, blocks)
        moves += copy_in(halves_of(buffers[1], mats[2:4]), sems, 14)
    else:
        mats[3][...] = pool_grad
    for move in moves:
        move.wait()


def early_entries(vec_ref, inner_ref, raised_ref, width, hidden, parts):
    once = 1.0 / parts
    sizes = [width, width, width, width, 3 * width, width, hidden, width, width]
    return (
        [(vec_ref, 0, width, 1.0), (vec_ref, 1, width, 1.0), (vec_ref, 2, hidden, 1.0)]
        + [(vec_ref, 3, width, 1.0), (vec_ref, 4, width, 1.0)]
        + [(inner_ref, row, size, once) for row, size in enumerate(sizes)]
        + [(raised_ref, 0, POOL * width, once)]
    )


def late_entries(vec_ref, width):
    return [(vec_ref, 0, width, 1.0), (vec_ref, 1, width, 1.0), (vec_ref, 2, 3 * width, 1.0)]


def outer_hidden(index, lows, gz, inner_vecs, raised_vecs, cot, middle, active, rate, mixed, gains, shifts, pool_w, reduce_w, expand_w,
                 out_w, parts, blocks):
    rows, width = middle.shape
    lows, gz, cot, middle, active, rate, mixed = map(
        far_away, (lows, gz, cot, middle, active, rate, mixed)
    )
    hidden = expand_w.shape[2]
    shapes = [(hidden, width), (width, hidden), (width, width)]
    packed = can_pack(shapes + [(POOL * width, width)], parts, blocks) and hidden // parts == width and width // parts == LANES
    vmem = pl.BlockSpec(memory_space=pltpu.VMEM)
    far = pl.BlockSpec(memory_space=pltpu.HBM)
    shape = outside
    if packed:
        held = packed_rows(shapes, parts, blocks) + 16
        mats = [shape((parts // 2, blocks, held, LANES), BF16) for _ in range(2)]
        buffers = [pltpu.VMEM((parts, blocks, held, LANES), BF16)]
        added = packed_rows([(POOL * width, width)], parts, blocks)
        mats += [shape((blocks // 2, added, LANES), BF16) for _ in range(2)]
        buffers += [pltpu.VMEM((blocks, added, LANES), BF16)]
    else:
        mats = [shape(member, BF16) for member in shapes]
        mats += [shape((POOL * width, width // parts), BF16)]
        buffers = []
    found = pl.pallas_call(
        functools.partial(outer_hidden_kernel, parts, blocks, packed),
        name="outer_hidden",
        in_specs=[pl.BlockSpec(memory_space=pltpu.SMEM)] + [far] * 2 + [vmem] * 2 + [far] * 5 + [vmem] * 2 + [far] * 4,
        out_specs=[far] + [vmem] * 2 + [far if packed else vmem] * len(mats),
        out_shape=[
            shape((rows, width), F32),
            shape((rows, width), BF16),
            shape((8, hidden), F32),
        ] + mats,
        scratch_shapes=[
            pltpu.VMEM((POOL * width, width), BF16),
            pltpu.VMEM((hidden, width), BF16),
            pltpu.VMEM((width, hidden), BF16),
            pltpu.VMEM((width, width), BF16),
            pltpu.VMEM((width // LANES, rows, LANES), F32),
            pltpu.VMEM((rows, width), F32),
            pltpu.VMEM((rows, width), BF16),
            pltpu.VMEM((rows, width), BF16),
            pltpu.VMEM((rows, hidden), BF16),
            pltpu.VMEM((rows, width), F32),
            pltpu.VMEM((gz.shape[0] - 16, POOL * width), BF16),
            pltpu.VMEM(lows.shape, BF16),
            pltpu.VMEM(gz.shape, BF16),
            pltpu.VMEM((rows, width), F32),
            pltpu.VMEM((rows, hidden), BF16),
            pltpu.VMEM((rows, hidden), BF16),
            pltpu.VMEM((rows, width), BF16),
            pltpu.VMEM((rows, width), F32),
            pltpu.VMEM((rows, width), BF16),
            pltpu.SemaphoreType.DMA((17,)),
        ]
        + buffers,
        compiler_params=pltpu.CompilerParams(vmem_limit_bytes=grant(44 if packed else 60)),
        cost_estimate=cost(14),
    )(index, lows, gz, inner_vecs, raised_vecs, cot, middle, active, rate, mixed, gains, shifts, pool_w, reduce_w, expand_w, out_w)
    return found[:3], found[3:], packed, shapes


def store_rows(out, index, first, member, own_block, parts, blocks):
    rows, tiles = member.shape[0] // blocks, member.shape[1] // LANES
    share = rows // parts
    for part in range(parts):
        spot = reversed_bits(jnp.bitwise_xor(index, part), parts)
        for block in range(blocks):
            place = spot_of(block, own_block, blocks)
            start = block * rows + part * share
            for tile in range(tiles):
                out[spot, place, first + tile * share : first + (tile + 1) * share, :] = member[
                    start : start + share, tile * LANES : (tile + 1) * LANES
                ]
    return first + tiles * share


def outer_attention_kernel(
    parts,
    blocks,
    packed,
    quad,
    last,
    anchors,
    index_ref,
    ids_ref,
    emb_ref,
    gains_ref,
    shifts_ref,
    qkv_w_any,
    q_ref,
    k_ref,
    kt_ref,
    v_ref,
    o_ref,
    lse_ref,
    go_ref,
    cos_ref,
    sin_ref,
    *rest,
):
    given = (4 if last else 0) + anchors
    if last:
        middle_ref, sums_in_ref, first_ref, table_in_ref = rest[:4]
    outs = rest[given : given + 3]
    (qkv_w, gq_ref, gk_ref, gv_ref, code_ref, acc_ref, sems, *buffers) = rest[given + 3 :]
    index, own_block = index_ref[0], index_ref[1]
    rows, width = o_ref.shape
    vocab = emb_ref.shape[0]
    chunk = rows // 2
    wide = QUAD * HD
    lanes = slice(quad * wide, (quad + 1) * wide)
    moves = copy_in(
        [
            (
                qkv_w_any.at[0, :, part * width + quad * wide : part * width + (quad + 1) * wide],
                qkv_w.at[part],
            )
            for part in range(3)
        ],
        sems,
    )

    def block_of(j):
        if isinstance(j, int):
            return slice(j * rows, (j + 1) * rows)
        return pl.ds(pl.multiple_of(j * rows, rows), rows)

    def clear(j):
        gk_ref[block_of(j), :] = jnp.zeros((rows, wide), F32)
        gv_ref[block_of(j), :] = jnp.zeros((rows, wide), F32)

    def part_back(which, full):
        own_rows = slice(which * chunk, (which + 1) * chunk)
        place = chunk_of(index, which, parts)
        tall_q = quad_rows(q_ref[own_rows, lanes])
        tall_g = quad_rows(go_ref[own_rows, lanes])
        row = which * (width // wide) + quad
        lse = lse_ref[row : row + 1, :]
        delta = head_sums(o_ref[own_rows, lanes].astype(F32) * go_ref[own_rows, lanes].astype(F32))

        def one(j, masked):
            keys = block_of(j)
            scores = dot_nt(k_ref[keys, lanes], tall_q)
            if masked:
                scores = causal(scores, j * rows, place * chunk)
            add_k, add_v, add_q = back_block(
                scores, lse, delta, tall_q, tall_g, kt_ref[lanes, keys], v_ref[keys, lanes]
            )
            gk_ref[keys, :] += add_k
            gv_ref[keys, :] += add_v
            return add_q

        acc_ref[which] = one(full, True)

        def further(j):
            acc_ref[which] += one(j, False)

        each(full, further)
        gq_ref[own_rows, :] = quad_fold(acc_ref[which].T) * HD**-0.5

    def attend_back(full, seen):
        each(seen, clear)
        for which in range(2):
            part_back(which, full[which])

    by_blocks(index, parts, attend_back)

    codes = lax.broadcasted_iota(jnp.int32, (vocab, rows), 0)
    own_ids = own_lanes(jnp.broadcast_to(ids_ref[...], (8, ids_ref.shape[1])), index, parts, chunk)
    own_hot = (codes == own_ids[0:1]).astype(F32).astype(BF16)

    def own_rows_of(table):
        return jnp.concatenate(
            [
                table[pl.ds(pl.multiple_of(chunk_of(index, which, parts) * chunk, chunk), chunk), :]
                for which in range(2)
            ],
            axis=0,
        )

    turned = turn_rows(gq_ref[...], own_rows_of(cos_ref), -own_rows_of(sin_ref)).astype(BF16)
    code_ref[:, 0:wide] = dot(own_hot, turned)
    code_ref[:, wide : 3 * wide] = jnp.zeros((vocab, 2 * wide), F32)

    def by_code(j):
        columns = block_of(j)
        hot = (codes == ids_ref[:, columns]).astype(F32).astype(BF16)
        turned = turn_rows(gk_ref[columns, :], cos_ref[columns, :], -sin_ref[columns, :])
        code_ref[:, wide : 2 * wide] += dot(hot, turned.astype(BF16))
        code_ref[:, 2 * wide : 3 * wide] += dot(hot, gv_ref[columns, :].astype(BF16))

    by_blocks(index, parts, lambda full, seen: each(seen, by_code))
    code = code_ref[...]
    code_low = code.astype(BF16)
    unit, inverse = unit_rows(emb_ref[...].astype(F32))
    normed = (unit * gains_ref[0, 0:1] + shifts_ref[0, 0:1]).astype(BF16)
    qkv_grad = dot_tn(normed, code_low).astype(BF16)
    grad_table = jnp.zeros((vocab, width), F32)
    for part in range(3):
        moves[part].wait()
        grad_table += dot_nt(code_low[:, part * wide : (part + 1) * wide], qkv_w[part])
    vec_ref = outs[0]
    if last:
        vec_ref[...] = sums_in_ref[...]
    else:
        vec_ref[...] = jnp.zeros(vec_ref.shape, F32)
    for part in range(3):
        start = part * width + quad * wide
        vec_ref[2:3, start : start + wide] = jnp.sum(
            code[:, part * wide : (part + 1) * wide], axis=0, keepdims=True
        )
    if not last:
        outs[1][...] = qkv_grad
        outs[2][...] = grad_table
        return
    grad_table += table_in_ref[...]
    high = middle_ref[...].astype(BF16)
    low = (middle_ref[...] - high.astype(F32)).astype(BF16)
    embed = dot(own_hot, high) + dot(own_hot, low)
    embed = embed + norm_back_rows(grad_table, unit, inverse, gains_ref[0, 0:1])
    embed = embed.astype(BF16)
    vec_ref[0:1, 0:width] = jnp.sum(grad_table * unit, axis=0, keepdims=True)
    vec_ref[1:2, 0:width] = jnp.sum(grad_table, axis=0, keepdims=True)
    if packed:
        out = buffers[0]
        place = store_rows(out, index, 0, first_ref[...], own_block, parts, blocks)
        place = store_rows(out, index, place, qkv_grad, own_block, parts, blocks)
        place = store_split(out, index, place, embed, own_block, parts, blocks)
        store_vectors(out, index, place, late_entries(vec_ref, width), own_block, parts, blocks)
        for move in copy_in(halves_of(out, outs[1:]), sems, 3):
            move.wait()
    else:
        outs[1][...] = qkv_grad
        outs[2][...] = embed


def outer_attention(quad, index, all_ids, embedding, gains, shifts, qkv_w, queries, keys, keys_t, values,
                    mixed, lse, go, ending, anchors, parts, blocks):
    rows, width = queries.shape
    length = all_ids.shape[1]
    vocab = embedding.shape[0]
    chunk = rows // 2
    wide = QUAD * HD
    last = ending is not None
    packed = width % (16 * parts * blocks) == 0 and vocab % (16 * blocks) == 0
    packed = packed and width % (LANES * parts) == 0 and parts == 4
    cosine, sine = row_tables(length)
    vmem = pl.BlockSpec(memory_space=pltpu.VMEM)
    anywhere = pl.BlockSpec(memory_space=pl.ANY)
    far = pl.BlockSpec(memory_space=pltpu.HBM)
    shape = outside
    outs, buffers = [shape((8, 3 * width), F32)], []
    if not last:
        outs += [shape((width, 3 * wide), BF16), shape((vocab, width), F32)]
    elif packed:
        held = 3 * width // LANES * (width // blocks // parts)
        held += vocab // blocks * (width // parts // LANES) + 16
        outs += [shape((parts // 2, blocks, held, LANES), BF16) for _ in range(2)]
        buffers = [pltpu.VMEM((parts, blocks, held, LANES), BF16)]
    else:
        outs += [shape((width, 3 * wide), BF16), shape((vocab, width), BF16)]
    ending = list(ending) if last else []
    return pl.pallas_call(
        functools.partial(outer_attention_kernel, parts, blocks, packed, quad, last, len(anchors)),
        name="outer_attention",
        in_specs=[pl.BlockSpec(memory_space=pltpu.SMEM)]
        + [vmem] * 4
        + [far]
        + [vmem] * 9
        + [vmem] * len(ending)
        + [anywhere] * len(anchors),
        out_specs=[vmem] + [anywhere if buffers else vmem] * 2,
        out_shape=outs,
        scratch_shapes=[
            pltpu.VMEM((3, width, wide), BF16),
            pltpu.VMEM((rows, wide), F32),
            pltpu.VMEM((length, wide), F32),
            pltpu.VMEM((length, wide), F32),
            pltpu.VMEM((vocab, 3 * wide), F32),
            pltpu.VMEM((2, wide, QUAD * chunk), F32),
            pltpu.SemaphoreType.DMA((5,)),
        ]
        + buffers,
        compiler_params=pltpu.CompilerParams(vmem_limit_bytes=grant(34, length // (4 * rows))),
        cost_estimate=cost(14),
    )(index, all_ids, embedding, gains, shifts, qkv_w, queries, keys, keys_t, values, mixed, lse, go,
      far_away(jnp.asarray(cosine)), far_away(jnp.asarray(sine)), *ending, *map(far_away, anchors)), packed


def add_kernel(count, anchors, index_slices, *refs):
    sources, outs = refs[:count], refs[count + anchors :]
    for out, piece in zip(outs, index_slices):
        total = sources[0][piece].astype(F32)
        for source in sources[1:]:
            total += source[piece].astype(F32)
        out[...] = total.astype(BF16)


def add(sources, pieces, anchors=(), shape_of=jax.ShapeDtypeStruct):
    shape = sources[0].shape
    found, slices = [], []
    for piece in pieces:
        if isinstance(piece, int):
            found, slices = found + [shape[1:]], slices + [piece]
        else:
            *first, start, stop = piece
            found += [(stop - start, *shape[1 + len(first) :])]
            slices += [(*first, slice(start, stop))]
    vmem = pl.BlockSpec(memory_space=pltpu.VMEM)
    return list(pl.pallas_call(
        functools.partial(add_kernel, len(sources), len(anchors), slices),
        name="add",
        in_specs=[vmem] * len(sources) + [pl.BlockSpec(memory_space=pl.ANY)] * len(anchors),
        out_specs=[vmem] * len(found),
        out_shape=[shape_of(member, BF16) for member in found],
        compiler_params=pltpu.CompilerParams(vmem_limit_bytes=grant(16)),
        cost_estimate=cost(3),
    )(*sources, *map(far_away, anchors)))


def merge_kernel(plan, split, count, *refs):
    sources, outs = refs[:count], refs[len(refs) - split :]
    for spot in range(sources[0].shape[0]):
        out = outs[spot] if split > 1 else outs[0].at[spot]
        at = 0
        for rows, members in plan:
            total = sources[members[0][0]][spot, members[0][1] : members[0][1] + rows].astype(F32)
            for source, start in members[1:]:
                total += sources[source][spot, start : start + rows].astype(F32)
            out[at : at + rows, :] = total.astype(BF16)
            at += rows


def merge(sources, plan, split, anchors=()):
    count = sources[0].shape[0]
    rows = sum(member[0] for member in plan)
    vmem = pl.BlockSpec(memory_space=pltpu.VMEM)
    shapes = [(rows, LANES)] * count if split else [(count, rows, LANES)]
    return list(
        pl.pallas_call(
            functools.partial(merge_kernel, plan, len(shapes), len(sources)),
            name="merge",
            in_specs=[vmem] * len(sources) + [pl.BlockSpec(memory_space=pl.ANY)] * len(anchors),
            out_specs=[vmem] * len(shapes),
            out_shape=[jax.ShapeDtypeStruct(member, BF16) for member in shapes],
            compiler_params=pltpu.CompilerParams(vmem_limit_bytes=grant(16)),
            cost_estimate=cost(3),
        )(*sources, *map(far_away, anchors))
    )


def total_kernel(counts, *refs):
    out, start, at = refs[-1], 0, 0
    for count in counts:
        total = refs[at][...].astype(F32)
        for ref in refs[at + 1 : at + count]:
            total += ref[...].astype(F32)
        out[start : start + total.shape[0], :] = total.astype(BF16)
        start, at = start + total.shape[0], at + count


def totals(groups, anchors=()):
    rows = sum(group[0].shape[0] for group in groups)
    vmem = pl.BlockSpec(memory_space=pltpu.VMEM)
    members = [member for group in groups for member in group]
    return pl.pallas_call(
        functools.partial(total_kernel, [len(group) for group in groups]),
        name="totals",
        in_specs=[vmem] * len(members) + [pl.BlockSpec(memory_space=pl.ANY)] * len(anchors),
        out_specs=vmem,
        out_shape=jax.ShapeDtypeStruct((rows, LANES), BF16),
        compiler_params=pltpu.CompilerParams(vmem_limit_bytes=grant(8)),
        cost_estimate=cost(3),
    )(*members, *map(far_away, anchors))


def assemble_kernel(parts, blocks, index_ref, *rest):
    early, late, outs = rest[:parts], rest[parts : 2 * parts], rest[2 * parts :]
    index, own_block = index_ref[0], index_ref[1]
    (embed, gains, shifts, qkv_w, qkv_b, out_w, out_b, expand_w, expand_b, reduce_w, reduce_b) = outs[:11]
    pool_w, pool_b, up_w, up_b = outs[11:]

    def place(group, start, out, height, columns):
        tiles = columns // parts // LANES
        for at in range(parts):
            part = jnp.bitwise_xor(index, at)
            for tile in range(tiles):
                lanes = pl.ds(pl.multiple_of((part * tiles + tile) * LANES, LANES), LANES)
                found = group[at][start + tile * height : start + (tile + 1) * height]
                out[:, lanes] = found.astype(F32)
        return start + tiles * height

    start = 0
    for out in (reduce_w.at[1], expand_w.at[1], up_w, out_w.at[1], qkv_w.at[1]):
        start = place(early, start, out, *out.shape)
    for out in (reduce_w.at[0], expand_w.at[0], out_w.at[0]):
        start = place(early, start, out, *out.shape)
    early_start = start
    place(early, start + 16, pool_w, *pool_w.shape)
    height, wide = qkv_w.shape[1] // parts, QUAD * HD
    start = 0
    for quad in range(qkv_w.shape[2] // 3 // wide):
        for third in range(3):
            for tile in range(wide // LANES):
                lane = third * (qkv_w.shape[2] // 3) + quad * wide + tile * LANES
                for distance in range(parts):
                    part = jnp.bitwise_xor(index, distance)
                    rows = pl.ds(pl.multiple_of(part * height, height), height)
                    qkv_w[0, rows, lane : lane + LANES] = late[distance][
                        start : start + height
                    ].astype(F32)
                start += height
    late_start = place(late, start, embed, *embed.shape)

    def vectors(group, start, sizes):
        entries = [(None, 0, size * blocks, 1.0) for size in sizes]
        total = len(vector_tiles(entries, 0, blocks))
        count = -(-total // parts)
        tiles = {}
        for distance in range(parts):
            tiles[distance] = group[distance][start : start + 16].astype(F32)
        rows = []
        for number in range(total):
            row = jnp.zeros((1, LANES), F32)
            for distance in range(parts):
                here = jnp.bitwise_xor(index, distance) == number // count
                row = jnp.where(here, tiles[distance][number % count : number % count + 1], row)
            rows.append(row)
        found, number = [], 0
        for size in sizes:
            held = len(vector_tiles([(None, 0, size * blocks, 1.0)], 0, blocks))
            wide = jnp.concatenate(rows[number : number + held], axis=1)
            number += held
            if size % LANES != 0:
                shift = own_block * size % LANES
                wide = pltpu.roll(wide, (wide.shape[1] - shift) % wide.shape[1], 1)
            found.append(wide[:, :size])
        return found

    width_b, hidden_b, three_b = out_b.shape[1], expand_b.shape[1], qkv_b.shape[1]
    low = vectors(
        early,
        early_start,
        [width_b, width_b, hidden_b, width_b, width_b]
        + [width_b] * 4
        + [three_b, width_b, hidden_b, width_b, width_b, three_b],
    )
    high = vectors(late, late_start, [width_b, width_b, three_b])
    gains[0, 0:1], shifts[0, 0:1], qkv_b[0:1] = high
    gains[0, 1:2], shifts[0, 1:2], expand_b[0:1], reduce_b[0:1], out_b[0:1] = low[:5]
    gains[1, 0:1], gains[1, 1:2], shifts[1, 0:1], shifts[1, 1:2] = low[5:9]
    qkv_b[1:2], out_b[1:2], expand_b[1:2], reduce_b[1:2] = low[9:13]
    pool_b[...], up_b[...] = low[13:]


def assemble(index, gathered, late, width, hidden, vocab, parts, blocks):
    vmem = pl.BlockSpec(memory_space=pltpu.VMEM)
    part = width // blocks
    shapes = [
        (vocab // blocks, width),
        (2, 2, part),
        (2, 2, part),
        (2, part, 3 * width),
        (2, 3 * part),
        (2, part, width),
        (2, part),
        (2, part, hidden),
        (2, hidden // blocks),
        (2, hidden // blocks, width),
        (2, part),
        (POOL * part, width),
        (1, part),
        (part, POOL * width),
        (1, POOL * part),
    ]
    return pl.pallas_call(
        functools.partial(assemble_kernel, parts, blocks),
        name="assemble",
        in_specs=[pl.BlockSpec(memory_space=pltpu.SMEM)] + [vmem] * (2 * parts),
        out_specs=[vmem] * 15,
        out_shape=[jax.ShapeDtypeStruct(member, F32) for member in shapes],
        compiler_params=pltpu.CompilerParams(vmem_limit_bytes=grant(16)),
        cost_estimate=cost(4),
    )(index, *gathered, *late)


def pack(members, parts, blocks):
    rows = []
    for member in members:
        height, width = member.shape
        split = member.reshape(blocks, height // blocks, parts, width // parts)
        rows.append(split.transpose(2, 0, 1, 3).reshape(parts, blocks, -1))
    buffer = jnp.concatenate(rows, axis=2)
    order = [reversed_bits(spot, parts) for spot in range(parts)]
    index = lax.axis_index("seq")
    buffer = jnp.stack([buffer[jnp.bitwise_xor(index, other)] for other in order])
    return buffer.reshape(parts, blocks, -1, LANES)


def in_spots(buffer):
    blocks = buffer.shape[-3]
    index = lax.axis_index("batch")
    order = [spot * 2 % blocks + spot * 2 // blocks for spot in range(blocks)]
    return jnp.stack(
        [
            lax.dynamic_index_in_dim(buffer, jnp.bitwise_xor(index, other), -3, keepdims=False)
            for other in order
        ],
        axis=-3,
    )


def exchange(member, axis, distance):
    pairs = [(peer, peer ^ distance) for peer in range(lax.axis_size(axis))]
    return lax.ppermute(member, axis, pairs)


def seq_near(keep, send, anchors=()):
    half = keep.shape[1] // 2
    pieces = [(part, start, start + half) for part in range(2) for start in (half, 0)]
    return add([keep, exchange(send, "seq", 1)], pieces, anchors, outside)


def seq_far_send(quarters, beside=(), anchors=()):
    near, far = quarters[0], quarters[2]
    rows = near.shape[1]
    sources = [near, exchange(far, "seq", 2)]
    plan = [(rows, ((0, 0), (1, 0)))]
    if beside:
        sources, plan = sources + [beside[1]], plan + [(beside[1].shape[1], ((2, 0),))]
    return merge(sources, plan, False, anchors)[0]


def seq_far_keep(quarters, leaving, beside=(), others=(), anchors=()):
    near, far = quarters[1], quarters[3]
    rows = near.shape[1]
    if others:
        far = behind(far, *others)
    sources = [near, exchange(far, "seq", 2), exchange(leaving, "batch", 1)]
    plan = [(rows, ((0, 0), (1, 0), (2, 0)))]
    if beside:
        sources, plan = sources + [beside[0]], plan + [(beside[0].shape[1], ((3, 0), (2, rows)))]
    return merge(sources, plan, True, anchors)


def batch_halves(keep, send, anchors=()):
    return add([keep, exchange(send, "batch", 1)], list(range(keep.shape[0])), anchors)


def batch_rest(sums):
    return [sums[0]] + [
        exchange(sums[spot], "batch", 2 * spot) for spot in range(1, len(sums))
    ]


def plain_sums(buffer):
    level = 1
    while buffer.shape[0] > 1:
        half = buffer.shape[0] // 2
        got = exchange(buffer[half:], "seq", level)
        buffer = (buffer[:half].astype(F32) + got.astype(F32)).astype(BF16)
        level *= 2
    return plain_batch(buffer[0])


def plain_batch(buffer):
    half = buffer.shape[0] // 2
    got = exchange(buffer[half:], "batch", 1)
    sums = (buffer[:half].astype(F32) + got.astype(F32)).astype(BF16)
    total = sums[0].astype(F32)
    for spot in range(1, half):
        total += exchange(sums[spot], "batch", 2 * spot).astype(F32)
    return total.astype(BF16)


def behind(member, *others):
    return lax.optimization_barrier((member, *others))[0]


def seq_gather(member, *between):
    parts = lax.axis_size("seq")
    found, level = {0: member}, parts // 2
    while level >= 1:
        for distance, held in list(found.items()):
            found[distance ^ level] = exchange(held, "seq", level)
        if level == parts // 2 and between:
            found[level] = behind(found[level], *between)
        level //= 2
    return [found[distance] for distance in range(parts)]


def in_order(found):
    found = jnp.stack(found)
    index = lax.axis_index("seq")
    return jnp.stack([found[jnp.bitwise_xor(index, part)] for part in range(len(found))])


def unpack(gathered, shapes, blocks):
    parts = gathered.shape[0]
    gathered = gathered.reshape(parts, -1)
    found, start = [], 0
    for height, width in shapes:
        height, columns = height // blocks, width // parts
        piece = gathered[:, start : start + height * columns]
        piece = piece.reshape(parts, height, columns).transpose(1, 0, 2)
        start += height * columns
        found.append(piece.reshape(height, width).astype(F32))
    return found


def local(
    byte_ids,
    embedding,
    norm_gains,
    norm_biases,
    qkv_weights,
    qkv_biases,
    out_weights,
    out_biases,
    expand_weights,
    expand_biases,
    reduce_weights,
    reduce_biases,
    pool_weight,
    pool_bias,
    upsample_weight,
    upsample_bias,
    cotangent,
):
    parts, blocks = lax.axis_size("seq"), lax.axis_size("batch")
    rows, width, hidden = byte_ids.shape[1], embedding.shape[1], expand_weights.shape[2]
    index = jnp.stack([lax.axis_index("seq"), lax.axis_index("batch")]).astype(jnp.int32)
    ids = seq_gather(byte_ids)
    all_cot = lax.all_gather(cotangent[0], "seq", axis=0, tiled=True)

    (embedding, norm_gains, norm_biases, qkv_weights, qkv_biases, out_weights, out_biases) = (
        far_away(member)
        for member in (
            embedding, norm_gains, norm_biases, qkv_weights, qkv_biases, out_weights, out_biases
        )
    )
    (expand_weights, expand_biases, reduce_weights, reduce_biases, pool_weight) = (
        far_away(member)
        for member in (expand_weights, expand_biases, reduce_weights, reduce_biases, pool_weight)
    )
    (pool_bias, upsample_weight, upsample_bias) = (
        far_away(member) for member in (pool_bias[None], upsample_weight, upsample_bias[None])
    )

    coarse, fine = byte_table(embedding, norm_gains, norm_biases, qkv_weights, qkv_biases)
    h1_low, share, queries, keys, keys_t, values, mixed, lse, middle, active, rate, all_ids = outer_forward(
        index, ids, embedding, norm_gains, norm_biases, coarse, fine, out_weights, out_biases,
        expand_weights, expand_biases, reduce_weights, reduce_biases, pool_weight, rows
    )
    raised_grad, grad_short, raised_sums = raised_back(all_cot, upsample_weight)
    shares = seq_gather(share, raised_sums)
    short_low, gz, inner_vecs, inner_found, inner_packed = inner_layer(
        index, shares, pool_bias, norm_gains, norm_biases, qkv_weights, qkv_biases,
        out_weights, out_biases, expand_weights, expand_biases, reduce_weights, reduce_biases,
        raised_grad, grad_short, parts, blocks
    )
    lows = lax.all_gather(behind(h1_low, shares[-1]), "seq", axis=0)
    output = raised_output(index, lows, short_low, upsample_weight, upsample_bias)

    (grad_middle, grad_mixed, hidden_vecs), early, early_packed, early_shapes = outer_hidden(
        index, lows, gz, inner_vecs, raised_sums, all_cot, middle, active, rate, mixed, norm_gains,
        norm_biases, pool_weight, reduce_weights, expand_weights, out_weights, parts, blocks
    )

    def attention_back(quad, ending, anchors):
        return outer_attention(
            quad, index, all_ids, embedding, norm_gains, norm_biases, qkv_weights, queries, keys,
            keys_t, values, mixed, lse, grad_mixed, ending, anchors, parts, blocks
        )

    anchors = []
    packed = inner_packed and early_packed
    if packed:
        quarters = seq_near(*early[0:2], [output])
        inner_sums = batch_halves(*inner_found, quarters[:1])
        anchors = inner_sums + quarters
    ending, late_packed = attention_back(0, None, anchors)
    if packed:
        leaving = seq_far_send(quarters, early[2:4], ending[:1])
        inner_rest = batch_rest(inner_sums)
        anchors = [inner_rest[1], leaving]
    (table_vecs, *late), _ = attention_back(1, [grad_middle] + list(ending), anchors)
    if packed and late_packed:
        early_sums = seq_far_keep(quarters, leaving, early[2:4], ending[:1])
        late_quarters = seq_near(*late, early_sums[:1])
        late_sums = seq_far_keep(late_quarters, seq_far_send(late_quarters))
        gathered = seq_gather(totals([[totals([inner_rest])], batch_rest(early_sums)]))
        late_total = totals([batch_rest(late_sums)])
        found = list(
            assemble(index, gathered, seq_gather(late_total), width, hidden, embedding.shape[0], parts, blocks)
        )
        found[12], found[14] = found[12][0], found[14][0]
        return (output, *found)

    inner_shapes = inner_shapes_of(width, hidden)
    inner_buffer = jnp.concatenate([member.reshape(blocks, -1) for member in inner_found], axis=1)
    inner_buffer = in_spots(inner_buffer.reshape(blocks, -1, LANES))
    inner_out = unpack(in_order(seq_gather(plain_batch(inner_buffer))), inner_shapes, blocks)
    pool_buffer = in_spots(early[3].reshape(blocks, -1, LANES))
    pool_out = unpack(
        in_order(seq_gather(plain_batch(pool_buffer))), [(POOL * width, width)], blocks
    )
    early_buffer = in_spots(pack(early[:3], parts, blocks))
    early_out = unpack(
        in_order(seq_gather(plain_sums(early_buffer))), early_shapes, blocks
    )
    wide = QUAD * HD
    qkv_grad = jnp.concatenate(
        [
            half[:, part * wide : (part + 1) * wide]
            for part in range(3)
            for half in (ending[1], late[0])
        ],
        axis=1,
    )
    late, late_shapes = [qkv_grad, late[1]], [qkv_grad.shape, late[1].shape]
    late_buffer = in_spots(pack(late, parts, blocks))
    late_out = unpack(
        in_order(seq_gather(plain_sums(late_buffer))), late_shapes, blocks
    )
    once = 1.0 / parts
    vectors = [
        table_vecs[0, :width],
        hidden_vecs[0, :width],
        table_vecs[1, :width],
        hidden_vecs[1, :width],
        table_vecs[2, : 3 * width],
        hidden_vecs[4, :width],
        hidden_vecs[2, :hidden],
        hidden_vecs[3, :width],
        inner_vecs[0, :width] * once,
        inner_vecs[1, :width] * once,
        inner_vecs[2, :width] * once,
        inner_vecs[3, :width] * once,
        inner_vecs[4, : 3 * width] * once,
        inner_vecs[5, :width] * once,
        inner_vecs[6, :hidden] * once,
        inner_vecs[7, :width] * once,
        inner_vecs[8, :width] * once,
        raised_sums[0] * once,
    ]
    flat = jnp.concatenate([member.reshape(blocks, -1) for member in vectors], axis=1)
    flat = lax.psum(flat.astype(BF16), ("seq", "batch")).astype(F32)
    flat = lax.dynamic_index_in_dim(flat, lax.axis_index("batch"), 0, keepdims=False)
    sums, start = [], 0
    for member in vectors:
        sums.append(flat[start : start + member.shape[0] // blocks])
        start += member.shape[0] // blocks
    return (
        output,
        late_out[1],
        jnp.stack([jnp.stack([sums[0], sums[1]]), jnp.stack([sums[8], sums[9]])]),
        jnp.stack([jnp.stack([sums[2], sums[3]]), jnp.stack([sums[10], sums[11]])]),
        jnp.stack([late_out[0], inner_out[4]]),
        jnp.stack([sums[4], sums[12]]),
        jnp.stack([early_out[2], inner_out[3]]),
        jnp.stack([sums[5], sums[13]]),
        jnp.stack([early_out[1], inner_out[1]]),
        jnp.stack([sums[6], sums[14]]),
        jnp.stack([early_out[0], inner_out[0]]),
        jnp.stack([sums[7], sums[15]]),
        pool_out[0],
        sums[16],
        inner_out[2],
        sums[17],
    )


def solution(mesh):
    whole = P()
    return jax.shard_map(
        local,
        mesh=mesh,
        in_specs=(P("batch", "seq"),) + (whole,) * 15 + (P("batch", "seq", None),),
        out_specs=(
            P("batch", "seq", None),
            P("batch", None),
            P(None, None, "batch"),
            P(None, None, "batch"),
            P(None, "batch", None),
            P(None, "batch"),
            P(None, "batch", None),
            P(None, "batch"),
            P(None, "batch", None),
            P(None, "batch"),
            P(None, "batch", None),
            P(None, "batch"),
            P("batch", None),
            P("batch"),
            P("batch", None),
            P("batch"),
        ),
        check_vma=False,
    )
```

```python
import functools

import jax
import jax.numpy as jnp
import numpy as np
from jax import lax
from jax.experimental import pallas as pl
from jax.experimental.pallas import tpu as pltpu
from jax.sharding import PartitionSpec as P

HD = 64
POOL = 3
QUAD = 4
LANES = 128
VMEM_LIMIT = 60 * 1024 * 1024
F32 = jnp.float32
BF16 = jnp.bfloat16


def dot(left, right):
    return jnp.dot(left, right, preferred_element_type=F32)


def dot_nt(left, right):
    return lax.dot_general(left, right, (((1,), (1,)), ((), ())), preferred_element_type=F32)


def dot_tn(left, right):
    return lax.dot_general(left, right, (((0,), (0,)), ((), ())), preferred_element_type=F32)


def gelu_parts(pre):
    slope = 0.7978845608028654
    square = pre * pre
    bent = jnp.tanh(slope * pre * (1.0 + 0.044715 * square))
    half = 0.5 * (1.0 + bent)
    value = pre * half
    rate = half + 0.5 * pre * (1.0 - bent * bent) * (slope * (1.0 + 3.0 * 0.044715 * square))
    return (value, rate)


def angle_rows(length):
    frequency = 10000.0 ** (-np.arange(HD // 2, dtype=np.float64) / (HD // 2))
    angles = np.arange(length, dtype=np.float64)[:, None] * frequency[None, :]
    return (np.cos(angles).astype(np.float32), np.sin(angles).astype(np.float32))


def cost(microseconds):
    microseconds *= 10
    return pl.CostEstimate(
        flops=int(microseconds * 1e9), bytes_accessed=int(microseconds * 1e6), transcendentals=0
    )


def grant(megabytes, factor=1):
    return min(int(megabytes * factor), 60) * 1024 * 1024


def outside(shape, dtype):
    return pltpu.HBM(shape, dtype)


def far_away(member):
    return pltpu.with_memory_space_constraint(member, pltpu.HBM)


def copy_in(pairs, sems, start=0):
    moves = [
        pltpu.make_async_copy(src, dst, sems.at[start + i]) for i, (src, dst) in enumerate(pairs)
    ]
    for move in moves:
        move.start()
    return moves


def chunk_of(index, which, parts):
    return index + which * (2 * parts - 1 - 2 * index)


def by_blocks(index, parts, body):
    if parts != 4:
        full = [chunk_of(index, which, parts) // 2 for which in range(2)]
        body(full, full[1] + 1)
        return

    @pl.when(index < 2)
    def _():
        body([0, 3], 4)

    @pl.when(index >= 2)
    def _():
        body([1, 2], 3)


def each(count, step):
    if isinstance(count, int):
        for i in range(count):
            step(i)
    else:
        lax.fori_loop(0, count, lambda i, carry: (step(i), carry)[1], 0)


def own_lanes(row, index, parts, chunk):
    length = row.shape[1]
    return jnp.concatenate(
        [
            pltpu.roll(row, (length - chunk_of(index, which, parts) * chunk) % length, 1)[:, :chunk]
            for which in range(2)
        ],
        axis=1,
    )


def quad_rows(rows):
    lane = lax.broadcasted_iota(jnp.int32, rows.shape, 1) // HD
    zero = jnp.zeros_like(rows)
    return jnp.concatenate([jnp.where(lane == head, rows, zero) for head in range(QUAD)], axis=0)


def quad_fold(tall):
    count = tall.shape[0] // QUAD
    lane = lax.broadcasted_iota(jnp.int32, (count, tall.shape[1]), 1) // HD
    folded = jnp.zeros((count, tall.shape[1]), tall.dtype)
    for head in range(QUAD):
        folded = jnp.where(lane == head, tall[head * count : (head + 1) * count], folded)
    return folded


def lanes_of(quad):
    return slice(quad * QUAD * HD, (quad + 1) * QUAD * HD)


def causal(scores, key_start, query_start):
    count = scores.shape[1] // QUAD
    key = key_start + lax.broadcasted_iota(jnp.int32, scores.shape, 0)
    query = lax.broadcasted_iota(jnp.int32, (1, scores.shape[1]), 1)
    for head in range(1, QUAD):
        query = jnp.where(query >= count, query - count, query)
    return jnp.where(key <= query + query_start, scores, -1e30)


def flash_quads(tall_q, keys_at, values_at, full, key_start_last, query_start, state):
    quads = range(len(tall_q))
    acc, peak, total = state

    def scores_of(j):
        return [dot_nt(keys_at(j, quad), tall_q[quad]) for quad in quads]

    scores = [causal(member, key_start_last, query_start) for member in scores_of(full)]
    tops = [jnp.max(member, axis=0, keepdims=True) for member in scores]
    raised = [jnp.exp(scores[quad] - tops[quad]) for quad in quads]
    for quad in quads:
        peak[quad] = tops[quad]
        total[quad] = jnp.sum(raised[quad], axis=0, keepdims=True)
        acc[quad] = dot(values_at(full, quad), raised[quad].astype(BF16))

    def block(j):
        scores = scores_of(j)
        tops = [
            jnp.maximum(peak[quad], jnp.max(scores[quad], axis=0, keepdims=True)) for quad in quads
        ]
        raised = [jnp.exp(scores[quad] - tops[quad]) for quad in quads]
        for quad in quads:
            shrink = jnp.exp(peak[quad] - tops[quad])
            peak[quad] = tops[quad]
            total[quad] = total[quad] * shrink + jnp.sum(raised[quad], axis=0, keepdims=True)
            acc[quad] = acc[quad] * shrink + dot(values_at(j, quad), raised[quad].astype(BF16))

    each(full, block)
    return [
        (quad_fold((acc[quad] / total[quad]).T), peak[quad] + jnp.log(total[quad]))
        for quad in quads
    ]


def every_third(split_ref, start, count):
    return jnp.concatenate(
        [split_ref[i, pl.ds(start, count, stride=POOL), :] for i in range(split_ref.shape[0])],
        axis=1,
    )


def unit_rows(stream):
    centred = stream - jnp.mean(stream, axis=-1, keepdims=True)
    inverse = lax.rsqrt(jnp.mean(centred * centred, axis=-1, keepdims=True) + 1e-05)
    return (centred * inverse, inverse)


def table_kernel(emb_ref, gains_ref, shifts_ref, qkv_w_any, qkv_b_ref, coarse_ref, fine_ref, qkv_w, sems):
    width = emb_ref.shape[1]
    moves = copy_in([(qkv_w_any.at[0], qkv_w)], sems)
    unit, _ = unit_rows(emb_ref[...].astype(F32))
    normed = (unit * gains_ref[0, 0:1] + shifts_ref[0, 0:1]).astype(BF16)
    moves[0].wait()
    table = (dot(normed, qkv_w[...]) + qkv_b_ref[0:1]).T
    coarse = table.astype(BF16)
    coarse_ref[...] = coarse
    fine_ref[...] = (table[: 2 * width] - coarse[: 2 * width].astype(F32)).astype(BF16)


def byte_table(embedding, gains, shifts, qkv_w, qkv_b):
    vocab, width = embedding.shape
    vmem = pl.BlockSpec(memory_space=pltpu.VMEM)
    far = pl.BlockSpec(memory_space=pltpu.HBM)
    return pl.pallas_call(
        table_kernel,
        name="byte_table",
        in_specs=[vmem, vmem, vmem, far, vmem],
        out_specs=[vmem, vmem],
        out_shape=[
            jax.ShapeDtypeStruct((3 * width, vocab), BF16),
            jax.ShapeDtypeStruct((2 * width, vocab), BF16),
        ],
        scratch_shapes=[pltpu.VMEM((width, 3 * width), BF16), pltpu.SemaphoreType.DMA((1,))],
        compiler_params=pltpu.CompilerParams(vmem_limit_bytes=grant(16)),
        cost_estimate=cost(4),
    )(embedding, gains, shifts, qkv_w, qkv_b)


def outer_forward_kernel(
    parts,
    index_ref,
    *rest,
):
    ids, rest = rest[:parts], rest[parts:]
    (
    emb_ref,
    gains_ref,
    shifts_ref,
    coarse_any,
    fine_any,
    out_w_any,
    out_b_ref,
    expand_w_any,
    expand_b_ref,
    reduce_w_any,
    reduce_b_ref,
    pool_w_any,
    cos_ref,
    sin_ref,
    low_ref,
    share_ref,
    q_any,
    k_any,
    kt_any,
    v_any,
    o_any,
    lse_ref,
    middle_any,
    active_any,
    rate_any,
    ids_ref,
    q_ref,
    k_ref,
    kt_ref,
    v_ref,
    o_ref,
    middle_ref,
    active_ref,
    rate_ref,
    out_w,
    expand_w,
    reduce_w,
    pool_w,
    coarse_ref,
    fine_ref,
    vt_ref,
    acc_ref,
    peak_ref,
    total_ref,
    second_ref,
    sum_ref,
    later_ref,
    split_ref,
    sems,
    ) = rest
    index = index_ref[0]
    rows, width = middle_ref.shape
    vocab = emb_ref.shape[0]
    chunk = rows // 2
    moves = copy_in(
        [
            (coarse_any, coarse_ref),
            (fine_any, fine_ref),
            (out_w_any.at[0], out_w),
            (expand_w_any.at[0], expand_w),
            (reduce_w_any.at[0], reduce_w),
            (pool_w_any, pool_w),
        ],
        sems,
    )

    for distance in range(parts):
        part = jnp.bitwise_xor(index, distance)
        ids_ref[:, pl.ds(pl.multiple_of(part * rows, rows), rows)] = ids[distance][...]
    moves[0].wait()
    moves[1].wait()

    def picked(start, hot):
        return dot(coarse_ref[start : start + width], hot) + dot(
            fine_ref[start : start + width], hot
        )

    def turned(member, cosine, sine):
        pieces = []
        for head in range(width // HD):
            first = member[head * HD : head * HD + HD // 2]
            second = member[head * HD + HD // 2 : (head + 1) * HD]
            pieces += [first * cosine - second * sine, first * sine + second * cosine]
        return jnp.concatenate(pieces, axis=0)

    codes = lax.broadcasted_iota(jnp.int32, (vocab, rows), 0)

    def block_of(j):
        if isinstance(j, int):
            return slice(j * rows, (j + 1) * rows)
        return pl.ds(pl.multiple_of(j * rows, rows), rows)

    def key_block(j):
        columns = block_of(j)
        hot = (codes == ids_ref[:, columns]).astype(F32).astype(BF16)
        keys = turned(picked(width, hot), cos_ref[:, columns], sin_ref[:, columns])
        kt_ref[:, columns] = keys.astype(BF16)
        k_ref[columns, :] = keys.T.astype(BF16)
        values = dot(coarse_ref[2 * width : 3 * width], hot)
        vt_ref[:, columns] = values.astype(BF16)
        v_ref[columns, :] = values.T.astype(BF16)

    by_blocks(index, parts, lambda full, seen: each(seen, key_block))
    moves += copy_in([(k_ref, k_any), (kt_ref, kt_any), (v_ref, v_any)], sems, 6)
    own_ids = own_lanes(jnp.broadcast_to(ids_ref[...], (8, ids_ref.shape[1])), index, parts, chunk)
    own = (codes == own_ids[0:1]).astype(F32)
    queries = turned(
        picked(0, own.astype(BF16)),
        own_lanes(cos_ref[...], index, parts, chunk),
        own_lanes(sin_ref[...], index, parts, chunk),
    )
    q_ref[...] = (queries * HD**-0.5).T.astype(BF16)
    middle_ref[...] = dot(own.T.astype(BF16), emb_ref[...])

    quads = width // (QUAD * HD)

    def attend(full, seen):
        for which in range(2):
            own_rows = slice(which * chunk, (which + 1) * chunk)
            place = chunk_of(index, which, parts)
            found = flash_quads(
                [quad_rows(q_ref[own_rows, lanes_of(quad)]) for quad in range(quads)],
                lambda j, quad: k_ref[block_of(j), lanes_of(quad)],
                lambda j, quad: vt_ref[lanes_of(quad), block_of(j)],
                full[which],
                full[which] * rows,
                place * chunk,
                (acc_ref.at[which], peak_ref.at[which], total_ref.at[which]),
            )
            for quad, (mixed, lse) in enumerate(found):
                o_ref[own_rows, lanes_of(quad)] = mixed.astype(BF16)
                row = which * quads + quad
                lse_ref[row : row + 1, :] = lse

    by_blocks(index, parts, attend)

    moves += copy_in([(q_ref, q_any), (o_ref, o_any)], sems, 9)
    moves[2].wait()
    middle = middle_ref[...] + dot(o_ref[...], out_w[...]) + out_b_ref[0:1]
    middle_ref[...] = middle
    moves += copy_in([(middle_ref, middle_any)], sems, 11)
    unit, _ = unit_rows(middle)
    second_ref[...] = (unit * gains_ref[0, 1:2] + shifts_ref[0, 1:2]).astype(BF16)
    sum_ref[...] = middle + reduce_b_ref[0:1]
    moves[3].wait()
    moves[4].wait()

    for c in range(expand_w.shape[1] // width):
        columns = slice(c * width, (c + 1) * width)
        pre = dot(second_ref[...], expand_w[:, columns]) + expand_b_ref[0:1, columns]
        value, rate = gelu_parts(pre)
        value = value.astype(BF16)
        active_ref[:, columns] = value
        rate_ref[:, columns] = rate.astype(BF16)
        moves += copy_in(
            [
                (active_ref.at[:, columns], active_any.at[:, columns]),
                (rate_ref.at[:, columns], rate_any.at[:, columns]),
            ],
            sems,
            12 + 2 * c,
        )
        sum_ref[...] += dot(value, reduce_w[columns, :])
    low_ref[...] = sum_ref[...].astype(BF16)

    moves[5].wait()
    third = rows // POOL

    for lane in range(width // LANES):
        split_ref[lane] = sum_ref[:, lane * LANES : (lane + 1) * LANES]

    def thirds(start):
        return every_third(split_ref, start, third).astype(BF16)

    later = dot(thirds(1), pool_w[0:width]) + dot(thirds(2), pool_w[width : 2 * width])
    same = dot(thirds(0), pool_w[2 * width : 3 * width])
    half = third // 2
    for which in range(2):
        start = which * (half + 8)
        later_ref[start : start + 8] = jnp.zeros((8, width), F32)
        later_ref[start + half : start + half + 8] = jnp.zeros((8, width), F32)
        later_ref[start + 1 : start + half + 1] = later[which * half : (which + 1) * half]
        share_ref[start : start + half] = (
            later_ref[start : start + half] + same[which * half : (which + 1) * half]
        ).astype(BF16)
        share_ref[start + half : start + half + 8] = later_ref[
            start + half : start + half + 8
        ].astype(BF16)
    for move in moves[6:]:
        move.wait()


def outer_forward(index, ids, embedding, gains, shifts, coarse, fine, out_w, out_b, expand_w,
                  expand_b, reduce_w, reduce_b, pool_w, rows):
    length = rows * len(ids)
    vocab, width = embedding.shape
    hidden = expand_w.shape[2]
    chunk, quads = rows // 2, width // (QUAD * HD)
    cosine, sine = angle_rows(length)
    vmem = pl.BlockSpec(memory_space=pltpu.VMEM)
    far = pl.BlockSpec(memory_space=pltpu.HBM)
    shape = outside
    third = rows // POOL
    kept = [
        shape((rows, width), BF16),
        shape((length, width), BF16),
        shape((width, length), BF16),
        shape((length, width), BF16),
        shape((rows, width), BF16),
        shape((rows, width), F32),
        shape((rows, hidden), BF16),
        shape((rows, hidden), BF16),
    ]
    return pl.pallas_call(
        functools.partial(outer_forward_kernel, length // rows),
        name="outer_forward",
        in_specs=[pl.BlockSpec(memory_space=pltpu.SMEM)] + [vmem] * (len(ids) + 3) + [far, far,
                  far, vmem, far, vmem, far, vmem, far, vmem, vmem],
        out_specs=[vmem] * 2 + [far] * 5 + [vmem] + [far] * 3 + [vmem],
        out_shape=[
            shape((rows, width), BF16),
            shape((third + 16, width), BF16),
        ]
        + kept[:5]
        + [shape((2 * quads, QUAD * chunk), F32)]
        + kept[5:]
        + [shape((1, length), jnp.int32)],
        scratch_shapes=[pltpu.VMEM(member.shape, member.dtype) for member in kept]
        + [
            pltpu.VMEM((width, width), BF16),
            pltpu.VMEM((width, hidden), BF16),
            pltpu.VMEM((hidden, width), BF16),
            pltpu.VMEM((POOL * width, width), BF16),
            pltpu.VMEM((3 * width, vocab), BF16),
            pltpu.VMEM((2 * width, vocab), BF16),
            pltpu.VMEM((width, length), BF16),
            pltpu.VMEM((2, quads, QUAD * HD, QUAD * chunk), F32),
            pltpu.VMEM((2, quads, 1, QUAD * chunk), F32),
            pltpu.VMEM((2, quads, 1, QUAD * chunk), F32),
            pltpu.VMEM((rows, width), BF16),
            pltpu.VMEM((rows, width), F32),
            pltpu.VMEM((third + 16, width), F32),
            pltpu.VMEM((width // LANES, rows, LANES), F32),
            pltpu.SemaphoreType.DMA((12 + 2 * (hidden // width),)),
        ],
        compiler_params=pltpu.CompilerParams(vmem_limit_bytes=grant(48 if length == 4 * rows else 60)),
        cost_estimate=cost(30),
    )(index, *ids, embedding, gains, shifts, coarse, fine, out_w, out_b, expand_w, expand_b,
      reduce_w, reduce_b, pool_w, far_away(jnp.asarray(cosine.T)), far_away(jnp.asarray(sine.T)))


def turn_rows(member, cosine, sine):
    pieces = []
    for start in range(0, member.shape[1], LANES):
        tile = member[:, start : start + LANES]
        lane = lax.broadcasted_iota(jnp.int32, tile.shape, 1) % HD
        other = jnp.where(
            lane < HD // 2,
            pltpu.roll(tile, LANES - HD // 2, 1),
            pltpu.roll(tile, HD // 2, 1),
        )
        pieces.append(tile * cosine + other * sine)
    return jnp.concatenate(pieces, axis=1)


def norm_back_rows(grad, unit, inverse, gain):
    scaled = grad * gain
    mean_one = jnp.mean(scaled, axis=-1, keepdims=True)
    mean_two = jnp.mean(scaled * unit, axis=-1, keepdims=True)
    return inverse * (scaled - mean_one - unit * mean_two)


def head_sums(product):
    tall = product.T
    return jnp.concatenate(
        [
            jnp.sum(tall[head * HD : (head + 1) * HD], axis=0, keepdims=True)
            for head in range(QUAD)
        ],
        axis=1,
    )


def back_block(scores, lse, delta, tall_q, tall_g, keys_t, values):
    probs = jnp.exp(scores - lse)
    low = (probs * (dot_nt(values, tall_g) - delta)).astype(BF16)
    return (dot(low, tall_q), dot(probs.astype(BF16), tall_g), dot(keys_t, low))


def share_columns(member_ref, index, parts):
    width = member_ref.shape[1] // parts
    if width % LANES == 0:
        return member_ref[:, pl.ds(pl.multiple_of(index * width, LANES), width)]
    full = member_ref.shape[1]
    row = lax.broadcasted_iota(jnp.int32, (full, width), 0)
    column = lax.broadcasted_iota(jnp.int32, (full, width), 1)
    picks = (row == column + index * width).astype(F32).astype(BF16)
    return dot(member_ref[...], picks).astype(BF16)


def can_pack(shapes, parts, blocks):
    return parts == 4 and all(
        rows % (16 * blocks) == 0 and columns % (LANES * parts) == 0 for rows, columns in shapes
    )


def packed_rows(shapes, parts, blocks):
    return sum(rows // blocks * (columns // parts // LANES) for rows, columns in shapes)


def spot_of(block, own_block, blocks):
    distance = jnp.bitwise_xor(own_block, block)
    return distance % 2 * (blocks // 2) + distance // 2


def store_packed(out, start, member, own_block, blocks):
    rows, columns = member.shape[0] // blocks, member.shape[1]
    for block in range(blocks):
        spot = spot_of(block, own_block, blocks)
        for tile in range(columns // LANES):
            out[spot, start + tile * rows : start + (tile + 1) * rows, :] = member[
                block * rows : (block + 1) * rows, tile * LANES : (tile + 1) * LANES
            ]
    return start + rows * (columns // LANES)


def inner_kernel(
    parts,
    blocks,
    packed,
    query_rows,
    index_ref,
    *rest,
):
    shares, rest = rest[:parts], rest[parts:]
    (
    pool_b_ref,
    gains_ref,
    shifts_ref,
    qkv_w_any,
    qkv_b_ref,
    out_w_any,
    out_b_ref,
    expand_w_any,
    expand_b_ref,
    reduce_w_any,
    reduce_b_ref,
    raised_grad_any,
    grad_any,
    cos_ref,
    sin_ref,
    ) = rest[:15]
    rest = rest[15:]
    outs = 2 if packed else 5
    low_ref, gz_ref, vec_ref = rest[:3]
    mats = rest[3 : 3 + outs]
    (
        qkv_w,
        out_w,
        expand_w,
        reduce_w,
        stream_ref,
        normed_ref,
        q_ref,
        k_ref,
        kt_ref,
        v_ref,
        vt_ref,
        o_ref,
        lse_ref,
        middle_ref,
        second_ref,
        active_ref,
        rate_ref,
        sum_ref,
        pre_ref,
        att_ref,
        go_ref,
        gk_ref,
        gv_ref,
        acc_ref,
        peak_ref,
        total_ref,
        raised_grad_ref,
        grad_ref,
        sems,
        *buffers,
    ) = rest[3 + outs :]
    index, own_block = index_ref[0], index_ref[1]
    rows, width = stream_ref.shape
    hidden_width = expand_w.shape[1]
    gq_ref, gqkv_ref = sum_ref, rate_ref.at[:, 0 : 3 * width]
    quads = width // (QUAD * HD)
    moves = copy_in(
        [
            (qkv_w_any.at[1], qkv_w),
            (out_w_any.at[1], out_w),
            (expand_w_any.at[1], expand_w),
            (reduce_w_any.at[1], reduce_w),
            (grad_any, grad_ref),
            (raised_grad_any, raised_grad_ref),
        ],
        sems,
    )
    share = rows // parts
    half = share // 2
    chunks = [
        (shares[distance], which * (half + 8), chunk_of(jnp.bitwise_xor(index, distance), which, parts))
        for distance in range(parts)
        for which in range(2)
    ]
    for given, start, place in chunks:
        own = pl.ds(pl.multiple_of(place * half, half), half)
        stream_ref[own] = given[start : start + half].astype(F32) + pool_b_ref[...]
    for given, start, place in chunks:

        @pl.when(place < 2 * parts - 1)
        def _():
            head = pl.ds(pl.multiple_of((place + 1) * half, half), 8)
            stream_ref[head] += given[start + half : start + half + 8].astype(F32)

    unit, _ = unit_rows(stream_ref[...])
    normed_ref[...] = (unit * gains_ref[1, 0:1] + shifts_ref[1, 0:1]).astype(BF16)
    moves[0].wait()

    def projected(part):
        columns = slice(part * width, (part + 1) * width)
        return dot(normed_ref[...], qkv_w[:, columns]) + qkv_b_ref[1:2, columns]

    cosine, sine = cos_ref[...], sin_ref[...]
    q_ref[...] = (turn_rows(projected(0), cosine, sine) * HD**-0.5).astype(BF16)
    keys = turn_rows(projected(1), cosine, sine)
    k_ref[...] = keys.astype(BF16)
    kt_ref[...] = keys.T.astype(BF16)
    values = projected(2)
    v_ref[...] = values.astype(BF16)
    vt_ref[...] = values.T.astype(BF16)

    def block_of(j):
        return pl.ds(pl.multiple_of(j * query_rows, query_rows), query_rows)

    def part(which, carry):
        own_rows = block_of(which)
        found = flash_quads(
            [quad_rows(q_ref[own_rows, lanes_of(quad)]) for quad in range(quads)],
            lambda j, quad: k_ref[block_of(j), lanes_of(quad)],
            lambda j, quad: vt_ref[lanes_of(quad), block_of(j)],
            which,
            which * query_rows,
            which * query_rows,
            (acc_ref, peak_ref, total_ref),
        )
        for quad, (mixed, lse) in enumerate(found):
            o_ref[own_rows, lanes_of(quad)] = mixed.astype(BF16)
            lse_ref[pl.ds(which * quads + quad, 1), :] = lse
        return carry

    lax.fori_loop(0, rows // query_rows, part, 0, unroll=parts == 4)
    moves[1].wait()
    middle = stream_ref[...] + dot(o_ref[...], out_w[...]) + out_b_ref[1:2]
    middle_ref[...] = middle
    unit, _ = unit_rows(middle)
    second_ref[...] = (unit * gains_ref[1, 1:2] + shifts_ref[1, 1:2]).astype(BF16)
    sum_ref[...] = middle + reduce_b_ref[1:2]
    moves[2].wait()
    moves[3].wait()

    def columns_of(c):
        return pl.ds(pl.multiple_of(c * width, width), width)

    def hidden(c, carry):
        columns = columns_of(c)
        pre = dot(second_ref[...], expand_w[:, columns]) + expand_b_ref[1:2, columns]
        value, rate = gelu_parts(pre)
        value = value.astype(BF16)
        active_ref[:, columns] = value
        rate_ref[:, columns] = rate.astype(BF16)
        sum_ref[...] += dot(value, reduce_w[columns, :])
        return carry

    lax.fori_loop(0, hidden_width // width, hidden, 0, unroll=parts == 4)
    low_ref[...] = sum_ref[...].astype(BF16)

    vec_ref[...] = jnp.zeros(vec_ref.shape, F32)

    def column_sum(row, member):
        vec_ref[row : row + 1, 0 : member.shape[1]] = jnp.sum(member, axis=0, keepdims=True)

    moves[4].wait()
    moves[5].wait()
    grad_low = grad_ref[...].astype(BF16)
    column_sum(7, grad_low.astype(F32))
    att_ref[...] = grad_low
    sum_ref[...] = jnp.zeros(sum_ref.shape, F32)

    def hidden_back(c, carry):
        columns = columns_of(c)
        pre = dot_nt(att_ref[...], reduce_w[columns, :]) * rate_ref[:, columns].astype(F32)
        low = pre.astype(BF16)
        pre_ref[:, columns] = low
        vec_ref[6:7, columns] = jnp.sum(low.astype(F32), axis=0, keepdims=True)
        sum_ref[...] += dot_nt(low, expand_w[:, columns])
        return carry

    lax.fori_loop(0, hidden_width // width, hidden_back, 0, unroll=parts == 4)
    if packed:
        place = store_packed(
            buffers[0], 0, dot_tn(active_ref[...], share_columns(att_ref, index, parts)).astype(BF16), own_block, blocks
        )
        place = store_packed(
            buffers[0], place, dot_tn(second_ref[...], share_columns(pre_ref, index, parts)).astype(BF16), own_block, blocks
        )
        place = store_packed(
            buffers[0], place, dot_tn(low_ref[...], share_columns(raised_grad_ref, index, parts)).astype(BF16), own_block, blocks
        )
    else:
        mats[0][...] = dot_tn(active_ref[...], share_columns(att_ref, index, parts)).astype(BF16)
        mats[1][...] = dot_tn(second_ref[...], share_columns(pre_ref, index, parts)).astype(BF16)
        mats[2][...] = dot_tn(low_ref[...], share_columns(raised_grad_ref, index, parts)).astype(BF16)

    unit, inverse = unit_rows(middle_ref[...])
    grad_second = sum_ref[...]
    column_sum(1, grad_second * unit)
    column_sum(3, grad_second)
    grad_middle = grad_ref[...] + norm_back_rows(grad_second, unit, inverse, gains_ref[1, 1:2])
    middle_ref[...] = grad_middle
    att_ref[...] = grad_middle.astype(BF16)
    column_sum(5, att_ref[...].astype(F32))
    go_ref[...] = dot_nt(att_ref[...], out_w[...]).astype(BF16)
    gk_ref[...] = jnp.zeros(gk_ref.shape, F32)
    gv_ref[...] = jnp.zeros(gv_ref.shape, F32)

    def part_back(which, carry):
        own_rows = block_of(which)
        every = range(quads)
        lanes = [lanes_of(quad) for quad in every]
        tall_q = [quad_rows(q_ref[own_rows, lane]) for lane in lanes]
        tall_g = [quad_rows(go_ref[own_rows, lane]) for lane in lanes]
        delta = [
            head_sums(o_ref[own_rows, lane].astype(F32) * go_ref[own_rows, lane].astype(F32))
            for lane in lanes
        ]

        def one(j, masked):
            keys = block_of(j)
            scores = [dot_nt(k_ref[keys, lanes[quad]], tall_q[quad]) for quad in every]
            if masked:
                scores = [
                    causal(member, j * query_rows, which * query_rows) for member in scores
                ]
            found = []
            for quad in every:
                lane = lanes[quad]
                add_k, add_v, add_q = back_block(
                    scores[quad],
                    lse_ref[pl.ds(which * quads + quad, 1), :],
                    delta[quad],
                    tall_q[quad],
                    tall_g[quad],
                    kt_ref[lane, keys],
                    v_ref[keys, lane],
                )
                gk_ref[keys, lane] += add_k
                gv_ref[keys, lane] += add_v
                found.append(add_q)
            return found

        for quad, found in enumerate(one(which, True)):
            acc_ref[quad] = found

        def full(j, inner_carry):
            for quad, found in enumerate(one(j, False)):
                acc_ref[quad] += found
            return inner_carry

        lax.fori_loop(0, which, full, 0)
        for quad in every:
            gq_ref[own_rows, lanes[quad]] = quad_fold(acc_ref[quad].T) * HD**-0.5
        return carry

    lax.fori_loop(0, rows // query_rows, part_back, 0, unroll=parts == 4)
    sine = -sin_ref[...]
    gqkv_ref[:, 0:width] = turn_rows(gq_ref[...], cosine, sine).astype(BF16)
    gqkv_ref[:, width : 2 * width] = turn_rows(gk_ref[...], cosine, sine).astype(BF16)
    gqkv_ref[:, 2 * width : 3 * width] = gv_ref[...].astype(BF16)
    column_sum(4, gqkv_ref[...].astype(F32))
    if packed:
        place = store_packed(
            buffers[0], place, dot_tn(o_ref[...], share_columns(att_ref, index, parts)).astype(BF16), own_block, blocks
        )
        store_packed(
            buffers[0], place, dot_tn(normed_ref[...], share_columns(gqkv_ref, index, parts)).astype(BF16), own_block, blocks
        )
    else:
        mats[3][...] = dot_tn(o_ref[...], share_columns(att_ref, index, parts)).astype(BF16)
        mats[4][...] = dot_tn(normed_ref[...], share_columns(gqkv_ref, index, parts)).astype(BF16)
    if packed:
        sent = copy_in(halves_of(buffers[0], mats), sems, 6)
    grad_normed = dot_nt(gqkv_ref[...], qkv_w[...])
    unit, inverse = unit_rows(stream_ref[...])
    column_sum(0, grad_normed * unit)
    column_sum(2, grad_normed)
    grad_in = middle_ref[...] + norm_back_rows(grad_normed, unit, inverse, gains_ref[1, 0:1])
    grad_in_low = grad_in.astype(BF16)
    gz_ref[0:rows] = grad_in_low
    gz_ref[rows : rows + 16] = jnp.zeros((16, width), BF16)
    column_sum(8, grad_in_low.astype(F32))
    if packed:
        for move in sent:
            move.wait()


def halves_of(buffer, outs):
    half = buffer.shape[0] // 2
    return [(buffer.at[0:half], outs[0]), (buffer.at[half : 2 * half], outs[1])]


def inner_shapes_of(width, hidden):
    return [
        (hidden, width),
        (width, hidden),
        (width, POOL * width),
        (width, width),
        (width, 3 * width),
    ]


def row_tables(length):
    cosine, sine = angle_rows(length)
    repeat = LANES // HD
    return (
        np.tile(np.concatenate([cosine, cosine], axis=1), (1, repeat)),
        np.tile(np.concatenate([-sine, sine], axis=1), (1, repeat)),
    )


def inner_layer(index, shares, pool_b, gains, shifts, qkv_w, qkv_b, out_w, out_b, expand_w, expand_b,
                reduce_w, reduce_b, raised_grad, grad, parts, blocks):
    rows, width = grad.shape
    raised_grad, grad = far_away(raised_grad), far_away(grad)
    hidden = expand_w.shape[2]
    quads = width // (QUAD * HD)
    query_rows = 256 if parts == 4 else 128
    shapes = inner_shapes_of(width, hidden)
    packed = can_pack(shapes, parts, blocks)
    cosine, sine = row_tables(rows)
    vmem = pl.BlockSpec(memory_space=pltpu.VMEM)
    anywhere = pl.BlockSpec(memory_space=pl.ANY)
    far = pl.BlockSpec(memory_space=pltpu.HBM)
    shape = outside
    if packed:
        held = packed_rows(shapes, parts, blocks)
        mats = [shape((blocks // 2, held, LANES), BF16) for _ in range(2)]
        buffers = [pltpu.VMEM((blocks, held, LANES), BF16)]
    else:
        mats = [shape((height, columns // parts), BF16) for height, columns in shapes]
        buffers = []
    found = pl.pallas_call(
        functools.partial(inner_kernel, parts, blocks, packed, query_rows),
        name="inner_layer",
        in_specs=[pl.BlockSpec(memory_space=pltpu.SMEM)] + [vmem] * parts + [vmem, vmem, vmem, far, vmem,
                  far, vmem, far, vmem, far, vmem, far, far, vmem, vmem],
        out_specs=[vmem] * 3 + [anywhere if packed else vmem] * len(mats),
        out_shape=[
            shape((rows, width), BF16),
            shape((rows + 16, width), BF16),
            shape((16, max(hidden, POOL * width)), F32),
        ] + mats,
        scratch_shapes=[
            pltpu.VMEM((width, 3 * width), BF16),
            pltpu.VMEM((width, width), BF16),
            pltpu.VMEM((width, hidden), BF16),
            pltpu.VMEM((hidden, width), BF16),
            pltpu.VMEM((rows, width), F32),
            pltpu.VMEM((rows, width), BF16),
            pltpu.VMEM((rows, width), BF16),
            pltpu.VMEM((rows, width), BF16),
            pltpu.VMEM((width, rows), BF16),
            pltpu.VMEM((rows, width), BF16),
            pltpu.VMEM((width, rows), BF16),
            pltpu.VMEM((rows, width), BF16),
            pltpu.VMEM((rows // query_rows * quads, QUAD * query_rows), F32),
            pltpu.VMEM((rows, width), F32),
            pltpu.VMEM((rows, width), BF16),
            pltpu.VMEM((rows, hidden), BF16),
            pltpu.VMEM((rows, hidden), BF16),
            pltpu.VMEM((rows, width), F32),
            pltpu.VMEM((rows, hidden), BF16),
            pltpu.VMEM((rows, width), BF16),
            pltpu.VMEM((rows, width), BF16),
            pltpu.VMEM((rows, width), F32),
            pltpu.VMEM((rows, width), F32),
            pltpu.VMEM((quads, QUAD * HD, QUAD * query_rows), F32),
            pltpu.VMEM((quads, 1, QUAD * query_rows), F32),
            pltpu.VMEM((quads, 1, QUAD * query_rows), F32),
            pltpu.VMEM(raised_grad.shape, BF16),
            pltpu.VMEM(grad.shape, F32),
            pltpu.SemaphoreType.DMA((8,)),
        ]
        + buffers,
        compiler_params=pltpu.CompilerParams(vmem_limit_bytes=grant(48 if parts == 4 else 60)),
        cost_estimate=cost(33),
    )(index, *shares, pool_b, gains, shifts, qkv_w, qkv_b, out_w, out_b, expand_w, expand_b, reduce_w,
      reduce_b, raised_grad, grad, far_away(jnp.asarray(cosine)), far_away(jnp.asarray(sine)))
    return found[0], found[1], found[2], found[3:], packed


def reversed_bits(value, size):
    found, bit = 0, 1
    while bit < size:
        found = found * 2 + (value // bit) % 2
        bit *= 2
    return found


def store_split(out, index, start, member, own_block, parts, blocks):
    columns = member.shape[1] // parts
    place = start
    for part in range(parts):
        spot = reversed_bits(jnp.bitwise_xor(index, part), parts)
        place = store_packed(
            out.at[spot],
            start,
            member[:, part * columns : (part + 1) * columns],
            own_block,
            blocks,
        )
    return place


def vector_tiles(entries, block, blocks):
    found = []
    for ref, row, length, scale in entries:
        size = length // blocks
        first, last = block * size // LANES, ((block + 1) * size - 1) // LANES
        found += [(ref, row, tile, scale) for tile in range(first, last + 1)]
    return found


def store_vectors(out, index, start, entries, own_block, parts, blocks):
    count = -(-len(vector_tiles(entries, 0, blocks)) // parts)
    for block in range(blocks):
        tiles = vector_tiles(entries, block, blocks)
        for part in range(parts):
            rows = [
                ref[row : row + 1, tile * LANES : (tile + 1) * LANES] * scale
                for ref, row, tile, scale in tiles[part * count : (part + 1) * count]
            ]
            rows += [jnp.zeros((16 - len(rows), LANES), F32)]
            spot = reversed_bits(jnp.bitwise_xor(index, part), parts)
            out[spot, spot_of(block, own_block, blocks), start : start + 16, :] = jnp.concatenate(
                rows, axis=0
            ).astype(BF16)


def split_lanes(split_ref, member):
    for lane in range(split_ref.shape[0]):
        split_ref[lane] = member[:, lane * LANES : (lane + 1) * LANES]


def joined_lanes(split_ref):
    return jnp.concatenate([split_ref[lane] for lane in range(split_ref.shape[0])], axis=1)


def add_third(split_ref, start, member):
    for lane in range(split_ref.shape[0]):
        rows = pl.ds(start, member.shape[0], stride=POOL)
        split_ref[lane, rows, :] = (
            split_ref[lane, rows, :] + member[:, lane * LANES : (lane + 1) * LANES]
        )


def raised_kernel(cot_ref, up_w_ref, joined_ref, grad_ref, sums_ref, split_ref):
    width = grad_ref.shape[1]
    split_lanes(split_ref, cot_ref[...].astype(F32))
    total = jnp.zeros(grad_ref.shape, F32)
    for slot in range(POOL):
        columns = slice(slot * width, (slot + 1) * width)
        rows = every_third(split_ref, slot, grad_ref.shape[0])
        sums_ref[:, columns] = jnp.sum(rows, axis=0, keepdims=True)
        rows = rows.astype(BF16)
        joined_ref[:, columns] = rows
        total += dot_nt(rows, up_w_ref[:, columns])
    grad_ref[...] = total


def raised_back(all_cot, up_w):
    length, width = all_cot.shape
    vmem = pl.BlockSpec(memory_space=pltpu.VMEM)
    shape = outside
    return pl.pallas_call(
        raised_kernel,
        name="raised_back",
        in_specs=[vmem] * 2,
        out_specs=[vmem] * 3,
        out_shape=[
            shape((length // POOL, POOL * width), BF16),
            shape((length // POOL, width), F32),
            shape((1, POOL * width), F32),
        ],
        scratch_shapes=[pltpu.VMEM((width // LANES, length, LANES), F32)],
        compiler_params=pltpu.CompilerParams(vmem_limit_bytes=grant(16, length // 1536)),
        cost_estimate=cost(4),
    )(all_cot, up_w)


def output_kernel(index_ref, lows_ref, low_ref, up_w_ref, up_b_ref, out_ref, split_ref):
    rows, width = out_ref.shape[1:]
    third = rows // POOL
    own = low_ref[pl.ds(pl.multiple_of(index_ref[0] * third, third), third), :]
    parts, chunk = lows_ref.shape[0], rows // 2
    found = []
    for which in range(2):
        place = 2 * index_ref[0] + which
        part = jnp.minimum(place, 2 * parts - 1 - place)
        start = jnp.where(place < parts, 0, chunk)
        found += [lows_ref[part, pl.ds(pl.multiple_of(start, chunk), chunk), :].astype(F32)]
    split_lanes(split_ref, jnp.concatenate(found, axis=0))
    for slot in range(POOL):
        columns = slice(slot * width, (slot + 1) * width)
        add_third(split_ref, slot, dot(own, up_w_ref[:, columns]) + up_b_ref[:, columns])
    out_ref[0] = joined_lanes(split_ref)


def raised_output(index, lows, low, up_w, up_b):
    rows, width = lows.shape[1:]
    vmem = pl.BlockSpec(memory_space=pltpu.VMEM)
    return pl.pallas_call(
        output_kernel,
        name="raised_output",
        in_specs=[pl.BlockSpec(memory_space=pltpu.SMEM)] + [vmem] * 4,
        out_specs=vmem,
        out_shape=jax.ShapeDtypeStruct((1, rows, width), F32),
        scratch_shapes=[pltpu.VMEM((width // LANES, rows, LANES), F32)],
        compiler_params=pltpu.CompilerParams(vmem_limit_bytes=grant(10)),
        cost_estimate=cost(3),
    )(index, lows, low, up_w, up_b)


def outer_hidden_kernel(
    parts,
    blocks,
    packed,
    index_ref,
    *rest,
):
    (
    lows_any,
    gz_any,
    inner_vec_ref,
    raised_vec_ref,
    cot_any,
    middle_in_any,
    active_any,
    rate_any,
    mixed_any,
    gains_ref,
    shifts_ref,
    pool_w_any,
    reduce_w_any,
    expand_w_any,
    out_w_any,
    ) = rest[:15]
    rest = rest[15:]
    outs = 4
    middle_any, go_ref, vec_ref = rest[:3]
    mats = rest[3 : 3 + outs]
    (
        pool_w,
        reduce_w,
        expand_w,
        out_w,
        split_ref,
        grad_ref,
        low_ref,
        second_ref,
        pre_ref,
        sum_ref,
        pooled_ref,
        lows_ref,
        gz_ref,
        middle_in_ref,
        active_ref,
        rate_ref,
        mixed_ref,
        middle_ref,
        att_ref,
        sems,
        *buffers,
    ) = rest[3 + outs :]
    index, own_block = index_ref[0], index_ref[1]
    rows, width = middle_in_ref.shape
    hidden_width = expand_w.shape[1]
    third = rows // POOL
    places = [chunk_of(index, which, parts) for which in range(2)]
    chunk = rows // 2
    coming = [(gz_any, gz_ref)] + [
        (
            cot_any.at[pl.ds(pl.multiple_of(place * chunk, chunk), chunk)],
            low_ref.at[which * chunk : (which + 1) * chunk],
        )
        for which, place in enumerate(places)
    ]
    coming += [
        (pool_w_any, pool_w),
        (rate_any, rate_ref),
        (reduce_w_any.at[0], reduce_w),
        (expand_w_any.at[0], expand_w),
        (middle_in_any, middle_in_ref),
        (active_any, active_ref),
        (out_w_any.at[0], out_w),
        (mixed_any, mixed_ref),
        (lows_any, lows_ref),
    ]
    coming = copy_in(coming, sems)
    moves = []
    half = third // 2
    coming[0].wait()
    tall = [
        gz_ref[pl.ds(pl.multiple_of(place * half, half), half + 16), :].astype(F32)
        for place in places
    ]
    here = jnp.concatenate([member[0:half] for member in tall], axis=0).astype(BF16)
    after = jnp.concatenate([member[1 : half + 1] for member in tall], axis=0).astype(BF16)

    coming[1].wait()
    coming[2].wait()
    split_lanes(split_ref, low_ref[...].astype(F32))
    coming[3].wait()
    add_third(split_ref, 0, dot_nt(here, pool_w[2 * width : 3 * width]))
    add_third(split_ref, 1, dot_nt(after, pool_w[0:width]))
    add_third(split_ref, 2, dot_nt(after, pool_w[width : 2 * width]))
    grad = joined_lanes(split_ref)
    grad_ref[...] = grad
    low_ref[...] = grad.astype(BF16)
    vec_ref[...] = jnp.zeros(vec_ref.shape, F32)

    def column_sum(row, member):
        vec_ref[row : row + 1, 0 : member.shape[1]] = jnp.sum(member, axis=0, keepdims=True)

    column_sum(3, low_ref[...].astype(F32))

    coming[7].wait()
    unit, inverse = unit_rows(middle_in_ref[...])
    second_ref[...] = (unit * gains_ref[0, 1:2] + shifts_ref[0, 1:2]).astype(BF16)
    sum_ref[...] = jnp.zeros(sum_ref.shape, F32)
    for move in coming[4:7] + coming[8:9]:
        move.wait()
    tiles = width // LANES

    def hidden_back(c, carry):
        columns = pl.ds(pl.multiple_of(c * width, width), width)
        pre = dot_nt(low_ref[...], reduce_w[columns, :]) * rate_ref[:, columns].astype(F32)
        low = pre.astype(BF16)
        vec_ref[2:3, columns] = jnp.sum(low.astype(F32), axis=0, keepdims=True)
        sum_ref[...] += dot_nt(low, expand_w[:, columns])
        reduce_grad = dot_tn(active_ref[:, columns], low_ref[...]).astype(BF16)
        expand_grad = dot_tn(second_ref[...], low).astype(BF16)
        if packed:
            out = buffers[0]
            height = hidden_width // blocks
            for part in range(parts):
                spot = reversed_bits(jnp.bitwise_xor(index, part), parts)
                for block in range(width // height):
                    place = spot_of(c * (width // height) + block, own_block, blocks)
                    out[spot, place, 0:height, :] = reduce_grad[
                        block * height : (block + 1) * height, part * LANES : (part + 1) * LANES
                    ]
            spot = reversed_bits(jnp.bitwise_xor(index, c), parts)
            store_packed(out.at[spot], height, expand_grad, own_block, blocks)
        else:
            mats[0][columns, :] = reduce_grad
            mats[1][:, columns] = expand_grad
        return carry

    lax.fori_loop(0, hidden_width // width, hidden_back, 0, unroll=True)
    grad_second = sum_ref[...]
    column_sum(0, grad_second * unit)
    column_sum(1, grad_second)
    grad_middle = grad_ref[...] + norm_back_rows(grad_second, unit, inverse, gains_ref[0, 1:2])
    middle_ref[...] = grad_middle
    moves += copy_in([(middle_ref, middle_any)], sems, 16)
    att_ref[...] = grad_middle.astype(BF16)
    column_sum(4, att_ref[...].astype(F32))
    coming[9].wait()
    coming[10].wait()
    go_ref[...] = dot_nt(att_ref[...], out_w[...]).astype(BF16)
    out_grad = dot_tn(mixed_ref[...], att_ref[...]).astype(BF16)
    if packed:
        place = hidden_width // blocks + tiles * (width // blocks)
        place = store_split(buffers[0], index, place, out_grad, own_block, parts, blocks)
        entries = early_entries(vec_ref, inner_vec_ref, raised_vec_ref, width, hidden_width, parts)
        store_vectors(buffers[0], index, place, entries, own_block, parts, blocks)
        moves += copy_in(halves_of(buffers[0], mats[0:2]), sems, 12)
    else:
        mats[2][...] = out_grad

    coming[11].wait()
    for part in range(parts):
        split_lanes(split_ref, lows_ref[part].astype(F32))
        for slot, first in ((0, 1), (1, 2), (2, 0)):
            found = every_third(split_ref, first, third).astype(BF16)
            for which in range(2):
                place = chunk_of(part, which, parts)
                own = slice(place * half, (place + 1) * half)
                pooled_ref[own, slot * width : (slot + 1) * width] = found[
                    which * half : (which + 1) * half
                ]
    shared = share_columns(gz_ref, index, parts).astype(F32)
    count = pooled_ref.shape[0]
    here, after = shared[0:count].astype(BF16), shared[1 : count + 1].astype(BF16)
    pool_grad = jnp.concatenate(
        [
            dot_tn(pooled_ref[:, slot * width : (slot + 1) * width], member).astype(BF16)
            for slot, member in ((0, after), (1, after), (2, here))
        ],
        axis=0,
    )
    if packed:
        store_packed(buffers[1], 0, pool_grad, own_block, blocks)
        moves += copy_in(halves_of(buffers[1], mats[2:4]), sems, 14)
    else:
        mats[3][...] = pool_grad
    for move in moves:
        move.wait()


def early_entries(vec_ref, inner_ref, raised_ref, width, hidden, parts):
    once = 1.0 / parts
    sizes = [width, width, width, width, 3 * width, width, hidden, width, width]
    return (
        [(vec_ref, 0, width, 1.0), (vec_ref, 1, width, 1.0), (vec_ref, 2, hidden, 1.0)]
        + [(vec_ref, 3, width, 1.0), (vec_ref, 4, width, 1.0)]
        + [(inner_ref, row, size, once) for row, size in enumerate(sizes)]
        + [(raised_ref, 0, POOL * width, once)]
    )


def late_entries(vec_ref, width):
    return [(vec_ref, 0, width, 1.0), (vec_ref, 1, width, 1.0), (vec_ref, 2, 3 * width, 1.0)]


def outer_hidden(index, lows, gz, inner_vecs, raised_vecs, cot, middle, active, rate, mixed, gains, shifts, pool_w, reduce_w, expand_w,
                 out_w, parts, blocks):
    rows, width = middle.shape
    lows, gz, cot, middle, active, rate, mixed = map(
        far_away, (lows, gz, cot, middle, active, rate, mixed)
    )
    hidden = expand_w.shape[2]
    shapes = [(hidden, width), (width, hidden), (width, width)]
    packed = can_pack(shapes + [(POOL * width, width)], parts, blocks) and hidden // parts == width and width // parts == LANES
    vmem = pl.BlockSpec(memory_space=pltpu.VMEM)
    far = pl.BlockSpec(memory_space=pltpu.HBM)
    shape = outside
    if packed:
        held = packed_rows(shapes, parts, blocks) + 16
        mats = [shape((parts // 2, blocks, held, LANES), BF16) for _ in range(2)]
        buffers = [pltpu.VMEM((parts, blocks, held, LANES), BF16)]
        added = packed_rows([(POOL * width, width)], parts, blocks)
        mats += [shape((blocks // 2, added, LANES), BF16) for _ in range(2)]
        buffers += [pltpu.VMEM((blocks, added, LANES), BF16)]
    else:
        mats = [shape(member, BF16) for member in shapes]
        mats += [shape((POOL * width, width // parts), BF16)]
        buffers = []
    found = pl.pallas_call(
        functools.partial(outer_hidden_kernel, parts, blocks, packed),
        name="outer_hidden",
        in_specs=[pl.BlockSpec(memory_space=pltpu.SMEM)] + [far] * 2 + [vmem] * 2 + [far] * 5 + [vmem] * 2 + [far] * 4,
        out_specs=[far] + [vmem] * 2 + [far if packed else vmem] * len(mats),
        out_shape=[
            shape((rows, width), F32),
            shape((rows, width), BF16),
            shape((8, hidden), F32),
        ] + mats,
        scratch_shapes=[
            pltpu.VMEM((POOL * width, width), BF16),
            pltpu.VMEM((hidden, width), BF16),
            pltpu.VMEM((width, hidden), BF16),
            pltpu.VMEM((width, width), BF16),
            pltpu.VMEM((width // LANES, rows, LANES), F32),
            pltpu.VMEM((rows, width), F32),
            pltpu.VMEM((rows, width), BF16),
            pltpu.VMEM((rows, width), BF16),
            pltpu.VMEM((rows, hidden), BF16),
            pltpu.VMEM((rows, width), F32),
            pltpu.VMEM((gz.shape[0] - 16, POOL * width), BF16),
            pltpu.VMEM(lows.shape, BF16),
            pltpu.VMEM(gz.shape, BF16),
            pltpu.VMEM((rows, width), F32),
            pltpu.VMEM((rows, hidden), BF16),
            pltpu.VMEM((rows, hidden), BF16),
            pltpu.VMEM((rows, width), BF16),
            pltpu.VMEM((rows, width), F32),
            pltpu.VMEM((rows, width), BF16),
            pltpu.SemaphoreType.DMA((17,)),
        ]
        + buffers,
        compiler_params=pltpu.CompilerParams(vmem_limit_bytes=grant(44 if packed else 60)),
        cost_estimate=cost(14),
    )(index, lows, gz, inner_vecs, raised_vecs, cot, middle, active, rate, mixed, gains, shifts, pool_w, reduce_w, expand_w, out_w)
    return found[:3], found[3:], packed, shapes


def store_rows(out, index, first, member, own_block, parts, blocks):
    rows, tiles = member.shape[0] // blocks, member.shape[1] // LANES
    share = rows // parts
    for part in range(parts):
        spot = reversed_bits(jnp.bitwise_xor(index, part), parts)
        for block in range(blocks):
            place = spot_of(block, own_block, blocks)
            start = block * rows + part * share
            for tile in range(tiles):
                out[spot, place, first + tile * share : first + (tile + 1) * share, :] = member[
                    start : start + share, tile * LANES : (tile + 1) * LANES
                ]
    return first + tiles * share


def outer_attention_kernel(
    parts,
    blocks,
    packed,
    quad,
    last,
    anchors,
    index_ref,
    ids_ref,
    emb_ref,
    gains_ref,
    shifts_ref,
    qkv_w_any,
    q_ref,
    k_ref,
    kt_ref,
    v_ref,
    o_ref,
    lse_ref,
    go_ref,
    cos_ref,
    sin_ref,
    *rest,
):
    given = (4 if last else 0) + anchors
    if last:
        middle_ref, sums_in_ref, first_ref, table_in_ref = rest[:4]
    outs = rest[given : given + 3]
    (qkv_w, gq_ref, gk_ref, gv_ref, code_ref, acc_ref, sems, *buffers) = rest[given + 3 :]
    index, own_block = index_ref[0], index_ref[1]
    rows, width = o_ref.shape
    vocab = emb_ref.shape[0]
    chunk = rows // 2
    wide = QUAD * HD
    lanes = slice(quad * wide, (quad + 1) * wide)
    moves = copy_in(
        [
            (
                qkv_w_any.at[0, :, part * width + quad * wide : part * width + (quad + 1) * wide],
                qkv_w.at[part],
            )
            for part in range(3)
        ],
        sems,
    )

    def block_of(j):
        if isinstance(j, int):
            return slice(j * rows, (j + 1) * rows)
        return pl.ds(pl.multiple_of(j * rows, rows), rows)

    def clear(j):
        gk_ref[block_of(j), :] = jnp.zeros((rows, wide), F32)
        gv_ref[block_of(j), :] = jnp.zeros((rows, wide), F32)

    def part_back(which, full):
        own_rows = slice(which * chunk, (which + 1) * chunk)
        place = chunk_of(index, which, parts)
        tall_q = quad_rows(q_ref[own_rows, lanes])
        tall_g = quad_rows(go_ref[own_rows, lanes])
        row = which * (width // wide) + quad
        lse = lse_ref[row : row + 1, :]
        delta = head_sums(o_ref[own_rows, lanes].astype(F32) * go_ref[own_rows, lanes].astype(F32))

        def one(j, masked):
            keys = block_of(j)
            scores = dot_nt(k_ref[keys, lanes], tall_q)
            if masked:
                scores = causal(scores, j * rows, place * chunk)
            add_k, add_v, add_q = back_block(
                scores, lse, delta, tall_q, tall_g, kt_ref[lanes, keys], v_ref[keys, lanes]
            )
            gk_ref[keys, :] += add_k
            gv_ref[keys, :] += add_v
            return add_q

        acc_ref[which] = one(full, True)

        def further(j):
            acc_ref[which] += one(j, False)

        each(full, further)
        gq_ref[own_rows, :] = quad_fold(acc_ref[which].T) * HD**-0.5

    def attend_back(full, seen):
        each(seen, clear)
        for which in range(2):
            part_back(which, full[which])

    by_blocks(index, parts, attend_back)

    codes = lax.broadcasted_iota(jnp.int32, (vocab, rows), 0)
    own_ids = own_lanes(jnp.broadcast_to(ids_ref[...], (8, ids_ref.shape[1])), index, parts, chunk)
    own_hot = (codes == own_ids[0:1]).astype(F32).astype(BF16)

    def own_rows_of(table):
        return jnp.concatenate(
            [
                table[pl.ds(pl.multiple_of(chunk_of(index, which, parts) * chunk, chunk), chunk), :]
                for which in range(2)
            ],
            axis=0,
        )

    turned = turn_rows(gq_ref[...], own_rows_of(cos_ref), -own_rows_of(sin_ref)).astype(BF16)
    code_ref[:, 0:wide] = dot(own_hot, turned)
    code_ref[:, wide : 3 * wide] = jnp.zeros((vocab, 2 * wide), F32)

    def by_code(j):
        columns = block_of(j)
        hot = (codes == ids_ref[:, columns]).astype(F32).astype(BF16)
        turned = turn_rows(gk_ref[columns, :], cos_ref[columns, :], -sin_ref[columns, :])
        code_ref[:, wide : 2 * wide] += dot(hot, turned.astype(BF16))
        code_ref[:, 2 * wide : 3 * wide] += dot(hot, gv_ref[columns, :].astype(BF16))

    by_blocks(index, parts, lambda full, seen: each(seen, by_code))
    code = code_ref[...]
    code_low = code.astype(BF16)
    unit, inverse = unit_rows(emb_ref[...].astype(F32))
    normed = (unit * gains_ref[0, 0:1] + shifts_ref[0, 0:1]).astype(BF16)
    qkv_grad = dot_tn(normed, code_low).astype(BF16)
    grad_table = jnp.zeros((vocab, width), F32)
    for part in range(3):
        moves[part].wait()
        grad_table += dot_nt(code_low[:, part * wide : (part + 1) * wide], qkv_w[part])
    vec_ref = outs[0]
    if last:
        vec_ref[...] = sums_in_ref[...]
    else:
        vec_ref[...] = jnp.zeros(vec_ref.shape, F32)
    for part in range(3):
        start = part * width + quad * wide
        vec_ref[2:3, start : start + wide] = jnp.sum(
            code[:, part * wide : (part + 1) * wide], axis=0, keepdims=True
        )
    if not last:
        outs[1][...] = qkv_grad
        outs[2][...] = grad_table
        return
    grad_table += table_in_ref[...]
    high = middle_ref[...].astype(BF16)
    low = (middle_ref[...] - high.astype(F32)).astype(BF16)
    embed = dot(own_hot, high) + dot(own_hot, low)
    embed = embed + norm_back_rows(grad_table, unit, inverse, gains_ref[0, 0:1])
    embed = embed.astype(BF16)
    vec_ref[0:1, 0:width] = jnp.sum(grad_table * unit, axis=0, keepdims=True)
    vec_ref[1:2, 0:width] = jnp.sum(grad_table, axis=0, keepdims=True)
    if packed:
        out = buffers[0]
        place = store_rows(out, index, 0, first_ref[...], own_block, parts, blocks)
        place = store_rows(out, index, place, qkv_grad, own_block, parts, blocks)
        place = store_split(out, index, place, embed, own_block, parts, blocks)
        store_vectors(out, index, place, late_entries(vec_ref, width), own_block, parts, blocks)
        for move in copy_in(halves_of(out, outs[1:]), sems, 3):
            move.wait()
    else:
        outs[1][...] = qkv_grad
        outs[2][...] = embed


def outer_attention(quad, index, all_ids, embedding, gains, shifts, qkv_w, queries, keys, keys_t, values,
                    mixed, lse, go, ending, anchors, parts, blocks):
    rows, width = queries.shape
    length = all_ids.shape[1]
    vocab = embedding.shape[0]
    chunk = rows // 2
    wide = QUAD * HD
    last = ending is not None
    packed = width % (16 * parts * blocks) == 0 and vocab % (16 * blocks) == 0
    packed = packed and width % (LANES * parts) == 0 and parts == 4
    cosine, sine = row_tables(length)
    vmem = pl.BlockSpec(memory_space=pltpu.VMEM)
    anywhere = pl.BlockSpec(memory_space=pl.ANY)
    far = pl.BlockSpec(memory_space=pltpu.HBM)
    shape = outside
    outs, buffers = [shape((8, 3 * width), F32)], []
    if not last:
        outs += [shape((width, 3 * wide), BF16), shape((vocab, width), F32)]
    elif packed:
        held = 3 * width // LANES * (width // blocks // parts)
        held += vocab // blocks * (width // parts // LANES) + 16
        outs += [shape((parts // 2, blocks, held, LANES), BF16) for _ in range(2)]
        buffers = [pltpu.VMEM((parts, blocks, held, LANES), BF16)]
    else:
        outs += [shape((width, 3 * wide), BF16), shape((vocab, width), BF16)]
    ending = list(ending) if last else []
    return pl.pallas_call(
        functools.partial(outer_attention_kernel, parts, blocks, packed, quad, last, len(anchors)),
        name="outer_attention",
        in_specs=[pl.BlockSpec(memory_space=pltpu.SMEM)]
        + [vmem] * 4
        + [far]
        + [vmem] * 9
        + [vmem] * len(ending)
        + [anywhere] * len(anchors),
        out_specs=[vmem] + [anywhere if buffers else vmem] * 2,
        out_shape=outs,
        scratch_shapes=[
            pltpu.VMEM((3, width, wide), BF16),
            pltpu.VMEM((rows, wide), F32),
            pltpu.VMEM((length, wide), F32),
            pltpu.VMEM((length, wide), F32),
            pltpu.VMEM((vocab, 3 * wide), F32),
            pltpu.VMEM((2, wide, QUAD * chunk), F32),
            pltpu.SemaphoreType.DMA((5,)),
        ]
        + buffers,
        compiler_params=pltpu.CompilerParams(vmem_limit_bytes=grant(34, length // (4 * rows))),
        cost_estimate=cost(14),
    )(index, all_ids, embedding, gains, shifts, qkv_w, queries, keys, keys_t, values, mixed, lse, go,
      far_away(jnp.asarray(cosine)), far_away(jnp.asarray(sine)), *ending, *map(far_away, anchors)), packed


def add_kernel(count, anchors, index_slices, *refs):
    sources, outs = refs[:count], refs[count + anchors :]
    for out, piece in zip(outs, index_slices):
        total = sources[0][piece].astype(F32)
        for source in sources[1:]:
            total += source[piece].astype(F32)
        out[...] = total.astype(BF16)


def add(sources, pieces, anchors=(), shape_of=jax.ShapeDtypeStruct):
    shape = sources[0].shape
    found, slices = [], []
    for piece in pieces:
        if isinstance(piece, int):
            found, slices = found + [shape[1:]], slices + [piece]
        else:
            *first, start, stop = piece
            found += [(stop - start, *shape[1 + len(first) :])]
            slices += [(*first, slice(start, stop))]
    vmem = pl.BlockSpec(memory_space=pltpu.VMEM)
    return list(pl.pallas_call(
        functools.partial(add_kernel, len(sources), len(anchors), slices),
        name="add",
        in_specs=[vmem] * len(sources) + [pl.BlockSpec(memory_space=pl.ANY)] * len(anchors),
        out_specs=[vmem] * len(found),
        out_shape=[shape_of(member, BF16) for member in found],
        compiler_params=pltpu.CompilerParams(vmem_limit_bytes=grant(16)),
        cost_estimate=cost(3),
    )(*sources, *map(far_away, anchors)))


def merge_kernel(plan, split, count, *refs):
    sources, outs = refs[:count], refs[len(refs) - split :]
    for spot in range(sources[0].shape[0]):
        out = outs[spot] if split > 1 else outs[0].at[spot]
        at = 0
        for rows, members in plan:
            total = sources[members[0][0]][spot, members[0][1] : members[0][1] + rows].astype(F32)
            for source, start in members[1:]:
                total += sources[source][spot, start : start + rows].astype(F32)
            out[at : at + rows, :] = total.astype(BF16)
            at += rows


def merge(sources, plan, split, anchors=()):
    count = sources[0].shape[0]
    rows = sum(member[0] for member in plan)
    vmem = pl.BlockSpec(memory_space=pltpu.VMEM)
    shapes = [(rows, LANES)] * count if split else [(count, rows, LANES)]
    return list(
        pl.pallas_call(
            functools.partial(merge_kernel, plan, len(shapes), len(sources)),
            name="merge",
            in_specs=[vmem] * len(sources) + [pl.BlockSpec(memory_space=pl.ANY)] * len(anchors),
            out_specs=[vmem] * len(shapes),
            out_shape=[jax.ShapeDtypeStruct(member, BF16) for member in shapes],
            compiler_params=pltpu.CompilerParams(vmem_limit_bytes=grant(16)),
            cost_estimate=cost(3),
        )(*sources, *map(far_away, anchors))
    )


def total_kernel(counts, *refs):
    out, start, at = refs[-1], 0, 0
    for count in counts:
        total = refs[at][...].astype(F32)
        for ref in refs[at + 1 : at + count]:
            total += ref[...].astype(F32)
        out[start : start + total.shape[0], :] = total.astype(BF16)
        start, at = start + total.shape[0], at + count


def totals(groups, anchors=()):
    rows = sum(group[0].shape[0] for group in groups)
    vmem = pl.BlockSpec(memory_space=pltpu.VMEM)
    members = [member for group in groups for member in group]
    return pl.pallas_call(
        functools.partial(total_kernel, [len(group) for group in groups]),
        name="totals",
        in_specs=[vmem] * len(members) + [pl.BlockSpec(memory_space=pl.ANY)] * len(anchors),
        out_specs=vmem,
        out_shape=jax.ShapeDtypeStruct((rows, LANES), BF16),
        compiler_params=pltpu.CompilerParams(vmem_limit_bytes=grant(8)),
        cost_estimate=cost(3),
    )(*members, *map(far_away, anchors))


def assemble_kernel(parts, blocks, index_ref, *rest):
    early, late, outs = rest[:parts], rest[parts : 2 * parts], rest[2 * parts :]
    index, own_block = index_ref[0], index_ref[1]
    (embed, gains, shifts, qkv_w, qkv_b, out_w, out_b, expand_w, expand_b, reduce_w, reduce_b) = outs[:11]
    pool_w, pool_b, up_w, up_b = outs[11:]

    def place(group, start, out, height, columns):
        tiles = columns // parts // LANES
        for at in range(parts):
            part = jnp.bitwise_xor(index, at)
            for tile in range(tiles):
                lanes = pl.ds(pl.multiple_of((part * tiles + tile) * LANES, LANES), LANES)
                found = group[at][start + tile * height : start + (tile + 1) * height]
                out[:, lanes] = found.astype(F32)
        return start + tiles * height

    start = 0
    for out in (reduce_w.at[1], expand_w.at[1], up_w, out_w.at[1], qkv_w.at[1]):
        start = place(early, start, out, *out.shape)
    for out in (reduce_w.at[0], expand_w.at[0], out_w.at[0]):
        start = place(early, start, out, *out.shape)
    early_start = start
    place(early, start + 16, pool_w, *pool_w.shape)
    height, wide = qkv_w.shape[1] // parts, QUAD * HD
    start = 0
    for quad in range(qkv_w.shape[2] // 3 // wide):
        for third in range(3):
            for tile in range(wide // LANES):
                lane = third * (qkv_w.shape[2] // 3) + quad * wide + tile * LANES
                for distance in range(parts):
                    part = jnp.bitwise_xor(index, distance)
                    rows = pl.ds(pl.multiple_of(part * height, height), height)
                    qkv_w[0, rows, lane : lane + LANES] = late[distance][
                        start : start + height
                    ].astype(F32)
                start += height
    late_start = place(late, start, embed, *embed.shape)

    def vectors(group, start, sizes):
        entries = [(None, 0, size * blocks, 1.0) for size in sizes]
        total = len(vector_tiles(entries, 0, blocks))
        count = -(-total // parts)
        tiles = {}
        for distance in range(parts):
            tiles[distance] = group[distance][start : start + 16].astype(F32)
        rows = []
        for number in range(total):
            row = jnp.zeros((1, LANES), F32)
            for distance in range(parts):
                here = jnp.bitwise_xor(index, distance) == number // count
                row = jnp.where(here, tiles[distance][number % count : number % count + 1], row)
            rows.append(row)
        found, number = [], 0
        for size in sizes:
            held = len(vector_tiles([(None, 0, size * blocks, 1.0)], 0, blocks))
            wide = jnp.concatenate(rows[number : number + held], axis=1)
            number += held
            if size % LANES != 0:
                shift = own_block * size % LANES
                wide = pltpu.roll(wide, (wide.shape[1] - shift) % wide.shape[1], 1)
            found.append(wide[:, :size])
        return found

    width_b, hidden_b, three_b = out_b.shape[1], expand_b.shape[1], qkv_b.shape[1]
    low = vectors(
        early,
        early_start,
        [width_b, width_b, hidden_b, width_b, width_b]
        + [width_b] * 4
        + [three_b, width_b, hidden_b, width_b, width_b, three_b],
    )
    high = vectors(late, late_start, [width_b, width_b, three_b])
    gains[0, 0:1], shifts[0, 0:1], qkv_b[0:1] = high
    gains[0, 1:2], shifts[0, 1:2], expand_b[0:1], reduce_b[0:1], out_b[0:1] = low[:5]
    gains[1, 0:1], gains[1, 1:2], shifts[1, 0:1], shifts[1, 1:2] = low[5:9]
    qkv_b[1:2], out_b[1:2], expand_b[1:2], reduce_b[1:2] = low[9:13]
    pool_b[...], up_b[...] = low[13:]


def assemble(index, gathered, late, width, hidden, vocab, parts, blocks):
    vmem = pl.BlockSpec(memory_space=pltpu.VMEM)
    part = width // blocks
    shapes = [
        (vocab // blocks, width),
        (2, 2, part),
        (2, 2, part),
        (2, part, 3 * width),
        (2, 3 * part),
        (2, part, width),
        (2, part),
        (2, part, hidden),
        (2, hidden // blocks),
        (2, hidden // blocks, width),
        (2, part),
        (POOL * part, width),
        (1, part),
        (part, POOL * width),
        (1, POOL * part),
    ]
    return pl.pallas_call(
        functools.partial(assemble_kernel, parts, blocks),
        name="assemble",
        in_specs=[pl.BlockSpec(memory_space=pltpu.SMEM)] + [vmem] * (2 * parts),
        out_specs=[vmem] * 15,
        out_shape=[jax.ShapeDtypeStruct(member, F32) for member in shapes],
        compiler_params=pltpu.CompilerParams(vmem_limit_bytes=grant(16)),
        cost_estimate=cost(4),
    )(index, *gathered, *late)


def pack(members, parts, blocks):
    rows = []
    for member in members:
        height, width = member.shape
        split = member.reshape(blocks, height // blocks, parts, width // parts)
        rows.append(split.transpose(2, 0, 1, 3).reshape(parts, blocks, -1))
    buffer = jnp.concatenate(rows, axis=2)
    order = [reversed_bits(spot, parts) for spot in range(parts)]
    index = lax.axis_index("seq")
    buffer = jnp.stack([buffer[jnp.bitwise_xor(index, other)] for other in order])
    return buffer.reshape(parts, blocks, -1, LANES)


def in_spots(buffer):
    blocks = buffer.shape[-3]
    index = lax.axis_index("batch")
    order = [spot * 2 % blocks + spot * 2 // blocks for spot in range(blocks)]
    return jnp.stack(
        [
            lax.dynamic_index_in_dim(buffer, jnp.bitwise_xor(index, other), -3, keepdims=False)
            for other in order
        ],
        axis=-3,
    )


def exchange(member, axis, distance):
    pairs = [(peer, peer ^ distance) for peer in range(lax.axis_size(axis))]
    return lax.ppermute(member, axis, pairs)


def seq_near(keep, send, anchors=()):
    half = keep.shape[1] // 2
    pieces = [(part, start, start + half) for part in range(2) for start in (half, 0)]
    return add([keep, exchange(send, "seq", 1)], pieces, anchors)


def seq_far_send(quarters, beside=(), anchors=()):
    near, far = quarters[0], quarters[2]
    rows = near.shape[1]
    sources = [near, exchange(far, "seq", 2)]
    plan = [(rows, ((0, 0), (1, 0)))]
    if beside:
        sources, plan = sources + [beside[1]], plan + [(beside[1].shape[1], ((2, 0),))]
    return merge(sources, plan, False, anchors)[0]


def seq_far_keep(quarters, leaving, beside=(), others=(), anchors=()):
    near, far = quarters[1], quarters[3]
    rows = near.shape[1]
    if others:
        far = behind(far, *others)
    sources = [near, exchange(far, "seq", 2), exchange(leaving, "batch", 1)]
    plan = [(rows, ((0, 0), (1, 0), (2, 0)))]
    if beside:
        sources, plan = sources + [beside[0]], plan + [(beside[0].shape[1], ((3, 0), (2, rows)))]
    return merge(sources, plan, True, anchors)


def batch_halves(keep, send, anchors=()):
    return add([keep, exchange(send, "batch", 1)], list(range(keep.shape[0])), anchors)


def batch_rest(sums):
    return [sums[0]] + [
        exchange(sums[spot], "batch", 2 * spot) for spot in range(1, len(sums))
    ]


def plain_sums(buffer):
    level = 1
    while buffer.shape[0] > 1:
        half = buffer.shape[0] // 2
        got = exchange(buffer[half:], "seq", level)
        buffer = (buffer[:half].astype(F32) + got.astype(F32)).astype(BF16)
        level *= 2
    return plain_batch(buffer[0])


def plain_batch(buffer):
    half = buffer.shape[0] // 2
    got = exchange(buffer[half:], "batch", 1)
    sums = (buffer[:half].astype(F32) + got.astype(F32)).astype(BF16)
    total = sums[0].astype(F32)
    for spot in range(1, half):
        total += exchange(sums[spot], "batch", 2 * spot).astype(F32)
    return total.astype(BF16)


def behind(member, *others):
    return lax.optimization_barrier((member, *others))[0]


def seq_gather(member, *between):
    parts = lax.axis_size("seq")
    found, level = {0: member}, parts // 2
    while level >= 1:
        for distance, held in list(found.items()):
            found[distance ^ level] = exchange(held, "seq", level)
        if level == parts // 2 and between:
            found[level] = behind(found[level], *between)
        level //= 2
    return [found[distance] for distance in range(parts)]


def in_order(found):
    found = jnp.stack(found)
    index = lax.axis_index("seq")
    return jnp.stack([found[jnp.bitwise_xor(index, part)] for part in range(len(found))])


def unpack(gathered, shapes, blocks):
    parts = gathered.shape[0]
    gathered = gathered.reshape(parts, -1)
    found, start = [], 0
    for height, width in shapes:
        height, columns = height // blocks, width // parts
        piece = gathered[:, start : start + height * columns]
        piece = piece.reshape(parts, height, columns).transpose(1, 0, 2)
        start += height * columns
        found.append(piece.reshape(height, width).astype(F32))
    return found


def local(
    byte_ids,
    embedding,
    norm_gains,
    norm_biases,
    qkv_weights,
    qkv_biases,
    out_weights,
    out_biases,
    expand_weights,
    expand_biases,
    reduce_weights,
    reduce_biases,
    pool_weight,
    pool_bias,
    upsample_weight,
    upsample_bias,
    cotangent,
):
    parts, blocks = lax.axis_size("seq"), lax.axis_size("batch")
    rows, width, hidden = byte_ids.shape[1], embedding.shape[1], expand_weights.shape[2]
    index = jnp.stack([lax.axis_index("seq"), lax.axis_index("batch")]).astype(jnp.int32)
    ids = seq_gather(byte_ids)
    all_cot = lax.all_gather(cotangent[0], "seq", axis=0, tiled=True)

    (embedding, norm_gains, norm_biases, qkv_weights, qkv_biases, out_weights, out_biases) = (
        far_away(member)
        for member in (
            embedding, norm_gains, norm_biases, qkv_weights, qkv_biases, out_weights, out_biases
        )
    )
    (expand_weights, expand_biases, reduce_weights, reduce_biases, pool_weight) = (
        far_away(member)
        for member in (expand_weights, expand_biases, reduce_weights, reduce_biases, pool_weight)
    )
    (pool_bias, upsample_weight, upsample_bias) = (
        far_away(member) for member in (pool_bias[None], upsample_weight, upsample_bias[None])
    )

    coarse, fine = byte_table(embedding, norm_gains, norm_biases, qkv_weights, qkv_biases)
    h1_low, share, queries, keys, keys_t, values, mixed, lse, middle, active, rate, all_ids = outer_forward(
        index, ids, embedding, norm_gains, norm_biases, coarse, fine, out_weights, out_biases,
        expand_weights, expand_biases, reduce_weights, reduce_biases, pool_weight, rows
    )
    raised_grad, grad_short, raised_sums = raised_back(all_cot, upsample_weight)
    shares = seq_gather(share, raised_sums)
    short_low, gz, inner_vecs, inner_found, inner_packed = inner_layer(
        index, shares, pool_bias, norm_gains, norm_biases, qkv_weights, qkv_biases,
        out_weights, out_biases, expand_weights, expand_biases, reduce_weights, reduce_biases,
        raised_grad, grad_short, parts, blocks
    )
    lows = lax.all_gather(behind(h1_low, shares[-1]), "seq", axis=0)
    output = raised_output(index, lows, short_low, upsample_weight, upsample_bias)

    (grad_middle, grad_mixed, hidden_vecs), early, early_packed, early_shapes = outer_hidden(
        index, lows, gz, inner_vecs, raised_sums, all_cot, middle, active, rate, mixed, norm_gains,
        norm_biases, pool_weight, reduce_weights, expand_weights, out_weights, parts, blocks
    )

    def attention_back(quad, ending, anchors):
        return outer_attention(
            quad, index, all_ids, embedding, norm_gains, norm_biases, qkv_weights, queries, keys,
            keys_t, values, mixed, lse, grad_mixed, ending, anchors, parts, blocks
        )

    anchors = []
    packed = inner_packed and early_packed
    if packed:
        quarters = seq_near(*early[0:2], [output])
        inner_sums = batch_halves(*inner_found, quarters[:1])
        anchors = inner_sums + quarters
    ending, late_packed = attention_back(0, None, anchors)
    if packed:
        leaving = seq_far_send(quarters, early[2:4], ending[:1])
        inner_rest = batch_rest(inner_sums)
        anchors = [inner_rest[1], leaving]
    (table_vecs, *late), _ = attention_back(1, [grad_middle] + list(ending), anchors)
    if packed and late_packed:
        early_sums = seq_far_keep(quarters, leaving, early[2:4], ending[:1])
        late_quarters = seq_near(*late, early_sums[:1])
        late_sums = seq_far_keep(late_quarters, seq_far_send(late_quarters))
        gathered = seq_gather(totals([[totals([inner_rest])], batch_rest(early_sums)]))
        late_total = totals([batch_rest(late_sums)])
        found = list(
            assemble(index, gathered, seq_gather(late_total), width, hidden, embedding.shape[0], parts, blocks)
        )
        found[12], found[14] = found[12][0], found[14][0]
        return (output, *found)

    inner_shapes = inner_shapes_of(width, hidden)
    inner_buffer = jnp.concatenate([member.reshape(blocks, -1) for member in inner_found], axis=1)
    inner_buffer = in_spots(inner_buffer.reshape(blocks, -1, LANES))
    inner_out = unpack(in_order(seq_gather(plain_batch(inner_buffer))), inner_shapes, blocks)
    pool_buffer = in_spots(early[3].reshape(blocks, -1, LANES))
    pool_out = unpack(
        in_order(seq_gather(plain_batch(pool_buffer))), [(POOL * width, width)], blocks
    )
    early_buffer = in_spots(pack(early[:3], parts, blocks))
    early_out = unpack(
        in_order(seq_gather(plain_sums(early_buffer))), early_shapes, blocks
    )
    wide = QUAD * HD
    qkv_grad = jnp.concatenate(
        [
            half[:, part * wide : (part + 1) * wide]
            for part in range(3)
            for half in (ending[1], late[0])
        ],
        axis=1,
    )
    late, late_shapes = [qkv_grad, late[1]], [qkv_grad.shape, late[1].shape]
    late_buffer = in_spots(pack(late, parts, blocks))
    late_out = unpack(
        in_order(seq_gather(plain_sums(late_buffer))), late_shapes, blocks
    )
    once = 1.0 / parts
    vectors = [
        table_vecs[0, :width],
        hidden_vecs[0, :width],
        table_vecs[1, :width],
        hidden_vecs[1, :width],
        table_vecs[2, : 3 * width],
        hidden_vecs[4, :width],
        hidden_vecs[2, :hidden],
        hidden_vecs[3, :width],
        inner_vecs[0, :width] * once,
        inner_vecs[1, :width] * once,
        inner_vecs[2, :width] * once,
        inner_vecs[3, :width] * once,
        inner_vecs[4, : 3 * width] * once,
        inner_vecs[5, :width] * once,
        inner_vecs[6, :hidden] * once,
        inner_vecs[7, :width] * once,
        inner_vecs[8, :width] * once,
        raised_sums[0] * once,
    ]
    flat = jnp.concatenate([member.reshape(blocks, -1) for member in vectors], axis=1)
    flat = lax.psum(flat.astype(BF16), ("seq", "batch")).astype(F32)
    flat = lax.dynamic_index_in_dim(flat, lax.axis_index("batch"), 0, keepdims=False)
    sums, start = [], 0
    for member in vectors:
        sums.append(flat[start : start + member.shape[0] // blocks])
        start += member.shape[0] // blocks
    return (
        output,
        late_out[1],
        jnp.stack([jnp.stack([sums[0], sums[1]]), jnp.stack([sums[8], sums[9]])]),
        jnp.stack([jnp.stack([sums[2], sums[3]]), jnp.stack([sums[10], sums[11]])]),
        jnp.stack([late_out[0], inner_out[4]]),
        jnp.stack([sums[4], sums[12]]),
        jnp.stack([early_out[2], inner_out[3]]),
        jnp.stack([sums[5], sums[13]]),
        jnp.stack([early_out[1], inner_out[1]]),
        jnp.stack([sums[6], sums[14]]),
        jnp.stack([early_out[0], inner_out[0]]),
        jnp.stack([sums[7], sums[15]]),
        pool_out[0],
        sums[16],
        inner_out[2],
        sums[17],
    )


def solution(mesh):
    whole = P()
    return jax.shard_map(
        local,
        mesh=mesh,
        in_specs=(P("batch", "seq"),) + (whole,) * 15 + (P("batch", "seq", None),),
        out_specs=(
            P("batch", "seq", None),
            P("batch", None),
            P(None, None, "batch"),
            P(None, None, "batch"),
            P(None, "batch", None),
            P(None, "batch"),
            P(None, "batch", None),
            P(None, "batch"),
            P(None, "batch", None),
            P(None, "batch"),
            P(None, "batch", None),
            P(None, "batch"),
            P("batch", None),
            P("batch"),
            P("batch", None),
            P("batch"),
        ),
        check_vma=False,
    )
```

```python
import functools

import jax
import jax.numpy as jnp
import numpy as np
from jax import lax
from jax.experimental import pallas as pl
from jax.experimental.pallas import tpu as pltpu
from jax.sharding import PartitionSpec as P

HD = 64
POOL = 3
QUAD = 4
LANES = 128
VMEM_LIMIT = 60 * 1024 * 1024
F32 = jnp.float32
BF16 = jnp.bfloat16


def dot(left, right):
    return jnp.dot(left, right, preferred_element_type=F32)


def dot_nt(left, right):
    return lax.dot_general(left, right, (((1,), (1,)), ((), ())), preferred_element_type=F32)


def dot_tn(left, right):
    return lax.dot_general(left, right, (((0,), (0,)), ((), ())), preferred_element_type=F32)


def gelu_parts(pre):
    slope = 0.7978845608028654
    square = pre * pre
    bent = jnp.tanh(slope * pre * (1.0 + 0.044715 * square))
    half = 0.5 * (1.0 + bent)
    value = pre * half
    rate = half + 0.5 * pre * (1.0 - bent * bent) * (slope * (1.0 + 3.0 * 0.044715 * square))
    return (value, rate)


def angle_rows(length):
    frequency = 10000.0 ** (-np.arange(HD // 2, dtype=np.float64) / (HD // 2))
    angles = np.arange(length, dtype=np.float64)[:, None] * frequency[None, :]
    return (np.cos(angles).astype(np.float32), np.sin(angles).astype(np.float32))


def cost(microseconds):
    microseconds *= 10
    return pl.CostEstimate(
        flops=int(microseconds * 1e9), bytes_accessed=int(microseconds * 1e6), transcendentals=0
    )


def grant(megabytes, factor=1):
    return min(int(megabytes * factor), 60) * 1024 * 1024


def outside(shape, dtype):
    return pltpu.HBM(shape, dtype)


def far_away(member):
    return pltpu.with_memory_space_constraint(member, pltpu.HBM)


def copy_in(pairs, sems, start=0):
    moves = [
        pltpu.make_async_copy(src, dst, sems.at[start + i]) for i, (src, dst) in enumerate(pairs)
    ]
    for move in moves:
        move.start()
    return moves


def chunk_of(index, which, parts):
    return index + which * (2 * parts - 1 - 2 * index)


def by_blocks(index, parts, body):
    if parts != 4:
        full = [chunk_of(index, which, parts) // 2 for which in range(2)]
        body(full, full[1] + 1)
        return

    @pl.when(index < 2)
    def _():
        body([0, 3], 4)

    @pl.when(index >= 2)
    def _():
        body([1, 2], 3)


def each(count, step):
    if isinstance(count, int):
        for i in range(count):
            step(i)
    else:
        lax.fori_loop(0, count, lambda i, carry: (step(i), carry)[1], 0)


def own_lanes(row, index, parts, chunk):
    length = row.shape[1]
    return jnp.concatenate(
        [
            pltpu.roll(row, (length - chunk_of(index, which, parts) * chunk) % length, 1)[:, :chunk]
            for which in range(2)
        ],
        axis=1,
    )


def quad_rows(rows):
    lane = lax.broadcasted_iota(jnp.int32, rows.shape, 1) // HD
    zero = jnp.zeros_like(rows)
    return jnp.concatenate([jnp.where(lane == head, rows, zero) for head in range(QUAD)], axis=0)


def quad_fold(tall):
    count = tall.shape[0] // QUAD
    lane = lax.broadcasted_iota(jnp.int32, (count, tall.shape[1]), 1) // HD
    folded = jnp.zeros((count, tall.shape[1]), tall.dtype)
    for head in range(QUAD):
        folded = jnp.where(lane == head, tall[head * count : (head + 1) * count], folded)
    return folded


def lanes_of(quad):
    return slice(quad * QUAD * HD, (quad + 1) * QUAD * HD)


def causal(scores, key_start, query_start):
    count = scores.shape[1] // QUAD
    key = key_start + lax.broadcasted_iota(jnp.int32, scores.shape, 0)
    query = lax.broadcasted_iota(jnp.int32, (1, scores.shape[1]), 1)
    for head in range(1, QUAD):
        query = jnp.where(query >= count, query - count, query)
    return jnp.where(key <= query + query_start, scores, -1e30)


def flash_quads(tall_q, keys_at, values_at, full, key_start_last, query_start, state):
    quads = range(len(tall_q))
    acc, peak, total = state

    def scores_of(j):
        return [dot_nt(keys_at(j, quad), tall_q[quad]) for quad in quads]

    scores = [causal(member, key_start_last, query_start) for member in scores_of(full)]
    tops = [jnp.max(member, axis=0, keepdims=True) for member in scores]
    raised = [jnp.exp(scores[quad] - tops[quad]) for quad in quads]
    for quad in quads:
        peak[quad] = tops[quad]
        total[quad] = jnp.sum(raised[quad], axis=0, keepdims=True)
        acc[quad] = dot(values_at(full, quad), raised[quad].astype(BF16))

    def block(j):
        scores = scores_of(j)
        tops = [
            jnp.maximum(peak[quad], jnp.max(scores[quad], axis=0, keepdims=True)) for quad in quads
        ]
        raised = [jnp.exp(scores[quad] - tops[quad]) for quad in quads]
        for quad in quads:
            shrink = jnp.exp(peak[quad] - tops[quad])
            peak[quad] = tops[quad]
            total[quad] = total[quad] * shrink + jnp.sum(raised[quad], axis=0, keepdims=True)
            acc[quad] = acc[quad] * shrink + dot(values_at(j, quad), raised[quad].astype(BF16))

    each(full, block)
    return [
        (quad_fold((acc[quad] / total[quad]).T), peak[quad] + jnp.log(total[quad]))
        for quad in quads
    ]


def every_third(split_ref, start, count):
    return jnp.concatenate(
        [split_ref[i, pl.ds(start, count, stride=POOL), :] for i in range(split_ref.shape[0])],
        axis=1,
    )


def unit_rows(stream):
    centred = stream - jnp.mean(stream, axis=-1, keepdims=True)
    inverse = lax.rsqrt(jnp.mean(centred * centred, axis=-1, keepdims=True) + 1e-05)
    return (centred * inverse, inverse)


def table_kernel(emb_ref, gains_ref, shifts_ref, qkv_w_any, qkv_b_ref, coarse_ref, fine_ref, qkv_w, sems):
    width = emb_ref.shape[1]
    moves = copy_in([(qkv_w_any.at[0], qkv_w)], sems)
    unit, _ = unit_rows(emb_ref[...].astype(F32))
    normed = (unit * gains_ref[0, 0:1] + shifts_ref[0, 0:1]).astype(BF16)
    moves[0].wait()
    table = (dot(normed, qkv_w[...]) + qkv_b_ref[0:1]).T
    coarse = table.astype(BF16)
    coarse_ref[...] = coarse
    fine_ref[...] = (table[: 2 * width] - coarse[: 2 * width].astype(F32)).astype(BF16)


def byte_table(embedding, gains, shifts, qkv_w, qkv_b):
    vocab, width = embedding.shape
    vmem = pl.BlockSpec(memory_space=pltpu.VMEM)
    far = pl.BlockSpec(memory_space=pltpu.HBM)
    return pl.pallas_call(
        table_kernel,
        name="byte_table",
        in_specs=[vmem, vmem, vmem, far, vmem],
        out_specs=[vmem, vmem],
        out_shape=[
            jax.ShapeDtypeStruct((3 * width, vocab), BF16),
            jax.ShapeDtypeStruct((2 * width, vocab), BF16),
        ],
        scratch_shapes=[pltpu.VMEM((width, 3 * width), BF16), pltpu.SemaphoreType.DMA((1,))],
        compiler_params=pltpu.CompilerParams(vmem_limit_bytes=grant(16)),
        cost_estimate=cost(4),
    )(embedding, gains, shifts, qkv_w, qkv_b)


def outer_forward_kernel(
    parts,
    index_ref,
    *rest,
):
    ids, rest = rest[:parts], rest[parts:]
    (
    emb_ref,
    gains_ref,
    shifts_ref,
    coarse_any,
    fine_any,
    out_w_any,
    out_b_ref,
    expand_w_any,
    expand_b_ref,
    reduce_w_any,
    reduce_b_ref,
    pool_w_any,
    cos_ref,
    sin_ref,
    low_ref,
    share_ref,
    q_any,
    k_any,
    kt_any,
    v_any,
    o_any,
    lse_ref,
    middle_any,
    active_any,
    rate_any,
    ids_ref,
    q_ref,
    k_ref,
    kt_ref,
    v_ref,
    o_ref,
    middle_ref,
    active_ref,
    rate_ref,
    out_w,
    expand_w,
    reduce_w,
    pool_w,
    coarse_ref,
    fine_ref,
    vt_ref,
    acc_ref,
    peak_ref,
    total_ref,
    second_ref,
    sum_ref,
    later_ref,
    split_ref,
    sems,
    ) = rest
    index = index_ref[0]
    rows, width = middle_ref.shape
    vocab = emb_ref.shape[0]
    chunk = rows // 2
    moves = copy_in(
        [
            (coarse_any, coarse_ref),
            (fine_any, fine_ref),
            (out_w_any.at[0], out_w),
            (expand_w_any.at[0], expand_w),
            (reduce_w_any.at[0], reduce_w),
            (pool_w_any, pool_w),
        ],
        sems,
    )

    for distance in range(parts):
        part = jnp.bitwise_xor(index, distance)
        ids_ref[:, pl.ds(pl.multiple_of(part * rows, rows), rows)] = ids[distance][...]
    moves[0].wait()
    moves[1].wait()

    def picked(start, hot):
        return dot(coarse_ref[start : start + width], hot) + dot(
            fine_ref[start : start + width], hot
        )

    def turned(member, cosine, sine):
        pieces = []
        for head in range(width // HD):
            first = member[head * HD : head * HD + HD // 2]
            second = member[head * HD + HD // 2 : (head + 1) * HD]
            pieces += [first * cosine - second * sine, first * sine + second * cosine]
        return jnp.concatenate(pieces, axis=0)

    codes = lax.broadcasted_iota(jnp.int32, (vocab, rows), 0)

    def block_of(j):
        if isinstance(j, int):
            return slice(j * rows, (j + 1) * rows)
        return pl.ds(pl.multiple_of(j * rows, rows), rows)

    def key_block(j):
        columns = block_of(j)
        hot = (codes == ids_ref[:, columns]).astype(F32).astype(BF16)
        keys = turned(picked(width, hot), cos_ref[:, columns], sin_ref[:, columns])
        kt_ref[:, columns] = keys.astype(BF16)
        k_ref[columns, :] = keys.T.astype(BF16)
        values = dot(coarse_ref[2 * width : 3 * width], hot)
        vt_ref[:, columns] = values.astype(BF16)
        v_ref[columns, :] = values.T.astype(BF16)

    by_blocks(index, parts, lambda full, seen: each(seen, key_block))
    moves += copy_in([(k_ref, k_any), (kt_ref, kt_any), (v_ref, v_any)], sems, 6)
    own_ids = own_lanes(jnp.broadcast_to(ids_ref[...], (8, ids_ref.shape[1])), index, parts, chunk)
    own = (codes == own_ids[0:1]).astype(F32)
    queries = turned(
        picked(0, own.astype(BF16)),
        own_lanes(cos_ref[...], index, parts, chunk),
        own_lanes(sin_ref[...], index, parts, chunk),
    )
    q_ref[...] = (queries * HD**-0.5).T.astype(BF16)
    middle_ref[...] = dot(own.T.astype(BF16), emb_ref[...])

    quads = width // (QUAD * HD)

    def attend(full, seen):
        for which in range(2):
            own_rows = slice(which * chunk, (which + 1) * chunk)
            place = chunk_of(index, which, parts)
            found = flash_quads(
                [quad_rows(q_ref[own_rows, lanes_of(quad)]) for quad in range(quads)],
                lambda j, quad: k_ref[block_of(j), lanes_of(quad)],
                lambda j, quad: vt_ref[lanes_of(quad), block_of(j)],
                full[which],
                full[which] * rows,
                place * chunk,
                (acc_ref.at[which], peak_ref.at[which], total_ref.at[which]),
            )
            for quad, (mixed, lse) in enumerate(found):
                o_ref[own_rows, lanes_of(quad)] = mixed.astype(BF16)
                row = which * quads + quad
                lse_ref[row : row + 1, :] = lse

    by_blocks(index, parts, attend)

    moves += copy_in([(q_ref, q_any), (o_ref, o_any)], sems, 9)
    moves[2].wait()
    middle = middle_ref[...] + dot(o_ref[...], out_w[...]) + out_b_ref[0:1]
    middle_ref[...] = middle
    moves += copy_in([(middle_ref, middle_any)], sems, 11)
    unit, _ = unit_rows(middle)
    second_ref[...] = (unit * gains_ref[0, 1:2] + shifts_ref[0, 1:2]).astype(BF16)
    sum_ref[...] = middle + reduce_b_ref[0:1]
    moves[3].wait()
    moves[4].wait()

    for c in range(expand_w.shape[1] // width):
        columns = slice(c * width, (c + 1) * width)
        pre = dot(second_ref[...], expand_w[:, columns]) + expand_b_ref[0:1, columns]
        value, rate = gelu_parts(pre)
        value = value.astype(BF16)
        active_ref[:, columns] = value
        rate_ref[:, columns] = rate.astype(BF16)
        moves += copy_in(
            [
                (active_ref.at[:, columns], active_any.at[:, columns]),
                (rate_ref.at[:, columns], rate_any.at[:, columns]),
            ],
            sems,
            12 + 2 * c,
        )
        sum_ref[...] += dot(value, reduce_w[columns, :])
    low_ref[...] = sum_ref[...].astype(BF16)

    moves[5].wait()
    third = rows // POOL

    for lane in range(width // LANES):
        split_ref[lane] = sum_ref[:, lane * LANES : (lane + 1) * LANES]

    def thirds(start):
        return every_third(split_ref, start, third).astype(BF16)

    later = dot(thirds(1), pool_w[0:width]) + dot(thirds(2), pool_w[width : 2 * width])
    same = dot(thirds(0), pool_w[2 * width : 3 * width])
    half = third // 2
    for which in range(2):
        start = which * (half + 8)
        later_ref[start : start + 8] = jnp.zeros((8, width), F32)
        later_ref[start + half : start + half + 8] = jnp.zeros((8, width), F32)
        later_ref[start + 1 : start + half + 1] = later[which * half : (which + 1) * half]
        share_ref[start : start + half] = (
            later_ref[start : start + half] + same[which * half : (which + 1) * half]
        ).astype(BF16)
        share_ref[start + half : start + half + 8] = later_ref[
            start + half : start + half + 8
        ].astype(BF16)
    for move in moves[6:]:
        move.wait()


def outer_forward(index, ids, embedding, gains, shifts, coarse, fine, out_w, out_b, expand_w,
                  expand_b, reduce_w, reduce_b, pool_w, rows):
    length = rows * len(ids)
    vocab, width = embedding.shape
    hidden = expand_w.shape[2]
    chunk, quads = rows // 2, width // (QUAD * HD)
    cosine, sine = angle_rows(length)
    vmem = pl.BlockSpec(memory_space=pltpu.VMEM)
    far = pl.BlockSpec(memory_space=pltpu.HBM)
    shape = outside
    third = rows // POOL
    kept = [
        shape((rows, width), BF16),
        shape((length, width), BF16),
        shape((width, length), BF16),
        shape((length, width), BF16),
        shape((rows, width), BF16),
        shape((rows, width), F32),
        shape((rows, hidden), BF16),
        shape((rows, hidden), BF16),
    ]
    return pl.pallas_call(
        functools.partial(outer_forward_kernel, length // rows),
        name="outer_forward",
        in_specs=[pl.BlockSpec(memory_space=pltpu.SMEM)] + [vmem] * (len(ids) + 3) + [far, far,
                  far, vmem, far, vmem, far, vmem, far, vmem, vmem],
        out_specs=[vmem] * 2 + [far] * 5 + [vmem] + [far] * 3 + [vmem],
        out_shape=[
            shape((rows, width), BF16),
            shape((third + 16, width), BF16),
        ]
        + kept[:5]
        + [shape((2 * quads, QUAD * chunk), F32)]
        + kept[5:]
        + [shape((1, length), jnp.int32)],
        scratch_shapes=[pltpu.VMEM(member.shape, member.dtype) for member in kept]
        + [
            pltpu.VMEM((width, width), BF16),
            pltpu.VMEM((width, hidden), BF16),
            pltpu.VMEM((hidden, width), BF16),
            pltpu.VMEM((POOL * width, width), BF16),
            pltpu.VMEM((3 * width, vocab), BF16),
            pltpu.VMEM((2 * width, vocab), BF16),
            pltpu.VMEM((width, length), BF16),
            pltpu.VMEM((2, quads, QUAD * HD, QUAD * chunk), F32),
            pltpu.VMEM((2, quads, 1, QUAD * chunk), F32),
            pltpu.VMEM((2, quads, 1, QUAD * chunk), F32),
            pltpu.VMEM((rows, width), BF16),
            pltpu.VMEM((rows, width), F32),
            pltpu.VMEM((third + 16, width), F32),
            pltpu.VMEM((width // LANES, rows, LANES), F32),
            pltpu.SemaphoreType.DMA((12 + 2 * (hidden // width),)),
        ],
        compiler_params=pltpu.CompilerParams(vmem_limit_bytes=grant(48 if length == 4 * rows else 60)),
        cost_estimate=cost(30),
    )(index, *ids, embedding, gains, shifts, coarse, fine, out_w, out_b, expand_w, expand_b,
      reduce_w, reduce_b, pool_w, far_away(jnp.asarray(cosine.T)), far_away(jnp.asarray(sine.T)))


def turn_rows(member, cosine, sine):
    pieces = []
    for start in range(0, member.shape[1], LANES):
        tile = member[:, start : start + LANES]
        lane = lax.broadcasted_iota(jnp.int32, tile.shape, 1) % HD
        other = jnp.where(
            lane < HD // 2,
            pltpu.roll(tile, LANES - HD // 2, 1),
            pltpu.roll(tile, HD // 2, 1),
        )
        pieces.append(tile * cosine + other * sine)
    return jnp.concatenate(pieces, axis=1)


def norm_back_rows(grad, unit, inverse, gain):
    scaled = grad * gain
    mean_one = jnp.mean(scaled, axis=-1, keepdims=True)
    mean_two = jnp.mean(scaled * unit, axis=-1, keepdims=True)
    return inverse * (scaled - mean_one - unit * mean_two)


def head_sums(product):
    tall = product.T
    return jnp.concatenate(
        [
            jnp.sum(tall[head * HD : (head + 1) * HD], axis=0, keepdims=True)
            for head in range(QUAD)
        ],
        axis=1,
    )


def back_block(scores, lse, delta, tall_q, tall_g, keys_t, values):
    probs = jnp.exp(scores - lse)
    low = (probs * (dot_nt(values, tall_g) - delta)).astype(BF16)
    return (dot(low, tall_q), dot(probs.astype(BF16), tall_g), dot(keys_t, low))


def share_columns(member_ref, index, parts):
    width = member_ref.shape[1] // parts
    if width % LANES == 0:
        return member_ref[:, pl.ds(pl.multiple_of(index * width, LANES), width)]
    full = member_ref.shape[1]
    row = lax.broadcasted_iota(jnp.int32, (full, width), 0)
    column = lax.broadcasted_iota(jnp.int32, (full, width), 1)
    picks = (row == column + index * width).astype(F32).astype(BF16)
    return dot(member_ref[...], picks).astype(BF16)


def can_pack(shapes, parts, blocks):
    return parts == 4 and all(
        rows % (16 * blocks) == 0 and columns % (LANES * parts) == 0 for rows, columns in shapes
    )


def packed_rows(shapes, parts, blocks):
    return sum(rows // blocks * (columns // parts // LANES) for rows, columns in shapes)


def spot_of(block, own_block, blocks):
    distance = jnp.bitwise_xor(own_block, block)
    return distance % 2 * (blocks // 2) + distance // 2


def store_packed(out, start, member, own_block, blocks):
    rows, columns = member.shape[0] // blocks, member.shape[1]
    for block in range(blocks):
        spot = spot_of(block, own_block, blocks)
        for tile in range(columns // LANES):
            out[spot, start + tile * rows : start + (tile + 1) * rows, :] = member[
                block * rows : (block + 1) * rows, tile * LANES : (tile + 1) * LANES
            ]
    return start + rows * (columns // LANES)


def inner_kernel(
    parts,
    blocks,
    packed,
    query_rows,
    index_ref,
    *rest,
):
    shares, rest = rest[:parts], rest[parts:]
    (
    pool_b_ref,
    gains_ref,
    shifts_ref,
    qkv_w_any,
    qkv_b_ref,
    out_w_any,
    out_b_ref,
    expand_w_any,
    expand_b_ref,
    reduce_w_any,
    reduce_b_ref,
    raised_grad_any,
    grad_any,
    cos_ref,
    sin_ref,
    ) = rest[:15]
    rest = rest[15:]
    outs = 2 if packed else 5
    low_ref, gz_ref, vec_ref = rest[:3]
    mats = rest[3 : 3 + outs]
    (
        qkv_w,
        out_w,
        expand_w,
        reduce_w,
        stream_ref,
        normed_ref,
        q_ref,
        k_ref,
        kt_ref,
        v_ref,
        vt_ref,
        o_ref,
        lse_ref,
        middle_ref,
        second_ref,
        active_ref,
        rate_ref,
        sum_ref,
        pre_ref,
        att_ref,
        go_ref,
        gk_ref,
        gv_ref,
        acc_ref,
        peak_ref,
        total_ref,
        raised_grad_ref,
        grad_ref,
        sems,
        *buffers,
    ) = rest[3 + outs :]
    index, own_block = index_ref[0], index_ref[1]
    rows, width = stream_ref.shape
    hidden_width = expand_w.shape[1]
    gq_ref, gqkv_ref = sum_ref, rate_ref.at[:, 0 : 3 * width]
    quads = width // (QUAD * HD)
    moves = copy_in(
        [
            (qkv_w_any.at[1], qkv_w),
            (out_w_any.at[1], out_w),
            (expand_w_any.at[1], expand_w),
            (reduce_w_any.at[1], reduce_w),
            (grad_any, grad_ref),
            (raised_grad_any, raised_grad_ref),
        ],
        sems,
    )
    share = rows // parts
    half = share // 2
    chunks = [
        (shares[distance], which * (half + 8), chunk_of(jnp.bitwise_xor(index, distance), which, parts))
        for distance in range(parts)
        for which in range(2)
    ]
    for given, start, place in chunks:
        own = pl.ds(pl.multiple_of(place * half, half), half)
        stream_ref[own] = given[start : start + half].astype(F32) + pool_b_ref[...]
    for given, start, place in chunks:

        @pl.when(place < 2 * parts - 1)
        def _():
            head = pl.ds(pl.multiple_of((place + 1) * half, half), 8)
            stream_ref[head] += given[start + half : start + half + 8].astype(F32)

    unit, _ = unit_rows(stream_ref[...])
    normed_ref[...] = (unit * gains_ref[1, 0:1] + shifts_ref[1, 0:1]).astype(BF16)
    moves[0].wait()

    def projected(part):
        columns = slice(part * width, (part + 1) * width)
        return dot(normed_ref[...], qkv_w[:, columns]) + qkv_b_ref[1:2, columns]

    cosine, sine = cos_ref[...], sin_ref[...]
    q_ref[...] = (turn_rows(projected(0), cosine, sine) * HD**-0.5).astype(BF16)
    keys = turn_rows(projected(1), cosine, sine)
    k_ref[...] = keys.astype(BF16)
    kt_ref[...] = keys.T.astype(BF16)
    values = projected(2)
    v_ref[...] = values.astype(BF16)
    vt_ref[...] = values.T.astype(BF16)

    def block_of(j):
        return pl.ds(pl.multiple_of(j * query_rows, query_rows), query_rows)

    def part(which, carry):
        own_rows = block_of(which)
        found = flash_quads(
            [quad_rows(q_ref[own_rows, lanes_of(quad)]) for quad in range(quads)],
            lambda j, quad: k_ref[block_of(j), lanes_of(quad)],
            lambda j, quad: vt_ref[lanes_of(quad), block_of(j)],
            which,
            which * query_rows,
            which * query_rows,
            (acc_ref, peak_ref, total_ref),
        )
        for quad, (mixed, lse) in enumerate(found):
            o_ref[own_rows, lanes_of(quad)] = mixed.astype(BF16)
            lse_ref[pl.ds(which * quads + quad, 1), :] = lse
        return carry

    lax.fori_loop(0, rows // query_rows, part, 0, unroll=parts == 4)
    moves[1].wait()
    middle = stream_ref[...] + dot(o_ref[...], out_w[...]) + out_b_ref[1:2]
    middle_ref[...] = middle
    unit, _ = unit_rows(middle)
    second_ref[...] = (unit * gains_ref[1, 1:2] + shifts_ref[1, 1:2]).astype(BF16)
    sum_ref[...] = middle + reduce_b_ref[1:2]
    moves[2].wait()
    moves[3].wait()

    def columns_of(c):
        return pl.ds(pl.multiple_of(c * width, width), width)

    def hidden(c, carry):
        columns = columns_of(c)
        pre = dot(second_ref[...], expand_w[:, columns]) + expand_b_ref[1:2, columns]
        value, rate = gelu_parts(pre)
        value = value.astype(BF16)
        active_ref[:, columns] = value
        rate_ref[:, columns] = rate.astype(BF16)
        sum_ref[...] += dot(value, reduce_w[columns, :])
        return carry

    lax.fori_loop(0, hidden_width // width, hidden, 0, unroll=parts == 4)
    low_ref[...] = sum_ref[...].astype(BF16)

    vec_ref[...] = jnp.zeros(vec_ref.shape, F32)

    def column_sum(row, member):
        vec_ref[row : row + 1, 0 : member.shape[1]] = jnp.sum(member, axis=0, keepdims=True)

    moves[4].wait()
    moves[5].wait()
    grad_low = grad_ref[...].astype(BF16)
    column_sum(7, grad_low.astype(F32))
    att_ref[...] = grad_low
    sum_ref[...] = jnp.zeros(sum_ref.shape, F32)

    def hidden_back(c, carry):
        columns = columns_of(c)
        pre = dot_nt(att_ref[...], reduce_w[columns, :]) * rate_ref[:, columns].astype(F32)
        low = pre.astype(BF16)
        pre_ref[:, columns] = low
        vec_ref[6:7, columns] = jnp.sum(low.astype(F32), axis=0, keepdims=True)
        sum_ref[...] += dot_nt(low, expand_w[:, columns])
        return carry

    lax.fori_loop(0, hidden_width // width, hidden_back, 0, unroll=parts == 4)
    if packed:
        place = store_packed(
            buffers[0], 0, dot_tn(active_ref[...], share_columns(att_ref, index, parts)).astype(BF16), own_block, blocks
        )
        place = store_packed(
            buffers[0], place, dot_tn(second_ref[...], share_columns(pre_ref, index, parts)).astype(BF16), own_block, blocks
        )
        place = store_packed(
            buffers[0], place, dot_tn(low_ref[...], share_columns(raised_grad_ref, index, parts)).astype(BF16), own_block, blocks
        )
    else:
        mats[0][...] = dot_tn(active_ref[...], share_columns(att_ref, index, parts)).astype(BF16)
        mats[1][...] = dot_tn(second_ref[...], share_columns(pre_ref, index, parts)).astype(BF16)
        mats[2][...] = dot_tn(low_ref[...], share_columns(raised_grad_ref, index, parts)).astype(BF16)

    unit, inverse = unit_rows(middle_ref[...])
    grad_second = sum_ref[...]
    column_sum(1, grad_second * unit)
    column_sum(3, grad_second)
    grad_middle = grad_ref[...] + norm_back_rows(grad_second, unit, inverse, gains_ref[1, 1:2])
    middle_ref[...] = grad_middle
    att_ref[...] = grad_middle.astype(BF16)
    column_sum(5, att_ref[...].astype(F32))
    go_ref[...] = dot_nt(att_ref[...], out_w[...]).astype(BF16)
    gk_ref[...] = jnp.zeros(gk_ref.shape, F32)
    gv_ref[...] = jnp.zeros(gv_ref.shape, F32)

    def part_back(which, carry):
        own_rows = block_of(which)
        every = range(quads)
        lanes = [lanes_of(quad) for quad in every]
        tall_q = [quad_rows(q_ref[own_rows, lane]) for lane in lanes]
        tall_g = [quad_rows(go_ref[own_rows, lane]) for lane in lanes]
        delta = [
            head_sums(o_ref[own_rows, lane].astype(F32) * go_ref[own_rows, lane].astype(F32))
            for lane in lanes
        ]

        def one(j, masked):
            keys = block_of(j)
            scores = [dot_nt(k_ref[keys, lanes[quad]], tall_q[quad]) for quad in every]
            if masked:
                scores = [
                    causal(member, j * query_rows, which * query_rows) for member in scores
                ]
            found = []
            for quad in every:
                lane = lanes[quad]
                add_k, add_v, add_q = back_block(
                    scores[quad],
                    lse_ref[pl.ds(which * quads + quad, 1), :],
                    delta[quad],
                    tall_q[quad],
                    tall_g[quad],
                    kt_ref[lane, keys],
                    v_ref[keys, lane],
                )
                gk_ref[keys, lane] += add_k
                gv_ref[keys, lane] += add_v
                found.append(add_q)
            return found

        for quad, found in enumerate(one(which, True)):
            acc_ref[quad] = found

        def full(j, inner_carry):
            for quad, found in enumerate(one(j, False)):
                acc_ref[quad] += found
            return inner_carry

        lax.fori_loop(0, which, full, 0)
        for quad in every:
            gq_ref[own_rows, lanes[quad]] = quad_fold(acc_ref[quad].T) * HD**-0.5
        return carry

    lax.fori_loop(0, rows // query_rows, part_back, 0, unroll=parts == 4)
    sine = -sin_ref[...]
    gqkv_ref[:, 0:width] = turn_rows(gq_ref[...], cosine, sine).astype(BF16)
    gqkv_ref[:, width : 2 * width] = turn_rows(gk_ref[...], cosine, sine).astype(BF16)
    gqkv_ref[:, 2 * width : 3 * width] = gv_ref[...].astype(BF16)
    column_sum(4, gqkv_ref[...].astype(F32))
    if packed:
        place = store_packed(
            buffers[0], place, dot_tn(o_ref[...], share_columns(att_ref, index, parts)).astype(BF16), own_block, blocks
        )
        store_packed(
            buffers[0], place, dot_tn(normed_ref[...], share_columns(gqkv_ref, index, parts)).astype(BF16), own_block, blocks
        )
    else:
        mats[3][...] = dot_tn(o_ref[...], share_columns(att_ref, index, parts)).astype(BF16)
        mats[4][...] = dot_tn(normed_ref[...], share_columns(gqkv_ref, index, parts)).astype(BF16)
    if packed:
        sent = copy_in(halves_of(buffers[0], mats), sems, 6)
    grad_normed = dot_nt(gqkv_ref[...], qkv_w[...])
    unit, inverse = unit_rows(stream_ref[...])
    column_sum(0, grad_normed * unit)
    column_sum(2, grad_normed)
    grad_in = middle_ref[...] + norm_back_rows(grad_normed, unit, inverse, gains_ref[1, 0:1])
    grad_in_low = grad_in.astype(BF16)
    gz_ref[0:rows] = grad_in_low
    gz_ref[rows : rows + 16] = jnp.zeros((16, width), BF16)
    column_sum(8, grad_in_low.astype(F32))
    if packed:
        for move in sent:
            move.wait()


def halves_of(buffer, outs):
    half = buffer.shape[0] // 2
    return [(buffer.at[0:half], outs[0]), (buffer.at[half : 2 * half], outs[1])]


def inner_shapes_of(width, hidden):
    return [
        (hidden, width),
        (width, hidden),
        (width, POOL * width),
        (width, width),
        (width, 3 * width),
    ]


def row_tables(length):
    cosine, sine = angle_rows(length)
    repeat = LANES // HD
    return (
        np.tile(np.concatenate([cosine, cosine], axis=1), (1, repeat)),
        np.tile(np.concatenate([-sine, sine], axis=1), (1, repeat)),
    )


def inner_layer(index, shares, pool_b, gains, shifts, qkv_w, qkv_b, out_w, out_b, expand_w, expand_b,
                reduce_w, reduce_b, raised_grad, grad, parts, blocks):
    rows, width = grad.shape
    raised_grad, grad = far_away(raised_grad), far_away(grad)
    hidden = expand_w.shape[2]
    quads = width // (QUAD * HD)
    query_rows = 256 if parts == 4 else 128
    shapes = inner_shapes_of(width, hidden)
    packed = can_pack(shapes, parts, blocks)
    cosine, sine = row_tables(rows)
    vmem = pl.BlockSpec(memory_space=pltpu.VMEM)
    anywhere = pl.BlockSpec(memory_space=pl.ANY)
    far = pl.BlockSpec(memory_space=pltpu.HBM)
    shape = outside
    if packed:
        held = packed_rows(shapes, parts, blocks)
        mats = [shape((blocks // 2, held, LANES), BF16) for _ in range(2)]
        buffers = [pltpu.VMEM((blocks, held, LANES), BF16)]
    else:
        mats = [shape((height, columns // parts), BF16) for height, columns in shapes]
        buffers = []
    found = pl.pallas_call(
        functools.partial(inner_kernel, parts, blocks, packed, query_rows),
        name="inner_layer",
        in_specs=[pl.BlockSpec(memory_space=pltpu.SMEM)] + [vmem] * parts + [vmem, vmem, vmem, far, vmem,
                  far, vmem, far, vmem, far, vmem, far, far, vmem, vmem],
        out_specs=[vmem] * 3 + [anywhere if packed else vmem] * len(mats),
        out_shape=[
            shape((rows, width), BF16),
            shape((rows + 16, width), BF16),
            shape((16, max(hidden, POOL * width)), F32),
        ] + mats,
        scratch_shapes=[
            pltpu.VMEM((width, 3 * width), BF16),
            pltpu.VMEM((width, width), BF16),
            pltpu.VMEM((width, hidden), BF16),
            pltpu.VMEM((hidden, width), BF16),
            pltpu.VMEM((rows, width), F32),
            pltpu.VMEM((rows, width), BF16),
            pltpu.VMEM((rows, width), BF16),
            pltpu.VMEM((rows, width), BF16),
            pltpu.VMEM((width, rows), BF16),
            pltpu.VMEM((rows, width), BF16),
            pltpu.VMEM((width, rows), BF16),
            pltpu.VMEM((rows, width), BF16),
            pltpu.VMEM((rows // query_rows * quads, QUAD * query_rows), F32),
            pltpu.VMEM((rows, width), F32),
            pltpu.VMEM((rows, width), BF16),
            pltpu.VMEM((rows, hidden), BF16),
            pltpu.VMEM((rows, hidden), BF16),
            pltpu.VMEM((rows, width), F32),
            pltpu.VMEM((rows, hidden), BF16),
            pltpu.VMEM((rows, width), BF16),
            pltpu.VMEM((rows, width), BF16),
            pltpu.VMEM((rows, width), F32),
            pltpu.VMEM((rows, width), F32),
            pltpu.VMEM((quads, QUAD * HD, QUAD * query_rows), F32),
            pltpu.VMEM((quads, 1, QUAD * query_rows), F32),
            pltpu.VMEM((quads, 1, QUAD * query_rows), F32),
            pltpu.VMEM(raised_grad.shape, BF16),
            pltpu.VMEM(grad.shape, F32),
            pltpu.SemaphoreType.DMA((8,)),
        ]
        + buffers,
        compiler_params=pltpu.CompilerParams(vmem_limit_bytes=grant(48 if parts == 4 else 60)),
        cost_estimate=cost(33),
    )(index, *shares, pool_b, gains, shifts, qkv_w, qkv_b, out_w, out_b, expand_w, expand_b, reduce_w,
      reduce_b, raised_grad, grad, far_away(jnp.asarray(cosine)), far_away(jnp.asarray(sine)))
    return found[0], found[1], found[2], found[3:], packed


def reversed_bits(value, size):
    found, bit = 0, 1
    while bit < size:
        found = found * 2 + (value // bit) % 2
        bit *= 2
    return found


def store_split(out, index, start, member, own_block, parts, blocks):
    columns = member.shape[1] // parts
    place = start
    for part in range(parts):
        spot = reversed_bits(jnp.bitwise_xor(index, part), parts)
        place = store_packed(
            out.at[spot],
            start,
            member[:, part * columns : (part + 1) * columns],
            own_block,
            blocks,
        )
    return place


def vector_tiles(entries, block, blocks):
    found = []
    for ref, row, length, scale in entries:
        size = length // blocks
        first, last = block * size // LANES, ((block + 1) * size - 1) // LANES
        found += [(ref, row, tile, scale) for tile in range(first, last + 1)]
    return found


def store_vectors(out, index, start, entries, own_block, parts, blocks):
    count = -(-len(vector_tiles(entries, 0, blocks)) // parts)
    for block in range(blocks):
        tiles = vector_tiles(entries, block, blocks)
        for part in range(parts):
            rows = [
                ref[row : row + 1, tile * LANES : (tile + 1) * LANES] * scale
                for ref, row, tile, scale in tiles[part * count : (part + 1) * count]
            ]
            rows += [jnp.zeros((16 - len(rows), LANES), F32)]
            spot = reversed_bits(jnp.bitwise_xor(index, part), parts)
            out[spot, spot_of(block, own_block, blocks), start : start + 16, :] = jnp.concatenate(
                rows, axis=0
            ).astype(BF16)


def split_lanes(split_ref, member):
    for lane in range(split_ref.shape[0]):
        split_ref[lane] = member[:, lane * LANES : (lane + 1) * LANES]


def joined_lanes(split_ref):
    return jnp.concatenate([split_ref[lane] for lane in range(split_ref.shape[0])], axis=1)


def add_third(split_ref, start, member):
    for lane in range(split_ref.shape[0]):
        rows = pl.ds(start, member.shape[0], stride=POOL)
        split_ref[lane, rows, :] = (
            split_ref[lane, rows, :] + member[:, lane * LANES : (lane + 1) * LANES]
        )


def raised_kernel(cot_ref, up_w_ref, joined_ref, grad_ref, sums_ref, split_ref):
    width = grad_ref.shape[1]
    split_lanes(split_ref, cot_ref[...].astype(F32))
    total = jnp.zeros(grad_ref.shape, F32)
    for slot in range(POOL):
        columns = slice(slot * width, (slot + 1) * width)
        rows = every_third(split_ref, slot, grad_ref.shape[0])
        sums_ref[:, columns] = jnp.sum(rows, axis=0, keepdims=True)
        rows = rows.astype(BF16)
        joined_ref[:, columns] = rows
        total += dot_nt(rows, up_w_ref[:, columns])
    grad_ref[...] = total


def raised_back(all_cot, up_w):
    length, width = all_cot.shape
    vmem = pl.BlockSpec(memory_space=pltpu.VMEM)
    shape = outside
    return pl.pallas_call(
        raised_kernel,
        name="raised_back",
        in_specs=[vmem] * 2,
        out_specs=[vmem] * 3,
        out_shape=[
            shape((length // POOL, POOL * width), BF16),
            shape((length // POOL, width), F32),
            shape((1, POOL * width), F32),
        ],
        scratch_shapes=[pltpu.VMEM((width // LANES, length, LANES), F32)],
        compiler_params=pltpu.CompilerParams(vmem_limit_bytes=grant(16, length // 1536)),
        cost_estimate=cost(4),
    )(all_cot, up_w)


def output_kernel(index_ref, lows_ref, low_ref, up_w_ref, up_b_ref, out_ref, split_ref):
    rows, width = out_ref.shape[1:]
    third = rows // POOL
    own = low_ref[pl.ds(pl.multiple_of(index_ref[0] * third, third), third), :]
    parts, chunk = lows_ref.shape[0], rows // 2
    found = []
    for which in range(2):
        place = 2 * index_ref[0] + which
        part = jnp.minimum(place, 2 * parts - 1 - place)
        start = jnp.where(place < parts, 0, chunk)
        found += [lows_ref[part, pl.ds(pl.multiple_of(start, chunk), chunk), :].astype(F32)]
    split_lanes(split_ref, jnp.concatenate(found, axis=0))
    for slot in range(POOL):
        columns = slice(slot * width, (slot + 1) * width)
        add_third(split_ref, slot, dot(own, up_w_ref[:, columns]) + up_b_ref[:, columns])
    out_ref[0] = joined_lanes(split_ref)


def raised_output(index, lows, low, up_w, up_b):
    rows, width = lows.shape[1:]
    vmem = pl.BlockSpec(memory_space=pltpu.VMEM)
    return pl.pallas_call(
        output_kernel,
        name="raised_output",
        in_specs=[pl.BlockSpec(memory_space=pltpu.SMEM)] + [vmem] * 4,
        out_specs=vmem,
        out_shape=jax.ShapeDtypeStruct((1, rows, width), F32),
        scratch_shapes=[pltpu.VMEM((width // LANES, rows, LANES), F32)],
        compiler_params=pltpu.CompilerParams(vmem_limit_bytes=grant(10)),
        cost_estimate=cost(3),
    )(index, lows, low, up_w, up_b)


def outer_hidden_kernel(
    parts,
    blocks,
    packed,
    index_ref,
    *rest,
):
    (
    lows_any,
    gz_any,
    inner_vec_ref,
    raised_vec_ref,
    cot_any,
    middle_in_any,
    active_any,
    rate_any,
    mixed_any,
    gains_ref,
    shifts_ref,
    pool_w_any,
    reduce_w_any,
    expand_w_any,
    out_w_any,
    ) = rest[:15]
    rest = rest[15:]
    outs = 4
    middle_any, go_ref, vec_ref = rest[:3]
    mats = rest[3 : 3 + outs]
    (
        pool_w,
        reduce_w,
        expand_w,
        out_w,
        split_ref,
        grad_ref,
        low_ref,
        second_ref,
        pre_ref,
        sum_ref,
        pooled_ref,
        lows_ref,
        gz_ref,
        middle_in_ref,
        active_ref,
        rate_ref,
        mixed_ref,
        middle_ref,
        att_ref,
        sems,
        *buffers,
    ) = rest[3 + outs :]
    index, own_block = index_ref[0], index_ref[1]
    rows, width = middle_in_ref.shape
    hidden_width = expand_w.shape[1]
    third = rows // POOL
    places = [chunk_of(index, which, parts) for which in range(2)]
    chunk = rows // 2
    coming = [(gz_any, gz_ref)] + [
        (
            cot_any.at[pl.ds(pl.multiple_of(place * chunk, chunk), chunk)],
            low_ref.at[which * chunk : (which + 1) * chunk],
        )
        for which, place in enumerate(places)
    ]
    coming += [
        (pool_w_any, pool_w),
        (rate_any, rate_ref),
        (reduce_w_any.at[0], reduce_w),
        (expand_w_any.at[0], expand_w),
        (middle_in_any, middle_in_ref),
        (active_any, active_ref),
        (out_w_any.at[0], out_w),
        (mixed_any, mixed_ref),
        (lows_any, lows_ref),
    ]
    coming = copy_in(coming, sems)
    moves = []
    half = third // 2
    coming[0].wait()
    tall = [
        gz_ref[pl.ds(pl.multiple_of(place * half, half), half + 16), :].astype(F32)
        for place in places
    ]
    here = jnp.concatenate([member[0:half] for member in tall], axis=0).astype(BF16)
    after = jnp.concatenate([member[1 : half + 1] for member in tall], axis=0).astype(BF16)

    coming[1].wait()
    coming[2].wait()
    split_lanes(split_ref, low_ref[...].astype(F32))
    coming[3].wait()
    add_third(split_ref, 0, dot_nt(here, pool_w[2 * width : 3 * width]))
    add_third(split_ref, 1, dot_nt(after, pool_w[0:width]))
    add_third(split_ref, 2, dot_nt(after, pool_w[width : 2 * width]))
    grad = joined_lanes(split_ref)
    grad_ref[...] = grad
    low_ref[...] = grad.astype(BF16)
    vec_ref[...] = jnp.zeros(vec_ref.shape, F32)

    def column_sum(row, member):
        vec_ref[row : row + 1, 0 : member.shape[1]] = jnp.sum(member, axis=0, keepdims=True)

    column_sum(3, low_ref[...].astype(F32))

    coming[7].wait()
    unit, inverse = unit_rows(middle_in_ref[...])
    second_ref[...] = (unit * gains_ref[0, 1:2] + shifts_ref[0, 1:2]).astype(BF16)
    sum_ref[...] = jnp.zeros(sum_ref.shape, F32)
    for move in coming[4:7] + coming[8:9]:
        move.wait()
    tiles = width // LANES

    def hidden_back(c, carry):
        columns = pl.ds(pl.multiple_of(c * width, width), width)
        pre = dot_nt(low_ref[...], reduce_w[columns, :]) * rate_ref[:, columns].astype(F32)
        low = pre.astype(BF16)
        vec_ref[2:3, columns] = jnp.sum(low.astype(F32), axis=0, keepdims=True)
        sum_ref[...] += dot_nt(low, expand_w[:, columns])
        reduce_grad = dot_tn(active_ref[:, columns], low_ref[...]).astype(BF16)
        expand_grad = dot_tn(second_ref[...], low).astype(BF16)
        if packed:
            out = buffers[0]
            height = hidden_width // blocks
            for part in range(parts):
                spot = reversed_bits(jnp.bitwise_xor(index, part), parts)
                for block in range(width // height):
                    place = spot_of(c * (width // height) + block, own_block, blocks)
                    out[spot, place, 0:height, :] = reduce_grad[
                        block * height : (block + 1) * height, part * LANES : (part + 1) * LANES
                    ]
            spot = reversed_bits(jnp.bitwise_xor(index, c), parts)
            store_packed(out.at[spot], height, expand_grad, own_block, blocks)
        else:
            mats[0][columns, :] = reduce_grad
            mats[1][:, columns] = expand_grad
        return carry

    lax.fori_loop(0, hidden_width // width, hidden_back, 0, unroll=True)
    grad_second = sum_ref[...]
    column_sum(0, grad_second * unit)
    column_sum(1, grad_second)
    grad_middle = grad_ref[...] + norm_back_rows(grad_second, unit, inverse, gains_ref[0, 1:2])
    middle_ref[...] = grad_middle
    moves += copy_in([(middle_ref, middle_any)], sems, 16)
    att_ref[...] = grad_middle.astype(BF16)
    column_sum(4, att_ref[...].astype(F32))
    coming[9].wait()
    coming[10].wait()
    go_ref[...] = dot_nt(att_ref[...], out_w[...]).astype(BF16)
    out_grad = dot_tn(mixed_ref[...], att_ref[...]).astype(BF16)
    if packed:
        place = hidden_width // blocks + tiles * (width // blocks)
        place = store_split(buffers[0], index, place, out_grad, own_block, parts, blocks)
        entries = early_entries(vec_ref, inner_vec_ref, raised_vec_ref, width, hidden_width, parts)
        store_vectors(buffers[0], index, place, entries, own_block, parts, blocks)
        moves += copy_in(halves_of(buffers[0], mats[0:2]), sems, 12)
    else:
        mats[2][...] = out_grad

    coming[11].wait()
    for part in range(parts):
        split_lanes(split_ref, lows_ref[part].astype(F32))
        for slot, first in ((0, 1), (1, 2), (2, 0)):
            found = every_third(split_ref, first, third).astype(BF16)
            for which in range(2):
                place = chunk_of(part, which, parts)
                own = slice(place * half, (place + 1) * half)
                pooled_ref[own, slot * width : (slot + 1) * width] = found[
                    which * half : (which + 1) * half
                ]
    shared = share_columns(gz_ref, index, parts).astype(F32)
    count = pooled_ref.shape[0]
    here, after = shared[0:count].astype(BF16), shared[1 : count + 1].astype(BF16)
    pool_grad = jnp.concatenate(
        [
            dot_tn(pooled_ref[:, slot * width : (slot + 1) * width], member).astype(BF16)
            for slot, member in ((0, after), (1, after), (2, here))
        ],
        axis=0,
    )
    if packed:
        store_packed(buffers[1], 0, pool_grad, own_block, blocks)
        moves += copy_in(halves_of(buffers[1], mats[2:4]), sems, 14)
    else:
        mats[3][...] = pool_grad
    for move in moves:
        move.wait()


def early_entries(vec_ref, inner_ref, raised_ref, width, hidden, parts):
    once = 1.0 / parts
    sizes = [width, width, width, width, 3 * width, width, hidden, width, width]
    return (
        [(vec_ref, 0, width, 1.0), (vec_ref, 1, width, 1.0), (vec_ref, 2, hidden, 1.0)]
        + [(vec_ref, 3, width, 1.0), (vec_ref, 4, width, 1.0)]
        + [(inner_ref, row, size, once) for row, size in enumerate(sizes)]
        + [(raised_ref, 0, POOL * width, once)]
    )


def late_entries(vec_ref, width):
    return [(vec_ref, 0, width, 1.0), (vec_ref, 1, width, 1.0), (vec_ref, 2, 3 * width, 1.0)]


def outer_hidden(index, lows, gz, inner_vecs, raised_vecs, cot, middle, active, rate, mixed, gains, shifts, pool_w, reduce_w, expand_w,
                 out_w, parts, blocks):
    rows, width = middle.shape
    lows, gz, cot, middle, active, rate, mixed = map(
        far_away, (lows, gz, cot, middle, active, rate, mixed)
    )
    hidden = expand_w.shape[2]
    shapes = [(hidden, width), (width, hidden), (width, width)]
    packed = can_pack(shapes + [(POOL * width, width)], parts, blocks) and hidden // parts == width and width // parts == LANES
    vmem = pl.BlockSpec(memory_space=pltpu.VMEM)
    far = pl.BlockSpec(memory_space=pltpu.HBM)
    shape = outside
    if packed:
        held = packed_rows(shapes, parts, blocks) + 16
        mats = [shape((parts // 2, blocks, held, LANES), BF16) for _ in range(2)]
        buffers = [pltpu.VMEM((parts, blocks, held, LANES), BF16)]
        added = packed_rows([(POOL * width, width)], parts, blocks)
        mats += [shape((blocks // 2, added, LANES), BF16) for _ in range(2)]
        buffers += [pltpu.VMEM((blocks, added, LANES), BF16)]
    else:
        mats = [shape(member, BF16) for member in shapes]
        mats += [shape((POOL * width, width // parts), BF16)]
        buffers = []
    found = pl.pallas_call(
        functools.partial(outer_hidden_kernel, parts, blocks, packed),
        name="outer_hidden",
        in_specs=[pl.BlockSpec(memory_space=pltpu.SMEM)] + [far] * 2 + [vmem] * 2 + [far] * 5 + [vmem] * 2 + [far] * 4,
        out_specs=[far] + [vmem] * 2 + [far if packed else vmem] * len(mats),
        out_shape=[
            shape((rows, width), F32),
            shape((rows, width), BF16),
            shape((8, hidden), F32),
        ] + mats,
        scratch_shapes=[
            pltpu.VMEM((POOL * width, width), BF16),
            pltpu.VMEM((hidden, width), BF16),
            pltpu.VMEM((width, hidden), BF16),
            pltpu.VMEM((width, width), BF16),
            pltpu.VMEM((width // LANES, rows, LANES), F32),
            pltpu.VMEM((rows, width), F32),
            pltpu.VMEM((rows, width), BF16),
            pltpu.VMEM((rows, width), BF16),
            pltpu.VMEM((rows, hidden), BF16),
            pltpu.VMEM((rows, width), F32),
            pltpu.VMEM((gz.shape[0] - 16, POOL * width), BF16),
            pltpu.VMEM(lows.shape, BF16),
            pltpu.VMEM(gz.shape, BF16),
            pltpu.VMEM((rows, width), F32),
            pltpu.VMEM((rows, hidden), BF16),
            pltpu.VMEM((rows, hidden), BF16),
            pltpu.VMEM((rows, width), BF16),
            pltpu.VMEM((rows, width), F32),
            pltpu.VMEM((rows, width), BF16),
            pltpu.SemaphoreType.DMA((17,)),
        ]
        + buffers,
        compiler_params=pltpu.CompilerParams(vmem_limit_bytes=grant(44 if packed else 60)),
        cost_estimate=cost(14),
    )(index, lows, gz, inner_vecs, raised_vecs, cot, middle, active, rate, mixed, gains, shifts, pool_w, reduce_w, expand_w, out_w)
    return found[:3], found[3:], packed, shapes


def store_rows(out, index, first, member, own_block, parts, blocks):
    rows, tiles = member.shape[0] // blocks, member.shape[1] // LANES
    share = rows // parts
    for part in range(parts):
        spot = reversed_bits(jnp.bitwise_xor(index, part), parts)
        for block in range(blocks):
            place = spot_of(block, own_block, blocks)
            start = block * rows + part * share
            for tile in range(tiles):
                out[spot, place, first + tile * share : first + (tile + 1) * share, :] = member[
                    start : start + share, tile * LANES : (tile + 1) * LANES
                ]
    return first + tiles * share


def outer_attention_kernel(
    parts,
    blocks,
    packed,
    quad,
    last,
    anchors,
    index_ref,
    ids_ref,
    emb_ref,
    gains_ref,
    shifts_ref,
    qkv_w_any,
    q_ref,
    k_ref,
    kt_ref,
    v_ref,
    o_ref,
    lse_ref,
    go_ref,
    cos_ref,
    sin_ref,
    *rest,
):
    given = (4 if last else 0) + anchors
    if last:
        middle_ref, sums_in_ref, first_ref, table_in_ref = rest[:4]
    outs = rest[given : given + 3]
    (qkv_w, gq_ref, gk_ref, gv_ref, code_ref, acc_ref, sems, *buffers) = rest[given + 3 :]
    index, own_block = index_ref[0], index_ref[1]
    rows, width = o_ref.shape
    vocab = emb_ref.shape[0]
    chunk = rows // 2
    wide = QUAD * HD
    lanes = slice(quad * wide, (quad + 1) * wide)
    moves = copy_in(
        [
            (
                qkv_w_any.at[0, :, part * width + quad * wide : part * width + (quad + 1) * wide],
                qkv_w.at[part],
            )
            for part in range(3)
        ],
        sems,
    )

    def block_of(j):
        if isinstance(j, int):
            return slice(j * rows, (j + 1) * rows)
        return pl.ds(pl.multiple_of(j * rows, rows), rows)

    def clear(j):
        gk_ref[block_of(j), :] = jnp.zeros((rows, wide), F32)
        gv_ref[block_of(j), :] = jnp.zeros((rows, wide), F32)

    def part_back(which, full):
        own_rows = slice(which * chunk, (which + 1) * chunk)
        place = chunk_of(index, which, parts)
        tall_q = quad_rows(q_ref[own_rows, lanes])
        tall_g = quad_rows(go_ref[own_rows, lanes])
        row = which * (width // wide) + quad
        lse = lse_ref[row : row + 1, :]
        delta = head_sums(o_ref[own_rows, lanes].astype(F32) * go_ref[own_rows, lanes].astype(F32))

        def one(j, masked):
            keys = block_of(j)
            scores = dot_nt(k_ref[keys, lanes], tall_q)
            if masked:
                scores = causal(scores, j * rows, place * chunk)
            add_k, add_v, add_q = back_block(
                scores, lse, delta, tall_q, tall_g, kt_ref[lanes, keys], v_ref[keys, lanes]
            )
            gk_ref[keys, :] += add_k
            gv_ref[keys, :] += add_v
            return add_q

        acc_ref[which] = one(full, True)

        def further(j):
            acc_ref[which] += one(j, False)

        each(full, further)
        gq_ref[own_rows, :] = quad_fold(acc_ref[which].T) * HD**-0.5

    def attend_back(full, seen):
        each(seen, clear)
        for which in range(2):
            part_back(which, full[which])

    by_blocks(index, parts, attend_back)

    codes = lax.broadcasted_iota(jnp.int32, (vocab, rows), 0)
    own_ids = own_lanes(jnp.broadcast_to(ids_ref[...], (8, ids_ref.shape[1])), index, parts, chunk)
    own_hot = (codes == own_ids[0:1]).astype(F32).astype(BF16)

    def own_rows_of(table):
        return jnp.concatenate(
            [
                table[pl.ds(pl.multiple_of(chunk_of(index, which, parts) * chunk, chunk), chunk), :]
                for which in range(2)
            ],
            axis=0,
        )

    turned = turn_rows(gq_ref[...], own_rows_of(cos_ref), -own_rows_of(sin_ref)).astype(BF16)
    code_ref[:, 0:wide] = dot(own_hot, turned)
    code_ref[:, wide : 3 * wide] = jnp.zeros((vocab, 2 * wide), F32)

    def by_code(j):
        columns = block_of(j)
        hot = (codes == ids_ref[:, columns]).astype(F32).astype(BF16)
        turned = turn_rows(gk_ref[columns, :], cos_ref[columns, :], -sin_ref[columns, :])
        code_ref[:, wide : 2 * wide] += dot(hot, turned.astype(BF16))
        code_ref[:, 2 * wide : 3 * wide] += dot(hot, gv_ref[columns, :].astype(BF16))

    by_blocks(index, parts, lambda full, seen: each(seen, by_code))
    code = code_ref[...]
    code_low = code.astype(BF16)
    unit, inverse = unit_rows(emb_ref[...].astype(F32))
    normed = (unit * gains_ref[0, 0:1] + shifts_ref[0, 0:1]).astype(BF16)
    qkv_grad = dot_tn(normed, code_low).astype(BF16)
    grad_table = jnp.zeros((vocab, width), F32)
    for part in range(3):
        moves[part].wait()
        grad_table += dot_nt(code_low[:, part * wide : (part + 1) * wide], qkv_w[part])
    vec_ref = outs[0]
    if last:
        vec_ref[...] = sums_in_ref[...]
    else:
        vec_ref[...] = jnp.zeros(vec_ref.shape, F32)
    for part in range(3):
        start = part * width + quad * wide
        vec_ref[2:3, start : start + wide] = jnp.sum(
            code[:, part * wide : (part + 1) * wide], axis=0, keepdims=True
        )
    if not last:
        outs[1][...] = qkv_grad
        outs[2][...] = grad_table
        return
    grad_table += table_in_ref[...]
    high = middle_ref[...].astype(BF16)
    low = (middle_ref[...] - high.astype(F32)).astype(BF16)
    embed = dot(own_hot, high) + dot(own_hot, low)
    embed = embed + norm_back_rows(grad_table, unit, inverse, gains_ref[0, 0:1])
    embed = embed.astype(BF16)
    vec_ref[0:1, 0:width] = jnp.sum(grad_table * unit, axis=0, keepdims=True)
    vec_ref[1:2, 0:width] = jnp.sum(grad_table, axis=0, keepdims=True)
    if packed:
        out = buffers[0]
        place = store_rows(out, index, 0, first_ref[...], own_block, parts, blocks)
        place = store_rows(out, index, place, qkv_grad, own_block, parts, blocks)
        place = store_split(out, index, place, embed, own_block, parts, blocks)
        store_vectors(out, index, place, late_entries(vec_ref, width), own_block, parts, blocks)
        for move in copy_in(halves_of(out, outs[1:]), sems, 3):
            move.wait()
    else:
        outs[1][...] = qkv_grad
        outs[2][...] = embed


def outer_attention(quad, index, all_ids, embedding, gains, shifts, qkv_w, queries, keys, keys_t, values,
                    mixed, lse, go, ending, anchors, parts, blocks):
    rows, width = queries.shape
    length = all_ids.shape[1]
    vocab = embedding.shape[0]
    chunk = rows // 2
    wide = QUAD * HD
    last = ending is not None
    packed = width % (16 * parts * blocks) == 0 and vocab % (16 * blocks) == 0
    packed = packed and width % (LANES * parts) == 0 and parts == 4
    cosine, sine = row_tables(length)
    vmem = pl.BlockSpec(memory_space=pltpu.VMEM)
    anywhere = pl.BlockSpec(memory_space=pl.ANY)
    far = pl.BlockSpec(memory_space=pltpu.HBM)
    shape = outside
    outs, buffers = [shape((8, 3 * width), F32)], []
    if not last:
        outs += [shape((width, 3 * wide), BF16), shape((vocab, width), F32)]
    elif packed:
        held = 3 * width // LANES * (width // blocks // parts)
        held += vocab // blocks * (width // parts // LANES) + 16
        outs += [shape((parts // 2, blocks, held, LANES), BF16) for _ in range(2)]
        buffers = [pltpu.VMEM((parts, blocks, held, LANES), BF16)]
    else:
        outs += [shape((width, 3 * wide), BF16), shape((vocab, width), BF16)]
    ending = list(ending) if last else []
    return pl.pallas_call(
        functools.partial(outer_attention_kernel, parts, blocks, packed, quad, last, len(anchors)),
        name="outer_attention",
        in_specs=[pl.BlockSpec(memory_space=pltpu.SMEM)]
        + [vmem] * 4
        + [far]
        + [vmem] * 9
        + [vmem] * len(ending)
        + [anywhere] * len(anchors),
        out_specs=[vmem] + [anywhere if buffers else vmem] * 2,
        out_shape=outs,
        scratch_shapes=[
            pltpu.VMEM((3, width, wide), BF16),
            pltpu.VMEM((rows, wide), F32),
            pltpu.VMEM((length, wide), F32),
            pltpu.VMEM((length, wide), F32),
            pltpu.VMEM((vocab, 3 * wide), F32),
            pltpu.VMEM((2, wide, QUAD * chunk), F32),
            pltpu.SemaphoreType.DMA((5,)),
        ]
        + buffers,
        compiler_params=pltpu.CompilerParams(vmem_limit_bytes=grant(34, length // (4 * rows))),
        cost_estimate=cost(14),
    )(index, all_ids, embedding, gains, shifts, qkv_w, queries, keys, keys_t, values, mixed, lse, go,
      far_away(jnp.asarray(cosine)), far_away(jnp.asarray(sine)), *ending, *map(far_away, anchors)), packed


def add_kernel(count, anchors, index_slices, *refs):
    sources, outs = refs[:count], refs[count + anchors :]
    for out, piece in zip(outs, index_slices):
        total = sources[0][piece].astype(F32)
        for source in sources[1:]:
            total += source[piece].astype(F32)
        out[...] = total.astype(BF16)


def add(sources, pieces, anchors=(), shape_of=jax.ShapeDtypeStruct):
    shape = sources[0].shape
    found, slices = [], []
    for piece in pieces:
        if isinstance(piece, int):
            found, slices = found + [shape[1:]], slices + [piece]
        else:
            *first, start, stop = piece
            found += [(stop - start, *shape[1 + len(first) :])]
            slices += [(*first, slice(start, stop))]
    vmem = pl.BlockSpec(memory_space=pltpu.VMEM)
    return list(pl.pallas_call(
        functools.partial(add_kernel, len(sources), len(anchors), slices),
        name="add",
        in_specs=[vmem] * len(sources) + [pl.BlockSpec(memory_space=pl.ANY)] * len(anchors),
        out_specs=[vmem] * len(found),
        out_shape=[shape_of(member, BF16) for member in found],
        compiler_params=pltpu.CompilerParams(vmem_limit_bytes=grant(16)),
        cost_estimate=cost(3),
    )(*sources, *map(far_away, anchors)))


def merge_kernel(plan, split, count, *refs):
    sources, outs = refs[:count], refs[len(refs) - split :]
    for spot in range(sources[0].shape[0]):
        out = outs[spot] if split > 1 else outs[0].at[spot]
        at = 0
        for rows, members in plan:
            total = sources[members[0][0]][spot, members[0][1] : members[0][1] + rows].astype(F32)
            for source, start in members[1:]:
                total += sources[source][spot, start : start + rows].astype(F32)
            out[at : at + rows, :] = total.astype(BF16)
            at += rows


def merge(sources, plan, split, anchors=()):
    count = sources[0].shape[0]
    rows = sum(member[0] for member in plan)
    vmem = pl.BlockSpec(memory_space=pltpu.VMEM)
    shapes = [(rows, LANES)] * count if split else [(count, rows, LANES)]
    return list(
        pl.pallas_call(
            functools.partial(merge_kernel, plan, len(shapes), len(sources)),
            name="merge",
            in_specs=[vmem] * len(sources) + [pl.BlockSpec(memory_space=pl.ANY)] * len(anchors),
            out_specs=[vmem] * len(shapes),
            out_shape=[jax.ShapeDtypeStruct(member, BF16) for member in shapes],
            compiler_params=pltpu.CompilerParams(vmem_limit_bytes=grant(16)),
            cost_estimate=cost(3),
        )(*sources, *map(far_away, anchors))
    )


def total_kernel(counts, *refs):
    out, start, at = refs[-1], 0, 0
    for count in counts:
        total = refs[at][...].astype(F32)
        for ref in refs[at + 1 : at + count]:
            total += ref[...].astype(F32)
        out[start : start + total.shape[0], :] = total.astype(BF16)
        start, at = start + total.shape[0], at + count


def totals(groups, anchors=()):
    rows = sum(group[0].shape[0] for group in groups)
    vmem = pl.BlockSpec(memory_space=pltpu.VMEM)
    members = [member for group in groups for member in group]
    return pl.pallas_call(
        functools.partial(total_kernel, [len(group) for group in groups]),
        name="totals",
        in_specs=[vmem] * len(members) + [pl.BlockSpec(memory_space=pl.ANY)] * len(anchors),
        out_specs=vmem,
        out_shape=jax.ShapeDtypeStruct((rows, LANES), BF16),
        compiler_params=pltpu.CompilerParams(vmem_limit_bytes=grant(8)),
        cost_estimate=cost(3),
    )(*members, *map(far_away, anchors))


def assemble_kernel(parts, blocks, index_ref, *rest):
    early, late, outs = rest[:parts], rest[parts : 2 * parts], rest[2 * parts :]
    index, own_block = index_ref[0], index_ref[1]
    (embed, gains, shifts, qkv_w, qkv_b, out_w, out_b, expand_w, expand_b, reduce_w, reduce_b) = outs[:11]
    pool_w, pool_b, up_w, up_b = outs[11:]

    def place(group, start, out, height, columns):
        tiles = columns // parts // LANES
        for at in range(parts):
            part = jnp.bitwise_xor(index, at)
            for tile in range(tiles):
                lanes = pl.ds(pl.multiple_of((part * tiles + tile) * LANES, LANES), LANES)
                found = group[at][start + tile * height : start + (tile + 1) * height]
                out[:, lanes] = found.astype(F32)
        return start + tiles * height

    start = 0
    for out in (reduce_w.at[1], expand_w.at[1], up_w, out_w.at[1], qkv_w.at[1], pool_w):
        start = place(early, start, out, *out.shape)
    for out in (reduce_w.at[0], expand_w.at[0], out_w.at[0]):
        start = place(early, start, out, *out.shape)
    early_start = start
    height, wide = qkv_w.shape[1] // parts, QUAD * HD
    start = 0
    for quad in range(qkv_w.shape[2] // 3 // wide):
        for third in range(3):
            for tile in range(wide // LANES):
                lane = third * (qkv_w.shape[2] // 3) + quad * wide + tile * LANES
                for distance in range(parts):
                    part = jnp.bitwise_xor(index, distance)
                    rows = pl.ds(pl.multiple_of(part * height, height), height)
                    qkv_w[0, rows, lane : lane + LANES] = late[distance][
                        start : start + height
                    ].astype(F32)
                start += height
    late_start = place(late, start, embed, *embed.shape)

    def vectors(group, start, sizes):
        entries = [(None, 0, size * blocks, 1.0) for size in sizes]
        total = len(vector_tiles(entries, 0, blocks))
        count = -(-total // parts)
        tiles = {}
        for distance in range(parts):
            tiles[distance] = group[distance][start : start + 16].astype(F32)
        rows = []
        for number in range(total):
            row = jnp.zeros((1, LANES), F32)
            for distance in range(parts):
                here = jnp.bitwise_xor(index, distance) == number // count
                row = jnp.where(here, tiles[distance][number % count : number % count + 1], row)
            rows.append(row)
        found, number = [], 0
        for size in sizes:
            held = len(vector_tiles([(None, 0, size * blocks, 1.0)], 0, blocks))
            wide = jnp.concatenate(rows[number : number + held], axis=1)
            number += held
            if size % LANES != 0:
                shift = own_block * size % LANES
                wide = pltpu.roll(wide, (wide.shape[1] - shift) % wide.shape[1], 1)
            found.append(wide[:, :size])
        return found

    width_b, hidden_b, three_b = out_b.shape[1], expand_b.shape[1], qkv_b.shape[1]
    low = vectors(
        early,
        early_start,
        [width_b, width_b, hidden_b, width_b, width_b]
        + [width_b] * 4
        + [three_b, width_b, hidden_b, width_b, width_b, three_b],
    )
    high = vectors(late, late_start, [width_b, width_b, three_b])
    gains[0, 0:1], shifts[0, 0:1], qkv_b[0:1] = high
    gains[0, 1:2], shifts[0, 1:2], expand_b[0:1], reduce_b[0:1], out_b[0:1] = low[:5]
    gains[1, 0:1], gains[1, 1:2], shifts[1, 0:1], shifts[1, 1:2] = low[5:9]
    qkv_b[1:2], out_b[1:2], expand_b[1:2], reduce_b[1:2] = low[9:13]
    pool_b[...], up_b[...] = low[13:]


def assemble(index, gathered, late, width, hidden, vocab, parts, blocks):
    vmem = pl.BlockSpec(memory_space=pltpu.VMEM)
    part = width // blocks
    shapes = [
        (vocab // blocks, width),
        (2, 2, part),
        (2, 2, part),
        (2, part, 3 * width),
        (2, 3 * part),
        (2, part, width),
        (2, part),
        (2, part, hidden),
        (2, hidden // blocks),
        (2, hidden // blocks, width),
        (2, part),
        (POOL * part, width),
        (1, part),
        (part, POOL * width),
        (1, POOL * part),
    ]
    return pl.pallas_call(
        functools.partial(assemble_kernel, parts, blocks),
        name="assemble",
        in_specs=[pl.BlockSpec(memory_space=pltpu.SMEM)] + [vmem] * (2 * parts),
        out_specs=[vmem] * 15,
        out_shape=[jax.ShapeDtypeStruct(member, F32) for member in shapes],
        compiler_params=pltpu.CompilerParams(vmem_limit_bytes=grant(16)),
        cost_estimate=cost(4),
    )(index, *gathered, *late)


def pack(members, parts, blocks):
    rows = []
    for member in members:
        height, width = member.shape
        split = member.reshape(blocks, height // blocks, parts, width // parts)
        rows.append(split.transpose(2, 0, 1, 3).reshape(parts, blocks, -1))
    buffer = jnp.concatenate(rows, axis=2)
    order = [reversed_bits(spot, parts) for spot in range(parts)]
    index = lax.axis_index("seq")
    buffer = jnp.stack([buffer[jnp.bitwise_xor(index, other)] for other in order])
    return buffer.reshape(parts, blocks, -1, LANES)


def in_spots(buffer):
    blocks = buffer.shape[-3]
    index = lax.axis_index("batch")
    order = [spot * 2 % blocks + spot * 2 // blocks for spot in range(blocks)]
    return jnp.stack(
        [
            lax.dynamic_index_in_dim(buffer, jnp.bitwise_xor(index, other), -3, keepdims=False)
            for other in order
        ],
        axis=-3,
    )


def exchange(member, axis, distance):
    pairs = [(peer, peer ^ distance) for peer in range(lax.axis_size(axis))]
    return lax.ppermute(member, axis, pairs)


def seq_near(keep, send, anchors=()):
    half = keep.shape[1] // 2
    pieces = [(part, start, start + half) for part in range(2) for start in (half, 0)]
    return add([keep, exchange(send, "seq", 1)], pieces, anchors)


def seq_far_send(quarters, beside=(), anchors=()):
    near, far = quarters[0], quarters[2]
    rows = near.shape[1]
    sources = [near, exchange(far, "seq", 2)]
    plan = [(rows, ((0, 0), (1, 0)))]
    if beside:
        sources, plan = sources + [beside[1]], plan + [(beside[1].shape[1], ((2, 0),))]
    return merge(sources, plan, False, anchors)[0]


def seq_far_keep(quarters, leaving, beside=(), others=(), anchors=()):
    near, far = quarters[1], quarters[3]
    rows = near.shape[1]
    if others:
        far = behind(far, *others)
    sources = [near, exchange(far, "seq", 2), exchange(leaving, "batch", 1)]
    plan = [(rows, ((0, 0), (1, 0), (2, 0)))]
    if beside:
        sources, plan = sources + [beside[0]], plan + [(beside[0].shape[1], ((3, 0), (2, rows)))]
    return merge(sources, plan, True, anchors)


def batch_halves(keep, send, anchors=()):
    return add([keep, exchange(send, "batch", 1)], list(range(keep.shape[0])), anchors)


def batch_rest(sums):
    return [sums[0]] + [
        exchange(sums[spot], "batch", 2 * spot) for spot in range(1, len(sums))
    ]


def plain_sums(buffer):
    level = 1
    while buffer.shape[0] > 1:
        half = buffer.shape[0] // 2
        got = exchange(buffer[half:], "seq", level)
        buffer = (buffer[:half].astype(F32) + got.astype(F32)).astype(BF16)
        level *= 2
    return plain_batch(buffer[0])


def plain_batch(buffer):
    half = buffer.shape[0] // 2
    got = exchange(buffer[half:], "batch", 1)
    sums = (buffer[:half].astype(F32) + got.astype(F32)).astype(BF16)
    total = sums[0].astype(F32)
    for spot in range(1, half):
        total += exchange(sums[spot], "batch", 2 * spot).astype(F32)
    return total.astype(BF16)


def behind(member, *others):
    return lax.optimization_barrier((member, *others))[0]


def seq_gather(member, *between):
    parts = lax.axis_size("seq")
    found, level = {0: member}, parts // 2
    while level >= 1:
        for distance, held in list(found.items()):
            found[distance ^ level] = exchange(held, "seq", level)
        if level == parts // 2 and between:
            found[level] = behind(found[level], *between)
        level //= 2
    return [found[distance] for distance in range(parts)]


def in_order(found):
    found = jnp.stack(found)
    index = lax.axis_index("seq")
    return jnp.stack([found[jnp.bitwise_xor(index, part)] for part in range(len(found))])


def unpack(gathered, shapes, blocks):
    parts = gathered.shape[0]
    gathered = gathered.reshape(parts, -1)
    found, start = [], 0
    for height, width in shapes:
        height, columns = height // blocks, width // parts
        piece = gathered[:, start : start + height * columns]
        piece = piece.reshape(parts, height, columns).transpose(1, 0, 2)
        start += height * columns
        found.append(piece.reshape(height, width).astype(F32))
    return found


def local(
    byte_ids,
    embedding,
    norm_gains,
    norm_biases,
    qkv_weights,
    qkv_biases,
    out_weights,
    out_biases,
    expand_weights,
    expand_biases,
    reduce_weights,
    reduce_biases,
    pool_weight,
    pool_bias,
    upsample_weight,
    upsample_bias,
    cotangent,
):
    parts, blocks = lax.axis_size("seq"), lax.axis_size("batch")
    rows, width, hidden = byte_ids.shape[1], embedding.shape[1], expand_weights.shape[2]
    index = jnp.stack([lax.axis_index("seq"), lax.axis_index("batch")]).astype(jnp.int32)
    ids = seq_gather(byte_ids)
    all_cot = lax.all_gather(cotangent[0], "seq", axis=0, tiled=True)

    (embedding, norm_gains, norm_biases, qkv_weights, qkv_biases, out_weights, out_biases) = (
        far_away(member)
        for member in (
            embedding, norm_gains, norm_biases, qkv_weights, qkv_biases, out_weights, out_biases
        )
    )
    (expand_weights, expand_biases, reduce_weights, reduce_biases, pool_weight) = (
        far_away(member)
        for member in (expand_weights, expand_biases, reduce_weights, reduce_biases, pool_weight)
    )
    (pool_bias, upsample_weight, upsample_bias) = (
        far_away(member) for member in (pool_bias[None], upsample_weight, upsample_bias[None])
    )

    coarse, fine = byte_table(embedding, norm_gains, norm_biases, qkv_weights, qkv_biases)
    h1_low, share, queries, keys, keys_t, values, mixed, lse, middle, active, rate, all_ids = outer_forward(
        index, ids, embedding, norm_gains, norm_biases, coarse, fine, out_weights, out_biases,
        expand_weights, expand_biases, reduce_weights, reduce_biases, pool_weight, rows
    )
    raised_grad, grad_short, raised_sums = raised_back(all_cot, upsample_weight)
    shares = seq_gather(share, raised_sums)
    short_low, gz, inner_vecs, inner_found, inner_packed = inner_layer(
        index, shares, pool_bias, norm_gains, norm_biases, qkv_weights, qkv_biases,
        out_weights, out_biases, expand_weights, expand_biases, reduce_weights, reduce_biases,
        raised_grad, grad_short, parts, blocks
    )
    lows = lax.all_gather(behind(h1_low, shares[-1]), "seq", axis=0)
    output = raised_output(index, lows, short_low, upsample_weight, upsample_bias)

    (grad_middle, grad_mixed, hidden_vecs), early, early_packed, early_shapes = outer_hidden(
        index, lows, gz, inner_vecs, raised_sums, all_cot, middle, active, rate, mixed, norm_gains,
        norm_biases, pool_weight, reduce_weights, expand_weights, out_weights, parts, blocks
    )

    def attention_back(quad, ending, anchors):
        return outer_attention(
            quad, index, all_ids, embedding, norm_gains, norm_biases, qkv_weights, queries, keys,
            keys_t, values, mixed, lse, grad_mixed, ending, anchors, parts, blocks
        )

    anchors = []
    packed = inner_packed and early_packed
    if packed:
        quarters = seq_near(*early[0:2], [output])
        inner_sums = merge(
            [
                inner_found[0],
                exchange(inner_found[1], "batch", 1),
                early[2],
                exchange(early[3], "batch", 1),
            ],
            [
                (inner_found[0].shape[1], ((0, 0), (1, 0))),
                (early[2].shape[1], ((2, 0), (3, 0))),
            ],
            True,
            quarters[:1],
        )
        anchors = inner_sums + quarters
    ending, late_packed = attention_back(0, None, anchors)
    if packed:
        leaving = seq_far_send(quarters, (), ending[:1])
        inner_rest = batch_rest(inner_sums)
        anchors = [inner_rest[1], leaving]
    (table_vecs, *late), _ = attention_back(1, [grad_middle] + list(ending), anchors)
    if packed and late_packed:
        early_sums = seq_far_keep(quarters, leaving, (), ending[:1], inner_rest[2:])
        late_quarters = seq_near(*late, early_sums[:1])
        late_sums = seq_far_keep(late_quarters, seq_far_send(late_quarters))
        gathered = seq_gather(totals([inner_rest, batch_rest(early_sums)]))
        late_total = totals([batch_rest(late_sums)])
        found = list(
            assemble(index, gathered, seq_gather(late_total), width, hidden, embedding.shape[0], parts, blocks)
        )
        found[12], found[14] = found[12][0], found[14][0]
        return (output, *found)

    inner_shapes = inner_shapes_of(width, hidden)
    inner_buffer = jnp.concatenate([member.reshape(blocks, -1) for member in inner_found], axis=1)
    inner_buffer = in_spots(inner_buffer.reshape(blocks, -1, LANES))
    inner_out = unpack(in_order(seq_gather(plain_batch(inner_buffer))), inner_shapes, blocks)
    pool_buffer = in_spots(early[3].reshape(blocks, -1, LANES))
    pool_out = unpack(
        in_order(seq_gather(plain_batch(pool_buffer))), [(POOL * width, width)], blocks
    )
    early_buffer = in_spots(pack(early[:3], parts, blocks))
    early_out = unpack(
        in_order(seq_gather(plain_sums(early_buffer))), early_shapes, blocks
    )
    wide = QUAD * HD
    qkv_grad = jnp.concatenate(
        [
            half[:, part * wide : (part + 1) * wide]
            for part in range(3)
            for half in (ending[1], late[0])
        ],
        axis=1,
    )
    late, late_shapes = [qkv_grad, late[1]], [qkv_grad.shape, late[1].shape]
    late_buffer = in_spots(pack(late, parts, blocks))
    late_out = unpack(
        in_order(seq_gather(plain_sums(late_buffer))), late_shapes, blocks
    )
    once = 1.0 / parts
    vectors = [
        table_vecs[0, :width],
        hidden_vecs[0, :width],
        table_vecs[1, :width],
        hidden_vecs[1, :width],
        table_vecs[2, : 3 * width],
        hidden_vecs[4, :width],
        hidden_vecs[2, :hidden],
        hidden_vecs[3, :width],
        inner_vecs[0, :width] * once,
        inner_vecs[1, :width] * once,
        inner_vecs[2, :width] * once,
        inner_vecs[3, :width] * once,
        inner_vecs[4, : 3 * width] * once,
        inner_vecs[5, :width] * once,
        inner_vecs[6, :hidden] * once,
        inner_vecs[7, :width] * once,
        inner_vecs[8, :width] * once,
        raised_sums[0] * once,
    ]
    flat = jnp.concatenate([member.reshape(blocks, -1) for member in vectors], axis=1)
    flat = lax.psum(flat.astype(BF16), ("seq", "batch")).astype(F32)
    flat = lax.dynamic_index_in_dim(flat, lax.axis_index("batch"), 0, keepdims=False)
    sums, start = [], 0
    for member in vectors:
        sums.append(flat[start : start + member.shape[0] // blocks])
        start += member.shape[0] // blocks
    return (
        output,
        late_out[1],
        jnp.stack([jnp.stack([sums[0], sums[1]]), jnp.stack([sums[8], sums[9]])]),
        jnp.stack([jnp.stack([sums[2], sums[3]]), jnp.stack([sums[10], sums[11]])]),
        jnp.stack([late_out[0], inner_out[4]]),
        jnp.stack([sums[4], sums[12]]),
        jnp.stack([early_out[2], inner_out[3]]),
        jnp.stack([sums[5], sums[13]]),
        jnp.stack([early_out[1], inner_out[1]]),
        jnp.stack([sums[6], sums[14]]),
        jnp.stack([early_out[0], inner_out[0]]),
        jnp.stack([sums[7], sums[15]]),
        pool_out[0],
        sums[16],
        inner_out[2],
        sums[17],
    )


def solution(mesh):
    whole = P()
    return jax.shard_map(
        local,
        mesh=mesh,
        in_specs=(P("batch", "seq"),) + (whole,) * 15 + (P("batch", "seq", None),),
        out_specs=(
            P("batch", "seq", None),
            P("batch", None),
            P(None, None, "batch"),
            P(None, None, "batch"),
            P(None, "batch", None),
            P(None, "batch"),
            P(None, "batch", None),
            P(None, "batch"),
            P(None, "batch", None),
            P(None, "batch"),
            P(None, "batch", None),
            P(None, "batch"),
            P("batch", None),
            P("batch"),
            P("batch", None),
            P("batch"),
        ),
        check_vma=False,
    )
```

```python
import functools

import jax
import jax.numpy as jnp
import numpy as np
from jax import lax
from jax.experimental import pallas as pl
from jax.experimental.pallas import tpu as pltpu
from jax.sharding import PartitionSpec as P

HD = 64
POOL = 3
QUAD = 4
LANES = 128
VMEM_LIMIT = 60 * 1024 * 1024
F32 = jnp.float32
BF16 = jnp.bfloat16


def dot(left, right):
    return jnp.dot(left, right, preferred_element_type=F32)


def dot_nt(left, right):
    return lax.dot_general(left, right, (((1,), (1,)), ((), ())), preferred_element_type=F32)


def dot_tn(left, right):
    return lax.dot_general(left, right, (((0,), (0,)), ((), ())), preferred_element_type=F32)


def gelu_parts(pre):
    slope = 0.7978845608028654
    square = pre * pre
    bent = jnp.tanh(slope * pre * (1.0 + 0.044715 * square))
    half = 0.5 * (1.0 + bent)
    value = pre * half
    rate = half + 0.5 * pre * (1.0 - bent * bent) * (slope * (1.0 + 3.0 * 0.044715 * square))
    return (value, rate)


def angle_rows(length):
    frequency = 10000.0 ** (-np.arange(HD // 2, dtype=np.float64) / (HD // 2))
    angles = np.arange(length, dtype=np.float64)[:, None] * frequency[None, :]
    return (np.cos(angles).astype(np.float32), np.sin(angles).astype(np.float32))


def cost(microseconds):
    microseconds *= 10
    return pl.CostEstimate(
        flops=int(microseconds * 1e9), bytes_accessed=int(microseconds * 1e6), transcendentals=0
    )


def grant(megabytes, factor=1):
    return min(int(megabytes * factor), 60) * 1024 * 1024


def outside(shape, dtype):
    return pltpu.HBM(shape, dtype)


def far_away(member):
    return pltpu.with_memory_space_constraint(member, pltpu.HBM)


def copy_in(pairs, sems, start=0):
    moves = [
        pltpu.make_async_copy(src, dst, sems.at[start + i]) for i, (src, dst) in enumerate(pairs)
    ]
    for move in moves:
        move.start()
    return moves


def chunk_of(index, which, parts):
    return index + which * (2 * parts - 1 - 2 * index)


def by_blocks(index, parts, body):
    if parts != 4:
        full = [chunk_of(index, which, parts) // 2 for which in range(2)]
        body(full, full[1] + 1)
        return

    @pl.when(index < 2)
    def _():
        body([0, 3], 4)

    @pl.when(index >= 2)
    def _():
        body([1, 2], 3)


def each(count, step):
    if isinstance(count, int):
        for i in range(count):
            step(i)
    else:
        lax.fori_loop(0, count, lambda i, carry: (step(i), carry)[1], 0)


def own_lanes(row, index, parts, chunk):
    length = row.shape[1]
    return jnp.concatenate(
        [
            pltpu.roll(row, (length - chunk_of(index, which, parts) * chunk) % length, 1)[:, :chunk]
            for which in range(2)
        ],
        axis=1,
    )


def quad_rows(rows):
    lane = lax.broadcasted_iota(jnp.int32, rows.shape, 1) // HD
    zero = jnp.zeros_like(rows)
    return jnp.concatenate([jnp.where(lane == head, rows, zero) for head in range(QUAD)], axis=0)


def quad_fold(tall):
    count = tall.shape[0] // QUAD
    lane = lax.broadcasted_iota(jnp.int32, (count, tall.shape[1]), 1) // HD
    folded = jnp.zeros((count, tall.shape[1]), tall.dtype)
    for head in range(QUAD):
        folded = jnp.where(lane == head, tall[head * count : (head + 1) * count], folded)
    return folded


def lanes_of(quad):
    return slice(quad * QUAD * HD, (quad + 1) * QUAD * HD)


def causal(scores, key_start, query_start):
    count = scores.shape[1] // QUAD
    key = key_start + lax.broadcasted_iota(jnp.int32, scores.shape, 0)
    query = lax.broadcasted_iota(jnp.int32, (1, scores.shape[1]), 1)
    for head in range(1, QUAD):
        query = jnp.where(query >= count, query - count, query)
    return jnp.where(key <= query + query_start, scores, -1e30)


def flash_quads(tall_q, keys_at, values_at, full, key_start_last, query_start, state):
    quads = range(len(tall_q))
    acc, peak, total = state

    def scores_of(j):
        return [dot_nt(keys_at(j, quad), tall_q[quad]) for quad in quads]

    scores = [causal(member, key_start_last, query_start) for member in scores_of(full)]
    tops = [jnp.max(member, axis=0, keepdims=True) for member in scores]
    raised = [jnp.exp(scores[quad] - tops[quad]) for quad in quads]
    for quad in quads:
        peak[quad] = tops[quad]
        total[quad] = jnp.sum(raised[quad], axis=0, keepdims=True)
        acc[quad] = dot(values_at(full, quad), raised[quad].astype(BF16))

    def block(j):
        scores = scores_of(j)
        tops = [
            jnp.maximum(peak[quad], jnp.max(scores[quad], axis=0, keepdims=True)) for quad in quads
        ]
        raised = [jnp.exp(scores[quad] - tops[quad]) for quad in quads]
        for quad in quads:
            shrink = jnp.exp(peak[quad] - tops[quad])
            peak[quad] = tops[quad]
            total[quad] = total[quad] * shrink + jnp.sum(raised[quad], axis=0, keepdims=True)
            acc[quad] = acc[quad] * shrink + dot(values_at(j, quad), raised[quad].astype(BF16))

    each(full, block)
    return [
        (quad_fold((acc[quad] / total[quad]).T), peak[quad] + jnp.log(total[quad]))
        for quad in quads
    ]


def every_third(split_ref, start, count):
    return jnp.concatenate(
        [split_ref[i, pl.ds(start, count, stride=POOL), :] for i in range(split_ref.shape[0])],
        axis=1,
    )


def unit_rows(stream):
    centred = stream - jnp.mean(stream, axis=-1, keepdims=True)
    inverse = lax.rsqrt(jnp.mean(centred * centred, axis=-1, keepdims=True) + 1e-05)
    return (centred * inverse, inverse)


def table_kernel(emb_ref, gains_ref, shifts_ref, qkv_w_any, qkv_b_ref, coarse_ref, fine_ref, qkv_w, sems):
    width = emb_ref.shape[1]
    moves = copy_in([(qkv_w_any.at[0], qkv_w)], sems)
    unit, _ = unit_rows(emb_ref[...].astype(F32))
    normed = (unit * gains_ref[0, 0:1] + shifts_ref[0, 0:1]).astype(BF16)
    moves[0].wait()
    table = (dot(normed, qkv_w[...]) + qkv_b_ref[0:1]).T
    coarse = table.astype(BF16)
    coarse_ref[...] = coarse
    fine_ref[...] = (table[: 2 * width] - coarse[: 2 * width].astype(F32)).astype(BF16)


def byte_table(embedding, gains, shifts, qkv_w, qkv_b):
    vocab, width = embedding.shape
    vmem = pl.BlockSpec(memory_space=pltpu.VMEM)
    far = pl.BlockSpec(memory_space=pltpu.HBM)
    return pl.pallas_call(
        table_kernel,
        name="byte_table",
        in_specs=[vmem, vmem, vmem, far, vmem],
        out_specs=[vmem, vmem],
        out_shape=[
            jax.ShapeDtypeStruct((3 * width, vocab), BF16),
            jax.ShapeDtypeStruct((2 * width, vocab), BF16),
        ],
        scratch_shapes=[pltpu.VMEM((width, 3 * width), BF16), pltpu.SemaphoreType.DMA((1,))],
        compiler_params=pltpu.CompilerParams(vmem_limit_bytes=grant(16)),
        cost_estimate=cost(4),
    )(embedding, gains, shifts, qkv_w, qkv_b)


def outer_forward_kernel(
    parts,
    index_ref,
    *rest,
):
    ids, rest = rest[:parts], rest[parts:]
    (
    emb_ref,
    gains_ref,
    shifts_ref,
    coarse_any,
    fine_any,
    out_w_any,
    out_b_ref,
    expand_w_any,
    expand_b_ref,
    reduce_w_any,
    reduce_b_ref,
    pool_w_any,
    cos_ref,
    sin_ref,
    low_ref,
    share_ref,
    q_any,
    k_any,
    kt_any,
    v_any,
    o_any,
    lse_ref,
    middle_any,
    active_any,
    rate_any,
    ids_ref,
    q_ref,
    k_ref,
    kt_ref,
    v_ref,
    o_ref,
    middle_ref,
    active_ref,
    rate_ref,
    out_w,
    expand_w,
    reduce_w,
    pool_w,
    coarse_ref,
    fine_ref,
    vt_ref,
    acc_ref,
    peak_ref,
    total_ref,
    second_ref,
    sum_ref,
    later_ref,
    split_ref,
    sems,
    ) = rest
    index = index_ref[0]
    rows, width = middle_ref.shape
    vocab = emb_ref.shape[0]
    chunk = rows // 2
    moves = copy_in(
        [
            (coarse_any, coarse_ref),
            (fine_any, fine_ref),
            (out_w_any.at[0], out_w),
            (expand_w_any.at[0], expand_w),
            (reduce_w_any.at[0], reduce_w),
            (pool_w_any, pool_w),
        ],
        sems,
    )

    for distance in range(parts):
        part = jnp.bitwise_xor(index, distance)
        ids_ref[:, pl.ds(pl.multiple_of(part * rows, rows), rows)] = ids[distance][...]
    moves[0].wait()
    moves[1].wait()

    def picked(start, hot):
        return dot(coarse_ref[start : start + width], hot) + dot(
            fine_ref[start : start + width], hot
        )

    def turned(member, cosine, sine):
        pieces = []
        for head in range(width // HD):
            first = member[head * HD : head * HD + HD // 2]
            second = member[head * HD + HD // 2 : (head + 1) * HD]
            pieces += [first * cosine - second * sine, first * sine + second * cosine]
        return jnp.concatenate(pieces, axis=0)

    codes = lax.broadcasted_iota(jnp.int32, (vocab, rows), 0)

    def block_of(j):
        if isinstance(j, int):
            return slice(j * rows, (j + 1) * rows)
        return pl.ds(pl.multiple_of(j * rows, rows), rows)

    def key_block(j):
        columns = block_of(j)
        hot = (codes == ids_ref[:, columns]).astype(F32).astype(BF16)
        keys = turned(picked(width, hot), cos_ref[:, columns], sin_ref[:, columns])
        kt_ref[:, columns] = keys.astype(BF16)
        k_ref[columns, :] = keys.T.astype(BF16)
        values = dot(coarse_ref[2 * width : 3 * width], hot)
        vt_ref[:, columns] = values.astype(BF16)
        v_ref[columns, :] = values.T.astype(BF16)

    by_blocks(index, parts, lambda full, seen: each(seen, key_block))
    moves += copy_in([(k_ref, k_any), (kt_ref, kt_any), (v_ref, v_any)], sems, 6)
    own_ids = own_lanes(jnp.broadcast_to(ids_ref[...], (8, ids_ref.shape[1])), index, parts, chunk)
    own = (codes == own_ids[0:1]).astype(F32)
    queries = turned(
        picked(0, own.astype(BF16)),
        own_lanes(cos_ref[...], index, parts, chunk),
        own_lanes(sin_ref[...], index, parts, chunk),
    )
    q_ref[...] = (queries * HD**-0.5).T.astype(BF16)
    middle_ref[...] = dot(own.T.astype(BF16), emb_ref[...])

    quads = width // (QUAD * HD)

    def attend(full, seen):
        for which in range(2):
            own_rows = slice(which * chunk, (which + 1) * chunk)
            place = chunk_of(index, which, parts)
            found = flash_quads(
                [quad_rows(q_ref[own_rows, lanes_of(quad)]) for quad in range(quads)],
                lambda j, quad: k_ref[block_of(j), lanes_of(quad)],
                lambda j, quad: vt_ref[lanes_of(quad), block_of(j)],
                full[which],
                full[which] * rows,
                place * chunk,
                (acc_ref.at[which], peak_ref.at[which], total_ref.at[which]),
            )
            for quad, (mixed, lse) in enumerate(found):
                o_ref[own_rows, lanes_of(quad)] = mixed.astype(BF16)
                row = which * quads + quad
                lse_ref[row : row + 1, :] = lse

    by_blocks(index, parts, attend)

    moves += copy_in([(q_ref, q_any), (o_ref, o_any)], sems, 9)
    moves[2].wait()
    middle = middle_ref[...] + dot(o_ref[...], out_w[...]) + out_b_ref[0:1]
    middle_ref[...] = middle
    moves += copy_in([(middle_ref, middle_any)], sems, 11)
    unit, _ = unit_rows(middle)
    second_ref[...] = (unit * gains_ref[0, 1:2] + shifts_ref[0, 1:2]).astype(BF16)
    sum_ref[...] = middle + reduce_b_ref[0:1]
    moves[3].wait()
    moves[4].wait()

    for c in range(expand_w.shape[1] // width):
        columns = slice(c * width, (c + 1) * width)
        pre = dot(second_ref[...], expand_w[:, columns]) + expand_b_ref[0:1, columns]
        value, rate = gelu_parts(pre)
        value = value.astype(BF16)
        active_ref[:, columns] = value
        rate_ref[:, columns] = rate.astype(BF16)
        moves += copy_in(
            [
                (active_ref.at[:, columns], active_any.at[:, columns]),
                (rate_ref.at[:, columns], rate_any.at[:, columns]),
            ],
            sems,
            12 + 2 * c,
        )
        sum_ref[...] += dot(value, reduce_w[columns, :])
    low_ref[...] = sum_ref[...].astype(BF16)

    moves[5].wait()
    third = rows // POOL

    for lane in range(width // LANES):
        split_ref[lane] = sum_ref[:, lane * LANES : (lane + 1) * LANES]

    def thirds(start):
        return every_third(split_ref, start, third).astype(BF16)

    later = dot(thirds(1), pool_w[0:width]) + dot(thirds(2), pool_w[width : 2 * width])
    same = dot(thirds(0), pool_w[2 * width : 3 * width])
    half = third // 2
    for which in range(2):
        start = which * (half + 8)
        later_ref[start : start + 8] = jnp.zeros((8, width), F32)
        later_ref[start + half : start + half + 8] = jnp.zeros((8, width), F32)
        later_ref[start + 1 : start + half + 1] = later[which * half : (which + 1) * half]
        share_ref[start : start + half] = (
            later_ref[start : start + half] + same[which * half : (which + 1) * half]
        ).astype(BF16)
        share_ref[start + half : start + half + 8] = later_ref[
            start + half : start + half + 8
        ].astype(BF16)
    for move in moves[6:]:
        move.wait()


def outer_forward(index, ids, embedding, gains, shifts, coarse, fine, out_w, out_b, expand_w,
                  expand_b, reduce_w, reduce_b, pool_w, rows):
    length = rows * len(ids)
    vocab, width = embedding.shape
    hidden = expand_w.shape[2]
    chunk, quads = rows // 2, width // (QUAD * HD)
    cosine, sine = angle_rows(length)
    vmem = pl.BlockSpec(memory_space=pltpu.VMEM)
    far = pl.BlockSpec(memory_space=pltpu.HBM)
    shape = outside
    third = rows // POOL
    kept = [
        shape((rows, width), BF16),
        shape((length, width), BF16),
        shape((width, length), BF16),
        shape((length, width), BF16),
        shape((rows, width), BF16),
        shape((rows, width), F32),
        shape((rows, hidden), BF16),
        shape((rows, hidden), BF16),
    ]
    return pl.pallas_call(
        functools.partial(outer_forward_kernel, length // rows),
        name="outer_forward",
        in_specs=[pl.BlockSpec(memory_space=pltpu.SMEM)] + [vmem] * (len(ids) + 3) + [far, far,
                  far, vmem, far, vmem, far, vmem, far, vmem, vmem],
        out_specs=[vmem] * 2 + [far] * 5 + [vmem] + [far] * 3 + [vmem],
        out_shape=[
            shape((rows, width), BF16),
            shape((third + 16, width), BF16),
        ]
        + kept[:5]
        + [shape((2 * quads, QUAD * chunk), F32)]
        + kept[5:]
        + [shape((1, length), jnp.int32)],
        scratch_shapes=[pltpu.VMEM(member.shape, member.dtype) for member in kept]
        + [
            pltpu.VMEM((width, width), BF16),
            pltpu.VMEM((width, hidden), BF16),
            pltpu.VMEM((hidden, width), BF16),
            pltpu.VMEM((POOL * width, width), BF16),
            pltpu.VMEM((3 * width, vocab), BF16),
            pltpu.VMEM((2 * width, vocab), BF16),
            pltpu.VMEM((width, length), BF16),
            pltpu.VMEM((2, quads, QUAD * HD, QUAD * chunk), F32),
            pltpu.VMEM((2, quads, 1, QUAD * chunk), F32),
            pltpu.VMEM((2, quads, 1, QUAD * chunk), F32),
            pltpu.VMEM((rows, width), BF16),
            pltpu.VMEM((rows, width), F32),
            pltpu.VMEM((third + 16, width), F32),
            pltpu.VMEM((width // LANES, rows, LANES), F32),
            pltpu.SemaphoreType.DMA((12 + 2 * (hidden // width),)),
        ],
        compiler_params=pltpu.CompilerParams(vmem_limit_bytes=grant(48 if length == 4 * rows else 60)),
        cost_estimate=cost(30),
    )(index, *ids, embedding, gains, shifts, coarse, fine, out_w, out_b, expand_w, expand_b,
      reduce_w, reduce_b, pool_w, far_away(jnp.asarray(cosine.T)), far_away(jnp.asarray(sine.T)))


def turn_rows(member, cosine, sine):
    pieces = []
    for start in range(0, member.shape[1], LANES):
        tile = member[:, start : start + LANES]
        lane = lax.broadcasted_iota(jnp.int32, tile.shape, 1) % HD
        other = jnp.where(
            lane < HD // 2,
            pltpu.roll(tile, LANES - HD // 2, 1),
            pltpu.roll(tile, HD // 2, 1),
        )
        pieces.append(tile * cosine + other * sine)
    return jnp.concatenate(pieces, axis=1)


def norm_back_rows(grad, unit, inverse, gain):
    scaled = grad * gain
    mean_one = jnp.mean(scaled, axis=-1, keepdims=True)
    mean_two = jnp.mean(scaled * unit, axis=-1, keepdims=True)
    return inverse * (scaled - mean_one - unit * mean_two)


def head_sums(product):
    tall = product.T
    return jnp.concatenate(
        [
            jnp.sum(tall[head * HD : (head + 1) * HD], axis=0, keepdims=True)
            for head in range(QUAD)
        ],
        axis=1,
    )


def back_block(scores, lse, delta, tall_q, tall_g, keys_t, values):
    probs = jnp.exp(scores - lse)
    low = (probs * (dot_nt(values, tall_g) - delta)).astype(BF16)
    return (dot(low, tall_q), dot(probs.astype(BF16), tall_g), dot(keys_t, low))


def share_columns(member_ref, index, parts):
    width = member_ref.shape[1] // parts
    if width % LANES == 0:
        return member_ref[:, pl.ds(pl.multiple_of(index * width, LANES), width)]
    full = member_ref.shape[1]
    row = lax.broadcasted_iota(jnp.int32, (full, width), 0)
    column = lax.broadcasted_iota(jnp.int32, (full, width), 1)
    picks = (row == column + index * width).astype(F32).astype(BF16)
    return dot(member_ref[...], picks).astype(BF16)


def can_pack(shapes, parts, blocks):
    return parts == 4 and all(
        rows % (16 * blocks) == 0 and columns % (LANES * parts) == 0 for rows, columns in shapes
    )


def packed_rows(shapes, parts, blocks):
    return sum(rows // blocks * (columns // parts // LANES) for rows, columns in shapes)


def spot_of(block, own_block, blocks):
    distance = jnp.bitwise_xor(own_block, block)
    return distance % 2 * (blocks // 2) + distance // 2


def store_packed(out, start, member, own_block, blocks):
    rows, columns = member.shape[0] // blocks, member.shape[1]
    for block in range(blocks):
        spot = spot_of(block, own_block, blocks)
        for tile in range(columns // LANES):
            out[spot, start + tile * rows : start + (tile + 1) * rows, :] = member[
                block * rows : (block + 1) * rows, tile * LANES : (tile + 1) * LANES
            ]
    return start + rows * (columns // LANES)


def inner_kernel(
    parts,
    blocks,
    packed,
    query_rows,
    index_ref,
    *rest,
):
    shares, rest = rest[:parts], rest[parts:]
    (
    pool_b_ref,
    gains_ref,
    shifts_ref,
    qkv_w_any,
    qkv_b_ref,
    out_w_any,
    out_b_ref,
    expand_w_any,
    expand_b_ref,
    reduce_w_any,
    reduce_b_ref,
    raised_grad_any,
    grad_any,
    cos_ref,
    sin_ref,
    ) = rest[:15]
    rest = rest[15:]
    outs = 2 if packed else 5
    low_ref, gz_ref, vec_ref = rest[:3]
    mats = rest[3 : 3 + outs]
    (
        qkv_w,
        out_w,
        expand_w,
        reduce_w,
        stream_ref,
        normed_ref,
        q_ref,
        k_ref,
        kt_ref,
        v_ref,
        vt_ref,
        o_ref,
        lse_ref,
        middle_ref,
        second_ref,
        active_ref,
        rate_ref,
        sum_ref,
        pre_ref,
        att_ref,
        go_ref,
        gk_ref,
        gv_ref,
        acc_ref,
        peak_ref,
        total_ref,
        raised_grad_ref,
        grad_ref,
        sems,
        *buffers,
    ) = rest[3 + outs :]
    index, own_block = index_ref[0], index_ref[1]
    rows, width = stream_ref.shape
    hidden_width = expand_w.shape[1]
    gq_ref, gqkv_ref = sum_ref, rate_ref.at[:, 0 : 3 * width]
    quads = width // (QUAD * HD)
    moves = copy_in(
        [
            (qkv_w_any.at[1], qkv_w),
            (out_w_any.at[1], out_w),
            (expand_w_any.at[1], expand_w),
            (reduce_w_any.at[1], reduce_w),
            (grad_any, grad_ref),
            (raised_grad_any, raised_grad_ref),
        ],
        sems,
    )
    share = rows // parts
    half = share // 2
    chunks = [
        (shares[distance], which * (half + 8), chunk_of(jnp.bitwise_xor(index, distance), which, parts))
        for distance in range(parts)
        for which in range(2)
    ]
    for given, start, place in chunks:
        own = pl.ds(pl.multiple_of(place * half, half), half)
        stream_ref[own] = given[start : start + half].astype(F32) + pool_b_ref[...]
    for given, start, place in chunks:

        @pl.when(place < 2 * parts - 1)
        def _():
            head = pl.ds(pl.multiple_of((place + 1) * half, half), 8)
            stream_ref[head] += given[start + half : start + half + 8].astype(F32)

    unit, _ = unit_rows(stream_ref[...])
    normed_ref[...] = (unit * gains_ref[1, 0:1] + shifts_ref[1, 0:1]).astype(BF16)
    moves[0].wait()

    def projected(part):
        columns = slice(part * width, (part + 1) * width)
        return dot(normed_ref[...], qkv_w[:, columns]) + qkv_b_ref[1:2, columns]

    cosine, sine = cos_ref[...], sin_ref[...]
    q_ref[...] = (turn_rows(projected(0), cosine, sine) * HD**-0.5).astype(BF16)
    keys = turn_rows(projected(1), cosine, sine)
    k_ref[...] = keys.astype(BF16)
    kt_ref[...] = keys.T.astype(BF16)
    values = projected(2)
    v_ref[...] = values.astype(BF16)
    vt_ref[...] = values.T.astype(BF16)

    def block_of(j):
        return pl.ds(pl.multiple_of(j * query_rows, query_rows), query_rows)

    def part(which, carry):
        own_rows = block_of(which)
        found = flash_quads(
            [quad_rows(q_ref[own_rows, lanes_of(quad)]) for quad in range(quads)],
            lambda j, quad: k_ref[block_of(j), lanes_of(quad)],
            lambda j, quad: vt_ref[lanes_of(quad), block_of(j)],
            which,
            which * query_rows,
            which * query_rows,
            (acc_ref, peak_ref, total_ref),
        )
        for quad, (mixed, lse) in enumerate(found):
            o_ref[own_rows, lanes_of(quad)] = mixed.astype(BF16)
            lse_ref[pl.ds(which * quads + quad, 1), :] = lse
        return carry

    lax.fori_loop(0, rows // query_rows, part, 0, unroll=parts == 4)
    moves[1].wait()
    middle = stream_ref[...] + dot(o_ref[...], out_w[...]) + out_b_ref[1:2]
    middle_ref[...] = middle
    unit, _ = unit_rows(middle)
    second_ref[...] = (unit * gains_ref[1, 1:2] + shifts_ref[1, 1:2]).astype(BF16)
    sum_ref[...] = middle + reduce_b_ref[1:2]
    moves[2].wait()
    moves[3].wait()

    def columns_of(c):
        return pl.ds(pl.multiple_of(c * width, width), width)

    def hidden(c, carry):
        columns = columns_of(c)
        pre = dot(second_ref[...], expand_w[:, columns]) + expand_b_ref[1:2, columns]
        value, rate = gelu_parts(pre)
        value = value.astype(BF16)
        active_ref[:, columns] = value
        rate_ref[:, columns] = rate.astype(BF16)
        sum_ref[...] += dot(value, reduce_w[columns, :])
        return carry

    lax.fori_loop(0, hidden_width // width, hidden, 0, unroll=parts == 4)
    low_ref[...] = sum_ref[...].astype(BF16)

    vec_ref[...] = jnp.zeros(vec_ref.shape, F32)

    def column_sum(row, member):
        vec_ref[row : row + 1, 0 : member.shape[1]] = jnp.sum(member, axis=0, keepdims=True)

    moves[4].wait()
    moves[5].wait()
    grad_low = grad_ref[...].astype(BF16)
    column_sum(7, grad_low.astype(F32))
    att_ref[...] = grad_low
    sum_ref[...] = jnp.zeros(sum_ref.shape, F32)

    def hidden_back(c, carry):
        columns = columns_of(c)
        pre = dot_nt(att_ref[...], reduce_w[columns, :]) * rate_ref[:, columns].astype(F32)
        low = pre.astype(BF16)
        pre_ref[:, columns] = low
        vec_ref[6:7, columns] = jnp.sum(low.astype(F32), axis=0, keepdims=True)
        sum_ref[...] += dot_nt(low, expand_w[:, columns])
        return carry

    lax.fori_loop(0, hidden_width // width, hidden_back, 0, unroll=parts == 4)
    if packed:
        place = store_packed(
            buffers[0], 0, dot_tn(active_ref[...], share_columns(att_ref, index, parts)).astype(BF16), own_block, blocks
        )
        place = store_packed(
            buffers[0], place, dot_tn(second_ref[...], share_columns(pre_ref, index, parts)).astype(BF16), own_block, blocks
        )
        place = store_packed(
            buffers[0], place, dot_tn(low_ref[...], share_columns(raised_grad_ref, index, parts)).astype(BF16), own_block, blocks
        )
    else:
        mats[0][...] = dot_tn(active_ref[...], share_columns(att_ref, index, parts)).astype(BF16)
        mats[1][...] = dot_tn(second_ref[...], share_columns(pre_ref, index, parts)).astype(BF16)
        mats[2][...] = dot_tn(low_ref[...], share_columns(raised_grad_ref, index, parts)).astype(BF16)

    unit, inverse = unit_rows(middle_ref[...])
    grad_second = sum_ref[...]
    column_sum(1, grad_second * unit)
    column_sum(3, grad_second)
    grad_middle = grad_ref[...] + norm_back_rows(grad_second, unit, inverse, gains_ref[1, 1:2])
    middle_ref[...] = grad_middle
    att_ref[...] = grad_middle.astype(BF16)
    column_sum(5, att_ref[...].astype(F32))
    go_ref[...] = dot_nt(att_ref[...], out_w[...]).astype(BF16)
    gk_ref[...] = jnp.zeros(gk_ref.shape, F32)
    gv_ref[...] = jnp.zeros(gv_ref.shape, F32)

    def part_back(which, carry):
        own_rows = block_of(which)
        every = range(quads)
        lanes = [lanes_of(quad) for quad in every]
        tall_q = [quad_rows(q_ref[own_rows, lane]) for lane in lanes]
        tall_g = [quad_rows(go_ref[own_rows, lane]) for lane in lanes]
        delta = [
            head_sums(o_ref[own_rows, lane].astype(F32) * go_ref[own_rows, lane].astype(F32))
            for lane in lanes
        ]

        def one(j, masked):
            keys = block_of(j)
            scores = [dot_nt(k_ref[keys, lanes[quad]], tall_q[quad]) for quad in every]
            if masked:
                scores = [
                    causal(member, j * query_rows, which * query_rows) for member in scores
                ]
            found = []
            for quad in every:
                lane = lanes[quad]
                add_k, add_v, add_q = back_block(
                    scores[quad],
                    lse_ref[pl.ds(which * quads + quad, 1), :],
                    delta[quad],
                    tall_q[quad],
                    tall_g[quad],
                    kt_ref[lane, keys],
                    v_ref[keys, lane],
                )
                gk_ref[keys, lane] += add_k
                gv_ref[keys, lane] += add_v
                found.append(add_q)
            return found

        for quad, found in enumerate(one(which, True)):
            acc_ref[quad] = found

        def full(j, inner_carry):
            for quad, found in enumerate(one(j, False)):
                acc_ref[quad] += found
            return inner_carry

        lax.fori_loop(0, which, full, 0)
        for quad in every:
            gq_ref[own_rows, lanes[quad]] = quad_fold(acc_ref[quad].T) * HD**-0.5
        return carry

    lax.fori_loop(0, rows // query_rows, part_back, 0, unroll=parts == 4)
    sine = -sin_ref[...]
    gqkv_ref[:, 0:width] = turn_rows(gq_ref[...], cosine, sine).astype(BF16)
    gqkv_ref[:, width : 2 * width] = turn_rows(gk_ref[...], cosine, sine).astype(BF16)
    gqkv_ref[:, 2 * width : 3 * width] = gv_ref[...].astype(BF16)
    column_sum(4, gqkv_ref[...].astype(F32))
    if packed:
        place = store_packed(
            buffers[0], place, dot_tn(o_ref[...], share_columns(att_ref, index, parts)).astype(BF16), own_block, blocks
        )
        store_packed(
            buffers[0], place, dot_tn(normed_ref[...], share_columns(gqkv_ref, index, parts)).astype(BF16), own_block, blocks
        )
    else:
        mats[3][...] = dot_tn(o_ref[...], share_columns(att_ref, index, parts)).astype(BF16)
        mats[4][...] = dot_tn(normed_ref[...], share_columns(gqkv_ref, index, parts)).astype(BF16)
    if packed:
        sent = copy_in(halves_of(buffers[0], mats), sems, 6)
    grad_normed = dot_nt(gqkv_ref[...], qkv_w[...])
    unit, inverse = unit_rows(stream_ref[...])
    column_sum(0, grad_normed * unit)
    column_sum(2, grad_normed)
    grad_in = middle_ref[...] + norm_back_rows(grad_normed, unit, inverse, gains_ref[1, 0:1])
    grad_in_low = grad_in.astype(BF16)
    gz_ref[0:rows] = grad_in_low
    gz_ref[rows : rows + 16] = jnp.zeros((16, width), BF16)
    column_sum(8, grad_in_low.astype(F32))
    if packed:
        for move in sent:
            move.wait()


def halves_of(buffer, outs):
    half = buffer.shape[0] // 2
    return [(buffer.at[0:half], outs[0]), (buffer.at[half : 2 * half], outs[1])]


def inner_shapes_of(width, hidden):
    return [
        (hidden, width),
        (width, hidden),
        (width, POOL * width),
        (width, width),
        (width, 3 * width),
    ]


def row_tables(length):
    cosine, sine = angle_rows(length)
    repeat = LANES // HD
    return (
        np.tile(np.concatenate([cosine, cosine], axis=1), (1, repeat)),
        np.tile(np.concatenate([-sine, sine], axis=1), (1, repeat)),
    )


def inner_layer(index, shares, pool_b, gains, shifts, qkv_w, qkv_b, out_w, out_b, expand_w, expand_b,
                reduce_w, reduce_b, raised_grad, grad, parts, blocks):
    rows, width = grad.shape
    raised_grad, grad = far_away(raised_grad), far_away(grad)
    hidden = expand_w.shape[2]
    quads = width // (QUAD * HD)
    query_rows = 256 if parts == 4 else 128
    shapes = inner_shapes_of(width, hidden)
    packed = can_pack(shapes, parts, blocks)
    cosine, sine = row_tables(rows)
    vmem = pl.BlockSpec(memory_space=pltpu.VMEM)
    anywhere = pl.BlockSpec(memory_space=pl.ANY)
    far = pl.BlockSpec(memory_space=pltpu.HBM)
    shape = outside
    if packed:
        held = packed_rows(shapes, parts, blocks)
        mats = [shape((blocks // 2, held, LANES), BF16) for _ in range(2)]
        buffers = [pltpu.VMEM((blocks, held, LANES), BF16)]
    else:
        mats = [shape((height, columns // parts), BF16) for height, columns in shapes]
        buffers = []
    found = pl.pallas_call(
        functools.partial(inner_kernel, parts, blocks, packed, query_rows),
        name="inner_layer",
        in_specs=[pl.BlockSpec(memory_space=pltpu.SMEM)] + [vmem] * parts + [vmem, vmem, vmem, far, vmem,
                  far, vmem, far, vmem, far, vmem, far, far, vmem, vmem],
        out_specs=[vmem] * 3 + [anywhere if packed else vmem] * len(mats),
        out_shape=[
            shape((rows, width), BF16),
            shape((rows + 16, width), BF16),
            shape((16, max(hidden, POOL * width)), F32),
        ] + mats,
        scratch_shapes=[
            pltpu.VMEM((width, 3 * width), BF16),
            pltpu.VMEM((width, width), BF16),
            pltpu.VMEM((width, hidden), BF16),
            pltpu.VMEM((hidden, width), BF16),
            pltpu.VMEM((rows, width), F32),
            pltpu.VMEM((rows, width), BF16),
            pltpu.VMEM((rows, width), BF16),
            pltpu.VMEM((rows, width), BF16),
            pltpu.VMEM((width, rows), BF16),
            pltpu.VMEM((rows, width), BF16),
            pltpu.VMEM((width, rows), BF16),
            pltpu.VMEM((rows, width), BF16),
            pltpu.VMEM((rows // query_rows * quads, QUAD * query_rows), F32),
            pltpu.VMEM((rows, width), F32),
            pltpu.VMEM((rows, width), BF16),
            pltpu.VMEM((rows, hidden), BF16),
            pltpu.VMEM((rows, hidden), BF16),
            pltpu.VMEM((rows, width), F32),
            pltpu.VMEM((rows, hidden), BF16),
            pltpu.VMEM((rows, width), BF16),
            pltpu.VMEM((rows, width), BF16),
            pltpu.VMEM((rows, width), F32),
            pltpu.VMEM((rows, width), F32),
            pltpu.VMEM((quads, QUAD * HD, QUAD * query_rows), F32),
            pltpu.VMEM((quads, 1, QUAD * query_rows), F32),
            pltpu.VMEM((quads, 1, QUAD * query_rows), F32),
            pltpu.VMEM(raised_grad.shape, BF16),
            pltpu.VMEM(grad.shape, F32),
            pltpu.SemaphoreType.DMA((8,)),
        ]
        + buffers,
        compiler_params=pltpu.CompilerParams(vmem_limit_bytes=grant(48 if parts == 4 else 60)),
        cost_estimate=cost(33),
    )(index, *shares, pool_b, gains, shifts, qkv_w, qkv_b, out_w, out_b, expand_w, expand_b, reduce_w,
      reduce_b, raised_grad, grad, far_away(jnp.asarray(cosine)), far_away(jnp.asarray(sine)))
    return found[0], found[1], found[2], found[3:], packed


def reversed_bits(value, size):
    found, bit = 0, 1
    while bit < size:
        found = found * 2 + (value // bit) % 2
        bit *= 2
    return found


def store_split(out, index, start, member, own_block, parts, blocks):
    columns = member.shape[1] // parts
    place = start
    for part in range(parts):
        spot = reversed_bits(jnp.bitwise_xor(index, part), parts)
        place = store_packed(
            out.at[spot],
            start,
            member[:, part * columns : (part + 1) * columns],
            own_block,
            blocks,
        )
    return place


def vector_tiles(entries, block, blocks):
    found = []
    for ref, row, length, scale in entries:
        size = length // blocks
        first, last = block * size // LANES, ((block + 1) * size - 1) // LANES
        found += [(ref, row, tile, scale) for tile in range(first, last + 1)]
    return found


def store_vectors(out, index, start, entries, own_block, parts, blocks):
    count = -(-len(vector_tiles(entries, 0, blocks)) // parts)
    for block in range(blocks):
        tiles = vector_tiles(entries, block, blocks)
        for part in range(parts):
            rows = [
                ref[row : row + 1, tile * LANES : (tile + 1) * LANES] * scale
                for ref, row, tile, scale in tiles[part * count : (part + 1) * count]
            ]
            rows += [jnp.zeros((16 - len(rows), LANES), F32)]
            spot = reversed_bits(jnp.bitwise_xor(index, part), parts)
            out[spot, spot_of(block, own_block, blocks), start : start + 16, :] = jnp.concatenate(
                rows, axis=0
            ).astype(BF16)


def split_lanes(split_ref, member):
    for lane in range(split_ref.shape[0]):
        split_ref[lane] = member[:, lane * LANES : (lane + 1) * LANES]


def joined_lanes(split_ref):
    return jnp.concatenate([split_ref[lane] for lane in range(split_ref.shape[0])], axis=1)


def add_third(split_ref, start, member):
    for lane in range(split_ref.shape[0]):
        rows = pl.ds(start, member.shape[0], stride=POOL)
        split_ref[lane, rows, :] = (
            split_ref[lane, rows, :] + member[:, lane * LANES : (lane + 1) * LANES]
        )


def raised_kernel(cot_ref, up_w_ref, joined_ref, grad_ref, sums_ref, split_ref):
    width = grad_ref.shape[1]
    split_lanes(split_ref, cot_ref[...].astype(F32))
    total = jnp.zeros(grad_ref.shape, F32)
    for slot in range(POOL):
        columns = slice(slot * width, (slot + 1) * width)
        rows = every_third(split_ref, slot, grad_ref.shape[0])
        sums_ref[:, columns] = jnp.sum(rows, axis=0, keepdims=True)
        rows = rows.astype(BF16)
        joined_ref[:, columns] = rows
        total += dot_nt(rows, up_w_ref[:, columns])
    grad_ref[...] = total


def raised_back(all_cot, up_w):
    length, width = all_cot.shape
    vmem = pl.BlockSpec(memory_space=pltpu.VMEM)
    shape = outside
    return pl.pallas_call(
        raised_kernel,
        name="raised_back",
        in_specs=[vmem] * 2,
        out_specs=[vmem] * 3,
        out_shape=[
            shape((length // POOL, POOL * width), BF16),
            shape((length // POOL, width), F32),
            shape((1, POOL * width), F32),
        ],
        scratch_shapes=[pltpu.VMEM((width // LANES, length, LANES), F32)],
        compiler_params=pltpu.CompilerParams(vmem_limit_bytes=grant(16, length // 1536)),
        cost_estimate=cost(4),
    )(all_cot, up_w)


def output_kernel(index_ref, lows_ref, low_ref, up_w_ref, up_b_ref, out_ref, split_ref):
    rows, width = out_ref.shape[1:]
    third = rows // POOL
    own = low_ref[pl.ds(pl.multiple_of(index_ref[0] * third, third), third), :]
    parts, chunk = lows_ref.shape[0], rows // 2
    found = []
    for which in range(2):
        place = 2 * index_ref[0] + which
        part = jnp.minimum(place, 2 * parts - 1 - place)
        start = jnp.where(place < parts, 0, chunk)
        found += [lows_ref[part, pl.ds(pl.multiple_of(start, chunk), chunk), :].astype(F32)]
    split_lanes(split_ref, jnp.concatenate(found, axis=0))
    for slot in range(POOL):
        columns = slice(slot * width, (slot + 1) * width)
        add_third(split_ref, slot, dot(own, up_w_ref[:, columns]) + up_b_ref[:, columns])
    out_ref[0] = joined_lanes(split_ref)


def raised_output(index, lows, low, up_w, up_b):
    rows, width = lows.shape[1:]
    vmem = pl.BlockSpec(memory_space=pltpu.VMEM)
    return pl.pallas_call(
        output_kernel,
        name="raised_output",
        in_specs=[pl.BlockSpec(memory_space=pltpu.SMEM)] + [vmem] * 4,
        out_specs=vmem,
        out_shape=jax.ShapeDtypeStruct((1, rows, width), F32),
        scratch_shapes=[pltpu.VMEM((width // LANES, rows, LANES), F32)],
        compiler_params=pltpu.CompilerParams(vmem_limit_bytes=grant(10)),
        cost_estimate=cost(3),
    )(index, lows, low, up_w, up_b)


def outer_hidden_kernel(
    parts,
    blocks,
    packed,
    index_ref,
    *rest,
):
    (
    lows_any,
    gz_any,
    inner_vec_ref,
    raised_vec_ref,
    cot_any,
    middle_in_any,
    active_any,
    rate_any,
    mixed_any,
    gains_ref,
    shifts_ref,
    pool_w_any,
    reduce_w_any,
    expand_w_any,
    out_w_any,
    ) = rest[:15]
    rest = rest[15:]
    outs = 4
    middle_any, go_ref, vec_ref = rest[:3]
    mats = rest[3 : 3 + outs]
    (
        pool_w,
        reduce_w,
        expand_w,
        out_w,
        split_ref,
        grad_ref,
        low_ref,
        second_ref,
        pre_ref,
        sum_ref,
        pooled_ref,
        lows_ref,
        gz_ref,
        middle_in_ref,
        active_ref,
        rate_ref,
        mixed_ref,
        middle_ref,
        att_ref,
        sems,
        *buffers,
    ) = rest[3 + outs :]
    index, own_block = index_ref[0], index_ref[1]
    rows, width = middle_in_ref.shape
    hidden_width = expand_w.shape[1]
    third = rows // POOL
    places = [chunk_of(index, which, parts) for which in range(2)]
    chunk = rows // 2
    coming = [(gz_any, gz_ref)] + [
        (
            cot_any.at[pl.ds(pl.multiple_of(place * chunk, chunk), chunk)],
            low_ref.at[which * chunk : (which + 1) * chunk],
        )
        for which, place in enumerate(places)
    ]
    coming += [
        (pool_w_any, pool_w),
        (rate_any, rate_ref),
        (reduce_w_any.at[0], reduce_w),
        (expand_w_any.at[0], expand_w),
        (middle_in_any, middle_in_ref),
        (active_any, active_ref),
        (out_w_any.at[0], out_w),
        (mixed_any, mixed_ref),
        (lows_any, lows_ref),
    ]
    coming = copy_in(coming, sems)
    moves = []
    half = third // 2
    coming[0].wait()
    tall = [
        gz_ref[pl.ds(pl.multiple_of(place * half, half), half + 16), :].astype(F32)
        for place in places
    ]
    here = jnp.concatenate([member[0:half] for member in tall], axis=0).astype(BF16)
    after = jnp.concatenate([member[1 : half + 1] for member in tall], axis=0).astype(BF16)

    coming[1].wait()
    coming[2].wait()
    split_lanes(split_ref, low_ref[...].astype(F32))
    coming[3].wait()
    add_third(split_ref, 0, dot_nt(here, pool_w[2 * width : 3 * width]))
    add_third(split_ref, 1, dot_nt(after, pool_w[0:width]))
    add_third(split_ref, 2, dot_nt(after, pool_w[width : 2 * width]))
    grad = joined_lanes(split_ref)
    grad_ref[...] = grad
    low_ref[...] = grad.astype(BF16)
    vec_ref[...] = jnp.zeros(vec_ref.shape, F32)

    def column_sum(row, member):
        vec_ref[row : row + 1, 0 : member.shape[1]] = jnp.sum(member, axis=0, keepdims=True)

    column_sum(3, low_ref[...].astype(F32))

    coming[7].wait()
    unit, inverse = unit_rows(middle_in_ref[...])
    second_ref[...] = (unit * gains_ref[0, 1:2] + shifts_ref[0, 1:2]).astype(BF16)
    sum_ref[...] = jnp.zeros(sum_ref.shape, F32)
    for move in coming[4:7] + coming[8:9]:
        move.wait()
    tiles = width // LANES

    def hidden_back(c, carry):
        columns = pl.ds(pl.multiple_of(c * width, width), width)
        pre = dot_nt(low_ref[...], reduce_w[columns, :]) * rate_ref[:, columns].astype(F32)
        low = pre.astype(BF16)
        vec_ref[2:3, columns] = jnp.sum(low.astype(F32), axis=0, keepdims=True)
        sum_ref[...] += dot_nt(low, expand_w[:, columns])
        reduce_grad = dot_tn(active_ref[:, columns], low_ref[...]).astype(BF16)
        expand_grad = dot_tn(second_ref[...], low).astype(BF16)
        if packed:
            out = buffers[0]
            height = hidden_width // blocks
            for part in range(parts):
                spot = reversed_bits(jnp.bitwise_xor(index, part), parts)
                for block in range(width // height):
                    place = spot_of(c * (width // height) + block, own_block, blocks)
                    out[spot, place, 0:height, :] = reduce_grad[
                        block * height : (block + 1) * height, part * LANES : (part + 1) * LANES
                    ]
            spot = reversed_bits(jnp.bitwise_xor(index, c), parts)
            store_packed(out.at[spot], height, expand_grad, own_block, blocks)
        else:
            mats[0][columns, :] = reduce_grad
            mats[1][:, columns] = expand_grad
        return carry

    lax.fori_loop(0, hidden_width // width, hidden_back, 0, unroll=True)
    grad_second = sum_ref[...]
    column_sum(0, grad_second * unit)
    column_sum(1, grad_second)
    grad_middle = grad_ref[...] + norm_back_rows(grad_second, unit, inverse, gains_ref[0, 1:2])
    middle_ref[...] = grad_middle
    moves += copy_in([(middle_ref, middle_any)], sems, 16)
    att_ref[...] = grad_middle.astype(BF16)
    column_sum(4, att_ref[...].astype(F32))
    coming[9].wait()
    coming[10].wait()
    go_ref[...] = dot_nt(att_ref[...], out_w[...]).astype(BF16)
    out_grad = dot_tn(mixed_ref[...], att_ref[...]).astype(BF16)
    if packed:
        place = hidden_width // blocks + tiles * (width // blocks)
        place = store_split(buffers[0], index, place, out_grad, own_block, parts, blocks)
        entries = early_entries(vec_ref, inner_vec_ref, raised_vec_ref, width, hidden_width, parts)
        store_vectors(buffers[0], index, place, entries, own_block, parts, blocks)
        moves += copy_in(halves_of(buffers[0], mats[0:2]), sems, 12)
    else:
        mats[2][...] = out_grad

    coming[11].wait()
    for part in range(parts):
        split_lanes(split_ref, lows_ref[part].astype(F32))
        for slot, first in ((0, 1), (1, 2), (2, 0)):
            found = every_third(split_ref, first, third).astype(BF16)
            for which in range(2):
                place = chunk_of(part, which, parts)
                own = slice(place * half, (place + 1) * half)
                pooled_ref[own, slot * width : (slot + 1) * width] = found[
                    which * half : (which + 1) * half
                ]
    shared = share_columns(gz_ref, index, parts).astype(F32)
    count = pooled_ref.shape[0]
    here, after = shared[0:count].astype(BF16), shared[1 : count + 1].astype(BF16)
    pool_grad = jnp.concatenate(
        [
            dot_tn(pooled_ref[:, slot * width : (slot + 1) * width], member).astype(BF16)
            for slot, member in ((0, after), (1, after), (2, here))
        ],
        axis=0,
    )
    if packed:
        store_packed(buffers[1], 0, pool_grad, own_block, blocks)
        moves += copy_in(halves_of(buffers[1], mats[2:4]), sems, 14)
    else:
        mats[3][...] = pool_grad
    for move in moves:
        move.wait()


def early_entries(vec_ref, inner_ref, raised_ref, width, hidden, parts):
    once = 1.0 / parts
    sizes = [width, width, width, width, 3 * width, width, hidden, width, width]
    return (
        [(vec_ref, 0, width, 1.0), (vec_ref, 1, width, 1.0), (vec_ref, 2, hidden, 1.0)]
        + [(vec_ref, 3, width, 1.0), (vec_ref, 4, width, 1.0)]
        + [(inner_ref, row, size, once) for row, size in enumerate(sizes)]
        + [(raised_ref, 0, POOL * width, once)]
    )


def late_entries(vec_ref, width):
    return [(vec_ref, 0, width, 1.0), (vec_ref, 1, width, 1.0), (vec_ref, 2, 3 * width, 1.0)]


def outer_hidden(index, lows, gz, inner_vecs, raised_vecs, cot, middle, active, rate, mixed, gains, shifts, pool_w, reduce_w, expand_w,
                 out_w, parts, blocks):
    rows, width = middle.shape
    lows, gz, cot, middle, active, rate, mixed = map(
        far_away, (lows, gz, cot, middle, active, rate, mixed)
    )
    hidden = expand_w.shape[2]
    shapes = [(hidden, width), (width, hidden), (width, width)]
    packed = can_pack(shapes + [(POOL * width, width)], parts, blocks) and hidden // parts == width and width // parts == LANES
    vmem = pl.BlockSpec(memory_space=pltpu.VMEM)
    far = pl.BlockSpec(memory_space=pltpu.HBM)
    shape = outside
    if packed:
        held = packed_rows(shapes, parts, blocks) + 16
        mats = [shape((parts // 2, blocks, held, LANES), BF16) for _ in range(2)]
        buffers = [pltpu.VMEM((parts, blocks, held, LANES), BF16)]
        added = packed_rows([(POOL * width, width)], parts, blocks)
        mats += [shape((blocks // 2, added, LANES), BF16) for _ in range(2)]
        buffers += [pltpu.VMEM((blocks, added, LANES), BF16)]
    else:
        mats = [shape(member, BF16) for member in shapes]
        mats += [shape((POOL * width, width // parts), BF16)]
        buffers = []
    found = pl.pallas_call(
        functools.partial(outer_hidden_kernel, parts, blocks, packed),
        name="outer_hidden",
        in_specs=[pl.BlockSpec(memory_space=pltpu.SMEM)] + [far] * 2 + [vmem] * 2 + [far] * 5 + [vmem] * 2 + [far] * 4,
        out_specs=[far] + [vmem] * 2 + [far if packed else vmem] * len(mats),
        out_shape=[
            shape((rows, width), F32),
            shape((rows, width), BF16),
            shape((8, hidden), F32),
        ] + mats,
        scratch_shapes=[
            pltpu.VMEM((POOL * width, width), BF16),
            pltpu.VMEM((hidden, width), BF16),
            pltpu.VMEM((width, hidden), BF16),
            pltpu.VMEM((width, width), BF16),
            pltpu.VMEM((width // LANES, rows, LANES), F32),
            pltpu.VMEM((rows, width), F32),
            pltpu.VMEM((rows, width), BF16),
            pltpu.VMEM((rows, width), BF16),
            pltpu.VMEM((rows, hidden), BF16),
            pltpu.VMEM((rows, width), F32),
            pltpu.VMEM((gz.shape[0] - 16, POOL * width), BF16),
            pltpu.VMEM(lows.shape, BF16),
            pltpu.VMEM(gz.shape, BF16),
            pltpu.VMEM((rows, width), F32),
            pltpu.VMEM((rows, hidden), BF16),
            pltpu.VMEM((rows, hidden), BF16),
            pltpu.VMEM((rows, width), BF16),
            pltpu.VMEM((rows, width), F32),
            pltpu.VMEM((rows, width), BF16),
            pltpu.SemaphoreType.DMA((17,)),
        ]
        + buffers,
        compiler_params=pltpu.CompilerParams(vmem_limit_bytes=grant(44 if packed else 60)),
        cost_estimate=cost(14),
    )(index, lows, gz, inner_vecs, raised_vecs, cot, middle, active, rate, mixed, gains, shifts, pool_w, reduce_w, expand_w, out_w)
    return found[:3], found[3:], packed, shapes


def store_rows(out, index, first, member, own_block, parts, blocks):
    rows, tiles = member.shape[0] // blocks, member.shape[1] // LANES
    share = rows // parts
    for part in range(parts):
        spot = reversed_bits(jnp.bitwise_xor(index, part), parts)
        for block in range(blocks):
            place = spot_of(block, own_block, blocks)
            start = block * rows + part * share
            for tile in range(tiles):
                out[spot, place, first + tile * share : first + (tile + 1) * share, :] = member[
                    start : start + share, tile * LANES : (tile + 1) * LANES
                ]
    return first + tiles * share


def outer_attention_kernel(
    parts,
    blocks,
    packed,
    quad,
    last,
    anchors,
    index_ref,
    ids_ref,
    emb_ref,
    gains_ref,
    shifts_ref,
    qkv_w_any,
    q_ref,
    k_ref,
    kt_ref,
    v_ref,
    o_ref,
    lse_ref,
    go_ref,
    cos_ref,
    sin_ref,
    *rest,
):
    given = (4 if last else 0) + anchors
    if last:
        middle_ref, sums_in_ref, first_ref, table_in_ref = rest[:4]
    outs = rest[given : given + 3]
    (qkv_w, gq_ref, gk_ref, gv_ref, code_ref, acc_ref, sems, *buffers) = rest[given + 3 :]
    index, own_block = index_ref[0], index_ref[1]
    rows, width = o_ref.shape
    vocab = emb_ref.shape[0]
    chunk = rows // 2
    wide = QUAD * HD
    lanes = slice(quad * wide, (quad + 1) * wide)
    moves = copy_in(
        [
            (
                qkv_w_any.at[0, :, part * width + quad * wide : part * width + (quad + 1) * wide],
                qkv_w.at[part],
            )
            for part in range(3)
        ],
        sems,
    )

    def block_of(j):
        if isinstance(j, int):
            return slice(j * rows, (j + 1) * rows)
        return pl.ds(pl.multiple_of(j * rows, rows), rows)

    def clear(j):
        gk_ref[block_of(j), :] = jnp.zeros((rows, wide), F32)
        gv_ref[block_of(j), :] = jnp.zeros((rows, wide), F32)

    def part_back(which, full):
        own_rows = slice(which * chunk, (which + 1) * chunk)
        place = chunk_of(index, which, parts)
        tall_q = quad_rows(q_ref[own_rows, lanes])
        tall_g = quad_rows(go_ref[own_rows, lanes])
        row = which * (width // wide) + quad
        lse = lse_ref[row : row + 1, :]
        delta = head_sums(o_ref[own_rows, lanes].astype(F32) * go_ref[own_rows, lanes].astype(F32))

        def one(j, masked):
            keys = block_of(j)
            scores = dot_nt(k_ref[keys, lanes], tall_q)
            if masked:
                scores = causal(scores, j * rows, place * chunk)
            add_k, add_v, add_q = back_block(
                scores, lse, delta, tall_q, tall_g, kt_ref[lanes, keys], v_ref[keys, lanes]
            )
            gk_ref[keys, :] += add_k
            gv_ref[keys, :] += add_v
            return add_q

        acc_ref[which] = one(full, True)

        def further(j):
            acc_ref[which] += one(j, False)

        each(full, further)
        gq_ref[own_rows, :] = quad_fold(acc_ref[which].T) * HD**-0.5

    def attend_back(full, seen):
        each(seen, clear)
        for which in range(2):
            part_back(which, full[which])

    by_blocks(index, parts, attend_back)

    codes = lax.broadcasted_iota(jnp.int32, (vocab, rows), 0)
    own_ids = own_lanes(jnp.broadcast_to(ids_ref[...], (8, ids_ref.shape[1])), index, parts, chunk)
    own_hot = (codes == own_ids[0:1]).astype(F32).astype(BF16)

    def own_rows_of(table):
        return jnp.concatenate(
            [
                table[pl.ds(pl.multiple_of(chunk_of(index, which, parts) * chunk, chunk), chunk), :]
                for which in range(2)
            ],
            axis=0,
        )

    turned = turn_rows(gq_ref[...], own_rows_of(cos_ref), -own_rows_of(sin_ref)).astype(BF16)
    code_ref[:, 0:wide] = dot(own_hot, turned)
    code_ref[:, wide : 3 * wide] = jnp.zeros((vocab, 2 * wide), F32)

    def by_code(j):
        columns = block_of(j)
        hot = (codes == ids_ref[:, columns]).astype(F32).astype(BF16)
        turned = turn_rows(gk_ref[columns, :], cos_ref[columns, :], -sin_ref[columns, :])
        code_ref[:, wide : 2 * wide] += dot(hot, turned.astype(BF16))
        code_ref[:, 2 * wide : 3 * wide] += dot(hot, gv_ref[columns, :].astype(BF16))

    by_blocks(index, parts, lambda full, seen: each(seen, by_code))
    code = code_ref[...]
    code_low = code.astype(BF16)
    unit, inverse = unit_rows(emb_ref[...].astype(F32))
    normed = (unit * gains_ref[0, 0:1] + shifts_ref[0, 0:1]).astype(BF16)
    qkv_grad = dot_tn(normed, code_low).astype(BF16)
    grad_table = jnp.zeros((vocab, width), F32)
    for part in range(3):
        moves[part].wait()
        grad_table += dot_nt(code_low[:, part * wide : (part + 1) * wide], qkv_w[part])
    vec_ref = outs[0]
    if last:
        vec_ref[...] = sums_in_ref[...]
    else:
        vec_ref[...] = jnp.zeros(vec_ref.shape, F32)
    for part in range(3):
        start = part * width + quad * wide
        vec_ref[2:3, start : start + wide] = jnp.sum(
            code[:, part * wide : (part + 1) * wide], axis=0, keepdims=True
        )
    if not last:
        outs[1][...] = qkv_grad
        outs[2][...] = grad_table
        return
    grad_table += table_in_ref[...]
    high = middle_ref[...].astype(BF16)
    low = (middle_ref[...] - high.astype(F32)).astype(BF16)
    embed = dot(own_hot, high) + dot(own_hot, low)
    embed = embed + norm_back_rows(grad_table, unit, inverse, gains_ref[0, 0:1])
    embed = embed.astype(BF16)
    vec_ref[0:1, 0:width] = jnp.sum(grad_table * unit, axis=0, keepdims=True)
    vec_ref[1:2, 0:width] = jnp.sum(grad_table, axis=0, keepdims=True)
    if packed:
        out = buffers[0]
        place = store_rows(out, index, 0, first_ref[...], own_block, parts, blocks)
        place = store_rows(out, index, place, qkv_grad, own_block, parts, blocks)
        place = store_split(out, index, place, embed, own_block, parts, blocks)
        store_vectors(out, index, place, late_entries(vec_ref, width), own_block, parts, blocks)
        for move in copy_in(halves_of(out, outs[1:]), sems, 3):
            move.wait()
    else:
        outs[1][...] = qkv_grad
        outs[2][...] = embed


def outer_attention(quad, index, all_ids, embedding, gains, shifts, qkv_w, queries, keys, keys_t, values,
                    mixed, lse, go, ending, anchors, parts, blocks):
    rows, width = queries.shape
    length = all_ids.shape[1]
    vocab = embedding.shape[0]
    chunk = rows // 2
    wide = QUAD * HD
    last = ending is not None
    packed = width % (16 * parts * blocks) == 0 and vocab % (16 * blocks) == 0
    packed = packed and width % (LANES * parts) == 0 and parts == 4
    cosine, sine = row_tables(length)
    vmem = pl.BlockSpec(memory_space=pltpu.VMEM)
    anywhere = pl.BlockSpec(memory_space=pl.ANY)
    far = pl.BlockSpec(memory_space=pltpu.HBM)
    shape = outside
    outs, buffers = [shape((8, 3 * width), F32)], []
    if not last:
        outs += [shape((width, 3 * wide), BF16), shape((vocab, width), F32)]
    elif packed:
        held = 3 * width // LANES * (width // blocks // parts)
        held += vocab // blocks * (width // parts // LANES) + 16
        outs += [shape((parts // 2, blocks, held, LANES), BF16) for _ in range(2)]
        buffers = [pltpu.VMEM((parts, blocks, held, LANES), BF16)]
    else:
        outs += [shape((width, 3 * wide), BF16), shape((vocab, width), BF16)]
    ending = list(ending) if last else []
    return pl.pallas_call(
        functools.partial(outer_attention_kernel, parts, blocks, packed, quad, last, len(anchors)),
        name="outer_attention",
        in_specs=[pl.BlockSpec(memory_space=pltpu.SMEM)]
        + [vmem] * 4
        + [far]
        + [vmem] * 9
        + [vmem] * len(ending)
        + [anywhere] * len(anchors),
        out_specs=[vmem] + [anywhere if buffers else vmem] * 2,
        out_shape=outs,
        scratch_shapes=[
            pltpu.VMEM((3, width, wide), BF16),
            pltpu.VMEM((rows, wide), F32),
            pltpu.VMEM((length, wide), F32),
            pltpu.VMEM((length, wide), F32),
            pltpu.VMEM((vocab, 3 * wide), F32),
            pltpu.VMEM((2, wide, QUAD * chunk), F32),
            pltpu.SemaphoreType.DMA((5,)),
        ]
        + buffers,
        compiler_params=pltpu.CompilerParams(vmem_limit_bytes=grant(34, length // (4 * rows))),
        cost_estimate=cost(14),
    )(index, all_ids, embedding, gains, shifts, qkv_w, queries, keys, keys_t, values, mixed, lse, go,
      far_away(jnp.asarray(cosine)), far_away(jnp.asarray(sine)), *ending, *map(far_away, anchors)), packed


def add_kernel(count, anchors, index_slices, *refs):
    sources, outs = refs[:count], refs[count + anchors :]
    for out, piece in zip(outs, index_slices):
        total = sources[0][piece].astype(F32)
        for source in sources[1:]:
            total += source[piece].astype(F32)
        out[...] = total.astype(BF16)


def add(sources, pieces, anchors=(), shape_of=jax.ShapeDtypeStruct):
    shape = sources[0].shape
    found, slices = [], []
    for piece in pieces:
        if isinstance(piece, int):
            found, slices = found + [shape[1:]], slices + [piece]
        else:
            *first, start, stop = piece
            found += [(stop - start, *shape[1 + len(first) :])]
            slices += [(*first, slice(start, stop))]
    vmem = pl.BlockSpec(memory_space=pltpu.VMEM)
    return list(pl.pallas_call(
        functools.partial(add_kernel, len(sources), len(anchors), slices),
        name="add",
        in_specs=[vmem] * len(sources) + [pl.BlockSpec(memory_space=pl.ANY)] * len(anchors),
        out_specs=[vmem] * len(found),
        out_shape=[shape_of(member, BF16) for member in found],
        compiler_params=pltpu.CompilerParams(vmem_limit_bytes=grant(16)),
        cost_estimate=cost(3),
    )(*sources, *map(far_away, anchors)))


def merge_kernel(plan, split, count, *refs):
    sources, outs = refs[:count], refs[len(refs) - split :]
    for spot in range(sources[0].shape[0]):
        out = outs[spot] if split > 1 else outs[0].at[spot]
        at = 0
        for rows, members in plan:
            total = sources[members[0][0]][spot, members[0][1] : members[0][1] + rows].astype(F32)
            for source, start in members[1:]:
                total += sources[source][spot, start : start + rows].astype(F32)
            out[at : at + rows, :] = total.astype(BF16)
            at += rows


def merge(sources, plan, split, anchors=()):
    count = sources[0].shape[0]
    rows = sum(member[0] for member in plan)
    vmem = pl.BlockSpec(memory_space=pltpu.VMEM)
    shapes = [(rows, LANES)] * count if split else [(count, rows, LANES)]
    return list(
        pl.pallas_call(
            functools.partial(merge_kernel, plan, len(shapes), len(sources)),
            name="merge",
            in_specs=[vmem] * len(sources) + [pl.BlockSpec(memory_space=pl.ANY)] * len(anchors),
            out_specs=[vmem] * len(shapes),
            out_shape=[jax.ShapeDtypeStruct(member, BF16) for member in shapes],
            compiler_params=pltpu.CompilerParams(vmem_limit_bytes=grant(16)),
            cost_estimate=cost(3),
        )(*sources, *map(far_away, anchors))
    )


def total_kernel(counts, *refs):
    out, start, at = refs[-1], 0, 0
    for count in counts:
        total = refs[at][...].astype(F32)
        for ref in refs[at + 1 : at + count]:
            total += ref[...].astype(F32)
        out[start : start + total.shape[0], :] = total.astype(BF16)
        start, at = start + total.shape[0], at + count


def totals(groups, anchors=()):
    rows = sum(group[0].shape[0] for group in groups)
    vmem = pl.BlockSpec(memory_space=pltpu.VMEM)
    members = [member for group in groups for member in group]
    return pl.pallas_call(
        functools.partial(total_kernel, [len(group) for group in groups]),
        name="totals",
        in_specs=[vmem] * len(members) + [pl.BlockSpec(memory_space=pl.ANY)] * len(anchors),
        out_specs=vmem,
        out_shape=jax.ShapeDtypeStruct((rows, LANES), BF16),
        compiler_params=pltpu.CompilerParams(vmem_limit_bytes=grant(8)),
        cost_estimate=cost(3),
    )(*members, *map(far_away, anchors))


def assemble_kernel(parts, blocks, index_ref, *rest):
    early, late, outs = rest[:parts], rest[parts : 2 * parts], rest[2 * parts :]
    index, own_block = index_ref[0], index_ref[1]
    (embed, gains, shifts, qkv_w, qkv_b, out_w, out_b, expand_w, expand_b, reduce_w, reduce_b) = outs[:11]
    pool_w, pool_b, up_w, up_b = outs[11:]

    def place(group, start, out, height, columns):
        tiles = columns // parts // LANES
        for at in range(parts):
            part = jnp.bitwise_xor(index, at)
            for tile in range(tiles):
                lanes = pl.ds(pl.multiple_of((part * tiles + tile) * LANES, LANES), LANES)
                found = group[at][start + tile * height : start + (tile + 1) * height]
                out[:, lanes] = found.astype(F32)
        return start + tiles * height

    start = 0
    for out in (reduce_w.at[1], expand_w.at[1], up_w, out_w.at[1], qkv_w.at[1], pool_w):
        start = place(early, start, out, *out.shape)
    for out in (reduce_w.at[0], expand_w.at[0], out_w.at[0]):
        start = place(early, start, out, *out.shape)
    early_start = start
    height, wide = qkv_w.shape[1] // parts, QUAD * HD
    start = 0
    for quad in range(qkv_w.shape[2] // 3 // wide):
        for third in range(3):
            for tile in range(wide // LANES):
                lane = third * (qkv_w.shape[2] // 3) + quad * wide + tile * LANES
                for distance in range(parts):
                    part = jnp.bitwise_xor(index, distance)
                    rows = pl.ds(pl.multiple_of(part * height, height), height)
                    qkv_w[0, rows, lane : lane + LANES] = late[distance][
                        start : start + height
                    ].astype(F32)
                start += height
    late_start = place(late, start, embed, *embed.shape)

    def vectors(group, start, sizes):
        entries = [(None, 0, size * blocks, 1.0) for size in sizes]
        total = len(vector_tiles(entries, 0, blocks))
        count = -(-total // parts)
        tiles = {}
        for distance in range(parts):
            tiles[distance] = group[distance][start : start + 16].astype(F32)
        rows = []
        for number in range(total):
            row = jnp.zeros((1, LANES), F32)
            for distance in range(parts):
                here = jnp.bitwise_xor(index, distance) == number // count
                row = jnp.where(here, tiles[distance][number % count : number % count + 1], row)
            rows.append(row)
        found, number = [], 0
        for size in sizes:
            held = len(vector_tiles([(None, 0, size * blocks, 1.0)], 0, blocks))
            wide = jnp.concatenate(rows[number : number + held], axis=1)
            number += held
            if size % LANES != 0:
                shift = own_block * size % LANES
                wide = pltpu.roll(wide, (wide.shape[1] - shift) % wide.shape[1], 1)
            found.append(wide[:, :size])
        return found

    width_b, hidden_b, three_b = out_b.shape[1], expand_b.shape[1], qkv_b.shape[1]
    low = vectors(
        early,
        early_start,
        [width_b, width_b, hidden_b, width_b, width_b]
        + [width_b] * 4
        + [three_b, width_b, hidden_b, width_b, width_b, three_b],
    )
    high = vectors(late, late_start, [width_b, width_b, three_b])
    gains[0, 0:1], shifts[0, 0:1], qkv_b[0:1] = high
    gains[0, 1:2], shifts[0, 1:2], expand_b[0:1], reduce_b[0:1], out_b[0:1] = low[:5]
    gains[1, 0:1], gains[1, 1:2], shifts[1, 0:1], shifts[1, 1:2] = low[5:9]
    qkv_b[1:2], out_b[1:2], expand_b[1:2], reduce_b[1:2] = low[9:13]
    pool_b[...], up_b[...] = low[13:]


def assemble(index, gathered, late, width, hidden, vocab, parts, blocks):
    vmem = pl.BlockSpec(memory_space=pltpu.VMEM)
    part = width // blocks
    shapes = [
        (vocab // blocks, width),
        (2, 2, part),
        (2, 2, part),
        (2, part, 3 * width),
        (2, 3 * part),
        (2, part, width),
        (2, part),
        (2, part, hidden),
        (2, hidden // blocks),
        (2, hidden // blocks, width),
        (2, part),
        (POOL * part, width),
        (1, part),
        (part, POOL * width),
        (1, POOL * part),
    ]
    return pl.pallas_call(
        functools.partial(assemble_kernel, parts, blocks),
        name="assemble",
        in_specs=[pl.BlockSpec(memory_space=pltpu.SMEM)] + [vmem] * (2 * parts),
        out_specs=[vmem] * 15,
        out_shape=[jax.ShapeDtypeStruct(member, F32) for member in shapes],
        compiler_params=pltpu.CompilerParams(vmem_limit_bytes=grant(16)),
        cost_estimate=cost(4),
    )(index, *gathered, *late)


def pack(members, parts, blocks):
    rows = []
    for member in members:
        height, width = member.shape
        split = member.reshape(blocks, height // blocks, parts, width // parts)
        rows.append(split.transpose(2, 0, 1, 3).reshape(parts, blocks, -1))
    buffer = jnp.concatenate(rows, axis=2)
    order = [reversed_bits(spot, parts) for spot in range(parts)]
    index = lax.axis_index("seq")
    buffer = jnp.stack([buffer[jnp.bitwise_xor(index, other)] for other in order])
    return buffer.reshape(parts, blocks, -1, LANES)


def in_spots(buffer):
    blocks = buffer.shape[-3]
    index = lax.axis_index("batch")
    order = [spot * 2 % blocks + spot * 2 // blocks for spot in range(blocks)]
    return jnp.stack(
        [
            lax.dynamic_index_in_dim(buffer, jnp.bitwise_xor(index, other), -3, keepdims=False)
            for other in order
        ],
        axis=-3,
    )


def exchange(member, axis, distance):
    pairs = [(peer, peer ^ distance) for peer in range(lax.axis_size(axis))]
    return lax.ppermute(member, axis, pairs)


def seq_near(keep, send, anchors=()):
    half = keep.shape[1] // 2
    pieces = [(part, start, start + half) for part in range(2) for start in (half, 0)]
    return add([keep, exchange(send, "seq", 1)], pieces, anchors)


def seq_far_send(quarters, beside=(), anchors=()):
    near, far = quarters[0], quarters[2]
    rows = near.shape[1]
    sources = [near, exchange(far, "seq", 2)]
    plan = [(rows, ((0, 0), (1, 0)))]
    if beside:
        sources, plan = sources + [beside[1]], plan + [(beside[1].shape[1], ((2, 0),))]
    return merge(sources, plan, False, anchors)[0]


def seq_far_keep(quarters, leaving, beside=(), others=(), anchors=()):
    near, far = quarters[1], quarters[3]
    rows = near.shape[1]
    if others:
        far = behind(far, *others)
    sources = [near, exchange(far, "seq", 2), exchange(leaving, "batch", 1)]
    plan = [(rows, ((0, 0), (1, 0), (2, 0)))]
    if beside:
        sources, plan = sources + [beside[0]], plan + [(beside[0].shape[1], ((3, 0), (2, rows)))]
    return merge(sources, plan, True, anchors)


def batch_halves(keep, send, anchors=()):
    return add([keep, exchange(send, "batch", 1)], list(range(keep.shape[0])), anchors)


def batch_rest(sums):
    return [sums[0]] + [
        exchange(sums[spot], "batch", 2 * spot) for spot in range(1, len(sums))
    ]


def plain_sums(buffer):
    level = 1
    while buffer.shape[0] > 1:
        half = buffer.shape[0] // 2
        got = exchange(buffer[half:], "seq", level)
        buffer = (buffer[:half].astype(F32) + got.astype(F32)).astype(BF16)
        level *= 2
    return plain_batch(buffer[0])


def plain_batch(buffer):
    half = buffer.shape[0] // 2
    got = exchange(buffer[half:], "batch", 1)
    sums = (buffer[:half].astype(F32) + got.astype(F32)).astype(BF16)
    total = sums[0].astype(F32)
    for spot in range(1, half):
        total += exchange(sums[spot], "batch", 2 * spot).astype(F32)
    return total.astype(BF16)


def behind(member, *others):
    return lax.optimization_barrier((member, *others))[0]


def seq_gather(member, *between):
    parts = lax.axis_size("seq")
    found, level = {0: member}, parts // 2
    while level >= 1:
        for distance, held in list(found.items()):
            found[distance ^ level] = exchange(held, "seq", level)
        if level == parts // 2 and between:
            found[level] = behind(found[level], *between)
        level //= 2
    return [found[distance] for distance in range(parts)]


def in_order(found):
    found = jnp.stack(found)
    index = lax.axis_index("seq")
    return jnp.stack([found[jnp.bitwise_xor(index, part)] for part in range(len(found))])


def unpack(gathered, shapes, blocks):
    parts = gathered.shape[0]
    gathered = gathered.reshape(parts, -1)
    found, start = [], 0
    for height, width in shapes:
        height, columns = height // blocks, width // parts
        piece = gathered[:, start : start + height * columns]
        piece = piece.reshape(parts, height, columns).transpose(1, 0, 2)
        start += height * columns
        found.append(piece.reshape(height, width).astype(F32))
    return found


def local(
    byte_ids,
    embedding,
    norm_gains,
    norm_biases,
    qkv_weights,
    qkv_biases,
    out_weights,
    out_biases,
    expand_weights,
    expand_biases,
    reduce_weights,
    reduce_biases,
    pool_weight,
    pool_bias,
    upsample_weight,
    upsample_bias,
    cotangent,
):
    parts, blocks = lax.axis_size("seq"), lax.axis_size("batch")
    rows, width, hidden = byte_ids.shape[1], embedding.shape[1], expand_weights.shape[2]
    index = jnp.stack([lax.axis_index("seq"), lax.axis_index("batch")]).astype(jnp.int32)
    ids = seq_gather(byte_ids)
    all_cot = lax.all_gather(cotangent[0], "seq", axis=0, tiled=True)

    (embedding, norm_gains, norm_biases, qkv_weights, qkv_biases, out_weights, out_biases) = (
        far_away(member)
        for member in (
            embedding, norm_gains, norm_biases, qkv_weights, qkv_biases, out_weights, out_biases
        )
    )
    (expand_weights, expand_biases, reduce_weights, reduce_biases, pool_weight) = (
        far_away(member)
        for member in (expand_weights, expand_biases, reduce_weights, reduce_biases, pool_weight)
    )
    (pool_bias, upsample_weight, upsample_bias) = (
        far_away(member) for member in (pool_bias[None], upsample_weight, upsample_bias[None])
    )

    coarse, fine = byte_table(embedding, norm_gains, norm_biases, qkv_weights, qkv_biases)
    h1_low, share, queries, keys, keys_t, values, mixed, lse, middle, active, rate, all_ids = outer_forward(
        index, ids, embedding, norm_gains, norm_biases, coarse, fine, out_weights, out_biases,
        expand_weights, expand_biases, reduce_weights, reduce_biases, pool_weight, rows
    )
    raised_grad, grad_short, raised_sums = raised_back(all_cot, upsample_weight)
    shares = seq_gather(share, raised_sums)
    short_low, gz, inner_vecs, inner_found, inner_packed = inner_layer(
        index, shares, pool_bias, norm_gains, norm_biases, qkv_weights, qkv_biases,
        out_weights, out_biases, expand_weights, expand_biases, reduce_weights, reduce_biases,
        raised_grad, grad_short, parts, blocks
    )
    lows = lax.all_gather(behind(h1_low, shares[-1]), "seq", axis=0)
    output = raised_output(index, lows, short_low, upsample_weight, upsample_bias)

    (grad_middle, grad_mixed, hidden_vecs), early, early_packed, early_shapes = outer_hidden(
        index, lows, gz, inner_vecs, raised_sums, all_cot, middle, active, rate, mixed, norm_gains,
        norm_biases, pool_weight, reduce_weights, expand_weights, out_weights, parts, blocks
    )

    def attention_back(quad, ending, anchors):
        return outer_attention(
            quad, index, all_ids, embedding, norm_gains, norm_biases, qkv_weights, queries, keys,
            keys_t, values, mixed, lse, grad_mixed, ending, anchors, parts, blocks
        )

    anchors = []
    packed = inner_packed and early_packed
    if packed:
        quarters = seq_near(*early[0:2], [output])
        inner_sums = merge(
            [
                inner_found[0],
                exchange(inner_found[1], "batch", 1),
                early[2],
                exchange(early[3], "batch", 1),
            ],
            [
                (inner_found[0].shape[1], ((0, 0), (1, 0))),
                (early[2].shape[1], ((2, 0), (3, 0))),
            ],
            True,
            quarters[3:],
        )
        anchors = inner_sums[1:] + quarters[2:]
    ending, late_packed = attention_back(0, None, anchors)
    if packed:
        leaving = seq_far_send(quarters, (), ending[:1])
        inner_rest = batch_rest(inner_sums)
        anchors = [inner_rest[1], leaving]
    (table_vecs, *late), _ = attention_back(1, [grad_middle] + list(ending), anchors)
    if packed and late_packed:
        early_sums = seq_far_keep(quarters, leaving, (), ending[:1], inner_rest[2:])
        late_quarters = seq_near(*late, early_sums[:1])
        late_sums = seq_far_keep(late_quarters, seq_far_send(late_quarters))
        gathered = seq_gather(totals([inner_rest, batch_rest(early_sums)]))
        late_total = totals([batch_rest(late_sums)])
        found = list(
            assemble(index, gathered, seq_gather(late_total), width, hidden, embedding.shape[0], parts, blocks)
        )
        found[12], found[14] = found[12][0], found[14][0]
        return (output, *found)

    inner_shapes = inner_shapes_of(width, hidden)
    inner_buffer = jnp.concatenate([member.reshape(blocks, -1) for member in inner_found], axis=1)
    inner_buffer = in_spots(inner_buffer.reshape(blocks, -1, LANES))
    inner_out = unpack(in_order(seq_gather(plain_batch(inner_buffer))), inner_shapes, blocks)
    pool_buffer = in_spots(early[3].reshape(blocks, -1, LANES))
    pool_out = unpack(
        in_order(seq_gather(plain_batch(pool_buffer))), [(POOL * width, width)], blocks
    )
    early_buffer = in_spots(pack(early[:3], parts, blocks))
    early_out = unpack(
        in_order(seq_gather(plain_sums(early_buffer))), early_shapes, blocks
    )
    wide = QUAD * HD
    qkv_grad = jnp.concatenate(
        [
            half[:, part * wide : (part + 1) * wide]
            for part in range(3)
            for half in (ending[1], late[0])
        ],
        axis=1,
    )
    late, late_shapes = [qkv_grad, late[1]], [qkv_grad.shape, late[1].shape]
    late_buffer = in_spots(pack(late, parts, blocks))
    late_out = unpack(
        in_order(seq_gather(plain_sums(late_buffer))), late_shapes, blocks
    )
    once = 1.0 / parts
    vectors = [
        table_vecs[0, :width],
        hidden_vecs[0, :width],
        table_vecs[1, :width],
        hidden_vecs[1, :width],
        table_vecs[2, : 3 * width],
        hidden_vecs[4, :width],
        hidden_vecs[2, :hidden],
        hidden_vecs[3, :width],
        inner_vecs[0, :width] * once,
        inner_vecs[1, :width] * once,
        inner_vecs[2, :width] * once,
        inner_vecs[3, :width] * once,
        inner_vecs[4, : 3 * width] * once,
        inner_vecs[5, :width] * once,
        inner_vecs[6, :hidden] * once,
        inner_vecs[7, :width] * once,
        inner_vecs[8, :width] * once,
        raised_sums[0] * once,
    ]
    flat = jnp.concatenate([member.reshape(blocks, -1) for member in vectors], axis=1)
    flat = lax.psum(flat.astype(BF16), ("seq", "batch")).astype(F32)
    flat = lax.dynamic_index_in_dim(flat, lax.axis_index("batch"), 0, keepdims=False)
    sums, start = [], 0
    for member in vectors:
        sums.append(flat[start : start + member.shape[0] // blocks])
        start += member.shape[0] // blocks
    return (
        output,
        late_out[1],
        jnp.stack([jnp.stack([sums[0], sums[1]]), jnp.stack([sums[8], sums[9]])]),
        jnp.stack([jnp.stack([sums[2], sums[3]]), jnp.stack([sums[10], sums[11]])]),
        jnp.stack([late_out[0], inner_out[4]]),
        jnp.stack([sums[4], sums[12]]),
        jnp.stack([early_out[2], inner_out[3]]),
        jnp.stack([sums[5], sums[13]]),
        jnp.stack([early_out[1], inner_out[1]]),
        jnp.stack([sums[6], sums[14]]),
        jnp.stack([early_out[0], inner_out[0]]),
        jnp.stack([sums[7], sums[15]]),
        pool_out[0],
        sums[16],
        inner_out[2],
        sums[17],
    )


def solution(mesh):
    whole = P()
    return jax.shard_map(
        local,
        mesh=mesh,
        in_specs=(P("batch", "seq"),) + (whole,) * 15 + (P("batch", "seq", None),),
        out_specs=(
            P("batch", "seq", None),
            P("batch", None),
            P(None, None, "batch"),
            P(None, None, "batch"),
            P(None, "batch", None),
            P(None, "batch"),
            P(None, "batch", None),
            P(None, "batch"),
            P(None, "batch", None),
            P(None, "batch"),
            P(None, "batch", None),
            P(None, "batch"),
            P("batch", None),
            P("batch"),
            P("batch", None),
            P("batch"),
        ),
        check_vma=False,
    )
```
